32 devices in a mesh: fsdp: 4 (over x, core), ctx: 4 (over z), tp: 2 (over y).
Axes of the slice: x: 2, y: 2, z: 4, core: 2. Of those that a mesh axis runs over, the one named last changes fastest.
Arguments:
- tokens: bfloat16 [4096, 2048], P(('fsdp', 'ctx')), may hold values from -7 to 7
- cotangent: bfloat16 [4096, 2048], P(('fsdp', 'ctx')), may hold values from -6 to 6
- attn_routes: int32 [4096, 2], P(('fsdp', 'ctx')), may hold values from 0 to 3, as said below
- ffn_routes: int32 [4096, 2], P(('fsdp', 'ctx')), may hold values from 0 to 3, as said below
- norm_gain1: float32 [2048], replicated, may hold values from 0.1 to 1.9
- norm_gain2: float32 [2048], replicated, may hold values from 0.1 to 1.9
- attn_router: bfloat16 [2048, 4], replicated, may hold values from -1 to 1
- ffn_router: bfloat16 [2048, 4], replicated, may hold values from -1 to 1
- key_proj: bfloat16 [2048, 2048], P(('fsdp', 'ctx'), 'tp'), may hold values from -0.125 to 0.125
- value_proj: bfloat16 [2048, 2048], P(('fsdp', 'ctx'), 'tp'), may hold values from -0.125 to 0.125
- query_proj: bfloat16 [4, 2048, 2048], P('ctx', 'fsdp', 'tp'), may hold values from -0.125 to 0.125
- out_proj: bfloat16 [4, 2048, 2048], P('ctx', 'tp', 'fsdp'), may hold values from -0.5 to 0.5
- gate_proj: bfloat16 [4, 2048, 5632], P('ctx', 'fsdp', 'tp'), may hold values from -0.125 to 0.125
- up_proj: bfloat16 [4, 2048, 5632], P('ctx', 'fsdp', 'tp'), may hold values from -0.125 to 0.125
- down_proj: bfloat16 [4, 5632, 2048], P('ctx', 'tp', 'fsdp'), may hold values from -0.078125 to 0.078125
Outputs:
- output: bfloat16 [4096, 2048], P(('fsdp', 'ctx'))
- input_grad: float32 [4096, 2048], P(('fsdp', 'ctx'))
- attn_loss: float32 [], replicated
- ffn_loss: float32 [], replicated
- gain1_grad: float32 [2048], replicated
- gain2_grad: float32 [2048], replicated
- attn_router_grad: float32 [2048, 4], replicated
- ffn_router_grad: float32 [2048, 4], replicated
- key_grad: float32 [2048, 2048], P(('fsdp', 'ctx'), 'tp')
- value_grad: float32 [2048, 2048], P(('fsdp', 'ctx'), 'tp')
- query_grad: float32 [4, 2048, 2048], P('ctx', 'fsdp', 'tp')
- out_proj_grad: float32 [4, 2048, 2048], P('ctx', 'tp', 'fsdp')
- gate_grad: float32 [4, 2048, 5632], P('ctx', 'fsdp', 'tp')
- up_grad: float32 [4, 2048, 5632], P('ctx', 'fsdp', 'tp')
- down_grad: float32 [4, 5632, 2048], P('ctx', 'tp', 'fsdp')
The draws below stay inside these ranges and needn't reach their ends.
Inputs may be any that keep to these rules, and one draw needn't show every extreme that they name: `attn_routes`: each row names 2 different attention experts; in each aligned block of 256 rows (the rows of one device) no expert is named more than 160 times, and some expert exactly 160 times; every expert is named by some row. `ffn_routes`: each row names 2 different feed-forward experts; in each aligned block of 256 rows (the rows of one device) no expert is named more than 160 times, and some expert exactly 160 times; every expert is named by some row.
All inputs are finite; a program needn't handle non-finite values.
Results may differ from the reference program's by a relative error of at most 0.023.
Values may be sent and summed in bfloat16 or wider, within the bound.
A program may use at most 256 MiB of HBM per device.

```python
import math
import jax
import jax.numpy as jnp
from jax import lax

D = 2048
HEADS = 16
HEAD = 128
FF = 5632
TOP = 2
BLOCK = 256
TOK_DEV = 256
EXPERTS = 4
HD = 2048
CAP = 160
SEQ = 1024
SEQS = 4
TOKENS = 4096


def route_table_draw(key):
    block_count = TOKENS // TOK_DEV
    pair_count = TOP * TOK_DEV
    hot_count = min(EXPERTS - 2, (pair_count - 2) // CAP)
    cold_count = EXPERTS - hot_count
    cold_total = pair_count - hot_count * CAP
    cold_base = cold_total // cold_count
    cold_extra = cold_total % cold_count
    key_shift, key_order, key_roll = jax.random.split(key, 3)
    shift = jax.random.randint(key_shift, (), 0, EXPERTS, dtype=jnp.int32)
    blocks = jnp.arange(block_count, dtype=jnp.int32)
    starts = (blocks * EXPERTS // block_count + shift) % EXPERTS
    ranks = (jnp.arange(EXPERTS, dtype=jnp.int32)[None, :] - starts[:, None]) % EXPERTS
    counts = jnp.where(ranks < hot_count, CAP, cold_base + (ranks - hot_count < cold_extra).astype(jnp.int32))
    ends = jnp.cumsum(counts, axis=1)
    positions = jnp.arange(pair_count, dtype=jnp.int32)
    labels = jnp.sum((positions[None, :, None] >= ends[:, None, :]).astype(jnp.int32), axis=2)
    table = jnp.transpose(labels.reshape(block_count, TOP, TOK_DEV), (0, 2, 1))
    scores = jax.random.randint(key_order, (block_count, TOK_DEV), 0, 1 << 16, dtype=jnp.int32) * TOK_DEV + jnp.arange(TOK_DEV, dtype=jnp.int32)[None, :]
    order = jnp.argsort(scores, axis=1, stable=True).astype(jnp.int32)
    table = jnp.take_along_axis(table, order[:, :, None], axis=1)
    roll = jax.random.randint(key_roll, (block_count, TOK_DEV, 1), 0, TOP, dtype=jnp.int32)
    columns = (jnp.arange(TOP, dtype=jnp.int32)[None, None, :] + roll) % TOP
    table = jnp.take_along_axis(table, columns, axis=2)
    return table.reshape(TOKENS, TOP).astype(jnp.int32)


def common_vector(key):
    base = jax.random.normal(jax.random.fold_in(key, 5), (D,), jnp.float32)
    return 0.4 * jnp.clip(base, -3.0, 3.0)


def column_scales(key):
    return jnp.exp(jax.random.uniform(key, (EXPERTS,), jnp.float32, math.log(0.5), math.log(1.5)))


def column_offsets(key):
    levels = jnp.linspace(-1.0, 1.0, EXPERTS).astype(jnp.float32)
    return jax.random.permutation(key, levels)


def scaled_router(base, scales, shared, offsets):
    length_sq = jnp.sum(shared * shared) / (1.0 + jnp.mean(shared * shared))
    along = shared[:, None] * offsets[None, :] * jnp.sqrt(1.0 + jnp.mean(shared * shared)) / length_sq
    return jnp.clip(base * scales[None, :] / math.sqrt(D) + along, -1.0, 1.0).astype(jnp.float32)


def draw_tokens(key, part):
    shared = common_vector(key)
    key = jax.random.fold_in(key, 53)
    base = jnp.clip(jax.random.normal(key, (TOKENS, D), jnp.float32), -5.0, 5.0)
    return (base + shared[None, :]).astype(jnp.bfloat16)


def draw_attn_routes(key, part):
    key = jax.random.fold_in(key, 11)
    return route_table_draw(key)


def draw_ffn_routes(key, part):
    key = jax.random.fold_in(key, 23)
    return route_table_draw(key)


def draw_attn_router(key, part):
    shared = common_vector(key)
    key = jax.random.fold_in(key, 37)
    key_scale, key_base, key_shift = jax.random.split(key, 3)
    base = jnp.clip(jax.random.normal(key_base, (D, EXPERTS), jnp.float32), -4.0, 4.0)
    return scaled_router(base, column_scales(key_scale), shared, column_offsets(key_shift)).astype(jnp.bfloat16)


def draw_ffn_router(key, part):
    shared = common_vector(key)
    key = jax.random.fold_in(key, 41)
    key_scale, key_base, key_shift = jax.random.split(key, 3)
    base = jnp.clip(jax.random.normal(key_base, (D, EXPERTS), jnp.float32), -4.0, 4.0)
    return scaled_router(base, column_scales(key_scale), shared, column_offsets(key_shift)).astype(jnp.bfloat16)


def level_of(rng, extent, cuts, low, top_value):
    def one(position, blocks):
        steps = jax.random.uniform(jax.random.fold_in(jax.random.fold_in(rng, 6), position), (blocks,), jnp.float32, low / len(cuts), top_value / len(cuts))
        return jnp.repeat(jnp.exp(steps), extent[position] // blocks).reshape((-1,) + (1,) * (len(extent) - position - 1))

    loudness = one(*cuts[0])
    for cut in cuts[1:]:
        loudness = loudness * one(*cut)
    return loudness


def noise(own_key, extent, scale, limit, shards=(), kind=jnp.bfloat16):
    array = jax.random.normal(own_key, extent, jnp.float32) * scale
    if len(shards) > 0:
        array = level_of(own_key, extent, shards, -0.22, 0.18) * array
    return jnp.clip(array, min=-limit, max=limit).astype(kind)


def setup_inputs(seed: int = 0) -> dict:
    arg_keys = jax.random.split(jax.random.key(seed), 16)
    return {
        "tokens": draw_tokens(jax.random.fold_in(arg_keys[15], 71), 0),
        "cotangent": noise(arg_keys[1], (TOKENS, D), 1.0, 6.0, ((0, 16),)),
        "attn_routes": draw_attn_routes(jax.random.fold_in(arg_keys[15], 71), 0),
        "ffn_routes": draw_ffn_routes(jax.random.fold_in(arg_keys[15], 71), 0),
        "norm_gain1": jnp.clip(1.0 + 0.18 * jax.random.normal(arg_keys[4], (D,), jnp.float32), 0.1, 1.9),
        "norm_gain2": jnp.clip(1.0 + 0.18 * jax.random.normal(arg_keys[5], (D,), jnp.float32), 0.1, 1.9),
        "attn_router": draw_attn_router(jax.random.fold_in(arg_keys[15], 71), 0),
        "ffn_router": draw_ffn_router(jax.random.fold_in(arg_keys[15], 71), 0),
        "key_proj": noise(arg_keys[8], (D, HD), D ** -0.5, 0.125, ((0, 16), (1, 2))),
        "value_proj": noise(arg_keys[9], (D, HD), D ** -0.5, 0.125, ((0, 16), (1, 2))),
        "query_proj": noise(arg_keys[10], (EXPERTS, D, HD), D ** -0.5, 0.125, ((0, 4), (1, 4), (2, 2))),
        "out_proj": noise(arg_keys[11], (EXPERTS, HD, D), (HD // 16) ** -0.5, 0.5, ((0, 4), (1, 2), (2, 4))),
        "gate_proj": noise(arg_keys[12], (EXPERTS, D, FF), D ** -0.5, 0.125, ((0, 4), (1, 4), (2, 2))),
        "up_proj": noise(arg_keys[13], (EXPERTS, D, FF), D ** -0.5, 0.125, ((0, 4), (1, 4), (2, 2))),
        "down_proj": noise(arg_keys[14], (EXPERTS, FF, D), FF ** -0.5, 0.078125, ((0, 4), (1, 2), (2, 4))),
    }


EPSILON = 1e-06
ROPE_BASE = 10000.0
AUX_WEIGHT = 0.1
MASKED = -1e+30
PRECISE = lax.Precision.HIGHEST

@jax.custom_vjp
def low(v):
    return lax.optimization_barrier(v.astype(jnp.bfloat16)).astype(jnp.float32)

@jax.custom_vjp
def low_back(v):
    return v

def low_keep(v):
    return (low(v), None)

def low_pass(kept, grad):
    return (grad,)

def back_keep(v):
    return (v, None)

def back_low(kept, grad):
    return (low(grad),)
low.defvjp(low_keep, low_pass)
low_back.defvjp(back_keep, back_low)

def dense(lhs_mat, rhs_mat):
    return jnp.dot(lhs_mat, rhs_mat, precision=PRECISE)

def rms_norm(values, gain_vec):
    return values * lax.rsqrt(lax.optimization_barrier(jnp.mean(values * values, axis=-1, keepdims=True)) + EPSILON) * gain_vec

def rotate(values, places):
    half_head = HEAD // 2
    frequency = ROPE_BASE ** (-jnp.arange(half_head, dtype=jnp.float32) * 2.0 / HEAD)
    angles = places.astype(jnp.float32)[:, None] * frequency[None, :]
    cos_table = jnp.cos(angles)[:, None, :]
    sin_table = jnp.sin(angles)[:, None, :]
    pieces = values.reshape(values.shape[0], -1, HEAD)
    first_half = pieces[..., :half_head]
    second = pieces[..., half_head:]
    turned = jnp.concatenate([first_half * cos_table - second * sin_table, second * cos_table + first_half * sin_table], axis=-1)
    return turned.reshape(values.shape)

def mixing(logits, routes):
    chosen = jnp.take_along_axis(logits, routes, axis=1)
    gate_mix = jax.nn.softmax(chosen, axis=-1)
    picked = (routes[:, :, None] == jnp.arange(EXPERTS, dtype=jnp.int32)[None, None, :]).astype(jnp.float32)
    return lax.optimization_barrier(jnp.sum(gate_mix[:, :, None] * picked, axis=1))

def balance(logits, routes):
    probs_all = jax.nn.softmax(logits, axis=-1)
    counts = lax.optimization_barrier(jnp.sum((routes[:, :, None] == jnp.arange(EXPERTS, dtype=jnp.int32)[None, None, :]).astype(jnp.float32), axis=(0, 1)))
    return EXPERTS * jnp.sum(counts / (TOKENS * TOP) * lax.optimization_barrier(jnp.mean(probs_all, axis=0)))

def attend(a_seq, mix_seq, key_w, value_w, query_w, output_w):
    places = jnp.arange(SEQ, dtype=jnp.int32)
    keys_seq = low(rotate(low_back(dense(a_seq, key_w)), places)).reshape(SEQ, HEADS, HEAD)
    values_seq = low(low_back(dense(a_seq, value_w))).reshape(SEQ, HEADS, HEAD)
    blocks_seq = places // BLOCK
    allowed = blocks_seq[None, :] <= blocks_seq[:, None]

    def one_expert(running, expert):
        a_copy = low_back(a_seq)
        queries = low(rotate(low_back(dense(a_copy, query_w[expert])), places)).reshape(SEQ, HEADS, HEAD)
        raw_scores = low_back(jnp.einsum('qhd,khd->hqk', queries, keys_seq, precision=PRECISE) / math.sqrt(HEAD))
        scores = jnp.where(allowed[None, :, :], raw_scores, MASKED)
        weights = low(jax.nn.softmax(scores, axis=-1))
        heads_out = jnp.einsum('hqk,khd->qhd', weights, values_seq, precision=PRECISE).reshape(SEQ, HD)
        expert_out = low(low_back(dense(low(low_back(heads_out)), output_w[expert])))
        return (running + mix_seq[:, expert][:, None] * expert_out, None)
    running, unused = lax.scan(jax.checkpoint(one_expert), jnp.zeros((SEQ, D), jnp.float32), jnp.arange(EXPERTS, dtype=jnp.int32))
    return running

def feed_forward(b_low, mix_ffn, gate_w, up_w, down_w):

    def one_expert(running, expert):
        b_copy = low_back(b_low)
        gate_act = low_back(dense(b_copy, gate_w[expert]))
        up_act = low_back(dense(b_copy, up_w[expert]))
        hidden = low(jax.nn.silu(gate_act) * up_act)
        expert_out = low(low_back(dense(hidden, down_w[expert])))
        return (running + mix_ffn[:, expert][:, None] * expert_out, None)
    running, unused = lax.scan(jax.checkpoint(one_expert), jnp.zeros((TOKENS, D), jnp.float32), jnp.arange(EXPERTS, dtype=jnp.int32))
    return running

def forward(params, routes_attn, routes_ffn):
    inputs, gain_one, gain_two, router_attn, router_ffn, key_w, value_w, query_w, output_w, gate_w, up_w, down_w = params
    a_low = low(rms_norm(inputs, gain_one))
    logits_attn = dense(a_low, router_attn)
    mix_attn = mixing(logits_attn, routes_attn)

    def attend_pair(pieces):
        return attend(pieces[0], pieces[1], key_w, value_w, query_w, output_w)
    attn_out = lax.map(attend_pair, (a_low.reshape(SEQS, SEQ, D), mix_attn.reshape(SEQS, SEQ, EXPERTS))).reshape(TOKENS, D)
    attended = inputs + attn_out
    b_low = low(rms_norm(attended, gain_two))
    logits_ffn = dense(b_low, router_ffn)
    mix_ffn = mixing(logits_ffn, routes_ffn)
    result = attended + feed_forward(b_low, mix_ffn, gate_w, up_w, down_w)
    return (result, balance(logits_attn, routes_attn), balance(logits_ffn, routes_ffn))

def reference(tokens, cotangent, attn_routes, ffn_routes, norm_gain1, norm_gain2, attn_router, ffn_router, key_proj, value_proj, query_proj, out_proj, gate_proj, up_proj, down_proj):
    params = tuple((item.astype(jnp.float32) for item in (tokens, norm_gain1, norm_gain2, attn_router, ffn_router, key_proj, value_proj, query_proj, out_proj, gate_proj, up_proj, down_proj)))

    def objective(*params_in):
        return forward(params_in, attn_routes, ffn_routes)
    (result, attn_loss, ffn_loss), pullback = jax.vjp(objective, *params)
    weight_in = jnp.asarray(AUX_WEIGHT, jnp.float32)
    grads = pullback((cotangent.astype(jnp.float32), weight_in, weight_in))
    return (result.astype(jnp.bfloat16), grads[0], attn_loss, ffn_loss, grads[1], grads[2], grads[3], grads[4], grads[5], grads[6], grads[7], grads[8], grads[9], grads[10], grads[11])
```

```python
import functools
import math

import jax
import jax.numpy as jnp
from jax import lax
from jax.experimental import pallas as pl
from jax.experimental.pallas import tpu as pltpu
from jax.sharding import PartitionSpec as P

HEAD = 128
EPSILON = 1e-06
ROPE_BASE = 10000.0
AUX_WEIGHT = 0.1
PRECISE = lax.Precision.HIGHEST
LOW = jnp.bfloat16
FULL = jnp.float32
VMEM_BYTES = 56 * 1024 * 1024


def matmul(lhs, rhs):
    return jnp.dot(lhs, rhs, preferred_element_type=FULL)


def matmul_tn(lhs, rhs):
    return lax.dot_general(lhs, rhs, (((0,), (0,)), ((), ())), preferred_element_type=FULL)


def matmul_nt(lhs, rhs):
    return lax.dot_general(lhs, rhs, (((1,), (1,)), ((), ())), preferred_element_type=FULL)


def precise_tn(lhs, rhs):
    return lax.dot_general(lhs, rhs, (((0,), (0,)), ((), ())), precision=PRECISE)


def swap(value, axis, distance):
    size = lax.axis_size(axis)
    return lax.ppermute(value, axis, [(i, i ^ distance) for i in range(size)])


def after(value, *earlier):
    return lax.optimization_barrier((value,) + earlier)[0]


def bits_down(size):
    bit = size // 2
    while bit >= 1:
        yield bit
        bit //= 2


def spread_order(size):
    order = [0]
    for bit in bits_down(size):
        order = order + [place | bit for place in order]
    return order


def gather_pieces(piece):
    pieces = [piece]
    for bit in bits_down(lax.axis_size("fsdp")):
        pieces = pieces + [swap(item, "fsdp", bit) for item in pieces]
    return pieces


def flip_blocks(value, axis, index, count):
    shape = value.shape
    width = shape[axis] // count
    for bit in bits_down(count):
        outer = shape[axis] // (2 * bit * width)
        split = value.reshape(shape[:axis] + (outer, 2, bit * width) + shape[axis + 1 :])
        turned = jnp.flip(split, axis + 1).reshape(shape)
        value = jnp.where((index // bit) % 2 == 1, turned, value)
    return value


def to_spread(value, axis):
    size = lax.axis_size("fsdp")
    value = flip_blocks(value, axis, lax.axis_index("fsdp"), size)
    parts = jnp.split(value, size, axis)
    return jnp.concatenate([parts[place] for place in spread_order(size)], axis)


def from_spread(value, axis):
    size = lax.axis_size("fsdp")
    parts = jnp.split(value, size, axis)
    order = spread_order(size)
    value = jnp.concatenate([parts[order.index(place)] for place in range(size)], axis)
    return flip_blocks(value, axis, lax.axis_index("fsdp"), size)


def my_half(value):
    width = value.shape[-1] // 2
    return jnp.where(lax.axis_index("tp") == 0, value[..., :width], value[..., width:])


def other_half(value):
    width = value.shape[-1] // 2
    return jnp.where(lax.axis_index("tp") == 0, value[..., width:], value[..., :width])


def join_halves(mine, other):
    first = lax.axis_index("tp") == 0
    return jnp.concatenate([jnp.where(first, mine, other), jnp.where(first, other, mine)], -1)


def tp_sum(value):
    return value + swap(value, "tp", 1)


def all_sum(value, axes):
    for axis in axes:
        for bit in bits_down(lax.axis_size(axis)):
            value = value + swap(value, axis, bit)
    return value


def far_first(size):
    return list(range(size // 2, size)) + list(range(size // 2 - 1, -1, -1))


def place_blocks(blocks):
    index = lax.axis_index("ctx")
    rows = blocks[0].shape[0]
    total = jnp.zeros((rows * len(blocks),) + blocks[0].shape[1:], blocks[0].dtype)
    for distance, block in enumerate(blocks):
        total = lax.dynamic_update_slice_in_dim(total, block, (index ^ distance) * rows, 0)
    return total


def block_for(value, distance):
    size = lax.axis_size("ctx")
    rows = value.shape[0] // size
    return lax.dynamic_slice_in_dim(value, (lax.axis_index("ctx") ^ distance) * rows, rows, 0)


def send_out(half_rows):
    size = lax.axis_size("ctx")
    blocks = [None] * size
    for distance in far_first(size):
        block = block_for(half_rows, distance)
        if distance:
            block = swap(block, "ctx", distance)
        blocks[distance] = join_halves(block, swap(block, "tp", 1))
    return place_blocks(blocks)


def send_home(partial_rows):
    size = lax.axis_size("ctx")
    blocks = [None] * size
    for distance in far_first(size):
        block = block_for(partial_rows, distance)
        arrived = swap(other_half(block).astype(LOW), "tp", 1)
        block = (my_half(block).astype(FULL) + arrived.astype(FULL)).astype(LOW)
        if distance:
            block = swap(block, "ctx", distance)
        blocks[distance] = block
    return blocks


def scatter_sum(keep, send, first_dim):
    size = lax.axis_size("fsdp")
    bit = 1
    while True:
        total = keep + swap(send, "fsdp", bit).astype(FULL)
        bit *= 2
        if bit >= size:
            return total
        width = total.shape[first_dim] // 2
        keep = lax.slice_in_dim(total, 0, width, axis=first_dim)
        send = lax.slice_in_dim(total, width, 2 * width, axis=first_dim).astype(LOW)


def turn_tables(places):
    half_head = HEAD // 2
    frequency = ROPE_BASE ** (-jnp.arange(half_head, dtype=FULL) * 2.0 / HEAD)
    angles = places.astype(FULL)[:, None] * frequency[None, :]
    cosine, sine = jnp.cos(angles), jnp.sin(angles)
    return jnp.concatenate([cosine, cosine, -sine, sine], axis=1)


def turn(value, table):
    return value * table[:, :HEAD] + pltpu.roll(value, HEAD // 2, 1) * table[:, HEAD:]


def turn_back(value, table):
    return value * table[:, :HEAD] - pltpu.roll(value, HEAD // 2, 1) * table[:, HEAD:]


def attend_kernel(
    groups, scale, q_lin, k_lin, v_lin, q_table, k_table, q_low, k_low, v_low, heads, log_sum
):
    q_low[...] = turn(q_lin[...], q_table[...]).astype(LOW)
    k_low[...] = turn(k_lin[...], k_table[...]).astype(LOW)
    v_low[...] = v_lin[...].astype(LOW)
    rows = q_low.shape[0] // groups
    block = k_low.shape[0] // groups
    for group in range(groups):
        span = slice(group * rows, (group + 1) * rows)
        seen = slice(0, (group + 1) * block)
        scores = matmul_nt(q_low[span, :], k_low[seen, :]) * scale
        top = jnp.max(scores, axis=1, keepdims=True)
        weights = jnp.exp(scores - top)
        total = jnp.sum(weights, axis=1, keepdims=True)
        weights = (weights * (1.0 / total)).astype(LOW)
        heads[span, :] = matmul(weights, v_low[seen, :]).astype(LOW)
        log_sum[span, :] = jnp.broadcast_to(top + jnp.log(total), (rows, HEAD))


def attend(query_lin, kv_lin, query_table, key_table, groups):
    slots, width = query_lin.shape
    length = kv_lin.shape[0]
    count = width // HEAD
    by_head = lambda rows: pl.BlockSpec((rows, HEAD), lambda h: (0, h))
    whole = lambda rows: pl.BlockSpec((rows, 2 * HEAD), lambda h: (0, 0))
    return pl.pallas_call(
        functools.partial(attend_kernel, groups, 1.0 / math.sqrt(HEAD)),
        grid=(count,),
        in_specs=[
            by_head(slots),
            by_head(length),
            pl.BlockSpec((length, HEAD), lambda h: (0, h + count)),
            whole(slots),
            whole(length),
        ],
        out_specs=[by_head(slots), by_head(length), by_head(length), by_head(slots), by_head(slots)],
        out_shape=[
            jax.ShapeDtypeStruct((slots, width), LOW),
            jax.ShapeDtypeStruct((length, width), LOW),
            jax.ShapeDtypeStruct((length, width), LOW),
            jax.ShapeDtypeStruct((slots, width), LOW),
            jax.ShapeDtypeStruct((slots, width), FULL),
        ],
        compiler_params=pltpu.CompilerParams(vmem_limit_bytes=VMEM_BYTES),
        cost_estimate=pl.CostEstimate(
            flops=3 * slots * length * width,
            bytes_accessed=20 * length * width,
            transcendentals=slots * length * count,
        ),
    )(query_lin, kv_lin, kv_lin, query_table, key_table)


def attend_back_kernel(
    groups, scale, q_low, k_low, v_low, d_heads, log_sum, q_table, k_table, dq, dk, dv, dk_sum, dv_sum
):
    dk_sum[...] = jnp.zeros_like(dk_sum)
    dv_sum[...] = jnp.zeros_like(dv_sum)
    rows = q_low.shape[0] // groups
    block = k_low.shape[0] // groups
    for group in range(groups):
        span = slice(group * rows, (group + 1) * rows)
        seen = slice(0, (group + 1) * block)
        query, keys = q_low[span, :], k_low[seen, :]
        grads = d_heads[span, :]
        scores = matmul_nt(query, keys) * scale
        weights = jnp.exp(scores - log_sum[span, :1])
        d_weights = matmul_nt(grads, v_low[seen, :])
        delta = jnp.sum(weights * d_weights, axis=1, keepdims=True)
        d_scores = (weights * (d_weights - delta)).astype(LOW)
        dq[span, :] = turn_back(matmul(d_scores, keys) * scale, q_table[span, :]).astype(LOW)
        dk_sum[seen, :] += matmul_tn(d_scores, query) * scale
        dv_sum[seen, :] += matmul_tn(weights.astype(LOW), grads)
    dk[...] = turn_back(dk_sum[...], k_table[...]).astype(LOW)
    dv[...] = dv_sum[...].astype(LOW)


def attend_back(q_low, k_low, v_low, d_heads, log_sum, query_table, key_table, groups):
    slots, width = q_low.shape
    length = k_low.shape[0]
    count = width // HEAD
    by_head = lambda rows: pl.BlockSpec((rows, HEAD), lambda h: (0, h))
    whole = lambda rows: pl.BlockSpec((rows, 2 * HEAD), lambda h: (0, 0))
    return pl.pallas_call(
        functools.partial(attend_back_kernel, groups, 1.0 / math.sqrt(HEAD)),
        grid=(count,),
        in_specs=[
            by_head(slots),
            by_head(length),
            by_head(length),
            by_head(slots),
            by_head(slots),
            whole(slots),
            whole(length),
        ],
        out_specs=[by_head(slots), by_head(length), by_head(length)],
        out_shape=[
            jax.ShapeDtypeStruct((slots, width), LOW),
            jax.ShapeDtypeStruct((length, width), LOW),
            jax.ShapeDtypeStruct((length, width), LOW),
        ],
        scratch_shapes=[pltpu.VMEM((length, HEAD), FULL), pltpu.VMEM((length, HEAD), FULL)],
        compiler_params=pltpu.CompilerParams(vmem_limit_bytes=VMEM_BYTES),
        cost_estimate=pl.CostEstimate(
            flops=7 * slots * length * width,
            bytes_accessed=14 * length * width,
            transcendentals=slots * length * count,
        ),
    )(q_low, k_low, v_low, d_heads, log_sum, query_table, key_table)


def chosen_picks(routes, expert_count, capacity):
    experts = jnp.arange(expert_count, dtype=jnp.int32)
    onehot = (routes[:, :, None] == experts[None, None, :]).astype(jnp.int32)
    order = jnp.cumsum(jnp.sum(onehot, axis=1), axis=0) - 1
    slot = routes * capacity + jnp.sum(onehot * order[:, None, :], axis=2)
    slots = jnp.arange(expert_count * capacity, dtype=jnp.int32)
    picks = [(slot[:, k : k + 1] == slots[None, :]).astype(LOW) for k in range(routes.shape[1])]
    return picks, onehot.astype(FULL)


def expert_picks(routes_seq, expert, capacity):
    named = jnp.any(routes_seq == expert, axis=1)
    order = jnp.cumsum(named.astype(jnp.int32), axis=1) - 1
    slot = jnp.where(named, order, -1)
    return (slot[:, None, :] == jnp.arange(capacity, dtype=jnp.int32)[None, :, None]).astype(LOW)


def mix_of(logits, onehot):
    chosen = jnp.sum(onehot * logits[:, None, :], axis=2)
    return jax.nn.softmax(chosen, axis=1)


def logits_back(mix, mix_grad, probs, onehot, share_grad):
    d_chosen = mix * (mix_grad - jnp.sum(mix * mix_grad, axis=1, keepdims=True))
    d_logits = jnp.sum(onehot * d_chosen[:, :, None], axis=1)
    inner = jnp.sum(probs * share_grad[None, :], axis=1, keepdims=True)
    return d_logits + probs * (share_grad[None, :] - inner)


def through_router(d_logits, router_half):
    total = d_logits[:, 0:1] * router_half[:, 0][None, :]
    for expert in range(1, d_logits.shape[1]):
        total = total + d_logits[:, expert : expert + 1] * router_half[:, expert][None, :]
    return total


def on_device(
    tokens,
    cotangent,
    attn_routes,
    ffn_routes,
    norm_gain1,
    norm_gain2,
    attn_router,
    ffn_router,
    key_proj,
    value_proj,
    query_proj,
    out_proj,
    gate_proj,
    up_proj,
    down_proj,
):
    rows_here, features = tokens.shape
    half_width = features // 2
    picks_each = attn_routes.shape[1]
    expert_count = attn_router.shape[1]
    groups = lax.axis_size("ctx")
    mine = lax.axis_index("ctx")
    capacity = rows_here * picks_each // expert_count * 5 // 4
    slots = groups * capacity
    all_tokens = rows_here * lax.axis_size("fsdp") * groups
    distances = far_first(groups)

    query_pieces = gather_pieces(query_proj[0])
    out_pieces = gather_pieces(out_proj[0])

    tokens_spread = to_spread(tokens, 1)
    token_half = my_half(tokens_spread)
    routes_mine = jnp.concatenate([attn_routes, ffn_routes], axis=1).T[None]
    kv_mine = jnp.concatenate([key_proj, value_proj], axis=1)
    token_blocks, route_blocks, kv_blocks = [None] * groups, [None] * groups, [None] * groups
    for distance in distances:
        if distance == 0:
            token_blocks[0], route_blocks[0], kv_blocks[0] = tokens_spread, routes_mine, kv_mine
            continue
        route_blocks[distance] = swap(routes_mine, "ctx", distance)
        token_blocks[distance] = swap(token_half, "ctx", distance)
        kv_blocks[distance] = swap(kv_mine, "ctx", distance)
    for distance in distances:
        if distance:
            token_blocks[distance] = join_halves(
                token_blocks[distance], swap(token_blocks[distance], "tp", 1)
            )
    seq_tokens = place_blocks(token_blocks).astype(FULL)
    seq_routes = place_blocks(route_blocks)
    kv_group = place_blocks(kv_blocks)
    kv_pieces = gather_pieces(kv_group)
    kv_full = jnp.concatenate(kv_pieces, axis=0)
    query_full = jnp.concatenate(query_pieces, axis=0)
    out_full = jnp.concatenate(out_pieces, axis=1)

    gate_pieces = gather_pieces(after(gate_proj[0], kv_group))
    up_pieces = gather_pieces(after(up_proj[0], kv_group, gate_pieces[0]))
    down_pieces = gather_pieces(after(down_proj[0], kv_group, up_pieces[0]))

    gain1 = to_spread(norm_gain1, 0)
    gain2_half = my_half(to_spread(norm_gain2, 0))
    router1 = to_spread(attn_router, 0)
    router2 = to_spread(ffn_router, 0)
    router1_half = my_half(router1.T).T.astype(FULL)
    router2_half = my_half(router2.T).T

    scale_seq = lax.rsqrt(jnp.mean(seq_tokens * seq_tokens, axis=1, keepdims=True) + EPSILON)
    a_seq = (seq_tokens * scale_seq * gain1).astype(LOW)
    a_mine = lax.dynamic_slice_in_dim(a_seq, mine * rows_here, rows_here, 0)
    scale_one = lax.dynamic_slice_in_dim(scale_seq, mine * rows_here, rows_here, 0)
    attn_logits = matmul(a_mine, router1)
    attn_probs = jax.nn.softmax(attn_logits, axis=1)
    attn_picks, attn_onehot = chosen_picks(attn_routes, expert_count, capacity)
    ffn_picks, ffn_onehot = chosen_picks(ffn_routes, expert_count, capacity)
    attn_mix = mix_of(attn_logits, attn_onehot)

    expert_onehot = expert_picks(seq_routes[:, :picks_each], mine, capacity)
    key_table = turn_tables(jnp.arange(groups * rows_here, dtype=jnp.int32))
    query_table = jnp.einsum(
        "bsr,brh->bsh",
        expert_onehot.astype(FULL),
        key_table.reshape(groups, rows_here, -1),
        precision=PRECISE,
    ).reshape(slots, -1)
    rows_in = (
        jnp.einsum(
            "bsr,brd->bsd",
            expert_onehot,
            a_seq.reshape(groups, rows_here, features),
            preferred_element_type=FULL,
        )
        .astype(LOW)
        .reshape(slots, features)
    )
    query_lin = matmul(rows_in, query_full)
    kv_lin = matmul(a_seq, kv_full)
    q_low, k_low, v_low, heads_low, log_sum = attend(
        query_lin, kv_lin, query_table, key_table, groups
    )
    attn_blocks = send_home(matmul(heads_low, out_full))
    attn_back = place_blocks(attn_blocks)

    cot_half = my_half(to_spread(cotangent, 1))
    ffn_pick = ffn_picks[0]
    for pick in ffn_picks[1:]:
        ffn_pick = ffn_pick + pick
    cot_rows = send_out(after(matmul_tn(ffn_pick, cot_half).astype(LOW), kv_group))

    input_half = my_half(tokens_spread).astype(FULL)
    attn_picked = [matmul(pick, attn_back) for pick in attn_picks]
    attended = input_half
    for k in range(picks_each):
        attended = attended + attn_mix[:, k : k + 1] * attn_picked[k]
    square_sum = tp_sum(jnp.sum(attended * attended, axis=1, keepdims=True))
    scale_two = lax.rsqrt(square_sum / features + EPSILON)
    b_half = (attended * scale_two * gain2_half).astype(LOW)
    ffn_rows = send_out(matmul_tn(ffn_pick, b_half).astype(LOW))
    ffn_logits = tp_sum(matmul(b_half, router2_half))
    ffn_probs = jax.nn.softmax(ffn_logits, axis=1)
    ffn_mix = mix_of(ffn_logits, ffn_onehot)
    mix_slots = jnp.zeros((slots,), FULL)
    for k in range(picks_each):
        mix_slots = mix_slots + jnp.sum(ffn_picks[k].astype(FULL) * ffn_mix[:, k : k + 1], axis=0)
    mix_slots = mix_slots.reshape(groups, 1, capacity)
    mix_rows = place_blocks(
        [
            swap(block_for(mix_slots, distance), "ctx", distance) if distance else block_for(mix_slots, 0)
            for distance in range(groups)
        ]
    ).reshape(slots, 1)

    gate_full = jnp.concatenate(gate_pieces, axis=0)
    up_full = jnp.concatenate(up_pieces, axis=0)
    down_full = jnp.concatenate(down_pieces, axis=1)
    gate_lin = matmul(ffn_rows, gate_full)
    up_lin = matmul(ffn_rows, up_full)
    sigmoid_gate = jax.nn.sigmoid(gate_lin)
    hidden = gate_lin * sigmoid_gate * up_lin
    hidden_low = hidden.astype(LOW)
    d_hidden = matmul_nt(cot_rows, down_full)
    mix_grad_rows = jnp.sum(hidden * d_hidden, axis=1)
    d_gated = d_hidden * mix_rows
    d_gate_low = (d_gated * up_lin * sigmoid_gate * (1.0 + gate_lin * (1.0 - sigmoid_gate))).astype(LOW)
    d_up_low = (d_gated * gate_lin * sigmoid_gate).astype(LOW)
    db_blocks = send_home(matmul_nt(d_gate_low, gate_full) + matmul_nt(d_up_low, up_full))
    mix_grad_blocks = mix_grad_rows.reshape(groups, 1, capacity)
    mix_grad_back = place_blocks(
        [
            tp_sum(
                swap(block_for(mix_grad_blocks, distance), "ctx", distance)
                if distance
                else block_for(mix_grad_blocks, 0)
            )
            for distance in range(groups)
        ]
    ).reshape(1, slots)
    dz_rows = (cot_rows.astype(FULL) * mix_rows).astype(LOW)
    near, far = slice(0, half_width), slice(half_width, features)
    down_grad = scatter_sum(
        matmul_tn(hidden_low, dz_rows[:, near]), matmul_tn(hidden_low, dz_rows[:, far]).astype(LOW), 1
    )
    gate_grad = scatter_sum(
        matmul_tn(ffn_rows[:, near], d_gate_low), matmul_tn(ffn_rows[:, far], d_gate_low).astype(LOW), 0
    )
    up_grad = scatter_sum(
        matmul_tn(ffn_rows[:, near], d_up_low), matmul_tn(ffn_rows[:, far], d_up_low).astype(LOW), 0
    )

    hits = all_sum(
        jnp.stack([jnp.sum(attn_onehot, axis=(0, 1)), jnp.sum(ffn_onehot, axis=(0, 1))]),
        ("fsdp", "ctx"),
    )
    share = hits / (all_tokens * picks_each)
    share_grad = AUX_WEIGHT * expert_count / all_tokens * share
    grad_half = cot_half.astype(FULL)
    db_back = place_blocks(db_blocks)
    d_normed2 = jnp.zeros((rows_here, half_width), FULL)
    ffn_mix_grad = []
    for pick in ffn_picks:
        d_normed2 = d_normed2 + matmul(pick, db_back)
        ffn_mix_grad.append(jnp.sum(pick.astype(FULL) * mix_grad_back, axis=1, keepdims=True))
    ffn_mix_grad = jnp.concatenate(ffn_mix_grad, axis=1)
    ffn_d_logits = logits_back(ffn_mix, ffn_mix_grad, ffn_probs, ffn_onehot, share_grad[1])
    d_normed2 = d_normed2 + through_router(ffn_d_logits, router2_half.astype(FULL))
    weighted2 = d_normed2 * gain2_half
    inner2 = tp_sum(jnp.sum(weighted2 * attended, axis=1, keepdims=True)) / features
    d_attended = grad_half + scale_two * weighted2 - attended * scale_two**3 * inner2
    gain2_part = jnp.sum(d_normed2 * attended * scale_two, axis=0)
    ffn_router_part = precise_tn(b_half.astype(FULL), ffn_d_logits)

    dy_slots = jnp.zeros((slots, half_width), FULL)
    for k in range(picks_each):
        dy_slots = dy_slots + matmul_tn(attn_picks[k], (attn_mix[:, k : k + 1] * d_attended).astype(LOW))
    dy_rows = send_out(dy_slots.astype(LOW))
    d_heads = matmul_nt(dy_rows, out_full).astype(LOW)
    dq_low, dk_low, dv_low = attend_back(
        q_low, k_low, v_low, d_heads, log_sum, query_table, key_table, groups
    )
    out_grad = scatter_sum(
        matmul_tn(heads_low, dy_rows[:, near]), matmul_tn(heads_low, dy_rows[:, far]).astype(LOW), 1
    )
    query_grad = scatter_sum(
        matmul_tn(rows_in[:, near], dq_low), matmul_tn(rows_in[:, far], dq_low).astype(LOW), 0
    )
    dkv_low = jnp.concatenate([dk_low, dv_low], axis=1)
    da_rows = matmul_nt(dq_low, query_full).astype(LOW).reshape(groups, capacity, features)
    da_seq = jnp.einsum("bsr,bsd->brd", expert_onehot, da_rows, preferred_element_type=FULL)
    da_seq = da_seq.reshape(groups * rows_here, features) + matmul_nt(dkv_low, kv_full)
    da_blocks = send_home(da_seq)
    kv_part = scatter_sum(
        matmul_tn(a_seq[:, near], dkv_low), matmul_tn(a_seq[:, far], dkv_low).astype(LOW), 0
    )
    kv_grad = block_for(kv_part, 0)
    kv_part_low = kv_part.astype(LOW)
    for distance in distances:
        if distance:
            kv_grad = kv_grad + swap(block_for(kv_part_low, distance), "ctx", distance).astype(FULL)
    key_width = key_proj.shape[1]

    ffn_back = place_blocks(send_home(matmul(hidden_low, down_full)))
    result = attended
    for k in range(picks_each):
        result = result + ffn_mix[:, k : k + 1] * matmul(ffn_picks[k], ffn_back)
    result_low = result.astype(LOW)
    output = from_spread(join_halves(result_low, swap(result_low, "tp", 1)), 1)

    attn_mix_grad = tp_sum(
        jnp.concatenate(
            [jnp.sum(d_attended * picked, axis=1, keepdims=True) for picked in attn_picked], axis=1
        )
    )
    attn_d_logits = logits_back(attn_mix, attn_mix_grad, attn_probs, attn_onehot, share_grad[0])
    a_half = my_half(a_mine)
    attn_router_part = precise_tn(a_half.astype(FULL), attn_d_logits)

    d_normed1 = through_router(attn_d_logits, router1_half)
    for block in da_blocks:
        d_normed1 = d_normed1 + block.astype(FULL)
    gain1_half = my_half(gain1)
    weighted1 = d_normed1 * gain1_half
    inner1 = tp_sum(jnp.sum(weighted1 * input_half, axis=1, keepdims=True)) / features
    input_grad = d_attended + scale_one * weighted1 - input_half * scale_one**3 * inner1
    input_grad_low = input_grad.astype(LOW)
    input_grad = from_spread(join_halves(input_grad_low, swap(input_grad_low, "tp", 1)), 1).astype(FULL)
    gain1_part = jnp.sum(d_normed1 * input_half * scale_one, axis=0)

    early = jnp.concatenate([gain2_part[None], ffn_router_part.T, attn_router_part.T], axis=0)
    early = from_spread(join_halves(early, swap(early, "tp", 1)), 1)
    early = all_sum(early, ("ctx", "fsdp"))
    late = gain1_part[None]
    late = from_spread(join_halves(late, swap(late, "tp", 1)), 1)
    late = all_sum(late, ("ctx", "fsdp"))
    prob_sums = all_sum(
        jnp.stack([jnp.sum(attn_probs, axis=0), jnp.sum(ffn_probs, axis=0)]), ("fsdp", "ctx")
    )
    losses = expert_count * jnp.sum(share * prob_sums / all_tokens, axis=1)
    return (
        output,
        input_grad,
        losses[0],
        losses[1],
        late[0],
        early[0],
        early[1 + expert_count :].T,
        early[1 : 1 + expert_count].T,
        kv_grad[:, :key_width],
        kv_grad[:, key_width:],
        query_grad[None],
        out_grad[None],
        gate_grad[None],
        up_grad[None],
        down_grad[None],
    )


def solution(mesh):
    by_token = P(("fsdp", "ctx"), None)
    by_row = P(("fsdp", "ctx"), "tp")
    inward = P("ctx", "fsdp", "tp")
    outward = P("ctx", "tp", "fsdp")
    weights = (by_row, by_row, inward, outward, inward, inward, outward)
    return jax.shard_map(
        on_device,
        mesh=mesh,
        in_specs=(by_token,) * 4 + (P(),) * 4 + weights,
        out_specs=(by_token,) * 2 + (P(),) * 6 + weights,
        check_vma=False,
    )
```

```python
import functools
import math

import jax
import jax.numpy as jnp
from jax import lax
from jax.experimental import pallas as pl
from jax.experimental.pallas import tpu as pltpu
from jax.sharding import PartitionSpec as P

HEAD = 128
EPSILON = 1e-06
ROPE_BASE = 10000.0
AUX_WEIGHT = 0.1
PRECISE = lax.Precision.HIGHEST
LOW = jnp.bfloat16
FULL = jnp.float32
VMEM_BYTES = 56 * 1024 * 1024


def matmul(lhs, rhs):
    return jnp.dot(lhs, rhs, preferred_element_type=FULL)


def matmul_tn(lhs, rhs):
    return lax.dot_general(lhs, rhs, (((0,), (0,)), ((), ())), preferred_element_type=FULL)


def matmul_nt(lhs, rhs):
    return lax.dot_general(lhs, rhs, (((1,), (1,)), ((), ())), preferred_element_type=FULL)


def precise_tn(lhs, rhs):
    return lax.dot_general(lhs, rhs, (((0,), (0,)), ((), ())), precision=PRECISE)


def swap(value, axis, distance):
    size = lax.axis_size(axis)
    return lax.ppermute(value, axis, [(i, i ^ distance) for i in range(size)])


def after(value, *earlier):
    return lax.optimization_barrier((value,) + earlier)[0]


def bits_down(size):
    bit = size // 2
    while bit >= 1:
        yield bit
        bit //= 2


def spread_order(size):
    order = [0]
    for bit in bits_down(size):
        order = order + [place | bit for place in order]
    return order


def gather_pieces(piece):
    pieces = [piece]
    for bit in bits_down(lax.axis_size("fsdp")):
        pieces = pieces + [swap(item, "fsdp", bit) for item in pieces]
    return pieces


def flip_blocks(value, axis, index, count):
    parts = jnp.split(value, count, axis)
    for bit in bits_down(count):
        turned = (index // bit) % 2 == 1
        parts = [jnp.where(turned, parts[n ^ bit], parts[n]) for n in range(count)]
    return jnp.concatenate(parts, axis)


def to_spread(value, axis):
    size = lax.axis_size("fsdp")
    value = flip_blocks(value, axis, lax.axis_index("fsdp"), size)
    parts = jnp.split(value, size, axis)
    return jnp.concatenate([parts[place] for place in spread_order(size)], axis)


def from_spread(value, axis):
    size = lax.axis_size("fsdp")
    parts = jnp.split(value, size, axis)
    order = spread_order(size)
    value = jnp.concatenate([parts[order.index(place)] for place in range(size)], axis)
    return flip_blocks(value, axis, lax.axis_index("fsdp"), size)


def my_half(value):
    width = value.shape[-1] // 2
    return jnp.where(lax.axis_index("tp") == 0, value[..., :width], value[..., width:])


def other_half(value):
    width = value.shape[-1] // 2
    return jnp.where(lax.axis_index("tp") == 0, value[..., width:], value[..., :width])


def join_halves(mine, other):
    first = lax.axis_index("tp") == 0
    return jnp.concatenate([jnp.where(first, mine, other), jnp.where(first, other, mine)], -1)


def tp_sum(value):
    return value + swap(value, "tp", 1)


def all_sum(value, axes):
    for axis in axes:
        for bit in bits_down(lax.axis_size(axis)):
            value = value + swap(value, axis, bit)
    return value


def far_first(size):
    return list(range(size // 2, size)) + list(range(size // 2 - 1, -1, -1))


def place_blocks(blocks):
    index = lax.axis_index("ctx")
    rows = blocks[0].shape[0]
    total = jnp.zeros((rows * len(blocks),) + blocks[0].shape[1:], blocks[0].dtype)
    for distance, block in enumerate(blocks):
        total = lax.dynamic_update_slice_in_dim(total, block, (index ^ distance) * rows, 0)
    return total


def block_for(value, distance):
    size = lax.axis_size("ctx")
    rows = value.shape[0] // size
    return lax.dynamic_slice_in_dim(value, (lax.axis_index("ctx") ^ distance) * rows, rows, 0)


def spread_out(half_rows):
    size = lax.axis_size("ctx")
    blocks = [None] * size
    for distance in far_first(size):
        block = block_for(half_rows, distance)
        if distance:
            block = swap(block, "ctx", distance)
        blocks[distance] = join_halves(block, swap(block, "tp", 1))
    return place_blocks(blocks)


def xor_index(index, distance):
    result = index
    bit = 1
    while bit <= distance:
        if distance & bit:
            result = result + bit - 2 * bit * ((index // bit) % 2)
        bit *= 2
    return result


def span(start, size):
    return pl.ds(pl.multiple_of(start * size, 16), size)


def meet(peers):
    barrier = pltpu.get_barrier_semaphore()
    for device in peers:
        pl.semaphore_signal(barrier, inc=1, device_id=device, device_id_type=pl.DeviceIdType.MESH)
    pl.semaphore_wait(barrier, len(peers))


def remote(source, target, sems, index, device):
    return pltpu.make_async_remote_copy(
        src_ref=source,
        dst_ref=target,
        send_sem=sems[0].at[index],
        recv_sem=sems[1].at[index],
        device_id=device,
        device_id_type=pl.DeviceIdType.MESH,
    )


def send_out_kernel(size, rows_ref, out_ref, z_land, y_land, z_send, z_recv, y_send, y_recv):
    mine, first = lax.axis_index("ctx"), lax.axis_index("tp") == 0
    other_tp = {"tp": 1 - lax.axis_index("tp")}
    rows, width = z_land.shape[1], z_land.shape[2]
    at = [xor_index(mine, distance) for distance in range(size)]
    meet([{"ctx": at[distance]} for distance in range(1, size)] + [other_tp])
    order = [distance for distance in far_first(size) if distance]
    across, beside = {}, {}
    for distance in order:
        across[distance] = remote(
            rows_ref.at[span(at[distance], rows)],
            z_land.at[distance],
            (z_send, z_recv),
            distance,
            {"ctx": at[distance]},
        )
        across[distance].start()
    beside[0] = remote(rows_ref.at[span(mine, rows)], y_land.at[0], (y_send, y_recv), 0, other_tp)
    beside[0].start()
    for distance in order:
        across[distance].wait_recv()
        beside[distance] = remote(
            z_land.at[distance], y_land.at[distance], (y_send, y_recv), distance, other_tp
        )
        beside[distance].start()
    for distance in [0] + order:
        beside[distance].wait_recv()
        own = z_land[distance] if distance else rows_ref[span(mine, rows), :]
        theirs = y_land[distance]
        out_ref[span(at[distance], rows), :width] = jnp.where(first, own, theirs)
        out_ref[span(at[distance], rows), width:] = jnp.where(first, theirs, own)
    for distance in order:
        across[distance].wait_send()
    for distance in [0] + order:
        beside[distance].wait_send()


def send_out(half_rows, number):
    size = lax.axis_size("ctx")
    total, width = half_rows.shape
    land = pltpu.VMEM((size, total // size, width), half_rows.dtype)
    return pl.pallas_call(
        functools.partial(send_out_kernel, size),
        in_specs=[pl.BlockSpec(memory_space=pltpu.VMEM)],
        out_specs=pl.BlockSpec(memory_space=pltpu.VMEM),
        out_shape=jax.ShapeDtypeStruct((total, 2 * width), half_rows.dtype),
        scratch_shapes=[land, land] + [pltpu.SemaphoreType.DMA((size,))] * 4,
        compiler_params=pltpu.CompilerParams(
            collective_id=number, has_side_effects=True, vmem_limit_bytes=VMEM_BYTES
        ),
        cost_estimate=pl.CostEstimate(flops=0, bytes_accessed=12 * total * width, transcendentals=0),
    )(half_rows)


def send_home_kernel(size, add_up, has_extra, *refs):
    part_ref, refs = refs[0], refs[1:]
    extra_ref, refs = (refs[0], refs[1:]) if has_extra else (None, refs)
    out_ref, refs = refs[0], refs[1:]
    extra_out, refs = (refs[0], refs[1:]) if has_extra else (None, refs)
    y_land, ready, z_land, y_send, y_recv, z_send, z_recv = refs[:7]
    mine, first = lax.axis_index("ctx"), lax.axis_index("tp") == 0
    place = lax.axis_index("tp")
    other_tp = {"tp": 1 - place}
    rows, width = z_land.shape[1], z_land.shape[2]
    at = [xor_index(mine, distance) for distance in range(size)]
    columns = pl.ds(pl.multiple_of((1 - place) * width, 128), width)
    meet([{"ctx": at[distance]} for distance in range(1, size)] + [other_tp])
    order = far_first(size)
    beside, across, extras = {}, {}, {}
    if has_extra:
        ey_land, e_ready, ez_land, ey_send, ey_recv, ez_send, ez_recv = refs[7:]
        extra_beside = remote(extra_ref, ey_land, (ey_send, ey_recv), 0, other_tp)
        extra_beside.start()
    for distance in order:
        beside[distance] = remote(
            part_ref.at[span(at[distance], rows), columns],
            y_land.at[distance],
            (y_send, y_recv),
            distance,
            other_tp,
        )
        beside[distance].start()
    if has_extra:
        extra_beside.wait_recv()
        e_ready[...] = extra_ref[...] + ey_land[...]
        for distance in order:
            if distance:
                extras[distance] = remote(
                    e_ready.at[at[distance]],
                    ez_land.at[distance],
                    (ez_send, ez_recv),
                    distance,
                    {"ctx": at[distance]},
                )
                extras[distance].start()
    for distance in order:
        beside[distance].wait_recv()
        whole = part_ref[span(at[distance], rows), :]
        own = jnp.where(first, whole[:, :width], whole[:, width:])
        total = (own.astype(FULL) + y_land[distance].astype(FULL)).astype(LOW)
        if distance:
            ready[distance] = total
            across[distance] = remote(
                ready.at[distance],
                z_land.at[distance],
                (z_send, z_recv),
                distance,
                {"ctx": at[distance]},
            )
            across[distance].start()
        elif add_up:
            out_ref[...] = total.astype(FULL)
        else:
            out_ref[span(mine, rows), :] = total
    for distance in order:
        if distance:
            across[distance].wait_recv()
            if add_up:
                out_ref[...] += z_land[distance].astype(FULL)
            else:
                out_ref[span(at[distance], rows), :] = z_land[distance]
    if has_extra:
        extra_out[mine] = e_ready[mine]
        for distance in order:
            if distance:
                extras[distance].wait_recv()
                extra_out[at[distance]] = ez_land[distance]
                extras[distance].wait_send()
        extra_beside.wait_send()
    for distance in order:
        beside[distance].wait_send()
        if distance:
            across[distance].wait_send()


def send_home(partial_rows, number, extra=None, add_up=False):
    size = lax.axis_size("ctx")
    total, width = partial_rows.shape[0], partial_rows.shape[1] // 2
    rows = total // size
    land = pltpu.VMEM((size, rows, width), LOW)
    sems = [pltpu.SemaphoreType.DMA((size,))] * 4
    shapes = [jax.ShapeDtypeStruct((rows, width), FULL) if add_up else jax.ShapeDtypeStruct((total, width), LOW)]
    operands, scratch = [partial_rows], [land, land, land] + sems
    if extra is not None:
        operands.append(extra)
        shapes.append(jax.ShapeDtypeStruct(extra.shape, FULL))
        scratch += [pltpu.VMEM(extra.shape, FULL)] * 3 + sems
    results = pl.pallas_call(
        functools.partial(send_home_kernel, size, add_up, extra is not None),
        in_specs=[pl.BlockSpec(memory_space=pltpu.VMEM)] * len(operands),
        out_specs=[pl.BlockSpec(memory_space=pltpu.VMEM)] * len(shapes),
        out_shape=shapes,
        scratch_shapes=scratch,
        compiler_params=pltpu.CompilerParams(
            collective_id=number, has_side_effects=True, vmem_limit_bytes=VMEM_BYTES
        ),
        cost_estimate=pl.CostEstimate(flops=0, bytes_accessed=12 * total * width, transcendentals=0),
    )(*operands)
    return results if extra is not None else results[0]


def prologue_kernel(sizes, *refs):
    groups, world = sizes
    half_in, own_in, routes_in, kv_in, query_in, out_in = refs[:6]
    seq_ref, routes_ref, kv_ref, query_ref, out_ref = refs[6:11]
    local_sem, zt, yt, zr, zk, xk, fr, fk, fq, fo = refs[11], *[
        (refs[12 + 2 * n], refs[13 + 2 * n]) for n in range(9)
    ]
    mine, place, spot = lax.axis_index("ctx"), lax.axis_index("tp"), lax.axis_index("fsdp")
    other_tp = {"tp": 1 - place}
    rows, width = half_in.shape
    sub = kv_in.shape[0]
    piece = sub * groups
    q_rows, o_columns = query_in.shape[0], out_in.shape[1]
    at = [xor_index(mine, distance) for distance in range(groups)]
    ctx_peer = [{"ctx": at[distance]} for distance in range(groups)]
    steps = list(bits_down(world))
    beside = {bit: {"fsdp": xor_index(spot, bit)} for bit in steps}
    meet(ctx_peer[1:] + [other_tp] + [beside[bit] for bit in steps])
    own_columns = pl.ds(pl.multiple_of(place * width, 128), width)
    order = [distance for distance in far_first(groups) if distance]
    locals_ = [
        pltpu.make_async_copy(own_in, seq_ref.at[span(mine, rows)], local_sem.at[0]),
        pltpu.make_async_copy(routes_in, routes_ref.at[0, mine], local_sem.at[1]),
        pltpu.make_async_copy(kv_in, kv_ref.at[span(mine, sub)], local_sem.at[2]),
        pltpu.make_async_copy(query_in, query_ref.at[pl.ds(0, q_rows)], local_sem.at[3]),
        pltpu.make_async_copy(out_in, out_ref.at[:, pl.ds(0, o_columns)], local_sem.at[4]),
    ]
    for copy in locals_:
        copy.start()
    started, landed = [], set()

    def go(copy):
        copy.start()
        started.append(copy)
        return copy

    def arrived(copy):
        if id(copy) not in landed:
            copy.wait_recv()
            landed.add(id(copy))

    first = steps[0]

    query_view = lambda n: query_ref.at[pl.ds(n * q_rows, q_rows)]
    out_view = lambda n: out_ref.at[:, pl.ds(n * o_columns, o_columns)]
    query_copies = {1: go(remote(query_in, query_view(1), fq, 1, beside[first]))}
    route_copies, kv_copies, token_copies = {}, {}, {}
    for distance in order:
        route_copies[distance] = go(
            remote(routes_in, routes_ref.at[0, mine], zr, distance, ctx_peer[distance])
        )
    for distance in order:
        kv_copies[distance] = go(
            remote(kv_in, kv_ref.at[span(mine, sub)], zk, distance, ctx_peer[distance])
        )
    for distance in order:
        token_copies[distance] = go(
            remote(
                half_in, seq_ref.at[span(mine, rows), own_columns], zt, distance, ctx_peer[distance]
            )
        )
    out_copies = {1: go(remote(out_in, out_view(1), fo, 1, beside[first]))}

    def kv_step(distance):
        if distance:
            arrived(kv_copies[distance])
            source = kv_ref.at[span(at[distance], sub)]
        else:
            source = kv_in
        target = kv_ref.at[pl.ds(pl.multiple_of(piece + at[distance] * sub, 16), sub)]
        return go(remote(source, target, xk, distance, beside[first]))

    kv_first = {0: kv_step(0)}
    half_copies = {}
    for distance in order:
        kv_first[distance] = kv_step(distance)
    for distance in order:
        arrived(token_copies[distance])
        view = seq_ref.at[span(at[distance], rows), own_columns]
        half_copies[distance] = go(remote(view, view, yt, distance, other_tp))
    for distance in order:
        arrived(route_copies[distance])
    for copy in locals_:
        copy.wait()
    kv_view = lambda n: kv_ref.at[pl.ds(n * piece, piece)]
    route_wait = {}
    kv_wait = {}
    count = 1
    for bit in steps:
        for n in range(count):
            peer = beside[bit]
            if n in route_wait:
                arrived(route_wait[n])
            route_wait[count + n] = go(
                remote(routes_ref.at[n], routes_ref.at[count + n], fr, count + n, peer)
            )
            if bit != first:
                if n:
                    arrived(query_copies[n])
                    arrived(out_copies[n])
                query_copies[count + n] = go(
                    remote(query_view(n), query_view(count + n), fq, count + n, peer)
                )
                out_copies[count + n] = go(remote(out_view(n), out_view(count + n), fo, count + n, peer))
                if n == 1:
                    for distance in range(groups):
                        arrived(kv_first[distance])
                if n > 1:
                    arrived(kv_wait[n])
                kv_wait[count + n] = go(remote(kv_view(n), kv_view(count + n), fk, count + n, peer))
        count *= 2
    for copy in started:
        arrived(copy)
    for copy in started:
        copy.wait_send()


def prologue(token_half, token_rows, routes, kv_rows, query_piece, out_piece, number):
    groups, world = lax.axis_size("ctx"), lax.axis_size("fsdp")
    any_space = pl.BlockSpec(memory_space=pl.ANY)
    rows, features = token_rows.shape
    pair = lambda count: [pltpu.SemaphoreType.DMA((count,))] * 2
    return pl.pallas_call(
        functools.partial(prologue_kernel, (groups, world)),
        in_specs=[any_space] * 6,
        out_specs=[any_space] * 5,
        out_shape=[
            jax.ShapeDtypeStruct((groups * rows, features), LOW),
            jax.ShapeDtypeStruct((world, groups) + routes.shape, jnp.int32),
            jax.ShapeDtypeStruct((world * groups * kv_rows.shape[0], kv_rows.shape[1]), LOW),
            jax.ShapeDtypeStruct((world * query_piece.shape[0], query_piece.shape[1]), LOW),
            jax.ShapeDtypeStruct((out_piece.shape[0], world * out_piece.shape[1]), LOW),
        ],
        scratch_shapes=[pltpu.SemaphoreType.DMA((5,))] + pair(groups) * 5 + pair(world) * 4,
        compiler_params=pltpu.CompilerParams(collective_id=number, has_side_effects=True),
        cost_estimate=pl.CostEstimate(flops=0, bytes_accessed=100000000, transcendentals=0),
    )(token_half, token_rows, routes, kv_rows, query_piece, out_piece)


def expert_kernel(world, *refs):
    rows_ref, cot_ref, mix_ref = refs[:3]
    gates, ups, downs = (refs[3 + n * world : 3 + (n + 1) * world] for n in range(3))
    hidden_ref, d_gate_ref, d_up_ref, db_ref, out_ref, mix_grad_ref = refs[3 + 3 * world : 9 + 3 * world]
    db_sum, out_sum = refs[9 + 3 * world :]
    step = pl.program_id(0)
    width = rows_ref.shape[1] // world

    @pl.when(step == 0)
    def _():
        db_sum[...] = jnp.zeros_like(db_sum)
        out_sum[...] = jnp.zeros_like(out_sum)
        mix_grad_ref[...] = jnp.zeros_like(mix_grad_ref)

    gate_lin, up_lin, d_hidden = None, None, None
    for n in range(world):
        columns = slice(n * width, (n + 1) * width)
        terms = (
            matmul(rows_ref[:, columns], gates[n][...]),
            matmul(rows_ref[:, columns], ups[n][...]),
            matmul_nt(cot_ref[:, columns], downs[n][...]),
        )
        if n:
            terms = (gate_lin + terms[0], up_lin + terms[1], d_hidden + terms[2])
        gate_lin, up_lin, d_hidden = terms
    sigmoid_gate = 1.0 / (1.0 + jnp.exp(-gate_lin))
    swish = gate_lin * sigmoid_gate
    hidden = swish * up_lin
    mix_grad_ref[...] += jnp.broadcast_to(
        jnp.sum(hidden * d_hidden, axis=1, keepdims=True), mix_grad_ref.shape
    )
    d_gated = d_hidden * mix_ref[:, :1]
    hidden_low = hidden.astype(LOW)
    d_gate = (d_gated * up_lin * sigmoid_gate * (1.0 + gate_lin * (1.0 - sigmoid_gate))).astype(LOW)
    d_up = (d_gated * swish).astype(LOW)
    hidden_ref[...] = hidden_low
    d_gate_ref[...] = d_gate
    d_up_ref[...] = d_up
    for n in range(world):
        columns = slice(n * width, (n + 1) * width)
        out_sum[:, columns] += matmul(hidden_low, downs[n][...])
        db_sum[:, columns] += matmul_nt(d_gate, gates[n][...]) + matmul_nt(d_up, ups[n][...])

    @pl.when(step == pl.num_programs(0) - 1)
    def _():
        db_ref[...] = db_sum[...].astype(LOW)
        out_ref[...] = out_sum[...].astype(LOW)


def expert_both_ways(rows, cot_rows, mix_rows, gate_pieces, up_pieces, down_pieces):
    world = len(gate_pieces)
    slots, features = rows.shape
    depth, hidden_width = gate_pieces[0].shape
    tile = 256
    once = pl.Buffered(1)
    whole = lambda width: pl.BlockSpec((slots, width), lambda i: (0, 0), pipeline_mode=once)
    kept = lambda width: pl.BlockSpec((slots, width), lambda i: (0, 0))
    tall = pl.BlockSpec((depth, tile), lambda i: (0, i))
    flat = pl.BlockSpec((tile, depth), lambda i: (i, 0))
    strip = pl.BlockSpec((slots, tile), lambda i: (0, i))
    low = lambda width: jax.ShapeDtypeStruct((slots, width), LOW)
    return pl.pallas_call(
        functools.partial(expert_kernel, world),
        grid=(hidden_width // tile,),
        in_specs=[whole(features), whole(features), whole(HEAD)]
        + [tall] * (2 * world)
        + [flat] * world,
        out_specs=[strip] * 3 + [kept(features)] * 2 + [kept(HEAD)],
        out_shape=[low(hidden_width)] * 3
        + [low(features)] * 2
        + [jax.ShapeDtypeStruct((slots, HEAD), FULL)],
        scratch_shapes=[pltpu.VMEM((slots, features), FULL)] * 2,
        compiler_params=pltpu.CompilerParams(vmem_limit_bytes=VMEM_BYTES),
        cost_estimate=pl.CostEstimate(
            flops=12 * slots * features * hidden_width,
            bytes_accessed=6 * features * hidden_width,
            transcendentals=slots * hidden_width,
        ),
    )(rows, cot_rows, mix_rows, *gate_pieces, *up_pieces, *down_pieces)


def scatter_sum(keep, send, first_dim):
    size = lax.axis_size("fsdp")
    bit = 1
    while True:
        total = keep + swap(send, "fsdp", bit).astype(FULL)
        bit *= 2
        if bit >= size:
            return total
        width = total.shape[first_dim] // 2
        keep = lax.slice_in_dim(total, 0, width, axis=first_dim)
        send = lax.slice_in_dim(total, width, 2 * width, axis=first_dim).astype(LOW)


def turn_tables(places):
    half_head = HEAD // 2
    frequency = ROPE_BASE ** (-jnp.arange(half_head, dtype=FULL) * 2.0 / HEAD)
    angles = places.astype(FULL)[:, None] * frequency[None, :]
    cosine, sine = jnp.cos(angles), jnp.sin(angles)
    return jnp.concatenate([cosine, cosine, -sine, sine], axis=1)


def turn(value, table):
    return value * table[:, :HEAD] + pltpu.roll(value, HEAD // 2, 1) * table[:, HEAD:]


def turn_back(value, table):
    return value * table[:, :HEAD] - pltpu.roll(value, HEAD // 2, 1) * table[:, HEAD:]


def attend_kernel(
    groups, scale, q_lin, k_lin, v_lin, q_table, k_table, q_low, k_low, v_low, heads, log_sum
):
    q_low[...] = turn(q_lin[...], q_table[...]).astype(LOW)
    k_low[...] = turn(k_lin[...], k_table[...]).astype(LOW)
    v_low[...] = v_lin[...].astype(LOW)
    rows = q_low.shape[0] // groups
    block = k_low.shape[0] // groups
    for group in range(groups):
        span = slice(group * rows, (group + 1) * rows)
        seen = slice(0, (group + 1) * block)
        scores = matmul_nt(q_low[span, :], k_low[seen, :]) * scale
        top = jnp.max(scores, axis=1, keepdims=True)
        weights = jnp.exp(scores - top)
        total = jnp.sum(weights, axis=1, keepdims=True)
        weights = (weights * (1.0 / total)).astype(LOW)
        heads[span, :] = matmul(weights, v_low[seen, :]).astype(LOW)
        log_sum[span, :] = jnp.broadcast_to(top + jnp.log(total), (rows, HEAD))


def attend(query_lin, kv_lin, query_table, key_table, groups):
    slots, width = query_lin.shape
    length = kv_lin.shape[0]
    count = width // HEAD
    by_head = lambda rows: pl.BlockSpec((rows, HEAD), lambda h: (0, h))
    whole = lambda rows: pl.BlockSpec((rows, 2 * HEAD), lambda h: (0, 0))
    return pl.pallas_call(
        functools.partial(attend_kernel, groups, 1.0 / math.sqrt(HEAD)),
        grid=(count,),
        in_specs=[
            by_head(slots),
            by_head(length),
            pl.BlockSpec((length, HEAD), lambda h: (0, h + count)),
            whole(slots),
            whole(length),
        ],
        out_specs=[by_head(slots), by_head(length), by_head(length), by_head(slots), by_head(slots)],
        out_shape=[
            jax.ShapeDtypeStruct((slots, width), LOW),
            jax.ShapeDtypeStruct((length, width), LOW),
            jax.ShapeDtypeStruct((length, width), LOW),
            jax.ShapeDtypeStruct((slots, width), LOW),
            jax.ShapeDtypeStruct((slots, width), FULL),
        ],
        compiler_params=pltpu.CompilerParams(vmem_limit_bytes=VMEM_BYTES),
        cost_estimate=pl.CostEstimate(
            flops=3 * slots * length * width,
            bytes_accessed=20 * length * width,
            transcendentals=slots * length * count,
        ),
    )(query_lin, kv_lin, kv_lin, query_table, key_table)


def attend_back_kernel(
    groups, scale, q_low, k_low, v_low, d_heads, log_sum, q_table, k_table, dq, dk, dv, dk_sum, dv_sum
):
    dk_sum[...] = jnp.zeros_like(dk_sum)
    dv_sum[...] = jnp.zeros_like(dv_sum)
    rows = q_low.shape[0] // groups
    block = k_low.shape[0] // groups
    for group in range(groups):
        span = slice(group * rows, (group + 1) * rows)
        seen = slice(0, (group + 1) * block)
        query, keys = q_low[span, :], k_low[seen, :]
        grads = d_heads[span, :]
        scores = matmul_nt(query, keys) * scale
        weights = jnp.exp(scores - log_sum[span, :1])
        d_weights = matmul_nt(grads, v_low[seen, :])
        delta = jnp.sum(weights * d_weights, axis=1, keepdims=True)
        d_scores = (weights * (d_weights - delta)).astype(LOW)
        dq[span, :] = turn_back(matmul(d_scores, keys) * scale, q_table[span, :]).astype(LOW)
        dk_sum[seen, :] += matmul_tn(d_scores, query) * scale
        dv_sum[seen, :] += matmul_tn(weights.astype(LOW), grads)
    dk[...] = turn_back(dk_sum[...], k_table[...]).astype(LOW)
    dv[...] = dv_sum[...].astype(LOW)


def attend_back(q_low, k_low, v_low, d_heads, log_sum, query_table, key_table, groups):
    slots, width = q_low.shape
    length = k_low.shape[0]
    count = width // HEAD
    by_head = lambda rows: pl.BlockSpec((rows, HEAD), lambda h: (0, h))
    whole = lambda rows: pl.BlockSpec((rows, 2 * HEAD), lambda h: (0, 0))
    return pl.pallas_call(
        functools.partial(attend_back_kernel, groups, 1.0 / math.sqrt(HEAD)),
        grid=(count,),
        in_specs=[
            by_head(slots),
            by_head(length),
            by_head(length),
            by_head(slots),
            by_head(slots),
            whole(slots),
            whole(length),
        ],
        out_specs=[by_head(slots), by_head(length), by_head(length)],
        out_shape=[
            jax.ShapeDtypeStruct((slots, width), LOW),
            jax.ShapeDtypeStruct((length, width), LOW),
            jax.ShapeDtypeStruct((length, width), LOW),
        ],
        scratch_shapes=[pltpu.VMEM((length, HEAD), FULL), pltpu.VMEM((length, HEAD), FULL)],
        compiler_params=pltpu.CompilerParams(vmem_limit_bytes=VMEM_BYTES),
        cost_estimate=pl.CostEstimate(
            flops=7 * slots * length * width,
            bytes_accessed=14 * length * width,
            transcendentals=slots * length * count,
        ),
    )(q_low, k_low, v_low, d_heads, log_sum, query_table, key_table)


def chosen_picks(routes, expert_count, capacity):
    experts = jnp.arange(expert_count, dtype=jnp.int32)
    onehot = (routes[:, :, None] == experts[None, None, :]).astype(jnp.int32)
    order = jnp.cumsum(jnp.sum(onehot, axis=1), axis=0) - 1
    slot = routes * capacity + jnp.sum(onehot * order[:, None, :], axis=2)
    slots = jnp.arange(expert_count * capacity, dtype=jnp.int32)
    picks = [(slot[:, k : k + 1] == slots[None, :]).astype(LOW) for k in range(routes.shape[1])]
    return picks, onehot.astype(FULL)


def expert_picks(routes_seq, expert, capacity):
    named = jnp.any(routes_seq == expert, axis=1)
    order = jnp.cumsum(named.astype(jnp.int32), axis=1) - 1
    slot = jnp.where(named, order, -1)
    return (slot[:, None, :] == jnp.arange(capacity, dtype=jnp.int32)[None, :, None]).astype(LOW)


def mix_of(logits, onehot):
    chosen = jnp.sum(onehot * logits[:, None, :], axis=2)
    return jax.nn.softmax(chosen, axis=1)


def logits_back(mix, mix_grad, probs, onehot, share_grad):
    d_chosen = mix * (mix_grad - jnp.sum(mix * mix_grad, axis=1, keepdims=True))
    d_logits = jnp.sum(onehot * d_chosen[:, :, None], axis=1)
    inner = jnp.sum(probs * share_grad[None, :], axis=1, keepdims=True)
    return d_logits + probs * (share_grad[None, :] - inner)


def through_router(d_logits, router_half):
    total = d_logits[:, 0:1] * router_half[:, 0][None, :]
    for expert in range(1, d_logits.shape[1]):
        total = total + d_logits[:, expert : expert + 1] * router_half[:, expert][None, :]
    return total


def on_device(
    tokens,
    cotangent,
    attn_routes,
    ffn_routes,
    norm_gain1,
    norm_gain2,
    attn_router,
    ffn_router,
    key_proj,
    value_proj,
    query_proj,
    out_proj,
    gate_proj,
    up_proj,
    down_proj,
):
    rows_here, features = tokens.shape
    half_width = features // 2
    picks_each = attn_routes.shape[1]
    expert_count = attn_router.shape[1]
    groups = lax.axis_size("ctx")
    mine = lax.axis_index("ctx")
    capacity = rows_here * picks_each // expert_count * 5 // 4
    slots = groups * capacity
    all_tokens = rows_here * lax.axis_size("fsdp") * groups

    tokens_spread = to_spread(tokens, 1)
    token_half = my_half(tokens_spread)
    routes_mine = jnp.concatenate([attn_routes.T, ffn_routes.T], axis=0)
    routes_mine = jnp.concatenate([routes_mine, jnp.zeros_like(routes_mine)], axis=0)
    kv_mine = jnp.concatenate([key_proj, value_proj], axis=1)
    seq_low, all_routes, kv_full, query_full, out_full = prologue(
        token_half, tokens_spread, routes_mine, kv_mine, query_proj[0], out_proj[0], 0
    )
    seq_routes = all_routes[0]
    seq_tokens = seq_low.astype(FULL)

    gate_pieces = gather_pieces(after(gate_proj[0], all_routes))
    up_pieces = gather_pieces(after(up_proj[0], all_routes))
    down_pieces = gather_pieces(after(down_proj[0], all_routes))

    gain1 = to_spread(norm_gain1, 0)
    gain2_half = my_half(to_spread(norm_gain2, 0))
    router1 = to_spread(attn_router, 0)
    router2 = to_spread(ffn_router, 0)
    router1_half = my_half(router1.T).T.astype(FULL)
    router2_half = my_half(router2.T).T

    scale_seq = lax.rsqrt(jnp.mean(seq_tokens * seq_tokens, axis=1, keepdims=True) + EPSILON)
    a_seq = (seq_tokens * scale_seq * gain1).astype(LOW)
    a_mine = lax.dynamic_slice_in_dim(a_seq, mine * rows_here, rows_here, 0)
    scale_one = lax.dynamic_slice_in_dim(scale_seq, mine * rows_here, rows_here, 0)
    attn_logits = matmul(a_mine, router1)
    attn_probs = jax.nn.softmax(attn_logits, axis=1)
    attn_picks, attn_onehot = chosen_picks(attn_routes, expert_count, capacity)
    ffn_picks, ffn_onehot = chosen_picks(ffn_routes, expert_count, capacity)
    attn_mix = mix_of(attn_logits, attn_onehot)

    expert_onehot = expert_picks(seq_routes[:, :picks_each], mine, capacity)
    key_table = turn_tables(jnp.arange(groups * rows_here, dtype=jnp.int32))
    query_table = jnp.einsum(
        "bsr,brh->bsh",
        expert_onehot.astype(FULL),
        key_table.reshape(groups, rows_here, -1),
        precision=PRECISE,
    ).reshape(slots, -1)
    rows_in = (
        jnp.einsum(
            "bsr,brd->bsd",
            expert_onehot,
            a_seq.reshape(groups, rows_here, features),
            preferred_element_type=FULL,
        )
        .astype(LOW)
        .reshape(slots, features)
    )
    query_lin = matmul(rows_in, query_full)
    kv_lin = matmul(a_seq, kv_full)
    q_low, k_low, v_low, heads_low, log_sum = attend(
        query_lin, kv_lin, query_table, key_table, groups
    )
    attn_back = send_home(matmul(heads_low, out_full).astype(LOW), 1)

    cot_half = my_half(to_spread(cotangent, 1))
    ffn_pick = ffn_picks[0]
    for pick in ffn_picks[1:]:
        ffn_pick = ffn_pick + pick
    cot_rows = spread_out(after(matmul_tn(ffn_pick, cot_half).astype(LOW), all_routes))

    input_half = my_half(tokens_spread).astype(FULL)
    attn_picked = [matmul(pick, attn_back) for pick in attn_picks]
    attended = input_half
    for k in range(picks_each):
        attended = attended + attn_mix[:, k : k + 1] * attn_picked[k]
    square_sum = tp_sum(jnp.sum(attended * attended, axis=1, keepdims=True))
    scale_two = lax.rsqrt(square_sum / features + EPSILON)
    b_half = (attended * scale_two * gain2_half).astype(LOW)
    ffn_rows = send_out(matmul_tn(ffn_pick, b_half).astype(LOW), 2)
    ffn_logits = tp_sum(matmul(b_half, router2_half))
    ffn_probs = jax.nn.softmax(ffn_logits, axis=1)
    ffn_mix = mix_of(ffn_logits, ffn_onehot)

    ffn_seq_routes = seq_routes[:, picks_each : 2 * picks_each]
    ffn_expert_onehot = expert_picks(ffn_seq_routes, mine, capacity).astype(FULL)
    row_routes = jnp.einsum(
        "bsr,bkr->bsk", ffn_expert_onehot, ffn_seq_routes.astype(FULL), precision=PRECISE
    ).reshape(slots, picks_each)
    row_onehot = row_routes[:, :, None] == jnp.arange(expert_count, dtype=FULL)[None, None, :]
    row_mix = mix_of(matmul(ffn_rows, router2), row_onehot.astype(FULL))
    mine_too = (row_routes == mine.astype(FULL)).astype(FULL)
    mix_rows = jnp.broadcast_to(jnp.sum(row_mix * mine_too, axis=1, keepdims=True), (slots, HEAD))
    hidden_low, d_gate_low, d_up_low, db_rows, ffn_out, mix_grad_rows = expert_both_ways(
        ffn_rows, cot_rows, mix_rows, gate_pieces, up_pieces, down_pieces
    )
    mix_grad_rows = jnp.pad(mix_grad_rows[:, 0].reshape(groups, 1, capacity), ((0, 0), (0, 7), (0, 256 - capacity)))
    db_back, mix_grad_back = send_home(db_rows, 3, extra=mix_grad_rows)
    mix_grad_back = mix_grad_back[:, 0, :capacity].reshape(1, slots)
    dz_rows = (cot_rows.astype(FULL) * mix_rows[:, :1]).astype(LOW)
    near, far = slice(0, half_width), slice(half_width, features)
    down_grad = scatter_sum(
        matmul_tn(hidden_low, dz_rows[:, near]), matmul_tn(hidden_low, dz_rows[:, far]).astype(LOW), 1
    )
    gate_grad = scatter_sum(
        matmul_tn(ffn_rows[:, near], d_gate_low), matmul_tn(ffn_rows[:, far], d_gate_low).astype(LOW), 0
    )
    up_grad = scatter_sum(
        matmul_tn(ffn_rows[:, near], d_up_low), matmul_tn(ffn_rows[:, far], d_up_low).astype(LOW), 0
    )

    experts = jnp.arange(expert_count, dtype=jnp.int32)
    named = (all_routes[..., None] == experts).astype(FULL)
    hits = jnp.stack(
        [
            jnp.sum(named[:, :, :picks_each], axis=(0, 1, 2, 3)),
            jnp.sum(named[:, :, picks_each : 2 * picks_each], axis=(0, 1, 2, 3)),
        ]
    )
    share = hits / (all_tokens * picks_each)
    share_grad = AUX_WEIGHT * expert_count / all_tokens * share
    grad_half = cot_half.astype(FULL)
    d_normed2 = jnp.zeros((rows_here, half_width), FULL)
    ffn_mix_grad = []
    for pick in ffn_picks:
        d_normed2 = d_normed2 + matmul(pick, db_back)
        ffn_mix_grad.append(jnp.sum(pick.astype(FULL) * mix_grad_back, axis=1, keepdims=True))
    ffn_mix_grad = jnp.concatenate(ffn_mix_grad, axis=1)
    ffn_d_logits = logits_back(ffn_mix, ffn_mix_grad, ffn_probs, ffn_onehot, share_grad[1])
    d_normed2 = d_normed2 + through_router(ffn_d_logits, router2_half.astype(FULL))
    weighted2 = d_normed2 * gain2_half
    inner2 = tp_sum(jnp.sum(weighted2 * attended, axis=1, keepdims=True)) / features
    d_attended = grad_half + scale_two * weighted2 - attended * scale_two**3 * inner2
    gain2_part = jnp.sum(d_normed2 * attended * scale_two, axis=0)
    ffn_router_part = precise_tn(b_half.astype(FULL), ffn_d_logits)

    dy_slots = jnp.zeros((slots, half_width), FULL)
    for k in range(picks_each):
        dy_slots = dy_slots + matmul_tn(attn_picks[k], (attn_mix[:, k : k + 1] * d_attended).astype(LOW))
    dy_rows = send_out(dy_slots.astype(LOW), 4)
    d_heads = matmul_nt(dy_rows, out_full).astype(LOW)
    dq_low, dk_low, dv_low = attend_back(
        q_low, k_low, v_low, d_heads, log_sum, query_table, key_table, groups
    )
    out_grad = scatter_sum(
        matmul_tn(heads_low, dy_rows[:, near]), matmul_tn(heads_low, dy_rows[:, far]).astype(LOW), 1
    )
    query_grad = scatter_sum(
        matmul_tn(rows_in[:, near], dq_low), matmul_tn(rows_in[:, far], dq_low).astype(LOW), 0
    )
    dkv_low = jnp.concatenate([dk_low, dv_low], axis=1)
    da_rows = matmul_nt(dq_low, query_full).astype(LOW).reshape(groups, capacity, features)
    da_seq = jnp.einsum("bsr,bsd->brd", expert_onehot, da_rows, preferred_element_type=FULL)
    da_seq = da_seq.reshape(groups * rows_here, features) + matmul_nt(dkv_low, kv_full)
    da_half = send_home(da_seq.astype(LOW), 5, add_up=True)
    kv_part = scatter_sum(
        matmul_tn(a_seq[:, near], dkv_low), matmul_tn(a_seq[:, far], dkv_low).astype(LOW), 0
    )
    kv_grad = block_for(kv_part, 0)
    kv_part_low = kv_part.astype(LOW)
    for distance in far_first(groups):
        if distance:
            kv_grad = kv_grad + swap(block_for(kv_part_low, distance), "ctx", distance).astype(FULL)
    key_width = key_proj.shape[1]

    ffn_back = send_home(ffn_out, 6)
    result = attended
    for k in range(picks_each):
        result = result + ffn_mix[:, k : k + 1] * matmul(ffn_picks[k], ffn_back)
    result_low = result.astype(LOW)
    output = from_spread(join_halves(result_low, swap(result_low, "tp", 1)), 1)

    attn_mix_grad = tp_sum(
        jnp.concatenate(
            [jnp.sum(d_attended * picked, axis=1, keepdims=True) for picked in attn_picked], axis=1
        )
    )
    attn_d_logits = logits_back(attn_mix, attn_mix_grad, attn_probs, attn_onehot, share_grad[0])
    a_half = my_half(a_mine)
    attn_router_part = precise_tn(a_half.astype(FULL), attn_d_logits)

    d_normed1 = da_half + through_router(attn_d_logits, router1_half)
    gain1_half = my_half(gain1)
    weighted1 = d_normed1 * gain1_half
    inner1 = tp_sum(jnp.sum(weighted1 * input_half, axis=1, keepdims=True)) / features
    input_grad = d_attended + scale_one * weighted1 - input_half * scale_one**3 * inner1
    input_grad_low = input_grad.astype(LOW)
    input_grad = from_spread(join_halves(input_grad_low, swap(input_grad_low, "tp", 1)), 1).astype(FULL)
    gain1_part = jnp.sum(d_normed1 * input_half * scale_one, axis=0)

    small = jnp.concatenate(
        [gain1_part[None], gain2_part[None], attn_router_part.T, ffn_router_part.T], axis=0
    )
    small = from_spread(join_halves(small, swap(small, "tp", 1)), 1)
    prob_sums = jnp.concatenate([jnp.sum(attn_probs, axis=0), jnp.sum(ffn_probs, axis=0)])
    small = jnp.concatenate([small, jnp.pad(prob_sums, (0, features - prob_sums.shape[0]))[None]], axis=0)
    small = all_sum(small, ("ctx", "fsdp"))
    prob_sums = small[-1, : 2 * expert_count].reshape(2, expert_count)
    losses = expert_count * jnp.sum(share * prob_sums / all_tokens, axis=1)
    return (
        output,
        input_grad,
        losses[0],
        losses[1],
        small[0],
        small[1],
        small[2 : 2 + expert_count].T,
        small[2 + expert_count : 2 + 2 * expert_count].T,
        kv_grad[:, :key_width],
        kv_grad[:, key_width:],
        query_grad[None],
        out_grad[None],
        gate_grad[None],
        up_grad[None],
        down_grad[None],
    )


def solution(mesh):
    by_token = P(("fsdp", "ctx"), None)
    by_row = P(("fsdp", "ctx"), "tp")
    inward = P("ctx", "fsdp", "tp")
    outward = P("ctx", "tp", "fsdp")
    weights = (by_row, by_row, inward, outward, inward, inward, outward)
    return jax.shard_map(
        on_device,
        mesh=mesh,
        in_specs=(by_token,) * 4 + (P(),) * 4 + weights,
        out_specs=(by_token,) * 2 + (P(),) * 6 + weights,
        check_vma=False,
    )
```

```python
import functools
import math

import jax
import jax.numpy as jnp
import numpy as np
from jax import lax
from jax.experimental import pallas as pl
from jax.experimental.pallas import tpu as pltpu
from jax.sharding import PartitionSpec as P

HEAD = 128
EPSILON = 1e-06
ROPE_BASE = 10000.0
AUX_WEIGHT = 0.1
PRECISE = lax.Precision.HIGHEST
LOW = jnp.bfloat16
FULL = jnp.float32
VMEM_BYTES = 56 * 1024 * 1024


def matmul(lhs, rhs):
    return jnp.dot(lhs, rhs, preferred_element_type=FULL)


def matmul_tn(lhs, rhs):
    return lax.dot_general(lhs, rhs, (((0,), (0,)), ((), ())), preferred_element_type=FULL)


def matmul_nt(lhs, rhs):
    return lax.dot_general(lhs, rhs, (((1,), (1,)), ((), ())), preferred_element_type=FULL)


def precise_tn(lhs, rhs):
    return lax.dot_general(lhs, rhs, (((0,), (0,)), ((), ())), precision=PRECISE)


def swap(value, axis, distance):
    size = lax.axis_size(axis)
    return lax.ppermute(value, axis, [(i, i ^ distance) for i in range(size)])


def after(value, *earlier):
    return lax.optimization_barrier((value,) + earlier)[0]


def bits_down(size):
    bit = size // 2
    while bit >= 1:
        yield bit
        bit //= 2


def spread_order(size):
    order = [0]
    for bit in bits_down(size):
        order = order + [place | bit for place in order]
    return order


def gather_pieces(piece):
    pieces = [piece]
    for bit in bits_down(lax.axis_size("fsdp")):
        if bit > 1:
            pieces = pieces + [swap(item, "fsdp", bit) for item in pieces]
    return pieces


def with_neighbours(pieces, *earlier):
    return pieces + [swap(after(item, *earlier), "fsdp", 1) for item in pieces]


def flip_blocks(value, axis, index, count):
    parts = jnp.split(value, count, axis)
    for bit in bits_down(count):
        turned = (index // bit) % 2 == 1
        parts = [jnp.where(turned, parts[n ^ bit], parts[n]) for n in range(count)]
    return jnp.concatenate(parts, axis)


def to_spread(value, axis):
    size = lax.axis_size("fsdp")
    value = flip_blocks(value, axis, lax.axis_index("fsdp"), size)
    parts = jnp.split(value, size, axis)
    return jnp.concatenate([parts[place] for place in spread_order(size)], axis)


def from_spread(value, axis):
    size = lax.axis_size("fsdp")
    parts = jnp.split(value, size, axis)
    order = spread_order(size)
    value = jnp.concatenate([parts[order.index(place)] for place in range(size)], axis)
    return flip_blocks(value, axis, lax.axis_index("fsdp"), size)


def my_half(value):
    width = value.shape[-1] // 2
    return jnp.where(lax.axis_index("tp") == 0, value[..., :width], value[..., width:])


def other_half(value):
    width = value.shape[-1] // 2
    return jnp.where(lax.axis_index("tp") == 0, value[..., width:], value[..., :width])


def join_halves(mine, other):
    first = lax.axis_index("tp") == 0
    return jnp.concatenate([jnp.where(first, mine, other), jnp.where(first, other, mine)], -1)


def tp_sum(value):
    return value + swap(value, "tp", 1)


def all_sum(value, axes):
    for axis in axes:
        for bit in bits_down(lax.axis_size(axis)):
            value = value + swap(value, axis, bit)
    return value


def far_first(size):
    return list(range(size // 2, size)) + list(range(size // 2 - 1, -1, -1))


def place_blocks(blocks):
    index = lax.axis_index("ctx")
    rows = blocks[0].shape[0]
    total = jnp.zeros((rows * len(blocks),) + blocks[0].shape[1:], blocks[0].dtype)
    for distance, block in enumerate(blocks):
        total = lax.dynamic_update_slice_in_dim(total, block, (index ^ distance) * rows, 0)
    return total


def block_for(value, distance):
    size = lax.axis_size("ctx")
    rows = value.shape[0] // size
    return lax.dynamic_slice_in_dim(value, (lax.axis_index("ctx") ^ distance) * rows, rows, 0)


def spread_out(half_rows):
    size = lax.axis_size("ctx")
    blocks = [None] * size
    for distance in far_first(size):
        block = block_for(half_rows, distance)
        if distance:
            block = swap(block, "ctx", distance)
        blocks[distance] = join_halves(block, swap(block, "tp", 1))
    return place_blocks(blocks)


def come_home(partial_rows):
    size = lax.axis_size("ctx")
    blocks = [None] * size
    for distance in far_first(size):
        block = block_for(partial_rows, distance)
        arrived = swap(other_half(block), "tp", 1)
        block = (my_half(block).astype(FULL) + arrived.astype(FULL)).astype(LOW)
        blocks[distance] = swap(block, "ctx", distance) if distance else block
    return place_blocks(blocks)


def xor_index(index, distance):
    result = index
    bit = 1
    while bit <= distance:
        if distance & bit:
            result = result + bit - 2 * bit * ((index // bit) % 2)
        bit *= 2
    return result


def span(start, size):
    return pl.ds(pl.multiple_of(start * size, 16), size)


def meet(peers):
    barrier = pltpu.get_barrier_semaphore()
    for device in peers:
        pl.semaphore_signal(barrier, inc=1, device_id=device, device_id_type=pl.DeviceIdType.MESH)
    pl.semaphore_wait(barrier, len(peers))


def remote(source, target, sems, index, device):
    return pltpu.make_async_remote_copy(
        src_ref=source,
        dst_ref=target,
        send_sem=sems[0].at[index],
        recv_sem=sems[1].at[index],
        device_id=device,
        device_id_type=pl.DeviceIdType.MESH,
    )


def near_first(size):
    return list(range(1, size))


def mixed_order(size):
    return [distance for distance in spread_order(size) if distance] + [0]


def send_out_kernel(size, rows_ref, out_ref, z_land, y_land, z_send, z_recv, y_send, y_recv):
    mine, first = lax.axis_index("ctx"), lax.axis_index("tp") == 0
    other_tp = {"tp": 1 - lax.axis_index("tp")}
    rows, width = z_land.shape[1], z_land.shape[2]
    at = [xor_index(mine, distance) for distance in range(size)]
    meet([{"ctx": at[distance]} for distance in range(1, size)] + [other_tp])
    order = near_first(size)
    across, beside = {}, {}
    for distance in order:
        across[distance] = remote(
            rows_ref.at[span(at[distance], rows)],
            z_land.at[distance],
            (z_send, z_recv),
            distance,
            {"ctx": at[distance]},
        )
        across[distance].start()
    beside[0] = remote(rows_ref.at[span(mine, rows)], y_land.at[0], (y_send, y_recv), 0, other_tp)
    beside[0].start()
    for distance in order:
        across[distance].wait_recv()
        beside[distance] = remote(
            z_land.at[distance], y_land.at[distance], (y_send, y_recv), distance, other_tp
        )
        beside[distance].start()
    for distance in [0] + order:
        beside[distance].wait_recv()
        own = z_land[distance] if distance else rows_ref[span(mine, rows), :]
        theirs = y_land[distance]
        out_ref[span(at[distance], rows), :width] = jnp.where(first, own, theirs)
        out_ref[span(at[distance], rows), width:] = jnp.where(first, theirs, own)
    for distance in order:
        across[distance].wait_send()
    for distance in [0] + order:
        beside[distance].wait_send()


def send_out(half_rows, number):
    size = lax.axis_size("ctx")
    total, width = half_rows.shape
    land = pltpu.VMEM((size, total // size, width), half_rows.dtype)
    return pl.pallas_call(
        functools.partial(send_out_kernel, size),
        in_specs=[pl.BlockSpec(memory_space=pltpu.VMEM)],
        out_specs=pl.BlockSpec(memory_space=pltpu.VMEM),
        out_shape=jax.ShapeDtypeStruct((total, 2 * width), half_rows.dtype),
        scratch_shapes=[land, land] + [pltpu.SemaphoreType.DMA((size,))] * 4,
        compiler_params=pltpu.CompilerParams(
            collective_id=number, has_side_effects=True, vmem_limit_bytes=VMEM_BYTES
        ),
        cost_estimate=pl.CostEstimate(flops=0, bytes_accessed=12 * total * width, transcendentals=0),
    )(half_rows)


def send_home_kernel(size, add_up, has_extra, cargoes, *refs):
    part_ref, refs = refs[0], refs[1:]
    extra_ref, refs = (refs[0], refs[1:]) if has_extra else (None, refs)
    cargo_in, refs = refs[:cargoes], refs[cargoes:]
    out_ref, refs = refs[0], refs[1:]
    extra_out, refs = (refs[0], refs[1:]) if has_extra else (None, refs)
    cargo_out, refs = refs[:cargoes], refs[cargoes:]
    y_land, ready, z_land, y_send, y_recv, z_send, z_recv = refs[:7]
    mine, first = lax.axis_index("ctx"), lax.axis_index("tp") == 0
    place = lax.axis_index("tp")
    other_tp = {"tp": 1 - place}
    rows, width = z_land.shape[1], z_land.shape[2]
    at = [xor_index(mine, distance) for distance in range(size)]
    columns = pl.ds(pl.multiple_of((1 - place) * width, 128), width)
    world = lax.axis_size("fsdp")
    along = [{"fsdp": xor_index(lax.axis_index("fsdp"), world // 2)}] if cargoes else []
    meet([{"ctx": at[distance]} for distance in range(1, size)] + [other_tp] + along)
    order = mixed_order(size)
    beside, across, extras = {}, {}, {}
    cargo = [
        remote(cargo_in[n], cargo_out[n], refs[-2:], n, along[0]) for n in range(cargoes)
    ]
    for copy in cargo:
        copy.start()
    if has_extra:
        ey_land, e_ready, ez_land, ey_send, ey_recv, ez_send, ez_recv = refs[7:14]
        extra_beside = remote(extra_ref, ey_land, (ey_send, ey_recv), 0, other_tp)
        extra_beside.start()
    for distance in order:
        beside[distance] = remote(
            part_ref.at[span(at[distance], rows), columns],
            y_land.at[distance],
            (y_send, y_recv),
            distance,
            other_tp,
        )
        beside[distance].start()
    if has_extra:
        extra_beside.wait_recv()
        e_ready[...] = extra_ref[...] + ey_land[...]
        for distance in order:
            if distance:
                extras[distance] = remote(
                    e_ready.at[at[distance]],
                    ez_land.at[distance],
                    (ez_send, ez_recv),
                    distance,
                    {"ctx": at[distance]},
                )
                extras[distance].start()
    for distance in order:
        beside[distance].wait_recv()
        whole = part_ref[span(at[distance], rows), :]
        own = jnp.where(first, whole[:, :width], whole[:, width:])
        total = (own.astype(FULL) + y_land[distance].astype(FULL)).astype(LOW)
        if distance:
            ready[distance] = total
            across[distance] = remote(
                ready.at[distance],
                z_land.at[distance],
                (z_send, z_recv),
                distance,
                {"ctx": at[distance]},
            )
            across[distance].start()
        elif add_up:
            out_ref[...] = total.astype(FULL)
        else:
            out_ref[span(mine, rows), :] = total
    for distance in order:
        if distance:
            across[distance].wait_recv()
            if add_up:
                out_ref[...] += z_land[distance].astype(FULL)
            else:
                out_ref[span(at[distance], rows), :] = z_land[distance]
    if has_extra:
        extra_out[mine] = e_ready[mine]
        for distance in order:
            if distance:
                extras[distance].wait_recv()
                extra_out[at[distance]] = ez_land[distance]
                extras[distance].wait_send()
        extra_beside.wait_send()
    for distance in order:
        beside[distance].wait_send()
        if distance:
            across[distance].wait_send()
    for copy in cargo:
        copy.wait()


def send_home(partial_rows, number, extra=None, cargo=(), add_up=False):
    size = lax.axis_size("ctx")
    total, width = partial_rows.shape[0], partial_rows.shape[1] // 2
    rows = total // size
    land = pltpu.VMEM((size, rows, width), LOW)
    sems = [pltpu.SemaphoreType.DMA((size,))] * 4
    shapes = [jax.ShapeDtypeStruct((rows, width), FULL) if add_up else jax.ShapeDtypeStruct((total, width), LOW)]
    operands, scratch = [partial_rows], [land, land, land] + sems
    if extra is not None:
        operands.append(extra)
        shapes.append(jax.ShapeDtypeStruct(extra.shape, FULL))
        scratch += [pltpu.VMEM(extra.shape, FULL)] * 3 + sems
    in_specs = [pl.BlockSpec(memory_space=pltpu.VMEM)] * len(operands)
    out_specs = [pl.BlockSpec(memory_space=pltpu.VMEM)] * len(shapes)
    for item in cargo:
        operands.append(item)
        shapes.append(jax.ShapeDtypeStruct(item.shape, item.dtype))
        in_specs.append(pl.BlockSpec(memory_space=pl.ANY))
        out_specs.append(pl.BlockSpec(memory_space=pl.ANY))
    if cargo:
        scratch += [pltpu.SemaphoreType.DMA((len(cargo),))] * 2
    results = pl.pallas_call(
        functools.partial(send_home_kernel, size, add_up, extra is not None, len(cargo)),
        in_specs=in_specs,
        out_specs=out_specs,
        out_shape=shapes,
        scratch_shapes=scratch,
        compiler_params=pltpu.CompilerParams(
            collective_id=number, has_side_effects=True, vmem_limit_bytes=VMEM_BYTES
        ),
        cost_estimate=pl.CostEstimate(flops=0, bytes_accessed=12 * total * width, transcendentals=0),
    )(*operands)
    return results if len(shapes) > 1 else results[0]


def prologue_kernel(sizes, *refs):
    groups, world = sizes
    half_in, own_in, routes_in, kv_in, query_in, out_in = refs[:6]
    seq_ref, routes_ref, kv_ref, query_ref, out_ref = refs[6:11]
    local_sem = refs[11]
    pairs = [(refs[12 + 2 * n], refs[13 + 2 * n]) for n in range(15)]
    token_line, route_line, kv_line, token_pass, kv_pass = (pairs[2 * n : 2 * n + 2] for n in range(5))
    kv_own, fr, fk, fq, fo = pairs[10:]
    mine, place, spot = lax.axis_index("ctx"), lax.axis_index("tp"), lax.axis_index("fsdp")
    other_tp = {"tp": 1 - place}
    rows, width = half_in.shape
    sub = kv_in.shape[0]
    piece = sub * groups
    q_rows = query_in.shape[0]
    steps = list(bits_down(world))
    beside = {bit: {"fsdp": xor_index(spot, bit)} for bit in steps}
    first = steps[0]
    meet(
        [{"ctx": xor_index(mine, distance)} for distance in range(1, groups)]
        + [other_tp]
        + [beside[bit] for bit in steps]
    )
    locals_ = [
        pltpu.make_async_copy(
            own_in.at[:, pl.ds(n * width, width)], seq_ref.at[n, span(mine, rows)], local_sem.at[n]
        )
        for n in range(2)
    ] + [
        pltpu.make_async_copy(routes_in, routes_ref.at[0, mine], local_sem.at[2]),
        pltpu.make_async_copy(kv_in, kv_ref.at[span(mine, sub)], local_sem.at[3]),
        pltpu.make_async_copy(query_in, query_ref.at[pl.ds(0, q_rows)], local_sem.at[4]),
        pltpu.make_async_copy(out_in, out_ref.at[0], local_sem.at[5]),
    ]
    started, landed = [], set()

    def go(copy):
        copy.start()
        started.append(copy)
        return copy

    def arrived(copy):
        if id(copy) not in landed:
            copy.wait_recv()
            landed.add(id(copy))

    def wrap(index):
        return lax.rem(index + groups, groups)

    def outgoing(step):
        yield 0, jnp.logical_and(mine < groups - 1, mine >= step), wrap(mine - step), wrap(mine + 1)
        yield 1, jnp.logical_and(mine > 0, mine + step < groups), wrap(mine + step), wrap(mine - 1)

    def incoming(step):
        yield 0, mine >= step + 1, wrap(mine - 1 - step)
        yield 1, mine + step + 1 < groups, wrap(mine + 1 + step)

    def line_copy(own, place_of, sems, step, way, block, target):
        source = place_of(block) if step else own
        return remote(source, place_of(block), sems[way], step, {"ctx": target})

    def line_start(own, place_of, sems, step):
        for way, happens, block, target in outgoing(step):

            @pl.when(happens)
            def _():
                line_copy(own, place_of, sems, step, way, block, target).start()

    def line_wait(place_of, sems, step, passed):
        for way, happens, block in incoming(step):

            @pl.when(happens)
            def _():
                remote(place_of(block), place_of(block), sems[way], step, other_tp).wait_recv()
                if passed is not None:
                    passed(step, way, block).start()

    def line_end(own, place_of, sems, step, passed):
        for way, happens, block, target in outgoing(step):

            @pl.when(happens)
            def _():
                line_copy(own, place_of, sems, step, way, block, target).wait_send()

        if passed is None:
            return
        for way, happens, block in incoming(step):

            @pl.when(happens)
            def _():
                passed(step, way, block).wait_send()

    def passed_wait(step, passed):
        for way, happens, block in incoming(step):

            @pl.when(happens)
            def _():
                passed(step, way, block).wait_recv()

    route_place = lambda n: routes_ref.at[0, n]
    kv_place = lambda n: kv_ref.at[span(n, sub)]
    token_place = lambda n: seq_ref.at[place, span(n, rows)]

    def kv_along(step, way, block):
        target = kv_ref.at[pl.ds(pl.multiple_of(piece + block * sub, 16), sub)]
        return remote(kv_place(block), target, kv_pass[way], step, beside[first])

    def token_along(step, way, block):
        return remote(token_place(block), token_place(block), token_pass[way], step, other_tp)

    def token_landed(step, way, block):
        view = seq_ref.at[1 - place, span(block, rows)]
        return remote(view, view, token_pass[way], step, other_tp)

    kv_first = go(
        remote(
            kv_in,
            kv_ref.at[pl.ds(pl.multiple_of(piece + mine * sub, 16), sub)],
            kv_own,
            0,
            beside[first],
        )
    )
    query_view = lambda n: query_ref.at[pl.ds(n * q_rows, q_rows)]
    out_view = lambda n: out_ref.at[n]
    kv_view = lambda n: kv_ref.at[pl.ds(n * piece, piece)]
    query_copies = {1: go(remote(query_in, query_view(1), fq, 1, beside[first]))}
    out_copies = {}
    for copy in locals_:
        copy.start()
    for step in range(groups - 1):
        line_start(kv_in, kv_place, kv_line, step)
        line_start(routes_in, route_place, route_line, step)
        line_start(half_in, token_place, token_line, step)
        if step == 0:
            for copy in locals_:
                copy.wait()
            for bit in steps[1:]:
                n = world // (2 * bit)
                query_copies[n] = go(remote(query_in, query_view(n), fq, n, beside[bit]))
                out_copies[n] = go(remote(out_in, out_view(n), fo, n, beside[bit]))
        line_wait(kv_place, kv_line, step, kv_along)
        if step == groups - 2:
            out_copies[1] = go(remote(out_in, out_view(1), fo, 1, beside[first]))
        line_wait(route_place, route_line, step, None)
        line_wait(token_place, token_line, step, token_along)
    route_wait, kv_wait = {}, {}
    count = 1
    for bit in steps:
        for n in range(count):
            peer = beside[bit]
            if n in route_wait:
                arrived(route_wait[n])
            route_wait[count + n] = go(
                remote(routes_ref.at[n], routes_ref.at[count + n], fr, count + n, peer)
            )
            if bit == first:
                continue
            if n:
                arrived(query_copies[n])
                query_copies[count + n] = go(
                    remote(query_view(n), query_view(count + n), fq, count + n, peer)
                )
            if n == 1 and count == 2:
                arrived(kv_first)
                for step in range(groups - 1):
                    passed_wait(step, kv_along)
            if n > 1:
                arrived(kv_wait[n])
            kv_wait[count + n] = go(remote(kv_view(n), kv_view(count + n), fk, count + n, peer))
            if n:
                arrived(out_copies[n])
                out_copies[count + n] = go(remote(out_view(n), out_view(count + n), fo, count + n, peer))
        count *= 2
    if world == 2:
        arrived(kv_first)
        for step in range(groups - 1):
            passed_wait(step, kv_along)
    for copy in started:
        arrived(copy)
    for step in range(groups - 1):
        passed_wait(step, token_landed)
        line_end(kv_in, kv_place, kv_line, step, kv_along)
        line_end(routes_in, route_place, route_line, step, None)
        line_end(half_in, token_place, token_line, step, token_along)
    for copy in started:
        copy.wait_send()


def prologue(token_half, token_rows, routes, kv_rows, query_piece, out_piece, number):
    groups, world = lax.axis_size("ctx"), lax.axis_size("fsdp")
    any_space = pl.BlockSpec(memory_space=pl.ANY)
    rows, features = token_rows.shape
    pair = lambda count: [pltpu.SemaphoreType.DMA((count,))] * 2
    return pl.pallas_call(
        functools.partial(prologue_kernel, (groups, world)),
        in_specs=[pl.BlockSpec(memory_space=pltpu.VMEM)] * 6,
        out_specs=[any_space] * 5,
        out_shape=[
            jax.ShapeDtypeStruct((2, groups * rows, features // 2), LOW),
            jax.ShapeDtypeStruct((world, groups) + routes.shape, jnp.int32),
            jax.ShapeDtypeStruct((world * groups * kv_rows.shape[0], kv_rows.shape[1]), LOW),
            jax.ShapeDtypeStruct((world * query_piece.shape[0], query_piece.shape[1]), LOW),
            jax.ShapeDtypeStruct((world,) + out_piece.shape, LOW),
        ],
        scratch_shapes=[pltpu.SemaphoreType.DMA((6,))] + pair(groups) * 10 + pair(1) + pair(world) * 4,
        compiler_params=pltpu.CompilerParams(
            collective_id=number, has_side_effects=True, vmem_limit_bytes=VMEM_BYTES
        ),
        cost_estimate=pl.CostEstimate(flops=0, bytes_accessed=100000000, transcendentals=0),
    )(token_half, token_rows, routes, kv_rows, query_piece, out_piece)


def expert_kernel(world, *refs):
    rows_ref, cot_ref, mix_ref = refs[:3]
    gates, ups, downs = (refs[3 + n * world : 3 + (n + 1) * world] for n in range(3))
    hidden_ref, d_gate_ref, d_up_ref, db_ref, out_ref, mix_grad_ref = refs[3 + 3 * world : 9 + 3 * world]
    db_sum, out_sum = refs[9 + 3 * world :]
    step = pl.program_id(0)
    width = rows_ref.shape[1] // world

    @pl.when(step == 0)
    def _():
        db_sum[...] = jnp.zeros_like(db_sum)
        out_sum[...] = jnp.zeros_like(out_sum)
        mix_grad_ref[...] = jnp.zeros_like(mix_grad_ref)

    gate_lin, up_lin, d_hidden = None, None, None
    for n in range(world):
        columns = slice(n * width, (n + 1) * width)
        terms = (
            matmul(rows_ref[:, columns], gates[n][...]),
            matmul(rows_ref[:, columns], ups[n][...]),
            matmul_nt(cot_ref[:, columns], downs[n][...]),
        )
        if n:
            terms = (gate_lin + terms[0], up_lin + terms[1], d_hidden + terms[2])
        gate_lin, up_lin, d_hidden = terms
    sigmoid_gate = 1.0 / (1.0 + jnp.exp(-gate_lin))
    swish = gate_lin * sigmoid_gate
    hidden = swish * up_lin
    mix_grad_ref[...] += jnp.broadcast_to(
        jnp.sum(hidden * d_hidden, axis=1, keepdims=True), mix_grad_ref.shape
    )
    d_gated = d_hidden * mix_ref[:, :1]
    hidden_low = hidden.astype(LOW)
    d_gate = (d_gated * up_lin * sigmoid_gate * (1.0 + gate_lin * (1.0 - sigmoid_gate))).astype(LOW)
    d_up = (d_gated * swish).astype(LOW)
    hidden_ref[...] = hidden_low
    d_gate_ref[...] = d_gate
    d_up_ref[...] = d_up
    for n in range(world):
        columns = slice(n * width, (n + 1) * width)
        out_sum[:, columns] += matmul(hidden_low, downs[n][...])
        db_sum[:, columns] += matmul_nt(d_gate, gates[n][...]) + matmul_nt(d_up, ups[n][...])

    @pl.when(step == pl.num_programs(0) - 1)
    def _():
        db_ref[...] = db_sum[...].astype(LOW)
        out_ref[...] = out_sum[...].astype(LOW)


def expert_both_ways(rows, cot_rows, mix_rows, gate_pieces, up_pieces, down_pieces):
    world = len(gate_pieces)
    slots, features = rows.shape
    depth, hidden_width = gate_pieces[0].shape
    tile = 256
    once = pl.Buffered(1)
    whole = lambda width: pl.BlockSpec((slots, width), lambda i: (0, 0), pipeline_mode=once)
    kept = lambda width: pl.BlockSpec((slots, width), lambda i: (0, 0))
    tall = pl.BlockSpec((depth, tile), lambda i: (0, i))
    flat = pl.BlockSpec((tile, depth), lambda i: (i, 0))
    strip = pl.BlockSpec((slots, tile), lambda i: (0, i))
    low = lambda width: jax.ShapeDtypeStruct((slots, width), LOW)
    return pl.pallas_call(
        functools.partial(expert_kernel, world),
        grid=(hidden_width // tile,),
        in_specs=[whole(features), whole(features), whole(HEAD)]
        + [tall] * (2 * world)
        + [flat] * world,
        out_specs=[strip] * 3 + [kept(features)] * 2 + [kept(HEAD)],
        out_shape=[low(hidden_width)] * 3
        + [low(features)] * 2
        + [jax.ShapeDtypeStruct((slots, HEAD), FULL)],
        scratch_shapes=[pltpu.VMEM((slots, features), FULL)] * 2,
        compiler_params=pltpu.CompilerParams(vmem_limit_bytes=VMEM_BYTES),
        cost_estimate=pl.CostEstimate(
            flops=12 * slots * features * hidden_width,
            bytes_accessed=6 * features * hidden_width,
            transcendentals=slots * hidden_width,
        ),
    )(rows, cot_rows, mix_rows, *gate_pieces, *up_pieces, *down_pieces)


def scatter_start(product, features, first_dim):
    pieces = lax.axis_size("fsdp")
    high, bit, arrived = features, 1, []

    def part(low, high):
        total = product(low, high)
        for block in arrived:
            total = total + lax.slice_in_dim(block, low, high, axis=first_dim).astype(FULL)
        return total

    while True:
        sent = part(high // 2, high).astype(LOW)
        high //= 2
        if 2 * bit >= pieces:
            break
        arrived.append(swap(sent, "fsdp", bit))
        bit *= 2

    def finish(last):
        arrived.append(last)
        return part(0, high)

    return sent, finish


def last_step(sent):
    return swap(sent, "fsdp", lax.axis_size("fsdp") // 2)


def turn_tables(length):
    half_head = HEAD // 2
    steps = np.arange(half_head, dtype=np.float32) * np.float32(2.0 / HEAD)
    frequency = np.power(np.float32(ROPE_BASE), -steps).astype(np.float32)
    angles = np.arange(length, dtype=np.float32)[:, None] * frequency[None, :]
    cosine = np.cos(angles.astype(np.float64)).astype(np.float32)
    sine = np.sin(angles.astype(np.float64)).astype(np.float32)
    return np.concatenate([cosine, cosine, -sine, sine], axis=1)


def turn(value, table):
    return value * table[:, :HEAD] + pltpu.roll(value, HEAD // 2, 1) * table[:, HEAD:]


def turn_back(value, table):
    return value * table[:, :HEAD] - pltpu.roll(value, HEAD // 2, 1) * table[:, HEAD:]


def attend_kernel(
    groups, scale, q_lin, k_lin, v_lin, q_table, k_table, q_low, k_low, v_low, heads, log_sum
):
    q_low[...] = turn(q_lin[...], q_table[...]).astype(LOW)
    k_low[...] = turn(k_lin[...], k_table[...]).astype(LOW)
    v_low[...] = v_lin[...].astype(LOW)
    rows = q_low.shape[0] // groups
    block = k_low.shape[0] // groups
    for group in range(groups):
        span = slice(group * rows, (group + 1) * rows)
        seen = slice(0, (group + 1) * block)
        scores = matmul_nt(q_low[span, :], k_low[seen, :]) * scale
        top = jnp.max(scores, axis=1, keepdims=True)
        weights = jnp.exp(scores - top)
        total = jnp.sum(weights, axis=1, keepdims=True)
        weights = (weights * (1.0 / total)).astype(LOW)
        heads[span, :] = matmul(weights, v_low[seen, :]).astype(LOW)
        log_sum[span, :] = jnp.broadcast_to(top + jnp.log(total), (rows, HEAD))


def attend(query_lin, kv_lin, query_table, key_table, groups):
    slots, width = query_lin.shape
    length = kv_lin.shape[0]
    count = width // HEAD
    by_head = lambda rows: pl.BlockSpec((rows, HEAD), lambda h: (0, h))
    whole = lambda rows: pl.BlockSpec((rows, 2 * HEAD), lambda h: (0, 0))
    return pl.pallas_call(
        functools.partial(attend_kernel, groups, 1.0 / math.sqrt(HEAD)),
        grid=(count,),
        in_specs=[
            by_head(slots),
            by_head(length),
            pl.BlockSpec((length, HEAD), lambda h: (0, h + count)),
            whole(slots),
            whole(length),
        ],
        out_specs=[by_head(slots), by_head(length), by_head(length), by_head(slots), by_head(slots)],
        out_shape=[
            jax.ShapeDtypeStruct((slots, width), LOW),
            jax.ShapeDtypeStruct((length, width), LOW),
            jax.ShapeDtypeStruct((length, width), LOW),
            jax.ShapeDtypeStruct((slots, width), LOW),
            jax.ShapeDtypeStruct((slots, width), FULL),
        ],
        compiler_params=pltpu.CompilerParams(vmem_limit_bytes=VMEM_BYTES),
        cost_estimate=pl.CostEstimate(
            flops=0, bytes_accessed=20 * length * width, transcendentals=0
        ),
    )(query_lin, kv_lin, kv_lin, query_table, key_table)


def attend_back_kernel(
    groups, scale, q_low, k_low, v_low, d_heads, log_sum, q_table, k_table, dq, dk, dv, dk_sum, dv_sum
):
    dk_sum[...] = jnp.zeros_like(dk_sum)
    dv_sum[...] = jnp.zeros_like(dv_sum)
    rows = q_low.shape[0] // groups
    block = k_low.shape[0] // groups
    for group in range(groups):
        span = slice(group * rows, (group + 1) * rows)
        seen = slice(0, (group + 1) * block)
        query, keys = q_low[span, :], k_low[seen, :]
        grads = d_heads[span, :]
        scores = matmul_nt(query, keys) * scale
        weights = jnp.exp(scores - log_sum[span, :1])
        d_weights = matmul_nt(grads, v_low[seen, :])
        delta = jnp.sum(weights * d_weights, axis=1, keepdims=True)
        d_scores = (weights * (d_weights - delta)).astype(LOW)
        dq[span, :] = turn_back(matmul(d_scores, keys) * scale, q_table[span, :]).astype(LOW)
        dk_sum[seen, :] += matmul_tn(d_scores, query) * scale
        dv_sum[seen, :] += matmul_tn(weights.astype(LOW), grads)
    dk[...] = turn_back(dk_sum[...], k_table[...]).astype(LOW)
    dv[...] = dv_sum[...].astype(LOW)


def attend_back(q_low, k_low, v_low, d_heads, log_sum, query_table, key_table, groups):
    slots, width = q_low.shape
    length = k_low.shape[0]
    count = width // HEAD
    by_head = lambda rows: pl.BlockSpec((rows, HEAD), lambda h: (0, h))
    whole = lambda rows: pl.BlockSpec((rows, 2 * HEAD), lambda h: (0, 0))
    return pl.pallas_call(
        functools.partial(attend_back_kernel, groups, 1.0 / math.sqrt(HEAD)),
        grid=(count,),
        in_specs=[
            by_head(slots),
            by_head(length),
            by_head(length),
            by_head(slots),
            by_head(slots),
            whole(slots),
            whole(length),
        ],
        out_specs=[by_head(slots), by_head(length), by_head(length)],
        out_shape=[
            jax.ShapeDtypeStruct((slots, width), LOW),
            jax.ShapeDtypeStruct((length, width), LOW),
            jax.ShapeDtypeStruct((length, width), LOW),
        ],
        scratch_shapes=[pltpu.VMEM((length, HEAD), FULL), pltpu.VMEM((length, HEAD), FULL)],
        compiler_params=pltpu.CompilerParams(vmem_limit_bytes=VMEM_BYTES),
        cost_estimate=pl.CostEstimate(
            flops=0, bytes_accessed=14 * length * width, transcendentals=0
        ),
    )(q_low, k_low, v_low, d_heads, log_sum, query_table, key_table)


def chosen_picks(routes, expert_count, capacity):
    experts = jnp.arange(expert_count, dtype=jnp.int32)
    onehot = (routes[:, :, None] == experts[None, None, :]).astype(jnp.int32)
    rows = routes.shape[0]
    below = (jnp.arange(rows)[:, None] > jnp.arange(rows)[None, :]).astype(LOW)
    order = matmul(below, jnp.sum(onehot, axis=1).astype(LOW)).astype(jnp.int32)
    slot = routes * capacity + jnp.sum(onehot * order[:, None, :], axis=2)
    slots = jnp.arange(expert_count * capacity, dtype=jnp.int32)
    picks = [(slot[:, k : k + 1] == slots[None, :]).astype(LOW) for k in range(routes.shape[1])]
    return picks, onehot.astype(FULL)


def expert_picks(routes_seq, expert, capacity):
    named = jnp.any(routes_seq == expert, axis=1)
    rows = named.shape[1]
    above = (jnp.arange(rows)[:, None] < jnp.arange(rows)[None, :]).astype(LOW)
    order = matmul(named.astype(LOW), above).astype(jnp.int32)
    slot = jnp.where(named, order, -1)
    return (slot[:, None, :] == jnp.arange(capacity, dtype=jnp.int32)[None, :, None]).astype(LOW)


def mix_of(logits, onehot):
    chosen = jnp.sum(onehot * logits[:, None, :], axis=2)
    return jax.nn.softmax(chosen, axis=1)


def logits_back(mix, mix_grad, probs, onehot, share_grad):
    d_chosen = mix * (mix_grad - jnp.sum(mix * mix_grad, axis=1, keepdims=True))
    d_logits = jnp.sum(onehot * d_chosen[:, :, None], axis=1)
    inner = jnp.sum(probs * share_grad[None, :], axis=1, keepdims=True)
    return d_logits + probs * (share_grad[None, :] - inner)


def through_router(d_logits, router_half):
    total = d_logits[:, 0:1] * router_half[:, 0][None, :]
    for expert in range(1, d_logits.shape[1]):
        total = total + d_logits[:, expert : expert + 1] * router_half[:, expert][None, :]
    return total


def on_device(
    tokens,
    cotangent,
    attn_routes,
    ffn_routes,
    norm_gain1,
    norm_gain2,
    attn_router,
    ffn_router,
    key_proj,
    value_proj,
    query_proj,
    out_proj,
    gate_proj,
    up_proj,
    down_proj,
):
    rows_here, features = tokens.shape
    half_width = features // 2
    picks_each = attn_routes.shape[1]
    expert_count = attn_router.shape[1]
    groups = lax.axis_size("ctx")
    mine = lax.axis_index("ctx")
    capacity = rows_here * picks_each // expert_count * 5 // 4
    slots = groups * capacity
    all_tokens = rows_here * lax.axis_size("fsdp") * groups

    tokens_spread = to_spread(tokens, 1)
    token_half = my_half(tokens_spread)
    routes_mine = jnp.concatenate([attn_routes.T, ffn_routes.T], axis=0)
    routes_mine = jnp.concatenate([routes_mine, jnp.zeros_like(routes_mine)], axis=0)
    kv_mine = jnp.concatenate([key_proj, value_proj], axis=1)
    seq_low, all_routes, kv_full, query_full, out_pieces = prologue(
        token_half, tokens_spread, routes_mine, kv_mine, query_proj[0], out_proj[0], 0
    )
    seq_routes = all_routes[0]
    seq_tokens = jnp.concatenate([seq_low[0], seq_low[1]], axis=1).astype(FULL)
    out_full = jnp.concatenate([out_pieces[n] for n in range(lax.axis_size("fsdp"))], axis=1)

    gate_pieces = gather_pieces(after(gate_proj[0], all_routes))
    up_pieces = gather_pieces(after(up_proj[0], all_routes))
    down_pieces = gather_pieces(after(down_proj[0], all_routes))

    gain1 = to_spread(norm_gain1, 0)
    gain2_half = my_half(to_spread(norm_gain2, 0))
    router1 = to_spread(attn_router, 0)
    router2 = to_spread(ffn_router, 0)
    router1_half = my_half(router1.T).T.astype(FULL)
    router2_half = my_half(router2.T).T

    scale_seq = lax.rsqrt(jnp.mean(seq_tokens * seq_tokens, axis=1, keepdims=True) + EPSILON)
    a_seq = (seq_tokens * scale_seq * gain1).astype(LOW)
    a_mine = lax.dynamic_slice_in_dim(a_seq, mine * rows_here, rows_here, 0)
    scale_one = lax.dynamic_slice_in_dim(scale_seq, mine * rows_here, rows_here, 0)
    attn_logits = matmul(a_mine, router1)
    attn_probs = jax.nn.softmax(attn_logits, axis=1)
    attn_picks, attn_onehot = chosen_picks(attn_routes, expert_count, capacity)
    ffn_picks, ffn_onehot = chosen_picks(ffn_routes, expert_count, capacity)
    attn_mix = mix_of(attn_logits, attn_onehot)

    cot_half = my_half(to_spread(cotangent, 1))
    ffn_pick = ffn_picks[0]
    for pick in ffn_picks[1:]:
        ffn_pick = ffn_pick + pick
    cot_rows = spread_out(after(matmul_tn(ffn_pick, cot_half).astype(LOW), all_routes))

    expert_onehot = expert_picks(seq_routes[:, :picks_each], mine, capacity)
    key_table = jnp.asarray(turn_tables(groups * rows_here))
    query_table = jnp.einsum(
        "bsr,brh->bsh",
        expert_onehot.astype(FULL),
        key_table.reshape(groups, rows_here, -1),
        precision=PRECISE,
    ).reshape(slots, -1)
    rows_in = (
        jnp.einsum(
            "bsr,brd->bsd",
            expert_onehot,
            a_seq.reshape(groups, rows_here, features),
            preferred_element_type=FULL,
        )
        .astype(LOW)
        .reshape(slots, features)
    )
    query_lin = matmul(rows_in, query_full)
    kv_lin = matmul(a_seq, kv_full)
    q_low, k_low, v_low, heads_low, log_sum = attend(
        query_lin, kv_lin, query_table, key_table, groups
    )
    attn_back = send_home(after(matmul(heads_low, out_full).astype(LOW), cot_rows), 1)

    input_half = my_half(tokens_spread).astype(FULL)
    attn_picked = [matmul(pick, attn_back) for pick in attn_picks]
    attended = input_half
    for k in range(picks_each):
        attended = attended + attn_mix[:, k : k + 1] * attn_picked[k]
    square_sum = tp_sum(jnp.sum(attended * attended, axis=1, keepdims=True))
    scale_two = lax.rsqrt(square_sum / features + EPSILON)
    b_half = (attended * scale_two * gain2_half).astype(LOW)
    gate_all = with_neighbours(gate_pieces, heads_low)
    up_all = with_neighbours(up_pieces, attn_back)
    b_slots = matmul_tn(ffn_pick, b_half).astype(LOW)
    ffn_rows = send_out(after(b_slots, *gate_all[1:], *up_all[1:]), 2)
    ffn_logits = tp_sum(matmul(b_half, router2_half))
    ffn_probs = jax.nn.softmax(ffn_logits, axis=1)
    ffn_mix = mix_of(ffn_logits, ffn_onehot)

    ffn_seq_routes = seq_routes[:, picks_each : 2 * picks_each]
    ffn_expert_onehot = expert_picks(ffn_seq_routes, mine, capacity).astype(FULL)
    row_routes = jnp.einsum(
        "bsr,bkr->bsk", ffn_expert_onehot, ffn_seq_routes.astype(FULL), precision=PRECISE
    ).reshape(slots, picks_each)
    row_onehot = row_routes[:, :, None] == jnp.arange(expert_count, dtype=FULL)[None, None, :]
    row_mix = mix_of(matmul(ffn_rows, router2), row_onehot.astype(FULL))
    mine_too = (row_routes == mine.astype(FULL)).astype(FULL)
    mix_rows = jnp.broadcast_to(jnp.sum(row_mix * mine_too, axis=1, keepdims=True), (slots, HEAD))
    hidden_low, d_gate_low, d_up_low, db_rows, ffn_out, mix_grad_rows = expert_both_ways(
        ffn_rows,
        cot_rows,
        mix_rows,
        gate_all,
        up_all,
        with_neighbours(down_pieces, ffn_rows),
    )
    mix_grad_rows = jnp.pad(
        mix_grad_rows[:, 0].reshape(groups, 1, capacity), ((0, 0), (0, 7), (0, 256 - capacity))
    )
    dz_rows = (cot_rows.astype(FULL) * mix_rows[:, :1]).astype(LOW)
    down_sent, down_finish = scatter_start(
        lambda low, high: matmul_tn(hidden_low, dz_rows[:, low:high]), features, 1
    )
    down_back = last_step(down_sent)
    d_both = jnp.concatenate([d_gate_low, d_up_low], axis=1)
    both_sent, both_finish = scatter_start(
        lambda low, high: matmul_tn(ffn_rows[:, low:high], d_both), features, 0
    )
    both_back = last_step(both_sent)
    db_back, mix_grad_back = send_home(after(db_rows, down_sent), 3, extra=mix_grad_rows)
    db_back = after(db_back, down_back)
    mix_grad_back = mix_grad_back[:, 0, :capacity].reshape(1, slots)

    experts = jnp.arange(expert_count, dtype=jnp.int32)
    named = (all_routes[..., None] == experts).astype(FULL)
    hits = jnp.stack(
        [
            jnp.sum(named[:, :, :picks_each], axis=(0, 1, 2, 3)),
            jnp.sum(named[:, :, picks_each : 2 * picks_each], axis=(0, 1, 2, 3)),
        ]
    )
    share = hits / (all_tokens * picks_each)
    share_grad = AUX_WEIGHT * expert_count / all_tokens * share
    grad_half = cot_half.astype(FULL)
    d_normed2 = jnp.zeros((rows_here, half_width), FULL)
    ffn_mix_grad = []
    for pick in ffn_picks:
        d_normed2 = d_normed2 + matmul(pick, db_back)
        ffn_mix_grad.append(jnp.sum(pick.astype(FULL) * mix_grad_back, axis=1, keepdims=True))
    ffn_mix_grad = jnp.concatenate(ffn_mix_grad, axis=1)
    ffn_d_logits = logits_back(ffn_mix, ffn_mix_grad, ffn_probs, ffn_onehot, share_grad[1])
    d_normed2 = d_normed2 + through_router(ffn_d_logits, router2_half.astype(FULL))
    weighted2 = d_normed2 * gain2_half
    inner2 = tp_sum(jnp.sum(weighted2 * attended, axis=1, keepdims=True)) / features
    d_attended = grad_half + scale_two * weighted2 - attended * scale_two**3 * inner2
    gain2_part = jnp.sum(d_normed2 * attended * scale_two, axis=0)
    ffn_router_part = precise_tn(b_half.astype(FULL), ffn_d_logits)

    dy_slots = jnp.zeros((slots, half_width), FULL)
    for k in range(picks_each):
        dy_slots = dy_slots + matmul_tn(attn_picks[k], (attn_mix[:, k : k + 1] * d_attended).astype(LOW))
    dy_rows = send_out(after(dy_slots.astype(LOW), both_sent), 4)
    d_heads = matmul_nt(dy_rows, out_full).astype(LOW)
    dq_low, dk_low, dv_low = attend_back(
        q_low, k_low, v_low, d_heads, log_sum, query_table, key_table, groups
    )
    dkv_low = jnp.concatenate([dk_low, dv_low], axis=1)
    da_rows = matmul_nt(dq_low, query_full).astype(LOW).reshape(groups, capacity, features)
    da_seq = jnp.einsum("bsr,bsd->brd", expert_onehot, da_rows, preferred_element_type=FULL)
    da_seq = da_seq.reshape(groups * rows_here, features) + matmul_nt(dkv_low, kv_full)
    out_sent, out_finish = scatter_start(
        lambda low, high: matmul_tn(heads_low, dy_rows[:, low:high]), features, 1
    )
    kv_sent, kv_finish = scatter_start(
        lambda low, high: matmul_tn(a_seq[:, low:high], dkv_low), features, 0
    )
    query_sent, query_finish = scatter_start(
        lambda low, high: matmul_tn(rows_in[:, low:high], dq_low), features, 0
    )
    ffn_back = come_home(after(ffn_out, dy_rows))
    da_half, kv_back, out_back = send_home(
        after(da_seq.astype(LOW), both_back, ffn_back, query_sent), 5, cargo=(kv_sent, out_sent), add_up=True
    )
    kv_part = kv_finish(kv_back)
    query_grad = query_finish(last_step(after(query_sent, da_half)))
    out_grad = out_finish(out_back)
    down_grad = down_finish(after(down_back, da_half))
    both_grad = both_finish(after(both_back, da_half))
    gate_grad, up_grad = jnp.split(both_grad, 2, axis=1)
    kv_grad = block_for(kv_part, 0)
    kv_part_low = kv_part.astype(LOW)
    for distance in far_first(groups):
        if distance:
            kv_grad = kv_grad + swap(block_for(kv_part_low, distance), "ctx", distance).astype(FULL)
    key_width = key_proj.shape[1]

    result = attended
    for k in range(picks_each):
        result = result + ffn_mix[:, k : k + 1] * matmul(ffn_picks[k], ffn_back)
    result_low = result.astype(LOW)
    output = from_spread(join_halves(result_low, swap(result_low, "tp", 1)), 1)

    attn_mix_grad = tp_sum(
        jnp.concatenate(
            [jnp.sum(d_attended * picked, axis=1, keepdims=True) for picked in attn_picked], axis=1
        )
    )
    attn_d_logits = logits_back(attn_mix, attn_mix_grad, attn_probs, attn_onehot, share_grad[0])
    a_half = my_half(a_mine)
    attn_router_part = precise_tn(a_half.astype(FULL), attn_d_logits)

    d_normed1 = da_half + through_router(attn_d_logits, router1_half)
    gain1_half = my_half(gain1)
    weighted1 = d_normed1 * gain1_half
    inner1 = tp_sum(jnp.sum(weighted1 * input_half, axis=1, keepdims=True)) / features
    input_grad = d_attended + scale_one * weighted1 - input_half * scale_one**3 * inner1
    input_grad_low = input_grad.astype(LOW)
    input_grad = from_spread(join_halves(input_grad_low, swap(input_grad_low, "tp", 1)), 1).astype(FULL)
    gain1_part = jnp.sum(d_normed1 * input_half * scale_one, axis=0)

    small = jnp.concatenate(
        [gain1_part[None], gain2_part[None], attn_router_part.T, ffn_router_part.T], axis=0
    )
    small = from_spread(join_halves(small, swap(small, "tp", 1)), 1)
    prob_sums = jnp.concatenate([jnp.sum(attn_probs, axis=0), jnp.sum(ffn_probs, axis=0)])
    small = jnp.concatenate([small, jnp.pad(prob_sums, (0, features - prob_sums.shape[0]))[None]], axis=0)
    small = all_sum(small, ("ctx", "fsdp"))
    prob_sums = small[-1, : 2 * expert_count].reshape(2, expert_count)
    losses = expert_count * jnp.sum(share * prob_sums / all_tokens, axis=1)
    return (
        output,
        input_grad,
        losses[0],
        losses[1],
        small[0],
        small[1],
        small[2 : 2 + expert_count].T,
        small[2 + expert_count : 2 + 2 * expert_count].T,
        kv_grad[:, :key_width],
        kv_grad[:, key_width:],
        query_grad[None],
        out_grad[None],
        gate_grad[None],
        up_grad[None],
        down_grad[None],
    )


def solution(mesh):
    by_token = P(("fsdp", "ctx"), None)
    by_row = P(("fsdp", "ctx"), "tp")
    inward = P("ctx", "fsdp", "tp")
    outward = P("ctx", "tp", "fsdp")
    weights = (by_row, by_row, inward, outward, inward, inward, outward)
    return jax.shard_map(
        on_device,
        mesh=mesh,
        in_specs=(by_token,) * 4 + (P(),) * 4 + weights,
        out_specs=(by_token,) * 2 + (P(),) * 6 + weights,
        check_vma=False,
    )
```

```python
import functools
import math

import jax
import jax.numpy as jnp
import numpy as np
from jax import lax
from jax.experimental import pallas as pl
from jax.experimental.pallas import tpu as pltpu
from jax.sharding import PartitionSpec as P

HEAD = 128
EPSILON = 1e-06
ROPE_BASE = 10000.0
AUX_WEIGHT = 0.1
PRECISE = lax.Precision.HIGHEST
LOW = jnp.bfloat16
FULL = jnp.float32
VMEM_BYTES = 58 * 1024 * 1024
TILE = 256


def matmul(lhs, rhs):
    return jnp.dot(lhs, rhs, preferred_element_type=FULL)


def matmul_tn(lhs, rhs):
    return lax.dot_general(lhs, rhs, (((0,), (0,)), ((), ())), preferred_element_type=FULL)


def matmul_nt(lhs, rhs):
    return lax.dot_general(lhs, rhs, (((1,), (1,)), ((), ())), preferred_element_type=FULL)


def precise_tn(lhs, rhs):
    return lax.dot_general(lhs, rhs, (((0,), (0,)), ((), ())), precision=PRECISE)


def swap(value, axis, distance):
    size = lax.axis_size(axis)
    return lax.ppermute(value, axis, [(i, i ^ distance) for i in range(size)])


def after(value, *earlier):
    return lax.optimization_barrier((value,) + earlier)[0]


def bits_down(size):
    bit = size // 2
    while bit >= 1:
        yield bit
        bit //= 2


def spread_order(size):
    order = [0]
    for bit in bits_down(size):
        order = order + [place | bit for place in order]
    return order


def gather_pieces(piece):
    pieces = [piece]
    for bit in bits_down(lax.axis_size("fsdp")):
        if bit > 1:
            pieces = pieces + [swap(item, "fsdp", bit) for item in pieces]
    return pieces


def with_neighbours(pieces, *earlier):
    return pieces + [swap(after(item, *earlier), "fsdp", 1) for item in pieces]


def flip_blocks(value, axis, index, count):
    parts = jnp.split(value, count, axis)
    for bit in bits_down(count):
        turned = (index // bit) % 2 == 1
        parts = [jnp.where(turned, parts[n ^ bit], parts[n]) for n in range(count)]
    return jnp.concatenate(parts, axis)


def to_spread(value, axis):
    size = lax.axis_size("fsdp")
    value = flip_blocks(value, axis, lax.axis_index("fsdp"), size)
    parts = jnp.split(value, size, axis)
    return jnp.concatenate([parts[place] for place in spread_order(size)], axis)


def from_spread(value, axis):
    size = lax.axis_size("fsdp")
    parts = jnp.split(value, size, axis)
    order = spread_order(size)
    value = jnp.concatenate([parts[order.index(place)] for place in range(size)], axis)
    return flip_blocks(value, axis, lax.axis_index("fsdp"), size)


def my_half(value):
    width = value.shape[-1] // 2
    return jnp.where(lax.axis_index("tp") == 0, value[..., :width], value[..., width:])


def other_half(value):
    width = value.shape[-1] // 2
    return jnp.where(lax.axis_index("tp") == 0, value[..., width:], value[..., :width])


def join_halves(mine, other):
    first = lax.axis_index("tp") == 0
    return jnp.concatenate([jnp.where(first, mine, other), jnp.where(first, other, mine)], -1)


def tp_sum(value):
    return value + swap(value, "tp", 1)


def all_sum(value, axes):
    for axis in axes:
        for bit in bits_down(lax.axis_size(axis)):
            value = value + swap(value, axis, bit)
    return value


def far_first(size):
    return list(range(size // 2, size)) + list(range(size // 2 - 1, -1, -1))


def place_blocks(blocks):
    index = lax.axis_index("ctx")
    rows = blocks[0].shape[0]
    total = jnp.zeros((rows * len(blocks),) + blocks[0].shape[1:], blocks[0].dtype)
    for distance, block in enumerate(blocks):
        total = lax.dynamic_update_slice_in_dim(total, block, (index ^ distance) * rows, 0)
    return total


def block_for(value, distance):
    size = lax.axis_size("ctx")
    rows = value.shape[0] // size
    return lax.dynamic_slice_in_dim(value, (lax.axis_index("ctx") ^ distance) * rows, rows, 0)


def spread_out(half_rows):
    size = lax.axis_size("ctx")
    blocks = [None] * size
    for distance in far_first(size):
        block = block_for(half_rows, distance)
        if distance:
            block = swap(block, "ctx", distance)
        blocks[distance] = join_halves(block, swap(block, "tp", 1))
    return place_blocks(blocks)


def xor_index(index, distance):
    result = index
    bit = 1
    while bit <= distance:
        if distance & bit:
            result = result + bit - 2 * bit * ((index // bit) % 2)
        bit *= 2
    return result


def span(start, size):
    return pl.ds(pl.multiple_of(start * size, 16), size)


def meet(peers):
    barrier = pltpu.get_barrier_semaphore()
    for device in peers:
        pl.semaphore_signal(barrier, inc=1, device_id=device, device_id_type=pl.DeviceIdType.MESH)
    pl.semaphore_wait(barrier, len(peers))


def remote(source, target, sems, index, device):
    return pltpu.make_async_remote_copy(
        src_ref=source,
        dst_ref=target,
        send_sem=sems[0].at[index],
        recv_sem=sems[1].at[index],
        device_id=device,
        device_id_type=pl.DeviceIdType.MESH,
    )


def near_first(size):
    return list(range(1, size))


def mixed_order(size):
    return [distance for distance in spread_order(size) if distance] + [0]


def send_out_kernel(size, rows_ref, out_ref, z_land, y_land, z_send, z_recv, y_send, y_recv):
    mine, first = lax.axis_index("ctx"), lax.axis_index("tp") == 0
    other_tp = {"tp": 1 - lax.axis_index("tp")}
    rows, width = z_land.shape[1], z_land.shape[2]
    at = [xor_index(mine, distance) for distance in range(size)]
    meet([{"ctx": at[distance]} for distance in range(1, size)] + [other_tp])
    order = near_first(size)
    across, beside = {}, {}
    for distance in order:
        across[distance] = remote(
            rows_ref.at[span(at[distance], rows)],
            z_land.at[distance],
            (z_send, z_recv),
            distance,
            {"ctx": at[distance]},
        )
        across[distance].start()
    beside[0] = remote(rows_ref.at[span(mine, rows)], y_land.at[0], (y_send, y_recv), 0, other_tp)
    beside[0].start()
    for distance in order:
        across[distance].wait_recv()
        beside[distance] = remote(
            z_land.at[distance], y_land.at[distance], (y_send, y_recv), distance, other_tp
        )
        beside[distance].start()
    for distance in [0] + order:
        beside[distance].wait_recv()
        own = z_land[distance] if distance else rows_ref[span(mine, rows), :]
        theirs = y_land[distance]
        out_ref[span(at[distance], rows), :width] = jnp.where(first, own, theirs)
        out_ref[span(at[distance], rows), width:] = jnp.where(first, theirs, own)
    for distance in order:
        across[distance].wait_send()
    for distance in [0] + order:
        beside[distance].wait_send()


def send_out(half_rows, number):
    size = lax.axis_size("ctx")
    total, width = half_rows.shape
    land = pltpu.VMEM((size, total // size, width), half_rows.dtype)
    return pl.pallas_call(
        functools.partial(send_out_kernel, size),
        in_specs=[pl.BlockSpec(memory_space=pltpu.VMEM)],
        out_specs=pl.BlockSpec(memory_space=pltpu.VMEM),
        out_shape=jax.ShapeDtypeStruct((total, 2 * width), half_rows.dtype),
        scratch_shapes=[land, land] + [pltpu.SemaphoreType.DMA((size,))] * 4,
        compiler_params=pltpu.CompilerParams(
            collective_id=number, has_side_effects=True, vmem_limit_bytes=VMEM_BYTES
        ),
        cost_estimate=pl.CostEstimate(flops=0, bytes_accessed=12 * total * width, transcendentals=0),
    )(half_rows)


def send_home_kernel(size, adds, has_extra, cargoes, *refs):
    streams = len(adds)
    parts, refs = refs[:streams], refs[streams:]
    extra_ref, refs = (refs[0], refs[1:]) if has_extra else (None, refs)
    cargo_in, refs = refs[:cargoes], refs[cargoes:]
    outs, refs = refs[:streams], refs[streams:]
    extra_out, refs = (refs[0], refs[1:]) if has_extra else (None, refs)
    cargo_out, refs = refs[:cargoes], refs[cargoes:]
    lands, refs = [refs[7 * n : 7 * n + 7] for n in range(streams)], refs[7 * streams :]
    mine, first = lax.axis_index("ctx"), lax.axis_index("tp") == 0
    place = lax.axis_index("tp")
    other_tp = {"tp": 1 - place}
    at = [xor_index(mine, distance) for distance in range(size)]
    world = lax.axis_size("fsdp")
    along = [{"fsdp": xor_index(lax.axis_index("fsdp"), world // 2)}] if cargoes else []
    meet([{"ctx": at[distance]} for distance in range(1, size)] + [other_tp] + along)
    order = mixed_order(size)
    beside, across, extras = {}, {}, {}
    cargo = [remote(cargo_in[n], cargo_out[n], refs[-2:], n, along[0]) for n in range(cargoes)]
    for copy in cargo:
        copy.start()
    if has_extra:
        ey_land, e_ready, ez_land, ey_send, ey_recv, ez_send, ez_recv = refs[:7]
        extra_beside = remote(extra_ref, ey_land, (ey_send, ey_recv), 0, other_tp)
        extra_beside.start()
    for n in range(streams):
        y_land, _, z_land, y_send, y_recv, _, _ = lands[n]
        rows, width = z_land.shape[1], z_land.shape[2]
        columns = pl.ds(pl.multiple_of((1 - place) * width, 128), width)
        for distance in order:
            beside[n, distance] = remote(
                parts[n].at[span(at[distance], rows), columns],
                y_land.at[distance],
                (y_send, y_recv),
                distance,
                other_tp,
            )
            beside[n, distance].start()
    if has_extra:
        extra_beside.wait_recv()
        e_ready[...] = extra_ref[...] + ey_land[...]
        for distance in order:
            if distance:
                extras[distance] = remote(
                    e_ready.at[at[distance]],
                    ez_land.at[distance],
                    (ez_send, ez_recv),
                    distance,
                    {"ctx": at[distance]},
                )
                extras[distance].start()
    for n in range(streams):
        y_land, ready, z_land, _, _, z_send, z_recv = lands[n]
        rows, width = z_land.shape[1], z_land.shape[2]
        for distance in order:
            beside[n, distance].wait_recv()
            whole = parts[n][span(at[distance], rows), :]
            own = jnp.where(first, whole[:, :width], whole[:, width:])
            total = (own.astype(FULL) + y_land[distance].astype(FULL)).astype(LOW)
            if distance:
                ready[distance] = total
                across[n, distance] = remote(
                    ready.at[distance],
                    z_land.at[distance],
                    (z_send, z_recv),
                    distance,
                    {"ctx": at[distance]},
                )
                across[n, distance].start()
            elif adds[n]:
                outs[n][...] = total.astype(FULL)
            else:
                outs[n][span(mine, rows), :] = total
    for n in range(streams):
        z_land = lands[n][2]
        rows = z_land.shape[1]
        for distance in order:
            if distance:
                across[n, distance].wait_recv()
                if adds[n]:
                    outs[n][...] += z_land[distance].astype(FULL)
                else:
                    outs[n][span(at[distance], rows), :] = z_land[distance]
    if has_extra:
        extra_out[mine] = e_ready[mine]
        for distance in order:
            if distance:
                extras[distance].wait_recv()
                extra_out[at[distance]] = ez_land[distance]
                extras[distance].wait_send()
        extra_beside.wait_send()
    for n in range(streams):
        for distance in order:
            beside[n, distance].wait_send()
            if distance:
                across[n, distance].wait_send()
    for copy in cargo:
        copy.wait()


def send_home(partial_rows, number, extra=None, cargo=(), add_up=False, more=None):
    size = lax.axis_size("ctx")
    operands = [partial_rows] if more is None else [partial_rows, more]
    adds = (add_up, False)[: len(operands)]
    sems = [pltpu.SemaphoreType.DMA((size,))] * 4
    shapes, scratch, moved = [], [], 0
    for item, added in zip(operands, adds):
        total, width = item.shape[0], item.shape[1] // 2
        rows = total // size
        moved += 12 * total * width
        shapes.append(
            jax.ShapeDtypeStruct((rows, width), FULL) if added else jax.ShapeDtypeStruct((total, width), LOW)
        )
        scratch += [pltpu.VMEM((size, rows, width), LOW)] * 3 + sems
    if extra is not None:
        operands.append(extra)
        shapes.append(jax.ShapeDtypeStruct(extra.shape, FULL))
        scratch += [pltpu.VMEM(extra.shape, FULL)] * 3 + sems
    in_specs = [pl.BlockSpec(memory_space=pltpu.VMEM)] * len(operands)
    out_specs = [pl.BlockSpec(memory_space=pltpu.VMEM)] * len(shapes)
    for item in cargo:
        operands.append(item)
        shapes.append(jax.ShapeDtypeStruct(item.shape, item.dtype))
        in_specs.append(pl.BlockSpec(memory_space=pl.ANY))
        out_specs.append(pl.BlockSpec(memory_space=pl.ANY))
    if cargo:
        scratch += [pltpu.SemaphoreType.DMA((len(cargo),))] * 2
    results = pl.pallas_call(
        functools.partial(send_home_kernel, size, adds, extra is not None, len(cargo)),
        in_specs=in_specs,
        out_specs=out_specs,
        out_shape=shapes,
        scratch_shapes=scratch,
        compiler_params=pltpu.CompilerParams(
            collective_id=number, has_side_effects=True, vmem_limit_bytes=VMEM_BYTES
        ),
        cost_estimate=pl.CostEstimate(flops=0, bytes_accessed=moved, transcendentals=0),
    )(*operands)
    return results if len(shapes) > 1 else results[0]


def prologue_kernel(sizes, *refs):
    groups, world = sizes
    half_in, own_in, routes_in, kv_in, query_in, out_in = refs[:6]
    seq_ref, routes_ref, kv_ref, query_ref, out_ref = refs[6:11]
    local_sem = refs[11]
    pairs = [(refs[12 + 2 * n], refs[13 + 2 * n]) for n in range(15)]
    token_line, route_line, kv_line, token_pass, kv_pass = (pairs[2 * n : 2 * n + 2] for n in range(5))
    kv_own, fr, fk, fq, fo = pairs[10:]
    mine, place, spot = lax.axis_index("ctx"), lax.axis_index("tp"), lax.axis_index("fsdp")
    other_tp = {"tp": 1 - place}
    rows, width = half_in.shape
    sub = kv_in.shape[0]
    piece = sub * groups
    q_rows = query_in.shape[0]
    steps = list(bits_down(world))
    beside = {bit: {"fsdp": xor_index(spot, bit)} for bit in steps}
    first = steps[0]
    meet(
        [{"ctx": xor_index(mine, distance)} for distance in range(1, groups)]
        + [other_tp]
        + [beside[bit] for bit in steps]
    )
    locals_ = [
        pltpu.make_async_copy(
            own_in.at[:, pl.ds(n * width, width)], seq_ref.at[n, span(mine, rows)], local_sem.at[n]
        )
        for n in range(2)
    ] + [
        pltpu.make_async_copy(routes_in, routes_ref.at[0, mine], local_sem.at[2]),
        pltpu.make_async_copy(kv_in, kv_ref.at[span(mine, sub)], local_sem.at[3]),
        pltpu.make_async_copy(query_in, query_ref.at[pl.ds(0, q_rows)], local_sem.at[4]),
        pltpu.make_async_copy(out_in, out_ref.at[0], local_sem.at[5]),
    ]
    started, landed = [], set()

    def go(copy):
        copy.start()
        started.append(copy)
        return copy

    def arrived(copy):
        if id(copy) not in landed:
            copy.wait_recv()
            landed.add(id(copy))

    def wrap(index):
        return lax.rem(index + groups, groups)

    def outgoing(step):
        yield 0, jnp.logical_and(mine < groups - 1, mine >= step), wrap(mine - step), wrap(mine + 1)
        yield 1, jnp.logical_and(mine > 0, mine + step < groups), wrap(mine + step), wrap(mine - 1)

    def incoming(step):
        yield 0, mine >= step + 1, wrap(mine - 1 - step)
        yield 1, mine + step + 1 < groups, wrap(mine + 1 + step)

    def line_copy(own, place_of, sems, step, way, block, target):
        source = place_of(block) if step else own
        return remote(source, place_of(block), sems[way], step, {"ctx": target})

    def line_start(own, place_of, sems, step):
        for way, happens, block, target in outgoing(step):

            @pl.when(happens)
            def _():
                line_copy(own, place_of, sems, step, way, block, target).start()

    def line_wait(place_of, sems, step, passed):
        for way, happens, block in incoming(step):

            @pl.when(happens)
            def _():
                remote(place_of(block), place_of(block), sems[way], step, other_tp).wait_recv()
                if passed is not None:
                    passed(step, way, block).start()

    def line_end(own, place_of, sems, step, passed):
        for way, happens, block, target in outgoing(step):

            @pl.when(happens)
            def _():
                line_copy(own, place_of, sems, step, way, block, target).wait_send()

        if passed is None:
            return
        for way, happens, block in incoming(step):

            @pl.when(happens)
            def _():
                passed(step, way, block).wait_send()

    def passed_wait(step, passed):
        for way, happens, block in incoming(step):

            @pl.when(happens)
            def _():
                passed(step, way, block).wait_recv()

    route_place = lambda n: routes_ref.at[0, n]
    kv_place = lambda n: kv_ref.at[span(n, sub)]
    token_place = lambda n: seq_ref.at[place, span(n, rows)]

    def kv_along(step, way, block):
        target = kv_ref.at[pl.ds(pl.multiple_of(piece + block * sub, 16), sub)]
        return remote(kv_place(block), target, kv_pass[way], step, beside[first])

    def token_along(step, way, block):
        return remote(token_place(block), token_place(block), token_pass[way], step, other_tp)

    def token_landed(step, way, block):
        view = seq_ref.at[1 - place, span(block, rows)]
        return remote(view, view, token_pass[way], step, other_tp)

    kv_first = go(
        remote(
            kv_in,
            kv_ref.at[pl.ds(pl.multiple_of(piece + mine * sub, 16), sub)],
            kv_own,
            0,
            beside[first],
        )
    )
    query_view = lambda n: query_ref.at[pl.ds(n * q_rows, q_rows)]
    out_view = lambda n: out_ref.at[n]
    kv_view = lambda n: kv_ref.at[pl.ds(n * piece, piece)]
    query_copies = {1: go(remote(query_in, query_view(1), fq, 1, beside[first]))}
    out_copies = {}
    for copy in locals_:
        copy.start()
    for step in range(groups - 1):
        line_start(kv_in, kv_place, kv_line, step)
        line_start(routes_in, route_place, route_line, step)
        line_start(half_in, token_place, token_line, step)
        if step == 0:
            for copy in locals_:
                copy.wait()
            for bit in steps[1:]:
                n = world // (2 * bit)
                query_copies[n] = go(remote(query_in, query_view(n), fq, n, beside[bit]))
                out_copies[n] = go(remote(out_in, out_view(n), fo, n, beside[bit]))
        line_wait(kv_place, kv_line, step, kv_along)
        if step == groups - 2:
            out_copies[1] = go(remote(out_in, out_view(1), fo, 1, beside[first]))
        line_wait(route_place, route_line, step, None)
        line_wait(token_place, token_line, step, token_along)
    route_wait, kv_wait = {}, {}
    count = 1
    for bit in steps:
        for n in range(count):
            peer = beside[bit]
            if n in route_wait:
                arrived(route_wait[n])
            route_wait[count + n] = go(
                remote(routes_ref.at[n], routes_ref.at[count + n], fr, count + n, peer)
            )
            if bit == first:
                continue
            if n:
                arrived(query_copies[n])
                query_copies[count + n] = go(
                    remote(query_view(n), query_view(count + n), fq, count + n, peer)
                )
            if n == 1 and count == 2:
                arrived(kv_first)
                for step in range(groups - 1):
                    passed_wait(step, kv_along)
            if n > 1:
                arrived(kv_wait[n])
            kv_wait[count + n] = go(remote(kv_view(n), kv_view(count + n), fk, count + n, peer))
            if n:
                arrived(out_copies[n])
                out_copies[count + n] = go(remote(out_view(n), out_view(count + n), fo, count + n, peer))
        count *= 2
    if world == 2:
        arrived(kv_first)
        for step in range(groups - 1):
            passed_wait(step, kv_along)
    for copy in started:
        arrived(copy)
    for step in range(groups - 1):
        passed_wait(step, token_landed)
        line_end(kv_in, kv_place, kv_line, step, kv_along)
        line_end(routes_in, route_place, route_line, step, None)
        line_end(half_in, token_place, token_line, step, token_along)
    for copy in started:
        copy.wait_send()


def prologue(token_half, token_rows, routes, kv_rows, query_piece, out_piece, number):
    groups, world = lax.axis_size("ctx"), lax.axis_size("fsdp")
    any_space = pl.BlockSpec(memory_space=pl.ANY)
    rows, features = token_rows.shape
    pair = lambda count: [pltpu.SemaphoreType.DMA((count,))] * 2
    return pl.pallas_call(
        functools.partial(prologue_kernel, (groups, world)),
        in_specs=[pl.BlockSpec(memory_space=pltpu.VMEM)] * 6,
        out_specs=[any_space] * 5,
        out_shape=[
            jax.ShapeDtypeStruct((2, groups * rows, features // 2), LOW),
            jax.ShapeDtypeStruct((world, groups) + routes.shape, jnp.int32),
            jax.ShapeDtypeStruct((world * groups * kv_rows.shape[0], kv_rows.shape[1]), LOW),
            jax.ShapeDtypeStruct((world * query_piece.shape[0], query_piece.shape[1]), LOW),
            jax.ShapeDtypeStruct((world,) + out_piece.shape, LOW),
        ],
        scratch_shapes=[pltpu.SemaphoreType.DMA((6,))] + pair(groups) * 10 + pair(1) + pair(world) * 4,
        compiler_params=pltpu.CompilerParams(
            collective_id=number, has_side_effects=True, vmem_limit_bytes=VMEM_BYTES
        ),
        cost_estimate=pl.CostEstimate(flops=0, bytes_accessed=100000000, transcendentals=0),
    )(token_half, token_rows, routes, kv_rows, query_piece, out_piece)


def expert_kernel(world, steps, *refs):
    rows_ref, cot_ref, mix_ref = refs[:3]
    gates, ups, downs = (refs[3 + n * world : 3 + (n + 1) * world] for n in range(3))
    near_ref, landed_ref, db_ref, out_ref, mix_grad_ref = refs[3 + 3 * world : 8 + 3 * world]
    db_sum, out_sum, rows_t_ref, cot_t_ref, far, send_sem, recv_sem = refs[8 + 3 * world :]
    step = pl.program_id(0)
    slot = lax.rem(step, 2)
    features = rows_ref.shape[1]
    width = features // world
    half = features // 2
    tile = near_ref.shape[2]
    other_core = {"fsdp": xor_index(lax.axis_index("fsdp"), 1)}

    def far_copy(at, place):
        columns = pl.ds(pl.multiple_of(at * tile, 128), tile)
        return pltpu.make_async_remote_copy(
            src_ref=far.at[place],
            dst_ref=landed_ref.at[:, :, columns],
            send_sem=send_sem.at[place],
            recv_sem=recv_sem.at[at],
            device_id=other_core,
            device_id_type=pl.DeviceIdType.MESH,
        )

    @pl.when(step == 0)
    def _():
        meet([other_core])
        db_sum[...] = jnp.zeros_like(db_sum)
        out_sum[...] = jnp.zeros_like(out_sum)
        mix_grad_ref[...] = jnp.zeros_like(mix_grad_ref)
        for at in range(0, features, tile):
            rows_t_ref[at : at + tile, :] = rows_ref[:, at : at + tile].T
            cot_t_ref[at : at + tile, :] = cot_ref[:, at : at + tile].T

    gate_lin, up_lin, d_hidden = None, None, None
    for n in range(world):
        columns = slice(n * width, (n + 1) * width)
        terms = (
            matmul(rows_ref[:, columns], gates[n][...]),
            matmul(rows_ref[:, columns], ups[n][...]),
            matmul_nt(cot_ref[:, columns], downs[n][...]),
        )
        if n:
            terms = (gate_lin + terms[0], up_lin + terms[1], d_hidden + terms[2])
        gate_lin, up_lin, d_hidden = terms
    sigmoid_gate = 1.0 / (1.0 + jnp.exp(-gate_lin))
    swish = gate_lin * sigmoid_gate
    hidden = swish * up_lin
    mix_grad = hidden * d_hidden
    for at in range(0, tile, HEAD):
        mix_grad_ref[...] += mix_grad[:, at : at + HEAD]
    mix = jnp.concatenate([mix_ref[...]] * (tile // HEAD), axis=1)
    d_gated = d_hidden * mix
    hidden_low = hidden.astype(LOW)
    mixed_low = (hidden * mix).astype(LOW)
    d_gate = (d_gated * up_lin * sigmoid_gate * (1.0 + gate_lin * (1.0 - sigmoid_gate))).astype(LOW)
    d_up = (d_gated * swish).astype(LOW)
    for n in range(world):
        columns = slice(n * width, (n + 1) * width)
        out_sum[:, columns] += matmul(hidden_low, downs[n][...])
        db_sum[:, columns] += matmul_nt(d_gate, gates[n][...]) + matmul_nt(d_up, ups[n][...])

    @pl.when(step >= 2)
    def _():
        far_copy(step - 2, slot).wait_send()

    pairs = ((rows_t_ref, d_gate), (rows_t_ref, d_up), (cot_t_ref, mixed_low))
    for n, (left, right) in enumerate(pairs):
        far[slot, n] = matmul(left[half:, :], right).astype(LOW)
    far_copy(step, slot).start()
    for n, (left, right) in enumerate(pairs):
        near_ref[n] = matmul(left[:half, :], right).astype(LOW)

    @pl.when(step == steps - 1)
    def _():
        db_ref[...] = db_sum[...].astype(LOW)
        out_ref[...] = out_sum[...].astype(LOW)
        for last in range(max(steps - 2, 0), steps):
            far_copy(last, last % 2).wait_send()
        for last in range(steps):
            far_copy(last, last % 2).wait_recv()


def expert_both_ways(rows, cot_rows, mix_rows, pieces, first, steps, number):
    gate_pieces, up_pieces, down_pieces = pieces
    world = len(gate_pieces)
    slots, features = rows.shape
    depth = gate_pieces[0].shape[0]
    tile = TILE
    once = pl.Buffered(1)
    whole = lambda value: pl.BlockSpec(value.shape, lambda i: (0, 0), pipeline_mode=once)
    kept = lambda width: pl.BlockSpec((slots, width), lambda i: (0, 0))
    tall = pl.BlockSpec((depth, tile), lambda i: (0, i + first))
    flat = pl.BlockSpec((tile, depth), lambda i: (i + first, 0))
    low = lambda *shape: jax.ShapeDtypeStruct(shape, LOW)
    grads = low(3, features // 2, steps * tile)
    return pl.pallas_call(
        functools.partial(expert_kernel, world, steps),
        grid=(steps,),
        in_specs=[whole(rows), whole(cot_rows), whole(mix_rows)]
        + [tall] * (2 * world)
        + [flat] * world,
        out_specs=[
            pl.BlockSpec((3, features // 2, tile), lambda i: (0, 0, i)),
            pl.BlockSpec(memory_space=pl.ANY),
            kept(features),
            kept(features),
            kept(HEAD),
        ],
        out_shape=[
            grads,
            grads,
            low(slots, features),
            low(slots, features),
            jax.ShapeDtypeStruct((slots, HEAD), FULL),
        ],
        scratch_shapes=[
            pltpu.VMEM((slots, features), FULL),
            pltpu.VMEM((slots, features), FULL),
            pltpu.VMEM((features, slots), LOW),
            pltpu.VMEM((features, slots), LOW),
            pltpu.VMEM((2, 3, features // 2, tile), LOW),
            pltpu.SemaphoreType.DMA((2,)),
            pltpu.SemaphoreType.DMA((steps,)),
        ],
        compiler_params=pltpu.CompilerParams(
            collective_id=number, has_side_effects=True, vmem_limit_bytes=VMEM_BYTES
        ),
        cost_estimate=pl.CostEstimate(
            flops=0, bytes_accessed=2 * slots * features, transcendentals=0
        ),
    )(rows, cot_rows, mix_rows, *gate_pieces, *up_pieces, *down_pieces)


def scatter_rest(near, landed):
    pieces = lax.axis_size("fsdp")
    arrived, high, bit = [landed], near.shape[1], 2

    def part(low, high):
        total = near[:, low:high].astype(FULL)
        for block in arrived:
            total = total + block[:, low:high].astype(FULL)
        return total

    while True:
        sent = part(high // 2, high).astype(LOW)
        high //= 2
        if 2 * bit >= pieces:
            break
        arrived.append(swap(sent, "fsdp", bit))
        bit *= 2

    def finish(last):
        arrived.append(last)
        return part(0, high)

    return sent, finish


def scatter_start(product, features, first_dim):
    pieces = lax.axis_size("fsdp")
    high, bit, arrived = features, 1, []

    def part(low, high):
        total = product(low, high)
        for block in arrived:
            total = total + lax.slice_in_dim(block, low, high, axis=first_dim).astype(FULL)
        return total

    while True:
        sent = part(high // 2, high).astype(LOW)
        high //= 2
        if 2 * bit >= pieces:
            break
        arrived.append(swap(sent, "fsdp", bit))
        bit *= 2

    def finish(last):
        arrived.append(last)
        return part(0, high)

    return sent, finish


def last_step(sent):
    return swap(sent, "fsdp", lax.axis_size("fsdp") // 2)


def turn_tables(length):
    half_head = HEAD // 2
    steps = np.arange(half_head, dtype=np.float32) * np.float32(2.0 / HEAD)
    frequency = np.power(np.float32(ROPE_BASE), -steps).astype(np.float32)
    angles = np.arange(length, dtype=np.float32)[:, None] * frequency[None, :]
    cosine = np.cos(angles.astype(np.float64)).astype(np.float32)
    sine = np.sin(angles.astype(np.float64)).astype(np.float32)
    return np.concatenate([cosine, cosine, -sine, sine], axis=1)


def turn(value, table):
    return value * table[:, :HEAD] + pltpu.roll(value, HEAD // 2, 1) * table[:, HEAD:]


def turn_back(value, table):
    return value * table[:, :HEAD] - pltpu.roll(value, HEAD // 2, 1) * table[:, HEAD:]


def attend_kernel(
    groups, scale, q_lin, k_lin, v_lin, q_table, k_table, q_low, k_low, v_low, heads, log_sum
):
    q_low[...] = turn(q_lin[...], q_table[...]).astype(LOW)
    k_low[...] = turn(k_lin[...], k_table[...]).astype(LOW)
    v_low[...] = v_lin[...].astype(LOW)
    rows = q_low.shape[0] // groups
    block = k_low.shape[0] // groups
    for group in range(groups):
        span = slice(group * rows, (group + 1) * rows)
        seen = slice(0, (group + 1) * block)
        scores = matmul_nt(q_low[span, :], k_low[seen, :]) * scale
        top = jnp.max(scores, axis=1, keepdims=True)
        weights = jnp.exp(scores - top)
        total = jnp.sum(weights, axis=1, keepdims=True)
        weights = (weights * (1.0 / total)).astype(LOW)
        heads[span, :] = matmul(weights, v_low[seen, :]).astype(LOW)
        log_sum[span, :] = jnp.broadcast_to(top + jnp.log(total), (rows, HEAD))


def attend(query_lin, kv_lin, query_table, key_table, groups):
    slots, width = query_lin.shape
    length = kv_lin.shape[0]
    count = width // HEAD
    by_head = lambda rows: pl.BlockSpec((rows, HEAD), lambda h: (0, h))
    whole = lambda rows: pl.BlockSpec((rows, 2 * HEAD), lambda h: (0, 0))
    return pl.pallas_call(
        functools.partial(attend_kernel, groups, 1.0 / math.sqrt(HEAD)),
        grid=(count,),
        in_specs=[
            by_head(slots),
            by_head(length),
            pl.BlockSpec((length, HEAD), lambda h: (0, h + count)),
            whole(slots),
            whole(length),
        ],
        out_specs=[by_head(slots), by_head(length), by_head(length), by_head(slots), by_head(slots)],
        out_shape=[
            jax.ShapeDtypeStruct((slots, width), LOW),
            jax.ShapeDtypeStruct((length, width), LOW),
            jax.ShapeDtypeStruct((length, width), LOW),
            jax.ShapeDtypeStruct((slots, width), LOW),
            jax.ShapeDtypeStruct((slots, width), FULL),
        ],
        compiler_params=pltpu.CompilerParams(vmem_limit_bytes=VMEM_BYTES),
        cost_estimate=pl.CostEstimate(
            flops=0, bytes_accessed=20 * length * width, transcendentals=0
        ),
    )(query_lin, kv_lin, kv_lin, query_table, key_table)


def attend_back_kernel(
    groups, scale, q_low, k_low, v_low, d_heads, log_sum, q_table, k_table, dq, dk, dv, dk_sum, dv_sum
):
    dk_sum[...] = jnp.zeros_like(dk_sum)
    dv_sum[...] = jnp.zeros_like(dv_sum)
    rows = q_low.shape[0] // groups
    block = k_low.shape[0] // groups
    for group in range(groups):
        span = slice(group * rows, (group + 1) * rows)
        seen = slice(0, (group + 1) * block)
        query, keys = q_low[span, :], k_low[seen, :]
        grads = d_heads[span, :]
        scores = matmul_nt(query, keys) * scale
        weights = jnp.exp(scores - log_sum[span, :1])
        d_weights = matmul_nt(grads, v_low[seen, :])
        delta = jnp.sum(weights * d_weights, axis=1, keepdims=True)
        d_scores = (weights * (d_weights - delta)).astype(LOW)
        dq[span, :] = turn_back(matmul(d_scores, keys) * scale, q_table[span, :]).astype(LOW)
        dk_sum[seen, :] += matmul_tn(d_scores, query) * scale
        dv_sum[seen, :] += matmul_tn(weights.astype(LOW), grads)
    dk[...] = turn_back(dk_sum[...], k_table[...]).astype(LOW)
    dv[...] = dv_sum[...].astype(LOW)


def attend_back(q_low, k_low, v_low, d_heads, log_sum, query_table, key_table, groups):
    slots, width = q_low.shape
    length = k_low.shape[0]
    count = width // HEAD
    by_head = lambda rows: pl.BlockSpec((rows, HEAD), lambda h: (0, h))
    whole = lambda rows: pl.BlockSpec((rows, 2 * HEAD), lambda h: (0, 0))
    return pl.pallas_call(
        functools.partial(attend_back_kernel, groups, 1.0 / math.sqrt(HEAD)),
        grid=(count,),
        in_specs=[
            by_head(slots),
            by_head(length),
            by_head(length),
            by_head(slots),
            by_head(slots),
            whole(slots),
            whole(length),
        ],
        out_specs=[by_head(slots), by_head(length), by_head(length)],
        out_shape=[
            jax.ShapeDtypeStruct((slots, width), LOW),
            jax.ShapeDtypeStruct((length, width), LOW),
            jax.ShapeDtypeStruct((length, width), LOW),
        ],
        scratch_shapes=[pltpu.VMEM((length, HEAD), FULL), pltpu.VMEM((length, HEAD), FULL)],
        compiler_params=pltpu.CompilerParams(vmem_limit_bytes=VMEM_BYTES),
        cost_estimate=pl.CostEstimate(
            flops=0, bytes_accessed=14 * length * width, transcendentals=0
        ),
    )(q_low, k_low, v_low, d_heads, log_sum, query_table, key_table)


def chosen_picks(routes, expert_count, capacity):
    experts = jnp.arange(expert_count, dtype=jnp.int32)
    onehot = (routes[:, :, None] == experts[None, None, :]).astype(jnp.int32)
    rows = routes.shape[0]
    below = (jnp.arange(rows)[:, None] > jnp.arange(rows)[None, :]).astype(LOW)
    order = matmul(below, jnp.sum(onehot, axis=1).astype(LOW)).astype(jnp.int32)
    slot = routes * capacity + jnp.sum(onehot * order[:, None, :], axis=2)
    slots = jnp.arange(expert_count * capacity, dtype=jnp.int32)
    picks = [(slot[:, k : k + 1] == slots[None, :]).astype(LOW) for k in range(routes.shape[1])]
    return picks, onehot.astype(FULL)


def expert_picks(routes_seq, expert, capacity):
    named = jnp.any(routes_seq == expert, axis=1)
    rows = named.shape[1]
    above = (jnp.arange(rows)[:, None] < jnp.arange(rows)[None, :]).astype(LOW)
    order = matmul(named.astype(LOW), above).astype(jnp.int32)
    slot = jnp.where(named, order, -1)
    return (slot[:, None, :] == jnp.arange(capacity, dtype=jnp.int32)[None, :, None]).astype(LOW)


def mix_of(logits, onehot):
    chosen = jnp.sum(onehot * logits[:, None, :], axis=2)
    return jax.nn.softmax(chosen, axis=1)


def logits_back(mix, mix_grad, probs, onehot, share_grad):
    d_chosen = mix * (mix_grad - jnp.sum(mix * mix_grad, axis=1, keepdims=True))
    d_logits = jnp.sum(onehot * d_chosen[:, :, None], axis=1)
    inner = jnp.sum(probs * share_grad[None, :], axis=1, keepdims=True)
    return d_logits + probs * (share_grad[None, :] - inner)


def through_router(d_logits, router_half):
    total = d_logits[:, 0:1] * router_half[:, 0][None, :]
    for expert in range(1, d_logits.shape[1]):
        total = total + d_logits[:, expert : expert + 1] * router_half[:, expert][None, :]
    return total


def on_device(
    tokens,
    cotangent,
    attn_routes,
    ffn_routes,
    norm_gain1,
    norm_gain2,
    attn_router,
    ffn_router,
    key_proj,
    value_proj,
    query_proj,
    out_proj,
    gate_proj,
    up_proj,
    down_proj,
):
    rows_here, features = tokens.shape
    half_width = features // 2
    picks_each = attn_routes.shape[1]
    expert_count = attn_router.shape[1]
    groups = lax.axis_size("ctx")
    mine = lax.axis_index("ctx")
    capacity = rows_here * picks_each // expert_count * 5 // 4
    slots = groups * capacity
    all_tokens = rows_here * lax.axis_size("fsdp") * groups

    tokens_spread = to_spread(tokens, 1)
    token_half = my_half(tokens_spread)
    routes_mine = jnp.concatenate([attn_routes.T, ffn_routes.T], axis=0)
    routes_mine = jnp.concatenate([routes_mine, jnp.zeros_like(routes_mine)], axis=0)
    kv_mine = jnp.concatenate([key_proj, value_proj], axis=1)
    seq_low, all_routes, kv_full, query_full, out_pieces = prologue(
        token_half, tokens_spread, routes_mine, kv_mine, query_proj[0], out_proj[0], 0
    )
    seq_routes = all_routes[0]
    seq_tokens = jnp.concatenate([seq_low[0], seq_low[1]], axis=1).astype(FULL)
    out_full = jnp.concatenate([out_pieces[n] for n in range(lax.axis_size("fsdp"))], axis=1)

    gate_pieces = gather_pieces(after(gate_proj[0], all_routes))
    up_pieces = gather_pieces(after(up_proj[0], all_routes))
    down_pieces = gather_pieces(after(down_proj[0], all_routes))

    gain1 = to_spread(norm_gain1, 0)
    gain2_half = my_half(to_spread(norm_gain2, 0))
    router1 = to_spread(attn_router, 0)
    router2 = to_spread(ffn_router, 0)
    router1_half = my_half(router1.T).T.astype(FULL)
    router2_half = my_half(router2.T).T

    scale_seq = lax.rsqrt(jnp.mean(seq_tokens * seq_tokens, axis=1, keepdims=True) + EPSILON)
    a_seq = (seq_tokens * scale_seq * gain1).astype(LOW)
    a_mine = lax.dynamic_slice_in_dim(a_seq, mine * rows_here, rows_here, 0)
    scale_one = lax.dynamic_slice_in_dim(scale_seq, mine * rows_here, rows_here, 0)
    attn_logits = matmul(a_mine, router1)
    attn_probs = jax.nn.softmax(attn_logits, axis=1)
    attn_picks, attn_onehot = chosen_picks(attn_routes, expert_count, capacity)
    ffn_picks, ffn_onehot = chosen_picks(ffn_routes, expert_count, capacity)
    attn_mix = mix_of(attn_logits, attn_onehot)

    cot_half = my_half(to_spread(cotangent, 1))
    ffn_pick = ffn_picks[0]
    for pick in ffn_picks[1:]:
        ffn_pick = ffn_pick + pick
    cot_rows = spread_out(after(matmul_tn(ffn_pick, cot_half).astype(LOW), all_routes))

    expert_onehot = expert_picks(seq_routes[:, :picks_each], mine, capacity)
    key_table = jnp.asarray(turn_tables(groups * rows_here))
    query_table = jnp.einsum(
        "bsr,brh->bsh",
        expert_onehot.astype(FULL),
        key_table.reshape(groups, rows_here, -1),
        precision=PRECISE,
    ).reshape(slots, -1)
    rows_in = (
        jnp.einsum(
            "bsr,brd->bsd",
            expert_onehot,
            a_seq.reshape(groups, rows_here, features),
            preferred_element_type=FULL,
        )
        .astype(LOW)
        .reshape(slots, features)
    )
    query_lin = matmul(rows_in, query_full)
    kv_lin = matmul(a_seq, kv_full)
    q_low, k_low, v_low, heads_low, log_sum = attend(
        query_lin, kv_lin, query_table, key_table, groups
    )
    attn_back = send_home(after(matmul(heads_low, out_full).astype(LOW), cot_rows), 1)

    input_half = my_half(tokens_spread).astype(FULL)
    attn_picked = [matmul(pick, attn_back) for pick in attn_picks]
    attended = input_half
    for k in range(picks_each):
        attended = attended + attn_mix[:, k : k + 1] * attn_picked[k]
    square_sum = tp_sum(jnp.sum(attended * attended, axis=1, keepdims=True))
    scale_two = lax.rsqrt(square_sum / features + EPSILON)
    b_half = (attended * scale_two * gain2_half).astype(LOW)
    gate_all = with_neighbours(gate_pieces, heads_low)
    up_all = with_neighbours(up_pieces, attn_back)
    b_slots = matmul_tn(ffn_pick, b_half).astype(LOW)
    ffn_rows = send_out(after(b_slots, *gate_all[1:], *up_all[1:]), 2)
    ffn_logits = tp_sum(matmul(b_half, router2_half))
    ffn_probs = jax.nn.softmax(ffn_logits, axis=1)
    ffn_mix = mix_of(ffn_logits, ffn_onehot)

    ffn_seq_routes = seq_routes[:, picks_each : 2 * picks_each]
    ffn_expert_onehot = expert_picks(ffn_seq_routes, mine, capacity).astype(FULL)
    row_routes = jnp.einsum(
        "bsr,bkr->bsk", ffn_expert_onehot, ffn_seq_routes.astype(FULL), precision=PRECISE
    ).reshape(slots, picks_each)
    row_onehot = row_routes[:, :, None] == jnp.arange(expert_count, dtype=FULL)[None, None, :]
    row_mix = mix_of(matmul(ffn_rows, router2), row_onehot.astype(FULL))
    mine_too = (row_routes == mine.astype(FULL)).astype(FULL)
    mix_rows = jnp.broadcast_to(jnp.sum(row_mix * mine_too, axis=1, keepdims=True), (slots, HEAD))
    pieces = (gate_all, up_all, with_neighbours(down_pieces, ffn_rows))
    tiles = gate_proj.shape[2] // TILE
    count_one = (tiles + 1) // 2
    near_one, landed_one, db_one, out_one, mix_grad_one = expert_both_ways(
        ffn_rows, cot_rows, mix_rows, pieces, 0, count_one, 7
    )
    sent_one, finish_one = scatter_rest(near_one, landed_one)
    back_one = last_step(sent_one)
    near_two, landed_two, db_two, out_two, mix_grad_two = expert_both_ways(
        after(ffn_rows, sent_one), cot_rows, mix_rows, pieces, count_one, tiles - count_one, 8
    )
    sent_two, finish_two = scatter_rest(near_two, landed_two)
    back_two = last_step(sent_two)
    db_rows = (db_one.astype(FULL) + db_two.astype(FULL)).astype(LOW)
    ffn_out = (out_one.astype(FULL) + out_two.astype(FULL)).astype(LOW)
    mix_grad_rows = jnp.pad(
        jnp.sum(mix_grad_one + mix_grad_two, axis=1).reshape(groups, 1, capacity),
        ((0, 0), (0, 7), (0, 256 - capacity)),
    )
    db_back, mix_grad_back = send_home(after(db_rows, sent_two), 3, extra=mix_grad_rows)
    db_back = after(db_back, back_one)
    mix_grad_back = mix_grad_back[:, 0, :capacity].reshape(1, slots)

    experts = jnp.arange(expert_count, dtype=jnp.int32)
    named = (all_routes[..., None] == experts).astype(FULL)
    hits = jnp.stack(
        [
            jnp.sum(named[:, :, :picks_each], axis=(0, 1, 2, 3)),
            jnp.sum(named[:, :, picks_each : 2 * picks_each], axis=(0, 1, 2, 3)),
        ]
    )
    share = hits / (all_tokens * picks_each)
    share_grad = AUX_WEIGHT * expert_count / all_tokens * share
    grad_half = cot_half.astype(FULL)
    d_normed2 = jnp.zeros((rows_here, half_width), FULL)
    ffn_mix_grad = []
    for pick in ffn_picks:
        d_normed2 = d_normed2 + matmul(pick, db_back)
        ffn_mix_grad.append(jnp.sum(pick.astype(FULL) * mix_grad_back, axis=1, keepdims=True))
    ffn_mix_grad = jnp.concatenate(ffn_mix_grad, axis=1)
    ffn_d_logits = logits_back(ffn_mix, ffn_mix_grad, ffn_probs, ffn_onehot, share_grad[1])
    d_normed2 = d_normed2 + through_router(ffn_d_logits, router2_half.astype(FULL))
    weighted2 = d_normed2 * gain2_half
    inner2 = tp_sum(jnp.sum(weighted2 * attended, axis=1, keepdims=True)) / features
    d_attended = grad_half + scale_two * weighted2 - attended * scale_two**3 * inner2
    gain2_part = jnp.sum(d_normed2 * attended * scale_two, axis=0)
    ffn_router_part = precise_tn(b_half.astype(FULL), ffn_d_logits)

    dy_slots = jnp.zeros((slots, half_width), FULL)
    for k in range(picks_each):
        dy_slots = dy_slots + matmul_tn(attn_picks[k], (attn_mix[:, k : k + 1] * d_attended).astype(LOW))
    dy_rows = send_out(dy_slots.astype(LOW), 4)
    d_heads = matmul_nt(dy_rows, out_full).astype(LOW)
    dq_low, dk_low, dv_low = attend_back(
        q_low, k_low, v_low, d_heads, log_sum, query_table, key_table, groups
    )
    dkv_low = after(jnp.concatenate([dk_low, dv_low], axis=1), back_two)
    da_rows = matmul_nt(dq_low, query_full).astype(LOW).reshape(groups, capacity, features)
    da_seq = jnp.einsum("bsr,bsd->brd", expert_onehot, da_rows, preferred_element_type=FULL)
    da_seq = da_seq.reshape(groups * rows_here, features) + matmul_nt(dkv_low, kv_full)
    out_sent, out_finish = scatter_start(
        lambda low, high: matmul_tn(heads_low, dy_rows[:, low:high]), features, 1
    )
    kv_sent, kv_finish = scatter_start(
        lambda low, high: matmul_tn(a_seq[:, low:high], dkv_low), features, 0
    )
    query_sent, query_finish = scatter_start(
        lambda low, high: matmul_tn(rows_in[:, low:high], dq_low), features, 0
    )
    da_half, ffn_back, kv_back, query_back, out_back = send_home(
        da_seq.astype(LOW), 5, cargo=(kv_sent, query_sent, out_sent), add_up=True, more=ffn_out
    )
    kv_part = kv_finish(kv_back)
    query_grad = query_finish(query_back)
    out_grad = out_finish(out_back)
    grads = jnp.concatenate(
        [finish_one(after(back_one, kv_part)), finish_two(after(back_two, kv_part))], axis=2
    )
    gate_grad, up_grad, down_grad = grads[0], grads[1], grads[2].T
    kv_grad = block_for(kv_part, 0)
    kv_part_low = kv_part.astype(LOW)
    for distance in far_first(groups):
        if distance:
            kv_grad = kv_grad + swap(block_for(kv_part_low, distance), "ctx", distance).astype(FULL)
    key_width = key_proj.shape[1]

    result = attended
    for k in range(picks_each):
        result = result + ffn_mix[:, k : k + 1] * matmul(ffn_picks[k], ffn_back)
    result_low = result.astype(LOW)
    output = from_spread(join_halves(result_low, swap(result_low, "tp", 1)), 1)

    attn_mix_grad = tp_sum(
        jnp.concatenate(
            [jnp.sum(d_attended * picked, axis=1, keepdims=True) for picked in attn_picked], axis=1
        )
    )
    attn_d_logits = logits_back(attn_mix, attn_mix_grad, attn_probs, attn_onehot, share_grad[0])
    a_half = my_half(a_mine)
    attn_router_part = precise_tn(a_half.astype(FULL), attn_d_logits)

    d_normed1 = da_half + through_router(attn_d_logits, router1_half)
    gain1_half = my_half(gain1)
    weighted1 = d_normed1 * gain1_half
    inner1 = tp_sum(jnp.sum(weighted1 * input_half, axis=1, keepdims=True)) / features
    input_grad = d_attended + scale_one * weighted1 - input_half * scale_one**3 * inner1
    input_grad_low = input_grad.astype(LOW)
    input_grad = from_spread(join_halves(input_grad_low, swap(input_grad_low, "tp", 1)), 1).astype(FULL)
    gain1_part = jnp.sum(d_normed1 * input_half * scale_one, axis=0)

    small = jnp.concatenate(
        [gain1_part[None], gain2_part[None], attn_router_part.T, ffn_router_part.T], axis=0
    )
    small = from_spread(join_halves(small, swap(small, "tp", 1)), 1)
    prob_sums = jnp.concatenate([jnp.sum(attn_probs, axis=0), jnp.sum(ffn_probs, axis=0)])
    small = jnp.concatenate([small, jnp.pad(prob_sums, (0, features - prob_sums.shape[0]))[None]], axis=0)
    small = all_sum(small, ("fsdp", "ctx"))
    prob_sums = small[-1, : 2 * expert_count].reshape(2, expert_count)
    losses = expert_count * jnp.sum(share * prob_sums / all_tokens, axis=1)
    return (
        output,
        input_grad,
        losses[0],
        losses[1],
        small[0],
        small[1],
        small[2 : 2 + expert_count].T,
        small[2 + expert_count : 2 + 2 * expert_count].T,
        kv_grad[:, :key_width],
        kv_grad[:, key_width:],
        query_grad[None],
        out_grad[None],
        gate_grad[None],
        up_grad[None],
        down_grad[None],
    )


def solution(mesh):
    by_token = P(("fsdp", "ctx"), None)
    by_row = P(("fsdp", "ctx"), "tp")
    inward = P("ctx", "fsdp", "tp")
    outward = P("ctx", "tp", "fsdp")
    weights = (by_row, by_row, inward, outward, inward, inward, outward)
    return jax.shard_map(
        on_device,
        mesh=mesh,
        in_specs=(by_token,) * 4 + (P(),) * 4 + weights,
        out_specs=(by_token,) * 2 + (P(),) * 6 + weights,
        check_vma=False,
    )
```

```python
import functools
import math

import jax
import jax.numpy as jnp
import numpy as np
from jax import lax
from jax.experimental import pallas as pl
from jax.experimental.pallas import tpu as pltpu
from jax.sharding import PartitionSpec as P

HEAD = 128
EPSILON = 1e-06
ROPE_BASE = 10000.0
AUX_WEIGHT = 0.1
PRECISE = lax.Precision.HIGHEST
LOW = jnp.bfloat16
FULL = jnp.float32
VMEM_BYTES = 58 * 1024 * 1024
TILE = 256


def matmul(lhs, rhs):
    return jnp.dot(lhs, rhs, preferred_element_type=FULL)


def matmul_tn(lhs, rhs):
    return lax.dot_general(lhs, rhs, (((0,), (0,)), ((), ())), preferred_element_type=FULL)


def matmul_nt(lhs, rhs):
    return lax.dot_general(lhs, rhs, (((1,), (1,)), ((), ())), preferred_element_type=FULL)


def precise_tn(lhs, rhs):
    return lax.dot_general(lhs, rhs, (((0,), (0,)), ((), ())), precision=PRECISE)


def swap(value, axis, distance):
    size = lax.axis_size(axis)
    return lax.ppermute(value, axis, [(i, i ^ distance) for i in range(size)])


def after(value, *earlier):
    return lax.optimization_barrier((value,) + earlier)[0]


def bits_down(size):
    bit = size // 2
    while bit >= 1:
        yield bit
        bit //= 2


def spread_order(size):
    order = [0]
    for bit in bits_down(size):
        order = order + [place | bit for place in order]
    return order


def gather_pieces(piece):
    pieces = [piece]
    for bit in bits_down(lax.axis_size("fsdp")):
        if bit > 1:
            pieces = pieces + [swap(item, "fsdp", bit) for item in pieces]
    return pieces


def with_neighbours(pieces, *earlier):
    return pieces + [swap(pieces[0], "fsdp", 1)] + [
        swap(after(item, *earlier), "fsdp", 1) for item in pieces[1:]
    ]


def flip_blocks(value, axis, index, count):
    parts = jnp.split(value, count, axis)
    for bit in bits_down(count):
        turned = (index // bit) % 2 == 1
        parts = [jnp.where(turned, parts[n ^ bit], parts[n]) for n in range(count)]
    return jnp.concatenate(parts, axis)


def to_spread(value, axis):
    size = lax.axis_size("fsdp")
    value = flip_blocks(value, axis, lax.axis_index("fsdp"), size)
    parts = jnp.split(value, size, axis)
    return jnp.concatenate([parts[place] for place in spread_order(size)], axis)


def from_spread(value, axis):
    size = lax.axis_size("fsdp")
    parts = jnp.split(value, size, axis)
    order = spread_order(size)
    value = jnp.concatenate([parts[order.index(place)] for place in range(size)], axis)
    return flip_blocks(value, axis, lax.axis_index("fsdp"), size)


def my_half(value):
    width = value.shape[-1] // 2
    return jnp.where(lax.axis_index("tp") == 0, value[..., :width], value[..., width:])


def other_half(value):
    width = value.shape[-1] // 2
    return jnp.where(lax.axis_index("tp") == 0, value[..., width:], value[..., :width])


def join_halves(mine, other):
    first = lax.axis_index("tp") == 0
    return jnp.concatenate([jnp.where(first, mine, other), jnp.where(first, other, mine)], -1)


def tp_sum(value):
    return value + swap(value, "tp", 1)


def all_sum(value, axes):
    for axis in axes:
        for bit in bits_down(lax.axis_size(axis)):
            value = value + swap(value, axis, bit)
    return value


def far_first(size):
    return list(range(size // 2, size)) + list(range(size // 2 - 1, -1, -1))


def place_blocks(blocks):
    index = lax.axis_index("ctx")
    rows = blocks[0].shape[0]
    total = jnp.zeros((rows * len(blocks),) + blocks[0].shape[1:], blocks[0].dtype)
    for distance, block in enumerate(blocks):
        total = lax.dynamic_update_slice_in_dim(total, block, (index ^ distance) * rows, 0)
    return total


def block_for(value, distance):
    size = lax.axis_size("ctx")
    rows = value.shape[0] // size
    return lax.dynamic_slice_in_dim(value, (lax.axis_index("ctx") ^ distance) * rows, rows, 0)


def spread_out(half_rows):
    blocks = [block_for(half_rows, distance) for distance in range(lax.axis_size("ctx"))]
    return blocks[:1] + [swap(blocks[distance], "ctx", distance) for distance in range(1, len(blocks))]


def xor_index(index, distance):
    result = index
    bit = 1
    while bit <= distance:
        if distance & bit:
            result = result + bit - 2 * bit * ((index // bit) % 2)
        bit *= 2
    return result


def span(start, size):
    return pl.ds(pl.multiple_of(start * size, 16), size)


def meet(peers):
    barrier = pltpu.get_barrier_semaphore()
    for device in peers:
        pl.semaphore_signal(barrier, inc=1, device_id=device, device_id_type=pl.DeviceIdType.MESH)
    pl.semaphore_wait(barrier, len(peers))


def remote(source, target, sems, index, device):
    return pltpu.make_async_remote_copy(
        src_ref=source,
        dst_ref=target,
        send_sem=sems[0].at[index],
        recv_sem=sems[1].at[index],
        device_id=device,
        device_id_type=pl.DeviceIdType.MESH,
    )


def near_first(size):
    return list(range(1, size))


def mixed_order(size):
    return [distance for distance in spread_order(size) if distance] + [0]


def send_out_kernel(size, rows_ref, out_ref, z_land, y_land, z_send, z_recv, y_send, y_recv):
    mine, first = lax.axis_index("ctx"), lax.axis_index("tp") == 0
    other_tp = {"tp": 1 - lax.axis_index("tp")}
    rows, width = z_land.shape[1], z_land.shape[2]
    at = [xor_index(mine, distance) for distance in range(size)]
    meet([{"ctx": at[distance]} for distance in range(1, size)] + [other_tp])
    order = near_first(size)
    across, beside = {}, {}
    for distance in order:
        across[distance] = remote(
            rows_ref.at[span(at[distance], rows)],
            z_land.at[distance],
            (z_send, z_recv),
            distance,
            {"ctx": at[distance]},
        )
        across[distance].start()
    beside[0] = remote(rows_ref.at[span(mine, rows)], y_land.at[0], (y_send, y_recv), 0, other_tp)
    beside[0].start()
    for distance in order:
        across[distance].wait_recv()
        beside[distance] = remote(
            z_land.at[distance], y_land.at[distance], (y_send, y_recv), distance, other_tp
        )
        beside[distance].start()
    for distance in [0] + order:
        beside[distance].wait_recv()
        own = z_land[distance] if distance else rows_ref[span(mine, rows), :]
        theirs = y_land[distance]
        out_ref[span(at[distance], rows), :width] = jnp.where(first, own, theirs)
        out_ref[span(at[distance], rows), width:] = jnp.where(first, theirs, own)
    for distance in order:
        across[distance].wait_send()
    for distance in [0] + order:
        beside[distance].wait_send()


def send_out(half_rows, number):
    size = lax.axis_size("ctx")
    total, width = half_rows.shape
    land = pltpu.VMEM((size, total // size, width), half_rows.dtype)
    return pl.pallas_call(
        functools.partial(send_out_kernel, size),
        in_specs=[pl.BlockSpec(memory_space=pltpu.VMEM)],
        out_specs=pl.BlockSpec(memory_space=pltpu.VMEM),
        out_shape=jax.ShapeDtypeStruct((total, 2 * width), half_rows.dtype),
        scratch_shapes=[land, land] + [pltpu.SemaphoreType.DMA((size,))] * 4,
        compiler_params=pltpu.CompilerParams(
            collective_id=number, has_side_effects=True, vmem_limit_bytes=VMEM_BYTES
        ),
        cost_estimate=pl.CostEstimate(flops=0, bytes_accessed=12 * total * width, transcendentals=0),
    )(half_rows)


def send_home_kernel(size, adds, has_extra, cargoes, *refs):
    streams = len(adds)
    parts, refs = refs[:streams], refs[streams:]
    extra_ref, refs = (refs[0], refs[1:]) if has_extra else (None, refs)
    cargo_in, refs = refs[:cargoes], refs[cargoes:]
    outs, refs = refs[:streams], refs[streams:]
    extra_out, refs = (refs[0], refs[1:]) if has_extra else (None, refs)
    cargo_out, refs = refs[:cargoes], refs[cargoes:]
    lands, refs = [refs[7 * n : 7 * n + 7] for n in range(streams)], refs[7 * streams :]
    mine, first = lax.axis_index("ctx"), lax.axis_index("tp") == 0
    place = lax.axis_index("tp")
    other_tp = {"tp": 1 - place}
    at = [xor_index(mine, distance) for distance in range(size)]
    world = lax.axis_size("fsdp")
    along = [{"fsdp": xor_index(lax.axis_index("fsdp"), world // 2)}] if cargoes else []
    meet([{"ctx": at[distance]} for distance in range(1, size)] + [other_tp] + along)
    order = mixed_order(size)
    beside, across, extras = {}, {}, {}
    cargo = [remote(cargo_in[n], cargo_out[n], refs[-2:], n, along[0]) for n in range(cargoes)]
    for copy in cargo:
        copy.start()
    if has_extra:
        ey_land, e_ready, ez_land, ey_send, ey_recv, ez_send, ez_recv = refs[:7]
        extra_beside = remote(extra_ref, ey_land, (ey_send, ey_recv), 0, other_tp)
        extra_beside.start()
    for n in range(streams):
        y_land, _, z_land, y_send, y_recv, _, _ = lands[n]
        rows, width = z_land.shape[1], z_land.shape[2]
        columns = pl.ds(pl.multiple_of((1 - place) * width, 128), width)
        for distance in order:
            beside[n, distance] = remote(
                parts[n].at[span(at[distance], rows), columns],
                y_land.at[distance],
                (y_send, y_recv),
                distance,
                other_tp,
            )
            beside[n, distance].start()
    if has_extra:
        extra_beside.wait_recv()
        e_ready[...] = extra_ref[...] + ey_land[...]
        for distance in order:
            if distance:
                extras[distance] = remote(
                    e_ready.at[at[distance]],
                    ez_land.at[distance],
                    (ez_send, ez_recv),
                    distance,
                    {"ctx": at[distance]},
                )
                extras[distance].start()
    for n in range(streams):
        y_land, ready, z_land, _, _, z_send, z_recv = lands[n]
        rows, width = z_land.shape[1], z_land.shape[2]
        for distance in order:
            beside[n, distance].wait_recv()
            whole = parts[n][span(at[distance], rows), :]
            own = jnp.where(first, whole[:, :width], whole[:, width:])
            total = (own.astype(FULL) + y_land[distance].astype(FULL)).astype(LOW)
            if distance:
                ready[distance] = total
                across[n, distance] = remote(
                    ready.at[distance],
                    z_land.at[distance],
                    (z_send, z_recv),
                    distance,
                    {"ctx": at[distance]},
                )
                across[n, distance].start()
            elif adds[n]:
                outs[n][...] = total.astype(FULL)
            else:
                outs[n][span(mine, rows), :] = total
    for n in range(streams):
        z_land = lands[n][2]
        rows = z_land.shape[1]
        for distance in order:
            if distance:
                across[n, distance].wait_recv()
                if adds[n]:
                    outs[n][...] += z_land[distance].astype(FULL)
                else:
                    outs[n][span(at[distance], rows), :] = z_land[distance]
    if has_extra:
        extra_out[mine] = e_ready[mine]
        for distance in order:
            if distance:
                extras[distance].wait_recv()
                extra_out[at[distance]] = ez_land[distance]
                extras[distance].wait_send()
        extra_beside.wait_send()
    for n in range(streams):
        for distance in order:
            beside[n, distance].wait_send()
            if distance:
                across[n, distance].wait_send()
    for copy in cargo:
        copy.wait()


def send_home(partial_rows, number, extra=None, cargo=(), add_up=False, more=None):
    size = lax.axis_size("ctx")
    operands = [partial_rows] if more is None else [partial_rows, more]
    adds = (add_up, False)[: len(operands)]
    sems = [pltpu.SemaphoreType.DMA((size,))] * 4
    shapes, scratch, moved = [], [], 0
    for item, added in zip(operands, adds):
        total, width = item.shape[0], item.shape[1] // 2
        rows = total // size
        moved += 12 * total * width
        shapes.append(
            jax.ShapeDtypeStruct((rows, width), FULL) if added else jax.ShapeDtypeStruct((total, width), LOW)
        )
        scratch += [pltpu.VMEM((size, rows, width), LOW)] * 3 + sems
    if extra is not None:
        operands.append(extra)
        shapes.append(jax.ShapeDtypeStruct(extra.shape, FULL))
        scratch += [pltpu.VMEM(extra.shape, FULL)] * 3 + sems
    in_specs = [pl.BlockSpec(memory_space=pltpu.VMEM)] * len(operands)
    out_specs = [pl.BlockSpec(memory_space=pltpu.VMEM)] * len(shapes)
    for item in cargo:
        operands.append(item)
        shapes.append(jax.ShapeDtypeStruct(item.shape, item.dtype))
        in_specs.append(pl.BlockSpec(memory_space=pl.ANY))
        out_specs.append(pl.BlockSpec(memory_space=pl.ANY))
    if cargo:
        scratch += [pltpu.SemaphoreType.DMA((len(cargo),))] * 2
    results = pl.pallas_call(
        functools.partial(send_home_kernel, size, adds, extra is not None, len(cargo)),
        in_specs=in_specs,
        out_specs=out_specs,
        out_shape=shapes,
        scratch_shapes=scratch,
        compiler_params=pltpu.CompilerParams(
            collective_id=number, has_side_effects=True, vmem_limit_bytes=VMEM_BYTES
        ),
        cost_estimate=pl.CostEstimate(flops=0, bytes_accessed=moved, transcendentals=0),
    )(*operands)
    return results if len(shapes) > 1 else results[0]


def prologue_kernel(sizes, *refs):
    groups, world = sizes
    half_in, own_in, routes_in, kv_in, query_in, out_in = refs[:6]
    seq_ref, routes_ref, kv_ref, query_ref, out_ref = refs[6:11]
    local_sem = refs[11]
    pairs = [(refs[12 + 2 * n], refs[13 + 2 * n]) for n in range(15)]
    token_line, route_line, kv_line, token_pass, kv_pass = (pairs[2 * n : 2 * n + 2] for n in range(5))
    kv_own, fr, fk, fq, fo = pairs[10:]
    mine, place, spot = lax.axis_index("ctx"), lax.axis_index("tp"), lax.axis_index("fsdp")
    other_tp = {"tp": 1 - place}
    rows, width = half_in.shape
    sub = kv_in.shape[0]
    piece = sub * groups
    q_rows = query_in.shape[0]
    steps = list(bits_down(world))
    beside = {bit: {"fsdp": xor_index(spot, bit)} for bit in steps}
    first = steps[0]
    meet(
        [{"ctx": xor_index(mine, distance)} for distance in range(1, groups)]
        + [other_tp]
        + [beside[bit] for bit in steps]
    )
    locals_ = [
        pltpu.make_async_copy(
            own_in.at[:, pl.ds(n * width, width)], seq_ref.at[n, span(mine, rows)], local_sem.at[n]
        )
        for n in range(2)
    ] + [
        pltpu.make_async_copy(routes_in, routes_ref.at[0, mine], local_sem.at[2]),
        pltpu.make_async_copy(kv_in, kv_ref.at[span(mine, sub)], local_sem.at[3]),
        pltpu.make_async_copy(query_in, query_ref.at[pl.ds(0, q_rows)], local_sem.at[4]),
        pltpu.make_async_copy(out_in, out_ref.at[0], local_sem.at[5]),
    ]
    started, landed = [], set()

    def go(copy):
        copy.start()
        started.append(copy)
        return copy

    def arrived(copy):
        if id(copy) not in landed:
            copy.wait_recv()
            landed.add(id(copy))

    def wrap(index):
        return lax.rem(index + groups, groups)

    def outgoing(step):
        yield 0, jnp.logical_and(mine < groups - 1, mine >= step), wrap(mine - step), wrap(mine + 1)
        yield 1, jnp.logical_and(mine > 0, mine + step < groups), wrap(mine + step), wrap(mine - 1)

    def incoming(step):
        yield 0, mine >= step + 1, wrap(mine - 1 - step)
        yield 1, mine + step + 1 < groups, wrap(mine + 1 + step)

    def line_copy(own, place_of, sems, step, way, block, target):
        source = place_of(block) if step else own
        return remote(source, place_of(block), sems[way], step, {"ctx": target})

    def line_start(own, place_of, sems, step):
        for way, happens, block, target in outgoing(step):

            @pl.when(happens)
            def _():
                line_copy(own, place_of, sems, step, way, block, target).start()

    def line_wait(place_of, sems, step, passed):
        for way, happens, block in incoming(step):

            @pl.when(happens)
            def _():
                remote(place_of(block), place_of(block), sems[way], step, other_tp).wait_recv()
                if passed is not None:
                    passed(step, way, block).start()

    def line_end(own, place_of, sems, step, passed):
        for way, happens, block, target in outgoing(step):

            @pl.when(happens)
            def _():
                line_copy(own, place_of, sems, step, way, block, target).wait_send()

        if passed is None:
            return
        for way, happens, block in incoming(step):

            @pl.when(happens)
            def _():
                passed(step, way, block).wait_send()

    def passed_wait(step, passed):
        for way, happens, block in incoming(step):

            @pl.when(happens)
            def _():
                passed(step, way, block).wait_recv()

    route_place = lambda n: routes_ref.at[0, n]
    kv_place = lambda n: kv_ref.at[span(n, sub)]
    token_place = lambda n: seq_ref.at[place, span(n, rows)]

    def kv_along(step, way, block):
        target = kv_ref.at[pl.ds(pl.multiple_of(piece + block * sub, 16), sub)]
        return remote(kv_place(block), target, kv_pass[way], step, beside[first])

    def token_along(step, way, block):
        return remote(token_place(block), token_place(block), token_pass[way], step, other_tp)

    def token_landed(step, way, block):
        view = seq_ref.at[1 - place, span(block, rows)]
        return remote(view, view, token_pass[way], step, other_tp)

    kv_first = go(
        remote(
            kv_in,
            kv_ref.at[pl.ds(pl.multiple_of(piece + mine * sub, 16), sub)],
            kv_own,
            0,
            beside[first],
        )
    )
    query_view = lambda n: query_ref.at[pl.ds(n * q_rows, q_rows)]
    out_view = lambda n: out_ref.at[n]
    kv_view = lambda n: kv_ref.at[pl.ds(n * piece, piece)]
    query_copies = {1: go(remote(query_in, query_view(1), fq, 1, beside[first]))}
    out_copies = {}
    for copy in locals_:
        copy.start()
    for step in range(groups - 1):
        line_start(kv_in, kv_place, kv_line, step)
        line_start(routes_in, route_place, route_line, step)
        line_start(half_in, token_place, token_line, step)
        if step == 0:
            for copy in locals_:
                copy.wait()
            for bit in steps[1:]:
                n = world // (2 * bit)
                query_copies[n] = go(remote(query_in, query_view(n), fq, n, beside[bit]))
                out_copies[n] = go(remote(out_in, out_view(n), fo, n, beside[bit]))
        line_wait(kv_place, kv_line, step, kv_along)
        if step == groups - 2:
            out_copies[1] = go(remote(out_in, out_view(1), fo, 1, beside[first]))
        line_wait(route_place, route_line, step, None)
        line_wait(token_place, token_line, step, token_along)
    route_wait, kv_wait = {}, {}
    count = 1
    for bit in steps:
        for n in range(count):
            peer = beside[bit]
            if n in route_wait:
                arrived(route_wait[n])
            route_wait[count + n] = go(
                remote(routes_ref.at[n], routes_ref.at[count + n], fr, count + n, peer)
            )
            if bit == first:
                continue
            if n:
                arrived(query_copies[n])
                query_copies[count + n] = go(
                    remote(query_view(n), query_view(count + n), fq, count + n, peer)
                )
            if n == 1 and count == 2:
                arrived(kv_first)
                for step in range(groups - 1):
                    passed_wait(step, kv_along)
            if n > 1:
                arrived(kv_wait[n])
            kv_wait[count + n] = go(remote(kv_view(n), kv_view(count + n), fk, count + n, peer))
            if n:
                arrived(out_copies[n])
                out_copies[count + n] = go(remote(out_view(n), out_view(count + n), fo, count + n, peer))
        count *= 2
    if world == 2:
        arrived(kv_first)
        for step in range(groups - 1):
            passed_wait(step, kv_along)
    for copy in started:
        arrived(copy)
    for step in range(groups - 1):
        passed_wait(step, token_landed)
        line_end(kv_in, kv_place, kv_line, step, kv_along)
        line_end(routes_in, route_place, route_line, step, None)
        line_end(half_in, token_place, token_line, step, token_along)
    for copy in started:
        copy.wait_send()


def prologue(token_half, token_rows, routes, kv_rows, query_piece, out_piece, number):
    groups, world = lax.axis_size("ctx"), lax.axis_size("fsdp")
    any_space = pl.BlockSpec(memory_space=pl.ANY)
    rows, features = token_rows.shape
    pair = lambda count: [pltpu.SemaphoreType.DMA((count,))] * 2
    return pl.pallas_call(
        functools.partial(prologue_kernel, (groups, world)),
        in_specs=[pl.BlockSpec(memory_space=pltpu.VMEM)] * 6,
        out_specs=[any_space] * 5,
        out_shape=[
            jax.ShapeDtypeStruct((2, groups * rows, features // 2), LOW),
            jax.ShapeDtypeStruct((world, groups) + routes.shape, jnp.int32),
            jax.ShapeDtypeStruct((world * groups * kv_rows.shape[0], kv_rows.shape[1]), LOW),
            jax.ShapeDtypeStruct((world * query_piece.shape[0], query_piece.shape[1]), LOW),
            jax.ShapeDtypeStruct((world,) + out_piece.shape, LOW),
        ],
        scratch_shapes=[pltpu.SemaphoreType.DMA((6,))] + pair(groups) * 10 + pair(1) + pair(world) * 4,
        compiler_params=pltpu.CompilerParams(
            collective_id=number, has_side_effects=True, vmem_limit_bytes=VMEM_BYTES
        ),
        cost_estimate=pl.CostEstimate(flops=0, bytes_accessed=100000000, transcendentals=0),
    )(token_half, token_rows, routes, kv_rows, query_piece, out_piece)


def expert_forward_kernel(world, size, *refs):
    rows_ref = refs[0]
    gates, ups = refs[1 : 1 + world], refs[1 + world : 1 + 2 * world]
    refs = refs[1 + 2 * world :]
    blocks, refs = refs[:size], refs[size:]
    hidden_ref, by_gate_ref, by_up_ref, cot_ref, y_land, y_send, y_recv = refs
    width = rows_ref.shape[1] // world
    mine, place = lax.axis_index("ctx"), lax.axis_index("tp")
    other_tp = {"tp": 1 - place}
    beside = [
        remote(blocks[distance], y_land.at[distance], (y_send, y_recv), distance, other_tp)
        for distance in range(size)
    ]

    @pl.when(pl.program_id(0) == 0)
    def _():
        meet([other_tp])
        for copy in beside:
            copy.start()

    gate_lin, up_lin = None, None
    for n in range(world):
        columns = slice(n * width, (n + 1) * width)
        gate_term = matmul(rows_ref[:, columns], gates[n][...])
        up_term = matmul(rows_ref[:, columns], ups[n][...])
        gate_lin = gate_lin + gate_term if n else gate_term
        up_lin = up_lin + up_term if n else up_term
    sigmoid_gate = 1.0 / (1.0 + jnp.exp(-gate_lin))
    swish = gate_lin * sigmoid_gate
    hidden_ref[...] = (swish * up_lin).astype(LOW)
    by_gate_ref[...] = (up_lin * sigmoid_gate * (1.0 + gate_lin * (1.0 - sigmoid_gate))).astype(LOW)
    by_up_ref[...] = swish.astype(LOW)

    @pl.when(pl.program_id(0) == pl.num_programs(0) - 1)
    def _():
        rows, half = y_land.shape[1], y_land.shape[2]
        for distance, copy in enumerate(beside):
            copy.wait_recv()
            own, theirs = blocks[distance][...], y_land[distance]
            here = span(xor_index(mine, distance), rows)
            cot_ref[here, :half] = jnp.where(place == 0, own, theirs)
            cot_ref[here, half:] = jnp.where(place == 0, theirs, own)
        for copy in beside:
            copy.wait_send()


def expert_forward(rows, gate_pieces, up_pieces, cot_blocks, number):
    world, size = len(gate_pieces), len(cot_blocks)
    slots, features = rows.shape
    depth, hidden_width = gate_pieces[0].shape
    tall = pl.BlockSpec((depth, TILE), lambda i: (0, i))
    strip = pl.BlockSpec((slots, TILE), lambda i: (0, i))
    whole = lambda value: pl.BlockSpec(value.shape, lambda i: (0, 0), pipeline_mode=pl.Buffered(1))
    return pl.pallas_call(
        functools.partial(expert_forward_kernel, world, size),
        grid=(hidden_width // TILE,),
        in_specs=[whole(rows)] + [tall] * (2 * world) + [whole(block) for block in cot_blocks],
        out_specs=[strip] * 3 + [pl.BlockSpec((slots, features), lambda i: (0, 0))],
        out_shape=[jax.ShapeDtypeStruct((slots, hidden_width), LOW)] * 3
        + [jax.ShapeDtypeStruct((slots, features), LOW)],
        scratch_shapes=[pltpu.VMEM((size,) + cot_blocks[0].shape, LOW)]
        + [pltpu.SemaphoreType.DMA((size,))] * 2,
        compiler_params=pltpu.CompilerParams(
            collective_id=number, has_side_effects=True, vmem_limit_bytes=VMEM_BYTES
        ),
        cost_estimate=pl.CostEstimate(flops=0, bytes_accessed=2 * slots * features, transcendentals=0),
    )(rows, *gate_pieces, *up_pieces, *cot_blocks)


def expert_back_kernel(world, steps, size, *refs):
    rows_ref, cot_ref, mix_ref, hidden_ref, by_gate_ref, by_up_ref = refs[:6]
    gates, ups, downs = (refs[6 + n * world : 6 + (n + 1) * world] for n in range(3))
    refs = refs[6 + 3 * world :]
    part_ref, refs = (refs[0], refs[1:]) if size else (None, refs)
    near_ref, landed_ref, db_ref, mix_grad_ref = refs[:4]
    home_ref, refs = (refs[4], refs[5:]) if size else (None, refs[4:])
    db_sum, rows_t_ref, cot_t_ref, far, send_sem, recv_sem = refs[:6]
    step = pl.program_id(0)
    slot = lax.rem(step, 2)
    features = rows_ref.shape[1]
    width = features // world
    half = features // 2
    tile = near_ref.shape[3]
    other_core = {"fsdp": xor_index(lax.axis_index("fsdp"), 1)}
    peers = [other_core]
    if size:
        y_land, ready, z_land, y_send, y_recv, z_send, z_recv = refs[6:]
        mine, place = lax.axis_index("ctx"), lax.axis_index("tp")
        other_tp = {"tp": 1 - place}
        at = [xor_index(mine, distance) for distance in range(size)]
        peers = peers + [other_tp] + [{"ctx": at[distance]} for distance in range(1, size)]
        home_rows, home_width = z_land.shape[1], z_land.shape[2]
        away = pl.ds(pl.multiple_of((1 - place) * home_width, 128), home_width)
        order = mixed_order(size)

        def beside(distance):
            return remote(
                part_ref.at[span(at[distance], home_rows), away],
                y_land.at[distance],
                (y_send, y_recv),
                distance,
                other_tp,
            )

        def across(distance):
            return remote(
                ready.at[distance],
                z_land.at[distance],
                (z_send, z_recv),
                distance,
                {"ctx": at[distance]},
            )

    def far_copy(at_step, at_slot):
        return pltpu.make_async_remote_copy(
            src_ref=far.at[at_slot],
            dst_ref=landed_ref.at[at_step],
            send_sem=send_sem.at[at_slot],
            recv_sem=recv_sem.at[at_step],
            device_id=other_core,
            device_id_type=pl.DeviceIdType.MESH,
        )

    @pl.when(step == 0)
    def _():
        meet(peers)
        if size:
            for distance in order:
                beside(distance).start()
        db_sum[...] = jnp.zeros_like(db_sum)
        mix_grad_ref[...] = jnp.zeros_like(mix_grad_ref)
        for place_at in range(0, features, tile):
            rows_t_ref[place_at : place_at + tile, :] = rows_ref[:, place_at : place_at + tile].T
            cot_t_ref[place_at : place_at + tile, :] = cot_ref[:, place_at : place_at + tile].T

    d_hidden = None
    for n in range(world):
        columns = slice(n * width, (n + 1) * width)
        term = matmul_nt(cot_ref[:, columns], downs[n][...])
        d_hidden = d_hidden + term if n else term
    hidden = hidden_ref[...].astype(FULL)
    mix_grad = hidden * d_hidden
    for place_at in range(0, tile, HEAD):
        mix_grad_ref[...] += mix_grad[:, place_at : place_at + HEAD]
    mix = jnp.concatenate([mix_ref[...]] * (tile // HEAD), axis=1)
    d_gated = d_hidden * mix
    mixed_low = (hidden * mix).astype(LOW)
    d_gate = (d_gated * by_gate_ref[...].astype(FULL)).astype(LOW)
    d_up = (d_gated * by_up_ref[...].astype(FULL)).astype(LOW)
    for n in range(world):
        columns = slice(n * width, (n + 1) * width)
        db_sum[:, columns] += matmul_nt(d_gate, gates[n][...]) + matmul_nt(d_up, ups[n][...])

    @pl.when(step >= 2)
    def _():
        far_copy(step - 2, slot).wait_send()

    pairs = ((rows_t_ref, d_gate), (rows_t_ref, d_up), (cot_t_ref, mixed_low))
    for n, (left, right) in enumerate(pairs):
        far[slot, n] = matmul(left[half:, :], right).astype(LOW)
    far_copy(step, slot).start()
    for n, (left, right) in enumerate(pairs):
        near_ref[0, n] = matmul(left[:half, :], right).astype(LOW)

    if size:
        for turn, distance in enumerate(order):

            @pl.when(step == min(turn + 1, steps - 1))
            def _():
                beside(distance).wait_recv()
                whole = part_ref[span(at[distance], home_rows), :]
                own = jnp.where(place == 0, whole[:, :home_width], whole[:, home_width:])
                total = (own.astype(FULL) + y_land[distance].astype(FULL)).astype(LOW)
                if distance:
                    ready[distance] = total
                    across(distance).start()
                else:
                    home_ref[span(mine, home_rows), :] = total

    @pl.when(step == steps - 1)
    def _():
        db_ref[...] = db_sum[...].astype(LOW)
        for last in range(max(steps - 2, 0), steps):
            far_copy(last, last % 2).wait_send()
        for last in range(steps):
            far_copy(last, last % 2).wait_recv()
        if size:
            for distance in order:
                beside(distance).wait_send()
                if distance:
                    across(distance).wait_recv()
                    home_ref[span(at[distance], home_rows), :] = z_land[distance]
                    across(distance).wait_send()


def expert_back(rows, cot_rows, mix_rows, forward, pieces, first, steps, number, going_home=None):
    gate_pieces, up_pieces, down_pieces = pieces
    world = len(gate_pieces)
    slots, features = rows.shape
    depth = gate_pieces[0].shape[0]
    tile = TILE
    once = pl.Buffered(1)
    whole = lambda value: pl.BlockSpec(value.shape, lambda i: (0, 0), pipeline_mode=once)
    kept = lambda width: pl.BlockSpec((slots, width), lambda i: (0, 0))
    tall = pl.BlockSpec((depth, tile), lambda i: (0, i + first))
    flat = pl.BlockSpec((tile, depth), lambda i: (i + first, 0))
    strip = pl.BlockSpec((slots, tile), lambda i: (0, i + first))
    low = lambda *shape: jax.ShapeDtypeStruct(shape, LOW)
    grads = low(steps, 3, features // 2, tile)
    operands = [rows, cot_rows, mix_rows, *forward, *gate_pieces, *up_pieces, *down_pieces]
    in_specs = [whole(rows), whole(cot_rows), whole(mix_rows)] + [strip] * 3
    in_specs += [tall] * (2 * world) + [flat] * world
    out_specs = [
        pl.BlockSpec((1, 3, features // 2, tile), lambda i: (i, 0, 0, 0)),
        pl.BlockSpec(memory_space=pl.ANY),
        kept(features),
        kept(HEAD),
    ]
    out_shape = [grads, grads, low(slots, features), jax.ShapeDtypeStruct((slots, HEAD), FULL)]
    scratch = [
        pltpu.VMEM((slots, features), FULL),
        pltpu.VMEM((features, slots), LOW),
        pltpu.VMEM((features, slots), LOW),
        pltpu.VMEM((2, 3, features // 2, tile), LOW),
        pltpu.SemaphoreType.DMA((2,)),
        pltpu.SemaphoreType.DMA((steps,)),
    ]
    size = 0
    if going_home is not None:
        size = lax.axis_size("ctx")
        operands.append(going_home)
        in_specs.append(whole(going_home))
        out_specs.append(kept(features // 2))
        out_shape.append(low(slots, features // 2))
        scratch += [pltpu.VMEM((size, slots // size, features // 2), LOW)] * 3
        scratch += [pltpu.SemaphoreType.DMA((size,))] * 4
    return pl.pallas_call(
        functools.partial(expert_back_kernel, world, steps, size),
        grid=(steps,),
        in_specs=in_specs,
        out_specs=out_specs,
        out_shape=out_shape,
        scratch_shapes=scratch,
        compiler_params=pltpu.CompilerParams(
            collective_id=number, has_side_effects=True, vmem_limit_bytes=VMEM_BYTES
        ),
        cost_estimate=pl.CostEstimate(
            flops=0, bytes_accessed=2 * slots * features, transcendentals=0
        ),
    )(*operands)


def scatter_rest(near, landed):
    pieces = lax.axis_size("fsdp")
    arrived, high, bit = [near, landed], near.shape[2], 2
    while True:
        total = arrived[0][:, :, high // 2 : high].astype(FULL)
        for block in arrived[1:]:
            total = total + block[:, :, high // 2 : high].astype(FULL)
        sent = total.astype(LOW)
        high //= 2
        if 2 * bit >= pieces:
            return sent, arrived
        arrived.append(swap(sent, "fsdp", bit))
        bit *= 2


def finish_kernel(count, steps_one, *refs):
    ones, twos = refs[:count], refs[count : 2 * count]
    outs = refs[2 * count :]

    def add_up(parts):
        for n, out in enumerate(outs):
            total = parts[0][0, n].astype(FULL)
            for part in parts[1:]:
                total = total + part[0, n].astype(FULL)
            out[...] = total.T if n == 2 else total

    @pl.when(pl.program_id(0) < steps_one)
    def _():
        add_up(ones)

    @pl.when(pl.program_id(0) >= steps_one)
    def _():
        add_up(twos)


def finish_experts(ones, twos):
    steps_one, steps_two = ones[0].shape[0], twos[0].shape[0]
    depth, tile = ones[-1].shape[2:]
    width = (steps_one + steps_two) * tile
    block = (1, 3, depth, tile)
    first = pl.BlockSpec(block, lambda i: (jnp.minimum(i, steps_one - 1), 0, 0, 0))
    second = pl.BlockSpec(block, lambda i: (jnp.maximum(i - steps_one, 0), 0, 0, 0))
    tall = pl.BlockSpec((depth, tile), lambda i: (0, i))
    return pl.pallas_call(
        functools.partial(finish_kernel, len(ones), steps_one),
        grid=(steps_one + steps_two,),
        in_specs=[first] * len(ones) + [second] * len(twos),
        out_specs=[tall, tall, pl.BlockSpec((tile, depth), lambda i: (i, 0))],
        out_shape=[jax.ShapeDtypeStruct((depth, width), FULL)] * 2
        + [jax.ShapeDtypeStruct((width, depth), FULL)],
        compiler_params=pltpu.CompilerParams(vmem_limit_bytes=VMEM_BYTES),
        cost_estimate=pl.CostEstimate(
            flops=0, bytes_accessed=30 * width * depth, transcendentals=0
        ),
    )(*ones, *twos)


def scatter_start(product, features, first_dim):
    pieces = lax.axis_size("fsdp")
    high, bit, arrived = features, 1, []

    def part(low, high):
        total = product(low, high)
        for block in arrived:
            total = total + lax.slice_in_dim(block, low, high, axis=first_dim).astype(FULL)
        return total

    while True:
        sent = part(high // 2, high).astype(LOW)
        high //= 2
        if 2 * bit >= pieces:
            break
        arrived.append(swap(sent, "fsdp", bit))
        bit *= 2

    def finish(last):
        arrived.append(last)
        return part(0, high)

    return sent, finish


def last_step(sent):
    return swap(sent, "fsdp", lax.axis_size("fsdp") // 2)


def turn_tables(length):
    half_head = HEAD // 2
    steps = np.arange(half_head, dtype=np.float32) * np.float32(2.0 / HEAD)
    frequency = np.power(np.float32(ROPE_BASE), -steps).astype(np.float32)
    angles = np.arange(length, dtype=np.float32)[:, None] * frequency[None, :]
    cosine = np.cos(angles.astype(np.float64)).astype(np.float32)
    sine = np.sin(angles.astype(np.float64)).astype(np.float32)
    return np.concatenate([cosine, cosine, -sine, sine], axis=1)


def turn(value, table):
    return value * table[:, :HEAD] + pltpu.roll(value, HEAD // 2, 1) * table[:, HEAD:]


def turn_back(value, table):
    return value * table[:, :HEAD] - pltpu.roll(value, HEAD // 2, 1) * table[:, HEAD:]


def attend_kernel(
    groups, scale, q_lin, k_lin, v_lin, q_table, k_table, q_low, k_low, v_low, heads, log_sum
):
    q_low[...] = turn(q_lin[...], q_table[...]).astype(LOW)
    k_low[...] = turn(k_lin[...], k_table[...]).astype(LOW)
    v_low[...] = v_lin[...].astype(LOW)
    rows = q_low.shape[0] // groups
    block = k_low.shape[0] // groups
    for group in range(groups):
        span = slice(group * rows, (group + 1) * rows)
        seen = slice(0, (group + 1) * block)
        scores = matmul_nt(q_low[span, :], k_low[seen, :]) * scale
        top = jnp.max(scores, axis=1, keepdims=True)
        weights = jnp.exp(scores - top)
        total = jnp.sum(weights, axis=1, keepdims=True)
        weights = (weights * (1.0 / total)).astype(LOW)
        heads[span, :] = matmul(weights, v_low[seen, :]).astype(LOW)
        log_sum[span, :] = jnp.broadcast_to(top + jnp.log(total), (rows, HEAD))


def attend(query_lin, kv_lin, query_table, key_table, groups):
    slots, width = query_lin.shape
    length = kv_lin.shape[0]
    count = width // HEAD
    by_head = lambda rows: pl.BlockSpec((rows, HEAD), lambda h: (0, h))
    whole = lambda rows: pl.BlockSpec((rows, 2 * HEAD), lambda h: (0, 0))
    return pl.pallas_call(
        functools.partial(attend_kernel, groups, 1.0 / math.sqrt(HEAD)),
        grid=(count,),
        in_specs=[
            by_head(slots),
            by_head(length),
            pl.BlockSpec((length, HEAD), lambda h: (0, h + count)),
            whole(slots),
            whole(length),
        ],
        out_specs=[by_head(slots), by_head(length), by_head(length), by_head(slots), by_head(slots)],
        out_shape=[
            jax.ShapeDtypeStruct((slots, width), LOW),
            jax.ShapeDtypeStruct((length, width), LOW),
            jax.ShapeDtypeStruct((length, width), LOW),
            jax.ShapeDtypeStruct((slots, width), LOW),
            jax.ShapeDtypeStruct((slots, width), FULL),
        ],
        compiler_params=pltpu.CompilerParams(vmem_limit_bytes=VMEM_BYTES),
        cost_estimate=pl.CostEstimate(
            flops=0, bytes_accessed=20 * length * width, transcendentals=0
        ),
    )(query_lin, kv_lin, kv_lin, query_table, key_table)


def attend_back_kernel(
    groups, scale, q_low, k_low, v_low, d_heads, log_sum, q_table, k_table, dq, dk, dv, dk_sum, dv_sum
):
    dk_sum[...] = jnp.zeros_like(dk_sum)
    dv_sum[...] = jnp.zeros_like(dv_sum)
    rows = q_low.shape[0] // groups
    block = k_low.shape[0] // groups
    for group in range(groups):
        span = slice(group * rows, (group + 1) * rows)
        seen = slice(0, (group + 1) * block)
        query, keys = q_low[span, :], k_low[seen, :]
        grads = d_heads[span, :]
        scores = matmul_nt(query, keys) * scale
        weights = jnp.exp(scores - log_sum[span, :1])
        d_weights = matmul_nt(grads, v_low[seen, :])
        delta = jnp.sum(weights * d_weights, axis=1, keepdims=True)
        d_scores = (weights * (d_weights - delta)).astype(LOW)
        dq[span, :] = turn_back(matmul(d_scores, keys) * scale, q_table[span, :]).astype(LOW)
        dk_sum[seen, :] += matmul_tn(d_scores, query) * scale
        dv_sum[seen, :] += matmul_tn(weights.astype(LOW), grads)
    dk[...] = turn_back(dk_sum[...], k_table[...]).astype(LOW)
    dv[...] = dv_sum[...].astype(LOW)


def attend_back(q_low, k_low, v_low, d_heads, log_sum, query_table, key_table, groups):
    slots, width = q_low.shape
    length = k_low.shape[0]
    count = width // HEAD
    by_head = lambda rows: pl.BlockSpec((rows, HEAD), lambda h: (0, h))
    whole = lambda rows: pl.BlockSpec((rows, 2 * HEAD), lambda h: (0, 0))
    return pl.pallas_call(
        functools.partial(attend_back_kernel, groups, 1.0 / math.sqrt(HEAD)),
        grid=(count,),
        in_specs=[
            by_head(slots),
            by_head(length),
            by_head(length),
            by_head(slots),
            by_head(slots),
            whole(slots),
            whole(length),
        ],
        out_specs=[by_head(slots), by_head(length), by_head(length)],
        out_shape=[
            jax.ShapeDtypeStruct((slots, width), LOW),
            jax.ShapeDtypeStruct((length, width), LOW),
            jax.ShapeDtypeStruct((length, width), LOW),
        ],
        scratch_shapes=[pltpu.VMEM((length, HEAD), FULL), pltpu.VMEM((length, HEAD), FULL)],
        compiler_params=pltpu.CompilerParams(vmem_limit_bytes=VMEM_BYTES),
        cost_estimate=pl.CostEstimate(
            flops=0, bytes_accessed=14 * length * width, transcendentals=0
        ),
    )(q_low, k_low, v_low, d_heads, log_sum, query_table, key_table)


def chosen_picks(routes, expert_count, capacity):
    experts = jnp.arange(expert_count, dtype=jnp.int32)
    onehot = (routes[:, :, None] == experts[None, None, :]).astype(jnp.int32)
    rows = routes.shape[0]
    below = (jnp.arange(rows)[:, None] > jnp.arange(rows)[None, :]).astype(LOW)
    order = matmul(below, jnp.sum(onehot, axis=1).astype(LOW)).astype(jnp.int32)
    slot = routes * capacity + jnp.sum(onehot * order[:, None, :], axis=2)
    slots = jnp.arange(expert_count * capacity, dtype=jnp.int32)
    picks = [(slot[:, k : k + 1] == slots[None, :]).astype(LOW) for k in range(routes.shape[1])]
    return picks, onehot.astype(FULL)


def expert_picks(routes_seq, expert, capacity):
    named = jnp.any(routes_seq == expert, axis=1)
    rows = named.shape[1]
    above = (jnp.arange(rows)[:, None] < jnp.arange(rows)[None, :]).astype(LOW)
    order = matmul(named.astype(LOW), above).astype(jnp.int32)
    slot = jnp.where(named, order, -1)
    return (slot[:, None, :] == jnp.arange(capacity, dtype=jnp.int32)[None, :, None]).astype(LOW)


def mix_of(logits, onehot):
    chosen = jnp.sum(onehot * logits[:, None, :], axis=2)
    return jax.nn.softmax(chosen, axis=1)


def logits_back(mix, mix_grad, probs, onehot, share_grad):
    d_chosen = mix * (mix_grad - jnp.sum(mix * mix_grad, axis=1, keepdims=True))
    d_logits = jnp.sum(onehot * d_chosen[:, :, None], axis=1)
    inner = jnp.sum(probs * share_grad[None, :], axis=1, keepdims=True)
    return d_logits + probs * (share_grad[None, :] - inner)


def through_router(d_logits, router_half):
    total = d_logits[:, 0:1] * router_half[:, 0][None, :]
    for expert in range(1, d_logits.shape[1]):
        total = total + d_logits[:, expert : expert + 1] * router_half[:, expert][None, :]
    return total


def on_device(
    tokens,
    cotangent,
    attn_routes,
    ffn_routes,
    norm_gain1,
    norm_gain2,
    attn_router,
    ffn_router,
    key_proj,
    value_proj,
    query_proj,
    out_proj,
    gate_proj,
    up_proj,
    down_proj,
):
    rows_here, features = tokens.shape
    half_width = features // 2
    picks_each = attn_routes.shape[1]
    expert_count = attn_router.shape[1]
    groups = lax.axis_size("ctx")
    mine = lax.axis_index("ctx")
    capacity = rows_here * picks_each // expert_count * 5 // 4
    slots = groups * capacity
    all_tokens = rows_here * lax.axis_size("fsdp") * groups

    tokens_spread = to_spread(tokens, 1)
    token_half = my_half(tokens_spread)
    routes_mine = jnp.concatenate([attn_routes.T, ffn_routes.T], axis=0)
    routes_mine = jnp.concatenate([routes_mine, jnp.zeros_like(routes_mine)], axis=0)
    kv_mine = jnp.concatenate([key_proj, value_proj], axis=1)
    seq_low, all_routes, kv_full, query_full, out_pieces = prologue(
        token_half, tokens_spread, routes_mine, kv_mine, query_proj[0], out_proj[0], 0
    )
    seq_routes = all_routes[0]
    seq_tokens = jnp.concatenate([seq_low[0], seq_low[1]], axis=1).astype(FULL)
    out_full = jnp.concatenate([out_pieces[n] for n in range(lax.axis_size("fsdp"))], axis=1)

    gate_pieces = gather_pieces(after(gate_proj[0], all_routes))
    up_pieces = gather_pieces(after(up_proj[0], all_routes))
    down_pieces = gather_pieces(after(down_proj[0], all_routes))

    gain1 = to_spread(norm_gain1, 0)
    gain2_half = my_half(to_spread(norm_gain2, 0))
    router1 = to_spread(attn_router, 0)
    router2 = to_spread(ffn_router, 0)
    router1_half = my_half(router1.T).T.astype(FULL)
    router2_half = my_half(router2.T).T

    scale_seq = lax.rsqrt(jnp.mean(seq_tokens * seq_tokens, axis=1, keepdims=True) + EPSILON)
    a_seq = (seq_tokens * scale_seq * gain1).astype(LOW)
    a_mine = lax.dynamic_slice_in_dim(a_seq, mine * rows_here, rows_here, 0)
    scale_one = lax.dynamic_slice_in_dim(scale_seq, mine * rows_here, rows_here, 0)
    attn_logits = matmul(a_mine, router1)
    attn_probs = jax.nn.softmax(attn_logits, axis=1)
    attn_picks, attn_onehot = chosen_picks(attn_routes, expert_count, capacity)
    ffn_picks, ffn_onehot = chosen_picks(ffn_routes, expert_count, capacity)
    attn_mix = mix_of(attn_logits, attn_onehot)

    cot_half = my_half(to_spread(cotangent, 1))
    ffn_pick = ffn_picks[0]
    for pick in ffn_picks[1:]:
        ffn_pick = ffn_pick + pick
    cot_blocks = spread_out(after(matmul_tn(ffn_pick, cot_half).astype(LOW), all_routes))

    expert_onehot = expert_picks(seq_routes[:, :picks_each], mine, capacity)
    key_table = jnp.asarray(turn_tables(groups * rows_here))
    query_table = jnp.einsum(
        "bsr,brh->bsh",
        expert_onehot.astype(FULL),
        key_table.reshape(groups, rows_here, -1),
        precision=PRECISE,
    ).reshape(slots, -1)
    rows_in = (
        jnp.einsum(
            "bsr,brd->bsd",
            expert_onehot,
            a_seq.reshape(groups, rows_here, features),
            preferred_element_type=FULL,
        )
        .astype(LOW)
        .reshape(slots, features)
    )
    query_lin = matmul(rows_in, query_full)
    kv_lin = matmul(a_seq, kv_full)
    q_low, k_low, v_low, heads_low, log_sum = attend(
        query_lin, kv_lin, query_table, key_table, groups
    )
    attn_back = send_home(after(matmul(heads_low, out_full).astype(LOW), *cot_blocks), 1)

    input_half = my_half(tokens_spread).astype(FULL)
    attn_picked = [matmul(pick, attn_back) for pick in attn_picks]
    attended = input_half
    for k in range(picks_each):
        attended = attended + attn_mix[:, k : k + 1] * attn_picked[k]
    square_sum = tp_sum(jnp.sum(attended * attended, axis=1, keepdims=True))
    scale_two = lax.rsqrt(square_sum / features + EPSILON)
    b_half = (attended * scale_two * gain2_half).astype(LOW)
    gate_all = with_neighbours(gate_pieces, heads_low)
    up_all = with_neighbours(up_pieces, attn_back)
    b_slots = matmul_tn(ffn_pick, b_half).astype(LOW)
    ffn_rows = send_out(after(b_slots, *gate_all[1:], *up_all[1:]), 2)
    ffn_logits = tp_sum(matmul(b_half, router2_half))
    ffn_probs = jax.nn.softmax(ffn_logits, axis=1)
    ffn_mix = mix_of(ffn_logits, ffn_onehot)

    ffn_seq_routes = seq_routes[:, picks_each : 2 * picks_each]
    ffn_expert_onehot = expert_picks(ffn_seq_routes, mine, capacity).astype(FULL)
    row_routes = jnp.einsum(
        "bsr,bkr->bsk", ffn_expert_onehot, ffn_seq_routes.astype(FULL), precision=PRECISE
    ).reshape(slots, picks_each)
    row_onehot = row_routes[:, :, None] == jnp.arange(expert_count, dtype=FULL)[None, None, :]
    row_mix = mix_of(matmul(ffn_rows, router2), row_onehot.astype(FULL))
    mine_too = (row_routes == mine.astype(FULL)).astype(FULL)
    mix_rows = jnp.broadcast_to(jnp.sum(row_mix * mine_too, axis=1, keepdims=True), (slots, HEAD))
    *forward, cot_rows = expert_forward(ffn_rows, gate_all, up_all, cot_blocks, 6)
    down_all = with_neighbours(down_pieces, forward[0])
    ffn_out = jnp.concatenate([matmul(forward[0], piece).astype(LOW) for piece in down_all], axis=1)
    pieces = (gate_all, up_all, down_all)
    tiles = gate_proj.shape[2] // TILE
    count_one = (tiles + 1) // 2
    near_one, landed_one, db_one, mix_grad_one, ffn_back = expert_back(
        ffn_rows, cot_rows, mix_rows, forward, pieces, 0, count_one, 7, going_home=ffn_out
    )
    sent_one, parts_one = scatter_rest(near_one, landed_one)
    back_one = last_step(sent_one)
    near_two, landed_two, db_two, mix_grad_two = expert_back(
        after(ffn_rows, sent_one), cot_rows, mix_rows, forward, pieces, count_one, tiles - count_one, 8
    )
    sent_two, parts_two = scatter_rest(near_two, landed_two)
    back_two = last_step(sent_two)
    db_rows = (db_one.astype(FULL) + db_two.astype(FULL)).astype(LOW)
    mix_grad_rows = jnp.pad(
        jnp.sum(mix_grad_one + mix_grad_two, axis=1).reshape(groups, 1, capacity),
        ((0, 0), (0, 7), (0, 256 - capacity)),
    )
    db_back, mix_grad_back = send_home(after(db_rows, sent_two), 3, extra=mix_grad_rows)
    db_back = after(db_back, back_one)
    mix_grad_back = mix_grad_back[:, 0, :capacity].reshape(1, slots)

    experts = jnp.arange(expert_count, dtype=jnp.int32)
    named = (all_routes[..., None] == experts).astype(FULL)
    hits = jnp.stack(
        [
            jnp.sum(named[:, :, :picks_each], axis=(0, 1, 2, 3)),
            jnp.sum(named[:, :, picks_each : 2 * picks_each], axis=(0, 1, 2, 3)),
        ]
    )
    share = hits / (all_tokens * picks_each)
    share_grad = AUX_WEIGHT * expert_count / all_tokens * share
    grad_half = cot_half.astype(FULL)
    d_normed2 = jnp.zeros((rows_here, half_width), FULL)
    ffn_mix_grad = []
    for pick in ffn_picks:
        d_normed2 = d_normed2 + matmul(pick, db_back)
        ffn_mix_grad.append(jnp.sum(pick.astype(FULL) * mix_grad_back, axis=1, keepdims=True))
    ffn_mix_grad = jnp.concatenate(ffn_mix_grad, axis=1)
    ffn_d_logits = logits_back(ffn_mix, ffn_mix_grad, ffn_probs, ffn_onehot, share_grad[1])
    d_normed2 = d_normed2 + through_router(ffn_d_logits, router2_half.astype(FULL))
    weighted2 = d_normed2 * gain2_half
    inner2 = tp_sum(jnp.sum(weighted2 * attended, axis=1, keepdims=True)) / features
    d_attended = grad_half + scale_two * weighted2 - attended * scale_two**3 * inner2
    gain2_part = jnp.sum(d_normed2 * attended * scale_two, axis=0)
    ffn_router_part = precise_tn(b_half.astype(FULL), ffn_d_logits)

    dy_slots = jnp.zeros((slots, half_width), FULL)
    for k in range(picks_each):
        dy_slots = dy_slots + matmul_tn(attn_picks[k], (attn_mix[:, k : k + 1] * d_attended).astype(LOW))
    dy_rows = send_out(dy_slots.astype(LOW), 4)
    d_heads = matmul_nt(dy_rows, out_full).astype(LOW)
    dq_low, dk_low, dv_low = attend_back(
        q_low, k_low, v_low, d_heads, log_sum, query_table, key_table, groups
    )
    dkv_low = after(jnp.concatenate([dk_low, dv_low], axis=1), back_two)
    da_rows = matmul_nt(dq_low, query_full).astype(LOW).reshape(groups, capacity, features)
    da_seq = jnp.einsum("bsr,bsd->brd", expert_onehot, da_rows, preferred_element_type=FULL)
    da_seq = da_seq.reshape(groups * rows_here, features) + matmul_nt(dkv_low, kv_full)
    out_sent, out_finish = scatter_start(
        lambda low, high: matmul_tn(heads_low, dy_rows[:, low:high]), features, 1
    )
    kv_sent, kv_finish = scatter_start(
        lambda low, high: matmul_tn(a_seq[:, low:high], dkv_low), features, 0
    )
    da_half, kv_back, out_back = send_home(
        da_seq.astype(LOW), 5, cargo=(kv_sent, out_sent), add_up=True
    )
    kv_part = kv_finish(kv_back)
    query_sent, query_finish = scatter_start(
        lambda low, high: matmul_tn(rows_in[:, low:high], after(dq_low, kv_part)), features, 0
    )
    query_back = last_step(query_sent)
    kv_grad = block_for(kv_part, 0)
    kv_part_low = kv_part.astype(LOW)
    for distance in far_first(groups):
        if distance:
            kv_arrived = swap(block_for(kv_part_low, distance), "ctx", distance)
            kv_grad = kv_grad + kv_arrived.astype(FULL)
    query_grad = query_finish(query_back)
    out_grad = out_finish(out_back)
    back_one, back_two = lax.optimization_barrier((back_one, back_two, query_back))[:2]
    gate_grad, up_grad, down_grad = finish_experts(parts_one + [back_one], parts_two + [back_two])
    key_width = key_proj.shape[1]

    result = attended
    for k in range(picks_each):
        result = result + ffn_mix[:, k : k + 1] * matmul(ffn_picks[k], ffn_back)
    result_low = result.astype(LOW)
    output = from_spread(join_halves(result_low, swap(result_low, "tp", 1)), 1)

    attn_mix_grad = tp_sum(
        jnp.concatenate(
            [jnp.sum(d_attended * picked, axis=1, keepdims=True) for picked in attn_picked], axis=1
        )
    )
    attn_d_logits = logits_back(attn_mix, attn_mix_grad, attn_probs, attn_onehot, share_grad[0])
    a_half = my_half(a_mine)
    attn_router_part = precise_tn(a_half.astype(FULL), attn_d_logits)

    d_normed1 = da_half + through_router(attn_d_logits, router1_half)
    gain1_half = my_half(gain1)
    weighted1 = d_normed1 * gain1_half
    inner1 = tp_sum(jnp.sum(weighted1 * input_half, axis=1, keepdims=True)) / features
    input_grad = d_attended + scale_one * weighted1 - input_half * scale_one**3 * inner1
    input_grad_low = input_grad.astype(LOW)
    input_grad = from_spread(join_halves(input_grad_low, swap(input_grad_low, "tp", 1)), 1).astype(FULL)
    gain1_part = jnp.sum(d_normed1 * input_half * scale_one, axis=0)

    small = jnp.concatenate(
        [gain1_part[None], gain2_part[None], attn_router_part.T, ffn_router_part.T], axis=0
    )
    small = from_spread(join_halves(small, swap(small, "tp", 1)), 1)
    prob_sums = jnp.concatenate([jnp.sum(attn_probs, axis=0), jnp.sum(ffn_probs, axis=0)])
    small = jnp.concatenate([small, jnp.pad(prob_sums, (0, features - prob_sums.shape[0]))[None]], axis=0)
    small = all_sum(after(all_sum(small, ("fsdp",)), query_back), ("ctx",))
    prob_sums = small[-1, : 2 * expert_count].reshape(2, expert_count)
    losses = expert_count * jnp.sum(share * prob_sums / all_tokens, axis=1)
    return (
        output,
        input_grad,
        losses[0],
        losses[1],
        small[0],
        small[1],
        small[2 : 2 + expert_count].T,
        small[2 + expert_count : 2 + 2 * expert_count].T,
        kv_grad[:, :key_width],
        kv_grad[:, key_width:],
        query_grad[None],
        out_grad[None],
        gate_grad[None],
        up_grad[None],
        down_grad[None],
    )


def solution(mesh):
    by_token = P(("fsdp", "ctx"), None)
    by_row = P(("fsdp", "ctx"), "tp")
    inward = P("ctx", "fsdp", "tp")
    outward = P("ctx", "tp", "fsdp")
    weights = (by_row, by_row, inward, outward, inward, inward, outward)
    return jax.shard_map(
        on_device,
        mesh=mesh,
        in_specs=(by_token,) * 4 + (P(),) * 4 + weights,
        out_specs=(by_token,) * 2 + (P(),) * 6 + weights,
        check_vma=False,
    )
```

```python
import functools
import math

import jax
import jax.numpy as jnp
import numpy as np
from jax import lax
from jax.experimental import pallas as pl
from jax.experimental.pallas import tpu as pltpu
from jax.sharding import PartitionSpec as P

HEAD = 128
EPSILON = 1e-06
ROPE_BASE = 10000.0
AUX_WEIGHT = 0.1
PRECISE = lax.Precision.HIGHEST
LOW = jnp.bfloat16
FULL = jnp.float32
VMEM_BYTES = 58 * 1024 * 1024
TILE = 256


def matmul(lhs, rhs):
    return jnp.dot(lhs, rhs, preferred_element_type=FULL)


def matmul_tn(lhs, rhs):
    return lax.dot_general(lhs, rhs, (((0,), (0,)), ((), ())), preferred_element_type=FULL)


def matmul_nt(lhs, rhs):
    return lax.dot_general(lhs, rhs, (((1,), (1,)), ((), ())), preferred_element_type=FULL)


def precise_tn(lhs, rhs):
    return lax.dot_general(lhs, rhs, (((0,), (0,)), ((), ())), precision=PRECISE)


def swap(value, axis, distance):
    size = lax.axis_size(axis)
    return lax.ppermute(value, axis, [(i, i ^ distance) for i in range(size)])


def after(value, *earlier):
    return lax.optimization_barrier((value,) + earlier)[0]


def bits_down(size):
    bit = size // 2
    while bit >= 1:
        yield bit
        bit //= 2


def spread_order(size):
    order = [0]
    for bit in bits_down(size):
        order = order + [place | bit for place in order]
    return order


def gather_pieces(piece):
    pieces = [piece]
    for bit in bits_down(lax.axis_size("fsdp")):
        if bit > 1:
            pieces = pieces + [swap(item, "fsdp", bit) for item in pieces]
    return pieces


def with_neighbours(pieces, known, *earlier):
    rest = [swap(after(item, *earlier), "fsdp", 1) for item in pieces[len(known) :]]
    return pieces + list(known) + rest


def flip_blocks(value, axis, index, count):
    parts = jnp.split(value, count, axis)
    for bit in bits_down(count):
        turned = (index // bit) % 2 == 1
        parts = [jnp.where(turned, parts[n ^ bit], parts[n]) for n in range(count)]
    return jnp.concatenate(parts, axis)


def to_spread(value, axis):
    size = lax.axis_size("fsdp")
    value = flip_blocks(value, axis, lax.axis_index("fsdp"), size)
    parts = jnp.split(value, size, axis)
    return jnp.concatenate([parts[place] for place in spread_order(size)], axis)


def from_spread(value, axis):
    size = lax.axis_size("fsdp")
    parts = jnp.split(value, size, axis)
    order = spread_order(size)
    value = jnp.concatenate([parts[order.index(place)] for place in range(size)], axis)
    return flip_blocks(value, axis, lax.axis_index("fsdp"), size)


def my_half(value):
    width = value.shape[-1] // 2
    return jnp.where(lax.axis_index("tp") == 0, value[..., :width], value[..., width:])


def other_half(value):
    width = value.shape[-1] // 2
    return jnp.where(lax.axis_index("tp") == 0, value[..., width:], value[..., :width])


def join_halves(mine, other):
    first = lax.axis_index("tp") == 0
    return jnp.concatenate([jnp.where(first, mine, other), jnp.where(first, other, mine)], -1)


def tp_sum(value):
    return value + swap(value, "tp", 1)


def all_sum(value, axes):
    for axis in axes:
        for bit in bits_down(lax.axis_size(axis)):
            value = value + swap(value, axis, bit)
    return value


def far_first(size):
    return list(range(size // 2, size)) + list(range(size // 2 - 1, -1, -1))


def place_blocks(blocks):
    index = lax.axis_index("ctx")
    rows = blocks[0].shape[0]
    total = jnp.zeros((rows * len(blocks),) + blocks[0].shape[1:], blocks[0].dtype)
    for distance, block in enumerate(blocks):
        total = lax.dynamic_update_slice_in_dim(total, block, (index ^ distance) * rows, 0)
    return total


def block_for(value, distance):
    size = lax.axis_size("ctx")
    rows = value.shape[0] // size
    return lax.dynamic_slice_in_dim(value, (lax.axis_index("ctx") ^ distance) * rows, rows, 0)


def spread_out(half_rows):
    blocks = [block_for(half_rows, distance) for distance in range(lax.axis_size("ctx"))]
    return blocks[:1] + [swap(blocks[distance], "ctx", distance) for distance in range(1, len(blocks))]


def xor_index(index, distance):
    result = index
    bit = 1
    while bit <= distance:
        if distance & bit:
            result = result + bit - 2 * bit * ((index // bit) % 2)
        bit *= 2
    return result


def span(start, size):
    return pl.ds(pl.multiple_of(start * size, 16), size)


def meet(peers):
    barrier = pltpu.get_barrier_semaphore()
    for device in peers:
        pl.semaphore_signal(barrier, inc=1, device_id=device, device_id_type=pl.DeviceIdType.MESH)
    pl.semaphore_wait(barrier, len(peers))


def remote(source, target, sems, index, device):
    return pltpu.make_async_remote_copy(
        src_ref=source,
        dst_ref=target,
        send_sem=sems[0].at[index],
        recv_sem=sems[1].at[index],
        device_id=device,
        device_id_type=pl.DeviceIdType.MESH,
    )


def near_first(size):
    return list(range(1, size))


def mixed_order(size):
    return [distance for distance in spread_order(size) if distance] + [0]


def cuts_of(rows):
    for count in (4, 2):
        if rows % (16 * count) == 0:
            return count
    return 1


def send_out_kernel(size, rows_ref, out_ref, z_land, y_land, z_send, z_recv, y_send, y_recv):
    mine, first = lax.axis_index("ctx"), lax.axis_index("tp") == 0
    other_tp = {"tp": 1 - lax.axis_index("tp")}
    rows, width = z_land.shape[1], z_land.shape[2]
    cuts = cuts_of(rows)
    part = rows // cuts
    at = [xor_index(mine, distance) for distance in range(size)]
    meet([{"ctx": at[distance]} for distance in range(1, size)] + [other_tp])
    order = [(distance, cut) for distance in near_first(size) for cut in range(cuts)]
    own = [(0, cut) for cut in range(cuts)]
    across, beside = {}, {}

    def source(distance, cut):
        start = pl.multiple_of(at[distance] * rows + cut * part, 16)
        return rows_ref.at[pl.ds(start, part)]

    def inside(distance, cut):
        return distance, pl.ds(cut * part, part)

    for distance, cut in order:
        across[distance, cut] = remote(
            source(distance, cut),
            z_land.at[inside(distance, cut)],
            (z_send, z_recv),
            distance * cuts + cut,
            {"ctx": at[distance]},
        )
        across[distance, cut].start()
    for distance, cut in own + order:
        if distance:
            across[distance, cut].wait_recv()
        beside[distance, cut] = remote(
            z_land.at[inside(distance, cut)] if distance else source(0, cut),
            y_land.at[inside(distance, cut)],
            (y_send, y_recv),
            distance * cuts + cut,
            other_tp,
        )
        beside[distance, cut].start()
    for distance, cut in own + order:
        beside[distance, cut].wait_recv()
        held = z_land[inside(distance, cut)] if distance else source(0, cut)[...]
        theirs = y_land[inside(distance, cut)]
        here = pl.ds(pl.multiple_of(at[distance] * rows + cut * part, 16), part)
        out_ref[here, :width] = jnp.where(first, held, theirs)
        out_ref[here, width:] = jnp.where(first, theirs, held)
    for item in order:
        across[item].wait_send()
    for item in own + order:
        beside[item].wait_send()


def send_out(half_rows, number):
    size = lax.axis_size("ctx")
    total, width = half_rows.shape
    land = pltpu.VMEM((size, total // size, width), half_rows.dtype)
    return pl.pallas_call(
        functools.partial(send_out_kernel, size),
        in_specs=[pl.BlockSpec(memory_space=pltpu.VMEM)],
        out_specs=pl.BlockSpec(memory_space=pltpu.VMEM),
        out_shape=jax.ShapeDtypeStruct((total, 2 * width), half_rows.dtype),
        scratch_shapes=[land, land] + [pltpu.SemaphoreType.DMA((size * cuts_of(total // size),))] * 4,
        compiler_params=pltpu.CompilerParams(
            collective_id=number, has_side_effects=True, vmem_limit_bytes=VMEM_BYTES
        ),
        cost_estimate=pl.CostEstimate(flops=0, bytes_accessed=12 * total * width, transcendentals=0),
    )(half_rows)


def send_home_kernel(size, adds, has_extra, cargo_axes, *refs):
    cargoes = len(cargo_axes)
    streams = len(adds)
    parts, refs = refs[:streams], refs[streams:]
    extra_ref, refs = (refs[0], refs[1:]) if has_extra else (None, refs)
    cargo_in, refs = refs[:cargoes], refs[cargoes:]
    outs, refs = refs[:streams], refs[streams:]
    extra_out, refs = (refs[0], refs[1:]) if has_extra else (None, refs)
    cargo_out, refs = refs[:cargoes], refs[cargoes:]
    lands, refs = [refs[7 * n : 7 * n + 7] for n in range(streams)], refs[7 * streams :]
    mine, first = lax.axis_index("ctx"), lax.axis_index("tp") == 0
    place = lax.axis_index("tp")
    other_tp = {"tp": 1 - place}
    at = [xor_index(mine, distance) for distance in range(size)]
    world = lax.axis_size("fsdp")
    spot = lax.axis_index("fsdp")
    along = {"tp": other_tp, "fsdp": {"fsdp": xor_index(spot, world // 2)}, "core": {"fsdp": xor_index(spot, 1)}}
    extra_peers = [along[axis] for axis in ("fsdp", "core") if axis in cargo_axes]
    meet([{"ctx": at[distance]} for distance in range(1, size)] + [other_tp] + extra_peers)
    order = mixed_order(size)
    beside, across, extras = {}, {}, {}
    cargo = [
        remote(cargo_in[n], cargo_out[n], refs[-2:], n, along[axis])
        for n, axis in enumerate(cargo_axes)
    ]
    for copy, axis in zip(cargo, cargo_axes):
        if axis != "tp":
            copy.start()
    if has_extra:
        ey_land, e_ready, ez_land, ey_send, ey_recv, ez_send, ez_recv = refs[:7]
        extra_beside = remote(extra_ref, ey_land, (ey_send, ey_recv), 0, other_tp)
        extra_beside.start()
    turns = []
    for n in range(streams):
        y_land, _, z_land, y_send, y_recv, _, _ = lands[n]
        rows, width = z_land.shape[1], z_land.shape[2]
        cuts = cuts_of(rows)
        part = rows // cuts
        columns = pl.ds(pl.multiple_of((1 - place) * width, 128), width)
        for distance in order:
            for cut in range(cuts):
                inside = distance, pl.ds(cut * part, part)
                here = pl.ds(pl.multiple_of(at[distance] * rows + cut * part, 16), part)
                number = distance * cuts + cut
                beside[n, number] = remote(
                    parts[n].at[here, columns], y_land.at[inside], (y_send, y_recv), number, other_tp
                )
                beside[n, number].start()
                turns.append((n, distance, cut, number, part, width, inside, here))
    for copy, axis in zip(cargo, cargo_axes):
        if axis == "tp":
            copy.start()
    if has_extra:
        extra_beside.wait_recv()
        e_ready[...] = extra_ref[...] + ey_land[...]
        for distance in order:
            if distance:
                extras[distance] = remote(
                    e_ready.at[at[distance]],
                    ez_land.at[distance],
                    (ez_send, ez_recv),
                    distance,
                    {"ctx": at[distance]},
                )
                extras[distance].start()
    for n, distance, cut, number, part, width, inside, here in turns:
        y_land, ready, z_land, _, _, z_send, z_recv = lands[n]
        beside[n, number].wait_recv()
        whole = parts[n][here, :]
        own = jnp.where(first, whole[:, :width], whole[:, width:])
        total = (own.astype(FULL) + y_land[inside].astype(FULL)).astype(LOW)
        if distance:
            ready[inside] = total
            across[n, number] = remote(
                ready.at[inside], z_land.at[inside], (z_send, z_recv), number, {"ctx": at[distance]}
            )
            across[n, number].start()
        elif adds[n]:
            outs[n][inside[1], :] = total.astype(FULL)
        else:
            outs[n][here, :] = total
    for n, distance, cut, number, part, width, inside, here in turns:
        if distance:
            across[n, number].wait_recv()
            if adds[n]:
                outs[n][inside[1], :] += lands[n][2][inside].astype(FULL)
            else:
                outs[n][here, :] = lands[n][2][inside]
    if has_extra:
        extra_out[mine] = e_ready[mine]
        for distance in order:
            if distance:
                extras[distance].wait_recv()
                extra_out[at[distance]] = ez_land[distance]
                extras[distance].wait_send()
        extra_beside.wait_send()
    for copy in list(beside.values()) + list(across.values()):
        copy.wait_send()
    for copy in cargo:
        copy.wait()


def send_home(partial_rows, number, extra=None, cargo=(), add_up=False, more=None):
    size = lax.axis_size("ctx")
    operands = [partial_rows] if more is None else [partial_rows, more]
    adds = (add_up, False)[: len(operands)]
    sems = [pltpu.SemaphoreType.DMA((size,))] * 4
    shapes, scratch, moved = [], [], 0
    for item, added in zip(operands, adds):
        total, width = item.shape[0], item.shape[1] // 2
        rows = total // size
        moved += 12 * total * width
        shapes.append(
            jax.ShapeDtypeStruct((rows, width), FULL) if added else jax.ShapeDtypeStruct((total, width), LOW)
        )
        scratch += [pltpu.VMEM((size, rows, width), LOW)] * 3
        scratch += [pltpu.SemaphoreType.DMA((size * cuts_of(rows),))] * 4
    if extra is not None:
        operands.append(extra)
        shapes.append(jax.ShapeDtypeStruct(extra.shape, FULL))
        scratch += [pltpu.VMEM(extra.shape, FULL)] * 3 + sems
    in_specs = [pl.BlockSpec(memory_space=pltpu.VMEM)] * len(operands)
    out_specs = [pl.BlockSpec(memory_space=pltpu.VMEM)] * len(shapes)
    for item, _ in cargo:
        operands.append(item)
        shapes.append(jax.ShapeDtypeStruct(item.shape, item.dtype))
        in_specs.append(pl.BlockSpec(memory_space=pl.ANY))
        out_specs.append(pl.BlockSpec(memory_space=pl.ANY))
    if cargo:
        scratch += [pltpu.SemaphoreType.DMA((len(cargo),))] * 2
    results = pl.pallas_call(
        functools.partial(send_home_kernel, size, adds, extra is not None, tuple(axis for _, axis in cargo)),
        in_specs=in_specs,
        out_specs=out_specs,
        out_shape=shapes,
        scratch_shapes=scratch,
        compiler_params=pltpu.CompilerParams(
            collective_id=number, has_side_effects=True, vmem_limit_bytes=VMEM_BYTES
        ),
        cost_estimate=pl.CostEstimate(flops=0, bytes_accessed=moved, transcendentals=0),
    )(*operands)
    return results if len(shapes) > 1 else results[0]


def prologue_kernel(sizes, *refs):
    groups, world = sizes
    half_in, own_in, routes_in, kv_in, query_in, out_in = refs[:6]
    seq_ref, routes_ref, kv_ref, query_ref, out_ref = refs[6:11]
    local_sem = refs[11]
    pairs = [(refs[12 + 2 * n], refs[13 + 2 * n]) for n in range(15)]
    token_line, route_line, kv_line, token_pass, kv_pass = (pairs[2 * n : 2 * n + 2] for n in range(5))
    kv_own, fr, fk, fq, fo = pairs[10:]
    mine, place, spot = lax.axis_index("ctx"), lax.axis_index("tp"), lax.axis_index("fsdp")
    other_tp = {"tp": 1 - place}
    rows, width = half_in.shape
    sub = kv_in.shape[0]
    piece = sub * groups
    q_rows = query_in.shape[0]
    steps = list(bits_down(world))
    beside = {bit: {"fsdp": xor_index(spot, bit)} for bit in steps}
    first = steps[0]
    meet(
        [{"ctx": xor_index(mine, distance)} for distance in range(1, groups)]
        + [other_tp]
        + [beside[bit] for bit in steps]
    )
    locals_ = [
        pltpu.make_async_copy(
            own_in.at[:, pl.ds(n * width, width)], seq_ref.at[n, span(mine, rows)], local_sem.at[n]
        )
        for n in range(2)
    ] + [
        pltpu.make_async_copy(routes_in, routes_ref.at[0, mine], local_sem.at[2]),
        pltpu.make_async_copy(kv_in, kv_ref.at[span(mine, sub)], local_sem.at[3]),
        pltpu.make_async_copy(query_in, query_ref.at[pl.ds(0, q_rows)], local_sem.at[4]),
        pltpu.make_async_copy(out_in, out_ref.at[0], local_sem.at[5]),
    ]
    started, landed = [], set()

    def go(copy):
        copy.start()
        started.append(copy)
        return copy

    def arrived(copy):
        if id(copy) not in landed:
            copy.wait_recv()
            landed.add(id(copy))

    def wrap(index):
        return lax.rem(index + groups, groups)

    def outgoing(step):
        yield 0, jnp.logical_and(mine < groups - 1, mine >= step), wrap(mine - step), wrap(mine + 1)
        yield 1, jnp.logical_and(mine > 0, mine + step < groups), wrap(mine + step), wrap(mine - 1)

    def incoming(step):
        yield 0, mine >= step + 1, wrap(mine - 1 - step)
        yield 1, mine + step + 1 < groups, wrap(mine + 1 + step)

    def line_copy(own, place_of, sems, step, way, block, target):
        source = place_of(block) if step else own
        return remote(source, place_of(block), sems[way], step, {"ctx": target})

    def line_start(own, place_of, sems, step):
        for way, happens, block, target in outgoing(step):

            @pl.when(happens)
            def _():
                line_copy(own, place_of, sems, step, way, block, target).start()

    def line_wait(place_of, sems, step, passed):
        for way, happens, block in incoming(step):

            @pl.when(happens)
            def _():
                remote(place_of(block), place_of(block), sems[way], step, other_tp).wait_recv()
                if passed is not None:
                    passed(step, way, block).start()

    def line_end(own, place_of, sems, step, passed):
        for way, happens, block, target in outgoing(step):

            @pl.when(happens)
            def _():
                line_copy(own, place_of, sems, step, way, block, target).wait_send()

        if passed is None:
            return
        for way, happens, block in incoming(step):

            @pl.when(happens)
            def _():
                passed(step, way, block).wait_send()

    def passed_wait(step, passed):
        for way, happens, block in incoming(step):

            @pl.when(happens)
            def _():
                passed(step, way, block).wait_recv()

    route_place = lambda n: routes_ref.at[0, n]
    kv_place = lambda n: kv_ref.at[span(n, sub)]
    token_place = lambda n: seq_ref.at[place, span(n, rows)]

    def kv_along(step, way, block):
        target = kv_ref.at[pl.ds(pl.multiple_of(piece + block * sub, 16), sub)]
        return remote(kv_place(block), target, kv_pass[way], step, beside[first])

    def token_along(step, way, block):
        return remote(token_place(block), token_place(block), token_pass[way], step, other_tp)

    def token_landed(step, way, block):
        view = seq_ref.at[1 - place, span(block, rows)]
        return remote(view, view, token_pass[way], step, other_tp)

    kv_first = go(
        remote(
            kv_in,
            kv_ref.at[pl.ds(pl.multiple_of(piece + mine * sub, 16), sub)],
            kv_own,
            0,
            beside[first],
        )
    )
    query_view = lambda n: query_ref.at[pl.ds(n * q_rows, q_rows)]
    out_view = lambda n: out_ref.at[n]
    kv_view = lambda n: kv_ref.at[pl.ds(n * piece, piece)]
    query_copies = {1: go(remote(query_in, query_view(1), fq, 1, beside[first]))}
    out_copies = {}
    for copy in locals_:
        copy.start()
    for step in range(groups - 1):
        line_start(kv_in, kv_place, kv_line, step)
        line_start(routes_in, route_place, route_line, step)
        line_start(half_in, token_place, token_line, step)
        if step == 0:
            for copy in locals_:
                copy.wait()
            for bit in steps[1:]:
                n = world // (2 * bit)
                query_copies[n] = go(remote(query_in, query_view(n), fq, n, beside[bit]))
                out_copies[n] = go(remote(out_in, out_view(n), fo, n, beside[bit]))
        line_wait(kv_place, kv_line, step, kv_along)
        if step == groups - 2:
            out_copies[1] = go(remote(out_in, out_view(1), fo, 1, beside[first]))
        line_wait(route_place, route_line, step, None)
        line_wait(token_place, token_line, step, token_along)
    route_wait, kv_wait = {}, {}
    count = 1
    for bit in steps:
        for n in range(count):
            peer = beside[bit]
            if n in route_wait:
                arrived(route_wait[n])
            route_wait[count + n] = go(
                remote(routes_ref.at[n], routes_ref.at[count + n], fr, count + n, peer)
            )
            if bit == first:
                continue
            if n:
                arrived(query_copies[n])
                query_copies[count + n] = go(
                    remote(query_view(n), query_view(count + n), fq, count + n, peer)
                )
            if n == 1 and count == 2:
                arrived(kv_first)
                for step in range(groups - 1):
                    passed_wait(step, kv_along)
            if n > 1:
                arrived(kv_wait[n])
            kv_wait[count + n] = go(remote(kv_view(n), kv_view(count + n), fk, count + n, peer))
            if n:
                arrived(out_copies[n])
                out_copies[count + n] = go(remote(out_view(n), out_view(count + n), fo, count + n, peer))
        count *= 2
    if world == 2:
        arrived(kv_first)
        for step in range(groups - 1):
            passed_wait(step, kv_along)
    for copy in started:
        arrived(copy)
    for step in range(groups - 1):
        passed_wait(step, token_landed)
        line_end(kv_in, kv_place, kv_line, step, kv_along)
        line_end(routes_in, route_place, route_line, step, None)
        line_end(half_in, token_place, token_line, step, token_along)
    for copy in started:
        copy.wait_send()


def prologue(token_half, token_rows, routes, kv_rows, query_piece, out_piece, number):
    groups, world = lax.axis_size("ctx"), lax.axis_size("fsdp")
    any_space = pl.BlockSpec(memory_space=pl.ANY)
    rows, features = token_rows.shape
    pair = lambda count: [pltpu.SemaphoreType.DMA((count,))] * 2
    return pl.pallas_call(
        functools.partial(prologue_kernel, (groups, world)),
        in_specs=[pl.BlockSpec(memory_space=pltpu.VMEM)] * 6,
        out_specs=[any_space] * 5,
        out_shape=[
            jax.ShapeDtypeStruct((2, groups * rows, features // 2), LOW),
            jax.ShapeDtypeStruct((world, groups) + routes.shape, jnp.int32),
            jax.ShapeDtypeStruct((world * groups * kv_rows.shape[0], kv_rows.shape[1]), LOW),
            jax.ShapeDtypeStruct((world * query_piece.shape[0], query_piece.shape[1]), LOW),
            jax.ShapeDtypeStruct((world,) + out_piece.shape, LOW),
        ],
        scratch_shapes=[pltpu.SemaphoreType.DMA((6,))] + pair(groups) * 10 + pair(1) + pair(world) * 4,
        compiler_params=pltpu.CompilerParams(
            collective_id=number, has_side_effects=True, vmem_limit_bytes=VMEM_BYTES
        ),
        cost_estimate=pl.CostEstimate(flops=0, bytes_accessed=100000000, transcendentals=0),
    )(token_half, token_rows, routes, kv_rows, query_piece, out_piece)


def expert_forward_kernel(world, size, *refs):
    rows_ref = refs[0]
    gates, ups = refs[1 : 1 + world], refs[1 + world : 1 + 2 * world]
    refs = refs[1 + 2 * world :]
    blocks, beside_ref, refs = refs[:size], refs[size], refs[size + 1 :]
    hidden_ref, by_gate_ref, by_up_ref, cot_ref, y_land, y_send, y_recv = refs
    width = rows_ref.shape[1] // world
    mine, place = lax.axis_index("ctx"), lax.axis_index("tp")
    other_tp = {"tp": 1 - place}
    beside = [
        remote(blocks[distance], y_land.at[distance], (y_send, y_recv), distance, other_tp)
        for distance in range(1, size)
    ]

    @pl.when(pl.program_id(0) == 0)
    def _():
        meet([other_tp])
        for copy in beside:
            copy.start()

    gate_lin, up_lin = None, None
    for n in range(world):
        columns = slice(n * width, (n + 1) * width)
        gate_term = matmul(rows_ref[:, columns], gates[n][...])
        up_term = matmul(rows_ref[:, columns], ups[n][...])
        gate_lin = gate_lin + gate_term if n else gate_term
        up_lin = up_lin + up_term if n else up_term
    sigmoid_gate = 1.0 / (1.0 + jnp.exp(-gate_lin))
    swish = gate_lin * sigmoid_gate
    hidden_ref[...] = (swish * up_lin).astype(LOW)
    by_gate_ref[...] = (up_lin * sigmoid_gate * (1.0 + gate_lin * (1.0 - sigmoid_gate))).astype(LOW)
    by_up_ref[...] = swish.astype(LOW)

    @pl.when(pl.program_id(0) == pl.num_programs(0) - 1)
    def _():
        rows, half = y_land.shape[1], y_land.shape[2]
        for distance in range(size):
            if distance:
                beside[distance - 1].wait_recv()
            own = blocks[distance][...]
            theirs = y_land[distance] if distance else beside_ref[...]
            here = span(xor_index(mine, distance), rows)
            cot_ref[here, :half] = jnp.where(place == 0, own, theirs)
            cot_ref[here, half:] = jnp.where(place == 0, theirs, own)
        for copy in beside:
            copy.wait_send()


def expert_forward(rows, gate_pieces, up_pieces, cot_blocks, cot_beside, number):
    world, size = len(gate_pieces), len(cot_blocks)
    slots, features = rows.shape
    depth, hidden_width = gate_pieces[0].shape
    tall = pl.BlockSpec((depth, TILE), lambda i: (0, i))
    strip = pl.BlockSpec((slots, TILE), lambda i: (0, i))
    whole = lambda value: pl.BlockSpec(value.shape, lambda i: (0, 0), pipeline_mode=pl.Buffered(1))
    return pl.pallas_call(
        functools.partial(expert_forward_kernel, world, size),
        grid=(hidden_width // TILE,),
        in_specs=[whole(rows)] + [tall] * (2 * world) + [whole(block) for block in cot_blocks] + [whole(cot_beside)],
        out_specs=[strip] * 3 + [pl.BlockSpec((slots, features), lambda i: (0, 0))],
        out_shape=[jax.ShapeDtypeStruct((slots, hidden_width), LOW)] * 3
        + [jax.ShapeDtypeStruct((slots, features), LOW)],
        scratch_shapes=[pltpu.VMEM((size,) + cot_blocks[0].shape, LOW)]
        + [pltpu.SemaphoreType.DMA((size,))] * 2,
        compiler_params=pltpu.CompilerParams(
            collective_id=number, has_side_effects=True, vmem_limit_bytes=VMEM_BYTES
        ),
        cost_estimate=pl.CostEstimate(flops=0, bytes_accessed=2 * slots * features, transcendentals=0),
    )(rows, *gate_pieces, *up_pieces, *cot_blocks, cot_beside)


def product_kernel(world, tiles, hidden_ref, *refs):
    downs, out_ref = refs[:world], refs[world]
    for n in range(world):

        @pl.when(pl.program_id(0) // tiles == n)
        def _():
            out_ref[...] = matmul(hidden_ref[...], downs[n][...]).astype(LOW)


def expert_product(hidden, down_pieces):
    world = len(down_pieces)
    depth, width = down_pieces[0].shape
    tiles = max(width // TILE, 1)
    tile = width // tiles

    def piece_spec(n):
        return pl.BlockSpec((depth, tile), lambda i: (0, jnp.clip(i - n * tiles, 0, tiles - 1)))

    return pl.pallas_call(
        functools.partial(product_kernel, world, tiles),
        grid=(world * tiles,),
        in_specs=[pl.BlockSpec(hidden.shape, lambda i: (0, 0), pipeline_mode=pl.Buffered(1))]
        + [piece_spec(n) for n in range(world)],
        out_specs=pl.BlockSpec((hidden.shape[0], tile), lambda i: (0, i)),
        out_shape=jax.ShapeDtypeStruct((hidden.shape[0], world * width), LOW),
        compiler_params=pltpu.CompilerParams(vmem_limit_bytes=VMEM_BYTES),
        cost_estimate=pl.CostEstimate(
            flops=2 * hidden.shape[0] * depth * world * width,
            bytes_accessed=2 * depth * world * width,
            transcendentals=0,
        ),
    )(hidden, *down_pieces)


def expert_back_kernel(world, steps, size, *refs):
    rows_ref, cot_ref, mix_ref, hidden_ref, by_gate_ref, by_up_ref = refs[:6]
    gates, ups, downs = (refs[6 + n * world : 6 + (n + 1) * world] for n in range(3))
    refs = refs[6 + 3 * world :]
    part_ref, refs = (refs[0], refs[1:]) if size else (None, refs)
    near_ref, landed_ref, db_ref, mix_grad_ref = refs[:4]
    home_ref, refs = (refs[4], refs[5:]) if size else (None, refs[4:])
    db_sum, rows_t_ref, cot_t_ref, far, send_sem, recv_sem = refs[:6]
    step = pl.program_id(0)
    slot = lax.rem(step, 2)
    features = rows_ref.shape[1]
    width = features // world
    half = features // 2
    tile = near_ref.shape[3]
    other_core = {"fsdp": xor_index(lax.axis_index("fsdp"), 1)}
    peers = [other_core]
    if size:
        y_land, ready, z_land, y_send, y_recv, z_send, z_recv = refs[6:]
        mine, place = lax.axis_index("ctx"), lax.axis_index("tp")
        other_tp = {"tp": 1 - place}
        at = [xor_index(mine, distance) for distance in range(size)]
        peers = peers + [other_tp] + [{"ctx": at[distance]} for distance in range(1, size)]
        home_rows, home_width = z_land.shape[1], z_land.shape[2]
        away = pl.ds(pl.multiple_of((1 - place) * home_width, 128), home_width)
        order = mixed_order(size)

        def beside(distance):
            return remote(
                part_ref.at[span(at[distance], home_rows), away],
                y_land.at[distance],
                (y_send, y_recv),
                distance,
                other_tp,
            )

        def across(distance):
            return remote(
                ready.at[distance],
                z_land.at[distance],
                (z_send, z_recv),
                distance,
                {"ctx": at[distance]},
            )

    def far_copy(at_step, at_slot):
        return pltpu.make_async_remote_copy(
            src_ref=far.at[at_slot],
            dst_ref=landed_ref.at[at_step],
            send_sem=send_sem.at[at_slot],
            recv_sem=recv_sem.at[at_step],
            device_id=other_core,
            device_id_type=pl.DeviceIdType.MESH,
        )

    @pl.when(step == 0)
    def _():
        meet(peers)
        if size:
            for distance in order:
                beside(distance).start()
        db_sum[...] = jnp.zeros_like(db_sum)
        mix_grad_ref[...] = jnp.zeros_like(mix_grad_ref)
        for place_at in range(0, features, tile):
            rows_t_ref[place_at : place_at + tile, :] = rows_ref[:, place_at : place_at + tile].T
            cot_t_ref[place_at : place_at + tile, :] = cot_ref[:, place_at : place_at + tile].T

    d_hidden = None
    for n in range(world):
        columns = slice(n * width, (n + 1) * width)
        term = matmul_nt(cot_ref[:, columns], downs[n][...])
        d_hidden = d_hidden + term if n else term
    hidden = hidden_ref[...].astype(FULL)
    mix_grad = hidden * d_hidden
    for place_at in range(0, tile, HEAD):
        mix_grad_ref[...] += mix_grad[:, place_at : place_at + HEAD]
    mix = jnp.concatenate([mix_ref[...]] * (tile // HEAD), axis=1)
    d_gated = d_hidden * mix
    mixed_low = (hidden * mix).astype(LOW)
    d_gate = (d_gated * by_gate_ref[...].astype(FULL)).astype(LOW)
    d_up = (d_gated * by_up_ref[...].astype(FULL)).astype(LOW)
    @pl.when(step >= 2)
    def _():
        far_copy(step - 2, slot).wait_send()

    pairs = ((rows_t_ref, d_gate), (rows_t_ref, d_up), (cot_t_ref, mixed_low))
    for n, (left, right) in enumerate(pairs):
        far[slot, n] = matmul(left[half:, :], right).astype(LOW)
    far_copy(step, slot).start()
    for n in range(world):
        columns = slice(n * width, (n + 1) * width)
        db_sum[:, columns] += matmul_nt(d_gate, gates[n][...]) + matmul_nt(d_up, ups[n][...])

    for n, (left, right) in enumerate(pairs):
        near_ref[0, n] = matmul(left[:half, :], right).astype(LOW)

    if size:
        for turn, distance in enumerate(order):

            @pl.when(step == min(turn + 1, steps - 1))
            def _():
                beside(distance).wait_recv()
                whole = part_ref[span(at[distance], home_rows), :]
                own = jnp.where(place == 0, whole[:, :home_width], whole[:, home_width:])
                total = (own.astype(FULL) + y_land[distance].astype(FULL)).astype(LOW)
                if distance:
                    ready[distance] = total
                    across(distance).start()
                else:
                    home_ref[span(mine, home_rows), :] = total

    @pl.when(step == steps - 1)
    def _():
        db_ref[...] = db_sum[...].astype(LOW)
        for last in range(max(steps - 2, 0), steps):
            far_copy(last, last % 2).wait_send()
        for last in range(steps):
            far_copy(last, last % 2).wait_recv()
        if size:
            for distance in order:
                beside(distance).wait_send()
                if distance:
                    across(distance).wait_recv()
                    home_ref[span(at[distance], home_rows), :] = z_land[distance]
                    across(distance).wait_send()


def expert_back(rows, cot_rows, mix_rows, forward, pieces, first, steps, number, going_home=None):
    gate_pieces, up_pieces, down_pieces = pieces
    world = len(gate_pieces)
    slots, features = rows.shape
    depth = gate_pieces[0].shape[0]
    tile = TILE
    once = pl.Buffered(1)
    whole = lambda value: pl.BlockSpec(value.shape, lambda i: (0, 0), pipeline_mode=once)
    kept = lambda width: pl.BlockSpec((slots, width), lambda i: (0, 0))
    tall = pl.BlockSpec((depth, tile), lambda i: (0, i + first))
    flat = pl.BlockSpec((tile, depth), lambda i: (i + first, 0))
    strip = pl.BlockSpec((slots, tile), lambda i: (0, i + first))
    low = lambda *shape: jax.ShapeDtypeStruct(shape, LOW)
    grads = low(steps, 3, features // 2, tile)
    operands = [rows, cot_rows, mix_rows, *forward, *gate_pieces, *up_pieces, *down_pieces]
    in_specs = [whole(rows), whole(cot_rows), whole(mix_rows)] + [strip] * 3
    in_specs += [tall] * (2 * world) + [flat] * world
    out_specs = [
        pl.BlockSpec((1, 3, features // 2, tile), lambda i: (i, 0, 0, 0)),
        pl.BlockSpec(memory_space=pl.ANY),
        kept(features),
        kept(HEAD),
    ]
    out_shape = [grads, grads, low(slots, features), jax.ShapeDtypeStruct((slots, HEAD), FULL)]
    scratch = [
        pltpu.VMEM((slots, features), FULL),
        pltpu.VMEM((features, slots), LOW),
        pltpu.VMEM((features, slots), LOW),
        pltpu.VMEM((2, 3, features // 2, tile), LOW),
        pltpu.SemaphoreType.DMA((2,)),
        pltpu.SemaphoreType.DMA((steps,)),
    ]
    size = 0
    if going_home is not None:
        size = lax.axis_size("ctx")
        operands.append(going_home)
        in_specs.append(whole(going_home))
        out_specs.append(kept(features // 2))
        out_shape.append(low(slots, features // 2))
        scratch += [pltpu.VMEM((size, slots // size, features // 2), LOW)] * 3
        scratch += [pltpu.SemaphoreType.DMA((size,))] * 4
    return pl.pallas_call(
        functools.partial(expert_back_kernel, world, steps, size),
        grid=(steps,),
        in_specs=in_specs,
        out_specs=out_specs,
        out_shape=out_shape,
        scratch_shapes=scratch,
        compiler_params=pltpu.CompilerParams(
            collective_id=number, has_side_effects=True, vmem_limit_bytes=VMEM_BYTES
        ),
        cost_estimate=pl.CostEstimate(
            flops=0, bytes_accessed=2 * slots * features, transcendentals=0
        ),
    )(*operands)


def scatter_rest(near, landed):
    pieces = lax.axis_size("fsdp")
    arrived, high, bit = [near, landed], near.shape[2], 2
    while True:
        total = arrived[0][:, :, high // 2 : high].astype(FULL)
        for block in arrived[1:]:
            total = total + block[:, :, high // 2 : high].astype(FULL)
        sent = total.astype(LOW)
        high //= 2
        if 2 * bit >= pieces:
            return sent, arrived
        arrived.append(swap(sent, "fsdp", bit))
        bit *= 2


def finish_kernel(count, steps_one, *refs):
    ones, twos = refs[:count], refs[count : 2 * count]
    outs = refs[2 * count :]

    def add_up(parts):
        for n, out in enumerate(outs):
            total = parts[0][0, n].astype(FULL)
            for part in parts[1:]:
                total = total + part[0, n].astype(FULL)
            out[...] = total.T if n == 2 else total

    @pl.when(pl.program_id(0) < steps_one)
    def _():
        add_up(ones)

    @pl.when(pl.program_id(0) >= steps_one)
    def _():
        add_up(twos)


def finish_experts(ones, twos):
    steps_one, steps_two = ones[0].shape[0], twos[0].shape[0]
    depth, tile = ones[-1].shape[2:]
    width = (steps_one + steps_two) * tile
    block = (1, 3, depth, tile)
    first = pl.BlockSpec(block, lambda i: (jnp.minimum(i, steps_one - 1), 0, 0, 0))
    second = pl.BlockSpec(block, lambda i: (jnp.maximum(i - steps_one, 0), 0, 0, 0))
    tall = pl.BlockSpec((depth, tile), lambda i: (0, i))
    return pl.pallas_call(
        functools.partial(finish_kernel, len(ones), steps_one),
        grid=(steps_one + steps_two,),
        in_specs=[first] * len(ones) + [second] * len(twos),
        out_specs=[tall, tall, pl.BlockSpec((tile, depth), lambda i: (i, 0))],
        out_shape=[jax.ShapeDtypeStruct((depth, width), FULL)] * 2
        + [jax.ShapeDtypeStruct((width, depth), FULL)],
        compiler_params=pltpu.CompilerParams(vmem_limit_bytes=VMEM_BYTES),
        cost_estimate=pl.CostEstimate(
            flops=0, bytes_accessed=30 * width * depth, transcendentals=0
        ),
    )(*ones, *twos)


def scatter_start(product, features, first_dim):
    pieces = lax.axis_size("fsdp")
    high, bit, arrived = features, 1, []

    def part(low, high):
        total = product(low, high)
        for block in arrived:
            total = total + lax.slice_in_dim(block, low, high, axis=first_dim).astype(FULL)
        return total

    while True:
        sent = part(high // 2, high).astype(LOW)
        high //= 2
        if 2 * bit >= pieces:
            break
        arrived.append(swap(sent, "fsdp", bit))
        bit *= 2

    def finish(last):
        arrived.append(last)
        return part(0, high)

    return sent, finish


def last_step(sent):
    return swap(sent, "fsdp", lax.axis_size("fsdp") // 2)


def turn_tables(length):
    half_head = HEAD // 2
    steps = np.arange(half_head, dtype=np.float32) * np.float32(2.0 / HEAD)
    frequency = np.power(np.float32(ROPE_BASE), -steps).astype(np.float32)
    angles = np.arange(length, dtype=np.float32)[:, None] * frequency[None, :]
    cosine = np.cos(angles.astype(np.float64)).astype(np.float32)
    sine = np.sin(angles.astype(np.float64)).astype(np.float32)
    return np.concatenate([cosine, cosine, -sine, sine], axis=1)


def turn(value, table):
    return value * table[:, :HEAD] + pltpu.roll(value, HEAD // 2, 1) * table[:, HEAD:]


def turn_back(value, table):
    return value * table[:, :HEAD] - pltpu.roll(value, HEAD // 2, 1) * table[:, HEAD:]


def attend_kernel(
    groups, scale, q_lin, k_lin, v_lin, q_table, k_table, q_low, k_low, v_low, heads, log_sum
):
    q_low[...] = turn(q_lin[...], q_table[...]).astype(LOW)
    k_low[...] = turn(k_lin[...], k_table[...]).astype(LOW)
    v_low[...] = v_lin[...].astype(LOW)
    rows = q_low.shape[0] // groups
    block = k_low.shape[0] // groups
    for group in range(groups):
        span = slice(group * rows, (group + 1) * rows)
        seen = slice(0, (group + 1) * block)
        scores = matmul_nt(q_low[span, :], k_low[seen, :]) * scale
        top = jnp.max(scores, axis=1, keepdims=True)
        weights = jnp.exp(scores - top)
        total = jnp.sum(weights, axis=1, keepdims=True)
        weights = (weights * (1.0 / total)).astype(LOW)
        heads[span, :] = matmul(weights, v_low[seen, :]).astype(LOW)
        log_sum[span, :] = jnp.broadcast_to(top + jnp.log(total), (rows, HEAD))


def attend(query_lin, kv_lin, query_table, key_table, groups):
    slots, width = query_lin.shape
    length = kv_lin.shape[0]
    count = width // HEAD
    by_head = lambda rows: pl.BlockSpec((rows, HEAD), lambda h: (0, h))
    whole = lambda rows: pl.BlockSpec((rows, 2 * HEAD), lambda h: (0, 0))
    return pl.pallas_call(
        functools.partial(attend_kernel, groups, 1.0 / math.sqrt(HEAD)),
        grid=(count,),
        in_specs=[
            by_head(slots),
            by_head(length),
            pl.BlockSpec((length, HEAD), lambda h: (0, h + count)),
            whole(slots),
            whole(length),
        ],
        out_specs=[by_head(slots), by_head(length), by_head(length), by_head(slots), by_head(slots)],
        out_shape=[
            jax.ShapeDtypeStruct((slots, width), LOW),
            jax.ShapeDtypeStruct((length, width), LOW),
            jax.ShapeDtypeStruct((length, width), LOW),
            jax.ShapeDtypeStruct((slots, width), LOW),
            jax.ShapeDtypeStruct((slots, width), FULL),
        ],
        compiler_params=pltpu.CompilerParams(vmem_limit_bytes=VMEM_BYTES),
        cost_estimate=pl.CostEstimate(
            flops=0, bytes_accessed=20 * length * width, transcendentals=0
        ),
    )(query_lin, kv_lin, kv_lin, query_table, key_table)


def attend_back_kernel(
    groups, scale, q_low, k_low, v_low, d_heads, log_sum, q_table, k_table, dq, dk, dv, dk_sum, dv_sum
):
    dk_sum[...] = jnp.zeros_like(dk_sum)
    dv_sum[...] = jnp.zeros_like(dv_sum)
    rows = q_low.shape[0] // groups
    block = k_low.shape[0] // groups
    for group in range(groups):
        span = slice(group * rows, (group + 1) * rows)
        seen = slice(0, (group + 1) * block)
        query, keys = q_low[span, :], k_low[seen, :]
        grads = d_heads[span, :]
        scores = matmul_nt(query, keys) * scale
        weights = jnp.exp(scores - log_sum[span, :1])
        d_weights = matmul_nt(grads, v_low[seen, :])
        delta = jnp.sum(weights * d_weights, axis=1, keepdims=True)
        d_scores = (weights * (d_weights - delta)).astype(LOW)
        dq[span, :] = turn_back(matmul(d_scores, keys) * scale, q_table[span, :]).astype(LOW)
        dk_sum[seen, :] += matmul_tn(d_scores, query) * scale
        dv_sum[seen, :] += matmul_tn(weights.astype(LOW), grads)
    dk[...] = turn_back(dk_sum[...], k_table[...]).astype(LOW)
    dv[...] = dv_sum[...].astype(LOW)


def attend_back(q_low, k_low, v_low, d_heads, log_sum, query_table, key_table, groups):
    slots, width = q_low.shape
    length = k_low.shape[0]
    count = width // HEAD
    by_head = lambda rows: pl.BlockSpec((rows, HEAD), lambda h: (0, h))
    whole = lambda rows: pl.BlockSpec((rows, 2 * HEAD), lambda h: (0, 0))
    return pl.pallas_call(
        functools.partial(attend_back_kernel, groups, 1.0 / math.sqrt(HEAD)),
        grid=(count,),
        in_specs=[
            by_head(slots),
            by_head(length),
            by_head(length),
            by_head(slots),
            by_head(slots),
            whole(slots),
            whole(length),
        ],
        out_specs=[by_head(slots), by_head(length), by_head(length)],
        out_shape=[
            jax.ShapeDtypeStruct((slots, width), LOW),
            jax.ShapeDtypeStruct((length, width), LOW),
            jax.ShapeDtypeStruct((length, width), LOW),
        ],
        scratch_shapes=[pltpu.VMEM((length, HEAD), FULL), pltpu.VMEM((length, HEAD), FULL)],
        compiler_params=pltpu.CompilerParams(vmem_limit_bytes=VMEM_BYTES),
        cost_estimate=pl.CostEstimate(
            flops=0, bytes_accessed=14 * length * width, transcendentals=0
        ),
    )(q_low, k_low, v_low, d_heads, log_sum, query_table, key_table)


def chosen_picks(routes, expert_count, capacity):
    experts = jnp.arange(expert_count, dtype=jnp.int32)
    onehot = (routes[:, :, None] == experts[None, None, :]).astype(jnp.int32)
    rows = routes.shape[0]
    below = (jnp.arange(rows)[:, None] > jnp.arange(rows)[None, :]).astype(LOW)
    order = matmul(below, jnp.sum(onehot, axis=1).astype(LOW)).astype(jnp.int32)
    slot = routes * capacity + jnp.sum(onehot * order[:, None, :], axis=2)
    slots = jnp.arange(expert_count * capacity, dtype=jnp.int32)
    picks = [(slot[:, k : k + 1] == slots[None, :]).astype(LOW) for k in range(routes.shape[1])]
    return picks, onehot.astype(FULL)


def expert_picks(routes_seq, expert, capacity):
    named = jnp.any(routes_seq == expert, axis=1)
    rows = named.shape[1]
    above = (jnp.arange(rows)[:, None] < jnp.arange(rows)[None, :]).astype(LOW)
    order = matmul(named.astype(LOW), above).astype(jnp.int32)
    slot = jnp.where(named, order, -1)
    return (slot[:, None, :] == jnp.arange(capacity, dtype=jnp.int32)[None, :, None]).astype(LOW)


def mix_of(logits, onehot):
    chosen = jnp.sum(onehot * logits[:, None, :], axis=2)
    return jax.nn.softmax(chosen, axis=1)


def logits_back(mix, mix_grad, probs, onehot, share_grad):
    d_chosen = mix * (mix_grad - jnp.sum(mix * mix_grad, axis=1, keepdims=True))
    d_logits = jnp.sum(onehot * d_chosen[:, :, None], axis=1)
    inner = jnp.sum(probs * share_grad[None, :], axis=1, keepdims=True)
    return d_logits + probs * (share_grad[None, :] - inner)


def through_router(d_logits, router_half):
    total = d_logits[:, 0:1] * router_half[:, 0][None, :]
    for expert in range(1, d_logits.shape[1]):
        total = total + d_logits[:, expert : expert + 1] * router_half[:, expert][None, :]
    return total


def on_device(
    tokens,
    cotangent,
    attn_routes,
    ffn_routes,
    norm_gain1,
    norm_gain2,
    attn_router,
    ffn_router,
    key_proj,
    value_proj,
    query_proj,
    out_proj,
    gate_proj,
    up_proj,
    down_proj,
):
    rows_here, features = tokens.shape
    half_width = features // 2
    picks_each = attn_routes.shape[1]
    expert_count = attn_router.shape[1]
    groups = lax.axis_size("ctx")
    mine = lax.axis_index("ctx")
    capacity = rows_here * picks_each // expert_count * 5 // 4
    slots = groups * capacity
    all_tokens = rows_here * lax.axis_size("fsdp") * groups

    tokens_spread = to_spread(tokens, 1)
    token_half = my_half(tokens_spread)
    routes_mine = jnp.concatenate([attn_routes.T, ffn_routes.T], axis=0)
    routes_mine = jnp.concatenate([routes_mine, jnp.zeros_like(routes_mine)], axis=0)
    kv_mine = jnp.concatenate([key_proj, value_proj], axis=1)
    seq_low, all_routes, kv_full, query_full, out_pieces = prologue(
        token_half, tokens_spread, routes_mine, kv_mine, query_proj[0], out_proj[0], 0
    )
    seq_routes = all_routes[0]
    seq_tokens = jnp.concatenate([seq_low[0], seq_low[1]], axis=1).astype(FULL)
    out_full = jnp.concatenate([out_pieces[n] for n in range(lax.axis_size("fsdp"))], axis=1)

    gate_pieces = gather_pieces(after(gate_proj[0], all_routes))
    up_pieces = gather_pieces(after(up_proj[0], all_routes))
    down_pieces = gather_pieces(after(down_proj[0], all_routes))

    gain1 = to_spread(norm_gain1, 0)
    gain2_half = my_half(to_spread(norm_gain2, 0))
    router1 = to_spread(attn_router, 0)
    router2 = to_spread(ffn_router, 0)
    router1_half = my_half(router1.T).T.astype(FULL)
    router2_half = my_half(router2.T).T

    scale_seq = lax.rsqrt(jnp.mean(seq_tokens * seq_tokens, axis=1, keepdims=True) + EPSILON)
    a_seq = (seq_tokens * scale_seq * gain1).astype(LOW)
    a_mine = lax.dynamic_slice_in_dim(a_seq, mine * rows_here, rows_here, 0)
    scale_one = lax.dynamic_slice_in_dim(scale_seq, mine * rows_here, rows_here, 0)
    attn_logits = matmul(a_mine, router1)
    attn_probs = jax.nn.softmax(attn_logits, axis=1)
    attn_picks, attn_onehot = chosen_picks(attn_routes, expert_count, capacity)
    ffn_picks, ffn_onehot = chosen_picks(ffn_routes, expert_count, capacity)
    attn_mix = mix_of(attn_logits, attn_onehot)

    cot_half = my_half(to_spread(cotangent, 1))
    ffn_pick = ffn_picks[0]
    for pick in ffn_picks[1:]:
        ffn_pick = ffn_pick + pick
    cot_blocks = spread_out(after(matmul_tn(ffn_pick, cot_half).astype(LOW), all_routes))

    expert_onehot = expert_picks(seq_routes[:, :picks_each], mine, capacity)
    key_table = jnp.asarray(turn_tables(groups * rows_here))
    query_table = jnp.einsum(
        "bsr,brh->bsh",
        expert_onehot.astype(FULL),
        key_table.reshape(groups, rows_here, -1),
        precision=PRECISE,
    ).reshape(slots, -1)
    rows_in = (
        jnp.einsum(
            "bsr,brd->bsd",
            expert_onehot,
            a_seq.reshape(groups, rows_here, features),
            preferred_element_type=FULL,
        )
        .astype(LOW)
        .reshape(slots, features)
    )
    query_lin = matmul(rows_in, query_full)
    kv_lin = matmul(a_seq, kv_full)
    q_low, k_low, v_low, heads_low, log_sum = attend(
        query_lin, kv_lin, query_table, key_table, groups
    )
    cargo = [(item, "core") for item in gate_pieces + [up_proj[0], down_proj[0]]]
    cargo = [(after(cot_blocks[0], *cot_blocks[1:]), "tp")] + cargo
    attn_back, cot_beside, *known = send_home(
        matmul(heads_low, out_full).astype(LOW), 1, cargo=cargo
    )
    gate_known, up_known, down_known = known[:-2], known[-2:-1], known[-1:]

    input_half = my_half(tokens_spread).astype(FULL)
    attn_picked = [matmul(pick, attn_back) for pick in attn_picks]
    attended = input_half
    for k in range(picks_each):
        attended = attended + attn_mix[:, k : k + 1] * attn_picked[k]
    square_sum = tp_sum(jnp.sum(attended * attended, axis=1, keepdims=True))
    scale_two = lax.rsqrt(square_sum / features + EPSILON)
    b_half = (attended * scale_two * gain2_half).astype(LOW)
    gate_all = with_neighbours(gate_pieces, gate_known)
    b_slots = matmul_tn(ffn_pick, b_half).astype(LOW)
    up_all = with_neighbours(up_pieces, up_known, b_slots)
    ffn_rows = send_out(after(b_slots, up_all[-1]), 2)
    ffn_logits = tp_sum(matmul(b_half, router2_half))
    ffn_probs = jax.nn.softmax(ffn_logits, axis=1)
    ffn_mix = mix_of(ffn_logits, ffn_onehot)

    ffn_seq_routes = seq_routes[:, picks_each : 2 * picks_each]
    ffn_expert_onehot = expert_picks(ffn_seq_routes, mine, capacity).astype(FULL)
    row_routes = jnp.einsum(
        "bsr,bkr->bsk", ffn_expert_onehot, ffn_seq_routes.astype(FULL), precision=PRECISE
    ).reshape(slots, picks_each)
    row_onehot = row_routes[:, :, None] == jnp.arange(expert_count, dtype=FULL)[None, None, :]
    row_mix = mix_of(matmul(ffn_rows, router2), row_onehot.astype(FULL))
    mine_too = (row_routes == mine.astype(FULL)).astype(FULL)
    mix_rows = jnp.broadcast_to(jnp.sum(row_mix * mine_too, axis=1, keepdims=True), (slots, HEAD))
    *forward, cot_rows = expert_forward(ffn_rows, gate_all, up_all, cot_blocks, cot_beside, 6)
    down_all = with_neighbours(down_pieces, down_known, forward[0])
    ffn_out = expert_product(forward[0], down_all)
    pieces = (gate_all, up_all, down_all)
    tiles = gate_proj.shape[2] // TILE
    count_one = (tiles + 1) // 2
    near_one, landed_one, db_one, mix_grad_one, ffn_back = expert_back(
        ffn_rows, cot_rows, mix_rows, forward, pieces, 0, count_one, 7, going_home=ffn_out
    )
    sent_one, parts_one = scatter_rest(near_one, landed_one)
    back_one = last_step(sent_one)
    near_two, landed_two, db_two, mix_grad_two = expert_back(
        after(ffn_rows, sent_one), cot_rows, mix_rows, forward, pieces, count_one, tiles - count_one, 8
    )
    sent_two, parts_two = scatter_rest(near_two, landed_two)
    back_two = last_step(sent_two)
    db_rows = (db_one.astype(FULL) + db_two.astype(FULL)).astype(LOW)
    mix_grad_rows = jnp.pad(
        jnp.sum(mix_grad_one + mix_grad_two, axis=1).reshape(groups, 1, capacity),
        ((0, 0), (0, 7), (0, 256 - capacity)),
    )
    db_back, mix_grad_back = send_home(after(db_rows, sent_two), 3, extra=mix_grad_rows)
    db_back = after(db_back, back_one)
    mix_grad_back = mix_grad_back[:, 0, :capacity].reshape(1, slots)

    experts = jnp.arange(expert_count, dtype=jnp.int32)
    named = (all_routes[..., None] == experts).astype(FULL)
    hits = jnp.stack(
        [
            jnp.sum(named[:, :, :picks_each], axis=(0, 1, 2, 3)),
            jnp.sum(named[:, :, picks_each : 2 * picks_each], axis=(0, 1, 2, 3)),
        ]
    )
    share = hits / (all_tokens * picks_each)
    share_grad = AUX_WEIGHT * expert_count / all_tokens * share
    grad_half = cot_half.astype(FULL)
    d_normed2 = jnp.zeros((rows_here, half_width), FULL)
    ffn_mix_grad = []
    for pick in ffn_picks:
        d_normed2 = d_normed2 + matmul(pick, db_back)
        ffn_mix_grad.append(jnp.sum(pick.astype(FULL) * mix_grad_back, axis=1, keepdims=True))
    ffn_mix_grad = jnp.concatenate(ffn_mix_grad, axis=1)
    ffn_d_logits = logits_back(ffn_mix, ffn_mix_grad, ffn_probs, ffn_onehot, share_grad[1])
    d_normed2 = d_normed2 + through_router(ffn_d_logits, router2_half.astype(FULL))
    weighted2 = d_normed2 * gain2_half
    inner2 = tp_sum(jnp.sum(weighted2 * attended, axis=1, keepdims=True)) / features
    d_attended = grad_half + scale_two * weighted2 - attended * scale_two**3 * inner2
    gain2_part = jnp.sum(d_normed2 * attended * scale_two, axis=0)
    ffn_router_part = precise_tn(b_half.astype(FULL), ffn_d_logits)

    dy_slots = jnp.zeros((slots, half_width), FULL)
    for k in range(picks_each):
        dy_slots = dy_slots + matmul_tn(attn_picks[k], (attn_mix[:, k : k + 1] * d_attended).astype(LOW))
    dy_rows = send_out(dy_slots.astype(LOW), 4)
    d_heads = matmul_nt(dy_rows, out_full).astype(LOW)
    dq_low, dk_low, dv_low = attend_back(
        q_low, k_low, v_low, d_heads, log_sum, query_table, key_table, groups
    )
    dkv_low = after(jnp.concatenate([dk_low, dv_low], axis=1), back_two)
    da_rows = matmul_nt(dq_low, query_full).astype(LOW).reshape(groups, capacity, features)
    da_seq = jnp.einsum("bsr,bsd->brd", expert_onehot, da_rows, preferred_element_type=FULL)
    da_seq = da_seq.reshape(groups * rows_here, features) + matmul_nt(dkv_low, kv_full)
    out_sent, out_finish = scatter_start(
        lambda low, high: matmul_tn(heads_low, dy_rows[:, low:high]), features, 1
    )
    kv_sent, kv_finish = scatter_start(
        lambda low, high: matmul_tn(a_seq[:, low:high], dkv_low), features, 0
    )
    result = attended
    for k in range(picks_each):
        result = result + ffn_mix[:, k : k + 1] * matmul(ffn_picks[k], ffn_back)
    result_low = result.astype(LOW)
    da_half, kv_back, out_back, result_other = send_home(
        da_seq.astype(LOW),
        5,
        cargo=((kv_sent, "fsdp"), (out_sent, "fsdp"), (result_low, "tp")),
        add_up=True,
    )
    output = from_spread(join_halves(result_low, result_other), 1)
    kv_part = kv_finish(kv_back)
    query_sent, query_finish = scatter_start(
        lambda low, high: matmul_tn(rows_in[:, low:high], after(dq_low, kv_part)), features, 0
    )
    query_back = last_step(query_sent)
    kv_grad = block_for(kv_part, 0)
    kv_part_low = kv_part.astype(LOW)
    for distance in far_first(groups):
        if distance:
            kv_arrived = swap(block_for(kv_part_low, distance), "ctx", distance)
            kv_grad = kv_grad + kv_arrived.astype(FULL)
    query_grad = query_finish(query_back)
    out_grad = out_finish(out_back)
    back_one, back_two = lax.optimization_barrier((back_one, back_two, query_sent))[:2]
    gate_grad, up_grad, down_grad = finish_experts(parts_one + [back_one], parts_two + [back_two])
    key_width = key_proj.shape[1]

    attn_mix_grad = tp_sum(
        jnp.concatenate(
            [jnp.sum(d_attended * picked, axis=1, keepdims=True) for picked in attn_picked], axis=1
        )
    )
    attn_d_logits = logits_back(attn_mix, attn_mix_grad, attn_probs, attn_onehot, share_grad[0])
    a_half = my_half(a_mine)
    attn_router_part = precise_tn(a_half.astype(FULL), attn_d_logits)

    d_normed1 = da_half + through_router(attn_d_logits, router1_half)
    gain1_half = my_half(gain1)
    weighted1 = d_normed1 * gain1_half
    inner1 = tp_sum(jnp.sum(weighted1 * input_half, axis=1, keepdims=True)) / features
    input_grad = d_attended + scale_one * weighted1 - input_half * scale_one**3 * inner1
    input_grad_low = input_grad.astype(LOW)
    input_grad = from_spread(join_halves(input_grad_low, swap(input_grad_low, "tp", 1)), 1).astype(FULL)
    gain1_part = jnp.sum(d_normed1 * input_half * scale_one, axis=0)

    small = jnp.concatenate(
        [gain1_part[None], gain2_part[None], attn_router_part.T, ffn_router_part.T], axis=0
    )
    small = from_spread(join_halves(small, swap(small, "tp", 1)), 1)
    prob_sums = jnp.concatenate([jnp.sum(attn_probs, axis=0), jnp.sum(ffn_probs, axis=0)])
    small = jnp.concatenate([small, jnp.pad(prob_sums, (0, features - prob_sums.shape[0]))[None]], axis=0)
    small = after(all_sum(small, ("fsdp",)), query_back)
    for bit in bits_down(groups):
        small = small + swap(small, "ctx", bit)
        if bit > 1:
            small = after(small, gate_grad)
    prob_sums = small[-1, : 2 * expert_count].reshape(2, expert_count)
    losses = expert_count * jnp.sum(share * prob_sums / all_tokens, axis=1)
    return (
        output,
        input_grad,
        losses[0],
        losses[1],
        small[0],
        small[1],
        small[2 : 2 + expert_count].T,
        small[2 + expert_count : 2 + 2 * expert_count].T,
        kv_grad[:, :key_width],
        kv_grad[:, key_width:],
        query_grad[None],
        out_grad[None],
        gate_grad[None],
        up_grad[None],
        down_grad[None],
    )


def solution(mesh):
    by_token = P(("fsdp", "ctx"), None)
    by_row = P(("fsdp", "ctx"), "tp")
    inward = P("ctx", "fsdp", "tp")
    outward = P("ctx", "tp", "fsdp")
    weights = (by_row, by_row, inward, outward, inward, inward, outward)
    return jax.shard_map(
        on_device,
        mesh=mesh,
        in_specs=(by_token,) * 4 + (P(),) * 4 + weights,
        out_specs=(by_token,) * 2 + (P(),) * 6 + weights,
        check_vma=False,
    )
```

```python
import functools
import math

import jax
import jax.numpy as jnp
import numpy as np
from jax import lax
from jax.experimental import pallas as pl
from jax.experimental.pallas import tpu as pltpu
from jax.sharding import PartitionSpec as P

HEAD = 128
EPSILON = 1e-06
ROPE_BASE = 10000.0
AUX_WEIGHT = 0.1
PRECISE = lax.Precision.HIGHEST
LOW = jnp.bfloat16
FULL = jnp.float32
VMEM_BYTES = 58 * 1024 * 1024
TILE = 256


def matmul(lhs, rhs):
    return jnp.dot(lhs, rhs, preferred_element_type=FULL)


def matmul_tn(lhs, rhs):
    return lax.dot_general(lhs, rhs, (((0,), (0,)), ((), ())), preferred_element_type=FULL)


def matmul_nt(lhs, rhs):
    return lax.dot_general(lhs, rhs, (((1,), (1,)), ((), ())), preferred_element_type=FULL)


def precise_tn(lhs, rhs):
    return lax.dot_general(lhs, rhs, (((0,), (0,)), ((), ())), precision=PRECISE)


def swap(value, axis, distance):
    size = lax.axis_size(axis)
    return lax.ppermute(value, axis, [(i, i ^ distance) for i in range(size)])


def after(value, *earlier):
    return lax.optimization_barrier((value,) + earlier)[0]


def bits_down(size):
    bit = size // 2
    while bit >= 1:
        yield bit
        bit //= 2


def spread_order(size):
    order = [0]
    for bit in bits_down(size):
        order = order + [place | bit for place in order]
    return order


def gather_pieces(piece):
    pieces = [piece]
    for bit in bits_down(lax.axis_size("fsdp")):
        if bit > 1:
            pieces = pieces + [swap(item, "fsdp", bit) for item in pieces]
    return pieces


def with_neighbours(pieces, known, *earlier):
    rest = [swap(after(item, *earlier), "fsdp", 1) for item in pieces[len(known) :]]
    return pieces + list(known) + rest


def flip_blocks(value, axis, index, count):
    parts = jnp.split(value, count, axis)
    for bit in bits_down(count):
        turned = (index // bit) % 2 == 1
        parts = [jnp.where(turned, parts[n ^ bit], parts[n]) for n in range(count)]
    return jnp.concatenate(parts, axis)


def to_spread(value, axis):
    size = lax.axis_size("fsdp")
    value = flip_blocks(value, axis, lax.axis_index("fsdp"), size)
    parts = jnp.split(value, size, axis)
    return jnp.concatenate([parts[place] for place in spread_order(size)], axis)


def from_spread(value, axis):
    size = lax.axis_size("fsdp")
    parts = jnp.split(value, size, axis)
    order = spread_order(size)
    value = jnp.concatenate([parts[order.index(place)] for place in range(size)], axis)
    return flip_blocks(value, axis, lax.axis_index("fsdp"), size)


def my_half(value):
    width = value.shape[-1] // 2
    return jnp.where(lax.axis_index("tp") == 0, value[..., :width], value[..., width:])


def other_half(value):
    width = value.shape[-1] // 2
    return jnp.where(lax.axis_index("tp") == 0, value[..., width:], value[..., :width])


def join_halves(mine, other):
    first = lax.axis_index("tp") == 0
    return jnp.concatenate([jnp.where(first, mine, other), jnp.where(first, other, mine)], -1)


def tp_sum(value):
    return value + swap(value, "tp", 1)


def all_sum(value, axes):
    for axis in axes:
        for bit in bits_down(lax.axis_size(axis)):
            value = value + swap(value, axis, bit)
    return value


def far_first(size):
    return list(range(size // 2, size)) + list(range(size // 2 - 1, -1, -1))


def place_blocks(blocks):
    index = lax.axis_index("ctx")
    rows = blocks[0].shape[0]
    total = jnp.zeros((rows * len(blocks),) + blocks[0].shape[1:], blocks[0].dtype)
    for distance, block in enumerate(blocks):
        total = lax.dynamic_update_slice_in_dim(total, block, (index ^ distance) * rows, 0)
    return total


def block_for(value, distance):
    size = lax.axis_size("ctx")
    rows = value.shape[0] // size
    return lax.dynamic_slice_in_dim(value, (lax.axis_index("ctx") ^ distance) * rows, rows, 0)


def xor_index(index, distance):
    result = index
    bit = 1
    while bit <= distance:
        if distance & bit:
            result = result + bit - 2 * bit * ((index // bit) % 2)
        bit *= 2
    return result


def span(start, size):
    return pl.ds(pl.multiple_of(start * size, 16), size)


def meet(peers):
    barrier = pltpu.get_barrier_semaphore()
    for device in peers:
        pl.semaphore_signal(barrier, inc=1, device_id=device, device_id_type=pl.DeviceIdType.MESH)
    pl.semaphore_wait(barrier, len(peers))


def remote(source, target, sems, index, device):
    return pltpu.make_async_remote_copy(
        src_ref=source,
        dst_ref=target,
        send_sem=sems[0].at[index],
        recv_sem=sems[1].at[index],
        device_id=device,
        device_id_type=pl.DeviceIdType.MESH,
    )


def near_first(size):
    return list(range(1, size))


def mixed_order(size):
    return [distance for distance in spread_order(size) if distance] + [0]


def cuts_of(rows):
    for count in (4, 2):
        if rows % (16 * count) == 0:
            return count
    return 1


def send_out_kernel(size, rows_ref, out_ref, z_land, y_land, z_send, z_recv, y_send, y_recv):
    mine, first = lax.axis_index("ctx"), lax.axis_index("tp") == 0
    other_tp = {"tp": 1 - lax.axis_index("tp")}
    rows, width = z_land.shape[1], z_land.shape[2]
    cuts = cuts_of(rows)
    part = rows // cuts
    at = [xor_index(mine, distance) for distance in range(size)]
    meet([{"ctx": at[distance]} for distance in range(1, size)] + [other_tp])
    order = [(distance, cut) for distance in near_first(size) for cut in range(cuts)]
    own = [(0, cut) for cut in range(cuts)]
    across, beside = {}, {}

    def source(distance, cut):
        start = pl.multiple_of(at[distance] * rows + cut * part, 16)
        return rows_ref.at[pl.ds(start, part)]

    def inside(distance, cut):
        return distance, pl.ds(cut * part, part)

    for distance, cut in order:
        across[distance, cut] = remote(
            source(distance, cut),
            z_land.at[inside(distance, cut)],
            (z_send, z_recv),
            distance * cuts + cut,
            {"ctx": at[distance]},
        )
        across[distance, cut].start()
    for distance, cut in own + order:
        if distance:
            across[distance, cut].wait_recv()
        beside[distance, cut] = remote(
            z_land.at[inside(distance, cut)] if distance else source(0, cut),
            y_land.at[inside(distance, cut)],
            (y_send, y_recv),
            distance * cuts + cut,
            other_tp,
        )
        beside[distance, cut].start()
    for distance, cut in own + order:
        beside[distance, cut].wait_recv()
        held = z_land[inside(distance, cut)] if distance else source(0, cut)[...]
        theirs = y_land[inside(distance, cut)]
        here = pl.ds(pl.multiple_of(at[distance] * rows + cut * part, 16), part)
        out_ref[here, :width] = jnp.where(first, held, theirs)
        out_ref[here, width:] = jnp.where(first, theirs, held)
    for item in order:
        across[item].wait_send()
    for item in own + order:
        beside[item].wait_send()


def send_out(half_rows, number):
    size = lax.axis_size("ctx")
    total, width = half_rows.shape
    land = pltpu.VMEM((size, total // size, width), half_rows.dtype)
    return pl.pallas_call(
        functools.partial(send_out_kernel, size),
        in_specs=[pl.BlockSpec(memory_space=pltpu.VMEM)],
        out_specs=pl.BlockSpec(memory_space=pltpu.VMEM),
        out_shape=jax.ShapeDtypeStruct((total, 2 * width), half_rows.dtype),
        scratch_shapes=[land, land] + [pltpu.SemaphoreType.DMA((size * cuts_of(total // size),))] * 4,
        compiler_params=pltpu.CompilerParams(
            collective_id=number, has_side_effects=True, vmem_limit_bytes=VMEM_BYTES
        ),
        cost_estimate=pl.CostEstimate(flops=0, bytes_accessed=12 * total * width, transcendentals=0),
    )(half_rows)


def send_home_kernel(size, adds, has_extra, cargo_axes, *refs):
    cargoes = len(cargo_axes)
    streams = len(adds)
    parts, refs = refs[:streams], refs[streams:]
    extra_ref, refs = (refs[0], refs[1:]) if has_extra else (None, refs)
    cargo_in, refs = refs[:cargoes], refs[cargoes:]
    outs, refs = refs[:streams], refs[streams:]
    extra_out, refs = (refs[0], refs[1:]) if has_extra else (None, refs)
    cargo_out, refs = refs[:cargoes], refs[cargoes:]
    lands, refs = [refs[7 * n : 7 * n + 7] for n in range(streams)], refs[7 * streams :]
    mine, first = lax.axis_index("ctx"), lax.axis_index("tp") == 0
    place = lax.axis_index("tp")
    other_tp = {"tp": 1 - place}
    at = [xor_index(mine, distance) for distance in range(size)]
    world = lax.axis_size("fsdp")
    spot = lax.axis_index("fsdp")
    along = {"tp": other_tp, "fsdp": {"fsdp": xor_index(spot, world // 2)}, "core": {"fsdp": xor_index(spot, 1)}}
    extra_peers = [along[axis] for axis in ("fsdp", "core") if axis in cargo_axes]
    meet([{"ctx": at[distance]} for distance in range(1, size)] + [other_tp] + extra_peers)
    order = mixed_order(size)
    beside, across, extras = {}, {}, {}
    cargo = [
        remote(cargo_in[n], cargo_out[n], refs[-2:], n, along[axis])
        for n, axis in enumerate(cargo_axes)
    ]
    for copy, axis in zip(cargo, cargo_axes):
        if axis != "tp":
            copy.start()
    if has_extra:
        ey_land, e_ready, ez_land, ey_send, ey_recv, ez_send, ez_recv = refs[:7]
        extra_beside = remote(extra_ref, ey_land, (ey_send, ey_recv), 0, other_tp)
        extra_beside.start()
    turns = []
    for n in range(streams):
        y_land, _, z_land, y_send, y_recv, _, _ = lands[n]
        rows, width = z_land.shape[1], z_land.shape[2]
        cuts = cuts_of(rows)
        part = rows // cuts
        columns = pl.ds(pl.multiple_of((1 - place) * width, 128), width)
        for distance in order:
            for cut in range(cuts):
                inside = distance, pl.ds(cut * part, part)
                here = pl.ds(pl.multiple_of(at[distance] * rows + cut * part, 16), part)
                number = distance * cuts + cut
                beside[n, number] = remote(
                    parts[n].at[here, columns], y_land.at[inside], (y_send, y_recv), number, other_tp
                )
                beside[n, number].start()
                turns.append((n, distance, cut, number, part, width, inside, here))
    for copy, axis in zip(cargo, cargo_axes):
        if axis == "tp":
            copy.start()
    if has_extra:
        extra_beside.wait_recv()
        e_ready[...] = extra_ref[...] + ey_land[...]
        for distance in order:
            if distance:
                extras[distance] = remote(
                    e_ready.at[at[distance]],
                    ez_land.at[distance],
                    (ez_send, ez_recv),
                    distance,
                    {"ctx": at[distance]},
                )
                extras[distance].start()
    for n, distance, cut, number, part, width, inside, here in turns:
        y_land, ready, z_land, _, _, z_send, z_recv = lands[n]
        beside[n, number].wait_recv()
        whole = parts[n][here, :]
        own = jnp.where(first, whole[:, :width], whole[:, width:])
        total = (own.astype(FULL) + y_land[inside].astype(FULL)).astype(LOW)
        if distance:
            ready[inside] = total
            across[n, number] = remote(
                ready.at[inside], z_land.at[inside], (z_send, z_recv), number, {"ctx": at[distance]}
            )
            across[n, number].start()
        elif adds[n]:
            outs[n][inside[1], :] = total.astype(FULL)
        else:
            outs[n][here, :] = total
    for n, distance, cut, number, part, width, inside, here in turns:
        if distance:
            across[n, number].wait_recv()
            if adds[n]:
                outs[n][inside[1], :] += lands[n][2][inside].astype(FULL)
            else:
                outs[n][here, :] = lands[n][2][inside]
    if has_extra:
        extra_out[mine] = e_ready[mine]
        for distance in order:
            if distance:
                extras[distance].wait_recv()
                extra_out[at[distance]] = ez_land[distance]
                extras[distance].wait_send()
        extra_beside.wait_send()
    for copy in list(beside.values()) + list(across.values()):
        copy.wait_send()
    for copy in cargo:
        copy.wait()


def send_home(partial_rows, number, extra=None, cargo=(), add_up=False, more=None):
    size = lax.axis_size("ctx")
    operands = [partial_rows] if more is None else [partial_rows, more]
    adds = (add_up, False)[: len(operands)]
    sems = [pltpu.SemaphoreType.DMA((size,))] * 4
    shapes, scratch, moved = [], [], 0
    for item, added in zip(operands, adds):
        total, width = item.shape[0], item.shape[1] // 2
        rows = total // size
        moved += 12 * total * width
        shapes.append(
            jax.ShapeDtypeStruct((rows, width), FULL) if added else jax.ShapeDtypeStruct((total, width), LOW)
        )
        scratch += [pltpu.VMEM((size, rows, width), LOW)] * 3
        scratch += [pltpu.SemaphoreType.DMA((size * cuts_of(rows),))] * 4
    if extra is not None:
        operands.append(extra)
        shapes.append(jax.ShapeDtypeStruct(extra.shape, FULL))
        scratch += [pltpu.VMEM(extra.shape, FULL)] * 3 + sems
    in_specs = [pl.BlockSpec(memory_space=pltpu.VMEM)] * len(operands)
    out_specs = [pl.BlockSpec(memory_space=pltpu.VMEM)] * len(shapes)
    for item, _ in cargo:
        operands.append(item)
        shapes.append(jax.ShapeDtypeStruct(item.shape, item.dtype))
        in_specs.append(pl.BlockSpec(memory_space=pl.ANY))
        out_specs.append(pl.BlockSpec(memory_space=pl.ANY))
    if cargo:
        scratch += [pltpu.SemaphoreType.DMA((len(cargo),))] * 2
    results = pl.pallas_call(
        functools.partial(send_home_kernel, size, adds, extra is not None, tuple(axis for _, axis in cargo)),
        in_specs=in_specs,
        out_specs=out_specs,
        out_shape=shapes,
        scratch_shapes=scratch,
        compiler_params=pltpu.CompilerParams(
            collective_id=number, has_side_effects=True, vmem_limit_bytes=VMEM_BYTES
        ),
        cost_estimate=pl.CostEstimate(flops=0, bytes_accessed=moved, transcendentals=0),
    )(*operands)
    return results if len(shapes) > 1 else results[0]


def prologue_kernel(sizes, *refs):
    groups, world = sizes
    half_in, own_in, routes_in, kv_in, query_in, out_in, cot_in = refs[:7]
    seq_ref, routes_ref, kv_ref, query_ref, out_ref, cot_ref = refs[7:13]
    local_sem = refs[13]
    pairs = [(refs[14 + 2 * n], refs[15 + 2 * n]) for n in range(16)]
    token_line, route_line, kv_line, token_pass, kv_pass = (pairs[2 * n : 2 * n + 2] for n in range(5))
    kv_own, fr, fk, fq, fo, cot_beside = pairs[10:]
    mine, place, spot = lax.axis_index("ctx"), lax.axis_index("tp"), lax.axis_index("fsdp")
    other_tp = {"tp": 1 - place}
    rows, width = half_in.shape
    sub = kv_in.shape[0]
    piece = sub * groups
    q_rows = query_in.shape[0]
    steps = list(bits_down(world))
    beside = {bit: {"fsdp": xor_index(spot, bit)} for bit in steps}
    first = steps[0]
    meet(
        [{"ctx": xor_index(mine, distance)} for distance in range(1, groups)]
        + [other_tp]
        + [beside[bit] for bit in steps]
    )
    locals_ = [
        pltpu.make_async_copy(
            own_in.at[:, pl.ds(n * width, width)], seq_ref.at[n, span(mine, rows)], local_sem.at[n]
        )
        for n in range(2)
    ] + [
        pltpu.make_async_copy(routes_in, routes_ref.at[0, mine], local_sem.at[2]),
        pltpu.make_async_copy(kv_in, kv_ref.at[span(mine, sub)], local_sem.at[3]),
        pltpu.make_async_copy(query_in, query_ref.at[pl.ds(0, q_rows)], local_sem.at[4]),
        pltpu.make_async_copy(out_in, out_ref.at[0], local_sem.at[5]),
    ]
    started, landed = [], set()

    def go(copy):
        copy.start()
        started.append(copy)
        return copy

    def arrived(copy):
        if id(copy) not in landed:
            copy.wait_recv()
            landed.add(id(copy))

    def wrap(index):
        return lax.rem(index + groups, groups)

    def outgoing(step):
        yield 0, jnp.logical_and(mine < groups - 1, mine >= step), wrap(mine - step), wrap(mine + 1)
        yield 1, jnp.logical_and(mine > 0, mine + step < groups), wrap(mine + step), wrap(mine - 1)

    def incoming(step):
        yield 0, mine >= step + 1, wrap(mine - 1 - step)
        yield 1, mine + step + 1 < groups, wrap(mine + 1 + step)

    def line_copy(own, place_of, sems, step, way, block, target):
        source = place_of(block) if step else own
        return remote(source, place_of(block), sems[way], step, {"ctx": target})

    def line_start(own, place_of, sems, step):
        for way, happens, block, target in outgoing(step):

            @pl.when(happens)
            def _():
                line_copy(own, place_of, sems, step, way, block, target).start()

    def line_wait(place_of, sems, step, passed):
        for way, happens, block in incoming(step):

            @pl.when(happens)
            def _():
                remote(place_of(block), place_of(block), sems[way], step, other_tp).wait_recv()
                if passed is not None:
                    passed(step, way, block).start()

    def line_end(own, place_of, sems, step, passed):
        for way, happens, block, target in outgoing(step):

            @pl.when(happens)
            def _():
                line_copy(own, place_of, sems, step, way, block, target).wait_send()

        if passed is None:
            return
        for way, happens, block in incoming(step):

            @pl.when(happens)
            def _():
                passed(step, way, block).wait_send()

    def passed_wait(step, passed):
        for way, happens, block in incoming(step):

            @pl.when(happens)
            def _():
                passed(step, way, block).wait_recv()

    route_place = lambda n: routes_ref.at[0, n]
    kv_place = lambda n: kv_ref.at[span(n, sub)]
    token_place = lambda n: seq_ref.at[place, span(n, rows)]

    def kv_along(step, way, block):
        target = kv_ref.at[pl.ds(pl.multiple_of(piece + block * sub, 16), sub)]
        return remote(kv_place(block), target, kv_pass[way], step, beside[first])

    def token_along(step, way, block):
        return remote(token_place(block), token_place(block), token_pass[way], step, other_tp)

    def token_landed(step, way, block):
        view = seq_ref.at[1 - place, span(block, rows)]
        return remote(view, view, token_pass[way], step, other_tp)

    kv_first = go(
        remote(
            kv_in,
            kv_ref.at[pl.ds(pl.multiple_of(piece + mine * sub, 16), sub)],
            kv_own,
            0,
            beside[first],
        )
    )
    query_view = lambda n: query_ref.at[pl.ds(n * q_rows, q_rows)]
    out_view = lambda n: out_ref.at[n]
    kv_view = lambda n: kv_ref.at[pl.ds(n * piece, piece)]
    query_copies = {1: go(remote(query_in, query_view(1), fq, 1, beside[first]))}
    out_copies = {}
    go(remote(cot_in, cot_ref, cot_beside, 0, other_tp))
    for copy in locals_:
        copy.start()
    for step in range(groups - 1):
        line_start(kv_in, kv_place, kv_line, step)
        line_start(routes_in, route_place, route_line, step)
        line_start(half_in, token_place, token_line, step)
        if step == 0:
            for copy in locals_:
                copy.wait()
            for bit in steps[1:]:
                n = world // (2 * bit)
                query_copies[n] = go(remote(query_in, query_view(n), fq, n, beside[bit]))
                out_copies[n] = go(remote(out_in, out_view(n), fo, n, beside[bit]))
        line_wait(kv_place, kv_line, step, kv_along)
        if step == groups - 2:
            out_copies[1] = go(remote(out_in, out_view(1), fo, 1, beside[first]))
        line_wait(route_place, route_line, step, None)
        line_wait(token_place, token_line, step, token_along)
    route_wait, kv_wait = {}, {}
    count = 1
    for bit in steps:
        for n in range(count):
            peer = beside[bit]
            if n in route_wait:
                arrived(route_wait[n])
            route_wait[count + n] = go(
                remote(routes_ref.at[n], routes_ref.at[count + n], fr, count + n, peer)
            )
            if bit == first:
                continue
            if n:
                arrived(query_copies[n])
                query_copies[count + n] = go(
                    remote(query_view(n), query_view(count + n), fq, count + n, peer)
                )
            if n == 1 and count == 2:
                arrived(kv_first)
                for step in range(groups - 1):
                    passed_wait(step, kv_along)
            if n > 1:
                arrived(kv_wait[n])
            kv_wait[count + n] = go(remote(kv_view(n), kv_view(count + n), fk, count + n, peer))
            if n:
                arrived(out_copies[n])
                out_copies[count + n] = go(remote(out_view(n), out_view(count + n), fo, count + n, peer))
        count *= 2
    if world == 2:
        arrived(kv_first)
        for step in range(groups - 1):
            passed_wait(step, kv_along)
    for copy in started:
        arrived(copy)
    for step in range(groups - 1):
        passed_wait(step, token_landed)
        line_end(kv_in, kv_place, kv_line, step, kv_along)
        line_end(routes_in, route_place, route_line, step, None)
        line_end(half_in, token_place, token_line, step, token_along)
    for copy in started:
        copy.wait_send()


def prologue(token_half, token_rows, routes, kv_rows, query_piece, out_piece, cot_block, number):
    groups, world = lax.axis_size("ctx"), lax.axis_size("fsdp")
    any_space = pl.BlockSpec(memory_space=pl.ANY)
    rows, features = token_rows.shape
    pair = lambda count: [pltpu.SemaphoreType.DMA((count,))] * 2
    return pl.pallas_call(
        functools.partial(prologue_kernel, (groups, world)),
        in_specs=[pl.BlockSpec(memory_space=pltpu.VMEM)] * 7,
        out_specs=[any_space] * 6,
        out_shape=[
            jax.ShapeDtypeStruct((2, groups * rows, features // 2), LOW),
            jax.ShapeDtypeStruct((world, groups) + routes.shape, jnp.int32),
            jax.ShapeDtypeStruct((world * groups * kv_rows.shape[0], kv_rows.shape[1]), LOW),
            jax.ShapeDtypeStruct((world * query_piece.shape[0], query_piece.shape[1]), LOW),
            jax.ShapeDtypeStruct((world,) + out_piece.shape, LOW),
            jax.ShapeDtypeStruct(cot_block.shape, LOW),
        ],
        scratch_shapes=[pltpu.SemaphoreType.DMA((6,))]
        + pair(groups) * 10
        + pair(1)
        + pair(world) * 4
        + pair(1),
        compiler_params=pltpu.CompilerParams(
            collective_id=number, has_side_effects=True, vmem_limit_bytes=VMEM_BYTES
        ),
        cost_estimate=pl.CostEstimate(flops=0, bytes_accessed=100000000, transcendentals=0),
    )(token_half, token_rows, routes, kv_rows, query_piece, out_piece, cot_block)


def expert_forward_kernel(world, size, *refs):
    rows_ref = refs[0]
    gates, ups = refs[1 : 1 + world], refs[1 + world : 1 + 2 * world]
    refs = refs[1 + 2 * world :]
    blocks, beside_ref, refs = refs[:size], refs[size], refs[size + 1 :]
    hidden_ref, by_gate_ref, by_up_ref, cot_ref, y_land, y_send, y_recv = refs
    width = rows_ref.shape[1] // world
    mine, place = lax.axis_index("ctx"), lax.axis_index("tp")
    other_tp = {"tp": 1 - place}
    beside = [
        remote(blocks[distance], y_land.at[distance], (y_send, y_recv), distance, other_tp)
        for distance in range(1, size)
    ]

    @pl.when(pl.program_id(0) == 0)
    def _():
        meet([other_tp])
        for copy in beside:
            copy.start()

    gate_lin, up_lin = None, None
    for n in range(world):
        columns = slice(n * width, (n + 1) * width)
        gate_term = matmul(rows_ref[:, columns], gates[n][...])
        up_term = matmul(rows_ref[:, columns], ups[n][...])
        gate_lin = gate_lin + gate_term if n else gate_term
        up_lin = up_lin + up_term if n else up_term
    sigmoid_gate = 1.0 / (1.0 + jnp.exp(-gate_lin))
    swish = gate_lin * sigmoid_gate
    hidden_ref[...] = (swish * up_lin).astype(LOW)
    by_gate_ref[...] = (up_lin * sigmoid_gate * (1.0 + gate_lin * (1.0 - sigmoid_gate))).astype(LOW)
    by_up_ref[...] = swish.astype(LOW)

    @pl.when(pl.program_id(0) == pl.num_programs(0) - 1)
    def _():
        rows, half = y_land.shape[1], y_land.shape[2]
        for distance in range(size):
            if distance:
                beside[distance - 1].wait_recv()
            own = blocks[distance][...]
            theirs = y_land[distance] if distance else beside_ref[...]
            here = span(xor_index(mine, distance), rows)
            cot_ref[here, :half] = jnp.where(place == 0, own, theirs)
            cot_ref[here, half:] = jnp.where(place == 0, theirs, own)
        for copy in beside:
            copy.wait_send()


def expert_forward(rows, gate_pieces, up_pieces, cot_blocks, cot_beside, number):
    world, size = len(gate_pieces), len(cot_blocks)
    slots, features = rows.shape
    depth, hidden_width = gate_pieces[0].shape
    tall = pl.BlockSpec((depth, TILE), lambda i: (0, i))
    strip = pl.BlockSpec((slots, TILE), lambda i: (0, i))
    whole = lambda value: pl.BlockSpec(value.shape, lambda i: (0, 0), pipeline_mode=pl.Buffered(1))
    return pl.pallas_call(
        functools.partial(expert_forward_kernel, world, size),
        grid=(hidden_width // TILE,),
        in_specs=[whole(rows)] + [tall] * (2 * world) + [whole(block) for block in cot_blocks] + [whole(cot_beside)],
        out_specs=[strip] * 3 + [pl.BlockSpec((slots, features), lambda i: (0, 0))],
        out_shape=[jax.ShapeDtypeStruct((slots, hidden_width), LOW)] * 3
        + [jax.ShapeDtypeStruct((slots, features), LOW)],
        scratch_shapes=[pltpu.VMEM((size,) + cot_blocks[0].shape, LOW)]
        + [pltpu.SemaphoreType.DMA((size,))] * 2,
        compiler_params=pltpu.CompilerParams(
            collective_id=number, has_side_effects=True, vmem_limit_bytes=VMEM_BYTES
        ),
        cost_estimate=pl.CostEstimate(flops=0, bytes_accessed=2 * slots * features, transcendentals=0),
    )(rows, *gate_pieces, *up_pieces, *cot_blocks, cot_beside)


def product_kernel(world, tiles, hidden_ref, *refs):
    downs, out_ref = refs[:world], refs[world]
    for n in range(world):

        @pl.when(pl.program_id(0) // tiles == n)
        def _():
            out_ref[...] = matmul(hidden_ref[...], downs[n][...]).astype(LOW)


def expert_product(hidden, down_pieces):
    world = len(down_pieces)
    depth, width = down_pieces[0].shape
    tiles = max(width // TILE, 1)
    tile = width // tiles

    def piece_spec(n):
        return pl.BlockSpec((depth, tile), lambda i: (0, jnp.clip(i - n * tiles, 0, tiles - 1)))

    return pl.pallas_call(
        functools.partial(product_kernel, world, tiles),
        grid=(world * tiles,),
        in_specs=[pl.BlockSpec(hidden.shape, lambda i: (0, 0), pipeline_mode=pl.Buffered(1))]
        + [piece_spec(n) for n in range(world)],
        out_specs=pl.BlockSpec((hidden.shape[0], tile), lambda i: (0, i)),
        out_shape=jax.ShapeDtypeStruct((hidden.shape[0], world * width), LOW),
        compiler_params=pltpu.CompilerParams(vmem_limit_bytes=VMEM_BYTES),
        cost_estimate=pl.CostEstimate(
            flops=2 * hidden.shape[0] * depth * world * width,
            bytes_accessed=2 * depth * world * width,
            transcendentals=0,
        ),
    )(hidden, *down_pieces)


def expert_back_kernel(world, steps, size, *refs):
    rows_ref, cot_ref, mix_ref, hidden_ref, by_gate_ref, by_up_ref = refs[:6]
    gates, ups, downs = (refs[6 + n * world : 6 + (n + 1) * world] for n in range(3))
    refs = refs[6 + 3 * world :]
    part_ref, refs = (refs[0], refs[1:]) if size else (None, refs)
    near_ref, landed_ref, db_ref, mix_grad_ref = refs[:4]
    home_ref, refs = (refs[4], refs[5:]) if size else (None, refs[4:])
    db_sum, rows_t_ref, cot_t_ref, far, send_sem, recv_sem = refs[:6]
    step = pl.program_id(0)
    slot = lax.rem(step, 2)
    features = rows_ref.shape[1]
    width = features // world
    half = features // 2
    tile = near_ref.shape[3]
    other_core = {"fsdp": xor_index(lax.axis_index("fsdp"), 1)}
    peers = [other_core]
    if size:
        y_land, ready, z_land, y_send, y_recv, z_send, z_recv = refs[6:]
        mine, place = lax.axis_index("ctx"), lax.axis_index("tp")
        other_tp = {"tp": 1 - place}
        at = [xor_index(mine, distance) for distance in range(size)]
        peers = peers + [other_tp] + [{"ctx": at[distance]} for distance in range(1, size)]
        home_rows, home_width = z_land.shape[1], z_land.shape[2]
        away = pl.ds(pl.multiple_of((1 - place) * home_width, 128), home_width)
        order = mixed_order(size)

        def beside(distance):
            return remote(
                part_ref.at[span(at[distance], home_rows), away],
                y_land.at[distance],
                (y_send, y_recv),
                distance,
                other_tp,
            )

        def across(distance):
            return remote(
                ready.at[distance],
                z_land.at[distance],
                (z_send, z_recv),
                distance,
                {"ctx": at[distance]},
            )

    def far_copy(at_step, at_slot):
        return pltpu.make_async_remote_copy(
            src_ref=far.at[at_slot],
            dst_ref=landed_ref.at[at_step],
            send_sem=send_sem.at[at_slot],
            recv_sem=recv_sem.at[at_step],
            device_id=other_core,
            device_id_type=pl.DeviceIdType.MESH,
        )

    @pl.when(step == 0)
    def _():
        meet(peers)
        if size:
            for distance in order:
                beside(distance).start()
        db_sum[...] = jnp.zeros_like(db_sum)
        mix_grad_ref[...] = jnp.zeros_like(mix_grad_ref)
        for place_at in range(0, features, tile):
            rows_t_ref[place_at : place_at + tile, :] = rows_ref[:, place_at : place_at + tile].T
            cot_t_ref[place_at : place_at + tile, :] = cot_ref[:, place_at : place_at + tile].T

    d_hidden = None
    for n in range(world):
        columns = slice(n * width, (n + 1) * width)
        term = matmul_nt(cot_ref[:, columns], downs[n][...])
        d_hidden = d_hidden + term if n else term
    hidden = hidden_ref[...].astype(FULL)
    mix_grad = hidden * d_hidden
    for place_at in range(0, tile, HEAD):
        mix_grad_ref[...] += mix_grad[:, place_at : place_at + HEAD]
    mix = jnp.concatenate([mix_ref[...]] * (tile // HEAD), axis=1)
    d_gated = d_hidden * mix
    mixed_low = (hidden * mix).astype(LOW)
    d_gate = (d_gated * by_gate_ref[...].astype(FULL)).astype(LOW)
    d_up = (d_gated * by_up_ref[...].astype(FULL)).astype(LOW)
    @pl.when(step >= 2)
    def _():
        far_copy(step - 2, slot).wait_send()

    pairs = ((rows_t_ref, d_gate), (rows_t_ref, d_up), (cot_t_ref, mixed_low))
    for n, (left, right) in enumerate(pairs):
        far[slot, n] = matmul(left[half:, :], right).astype(LOW)
    far_copy(step, slot).start()
    for n in range(world):
        columns = slice(n * width, (n + 1) * width)
        db_sum[:, columns] += matmul_nt(d_gate, gates[n][...]) + matmul_nt(d_up, ups[n][...])

    for n, (left, right) in enumerate(pairs):
        near_ref[0, n] = matmul(left[:half, :], right).astype(LOW)

    if size:
        for turn, distance in enumerate(order):

            @pl.when(step == min(turn + 1, steps - 1))
            def _():
                beside(distance).wait_recv()
                whole = part_ref[span(at[distance], home_rows), :]
                own = jnp.where(place == 0, whole[:, :home_width], whole[:, home_width:])
                total = (own.astype(FULL) + y_land[distance].astype(FULL)).astype(LOW)
                if distance:
                    ready[distance] = total
                    across(distance).start()
                else:
                    home_ref[span(mine, home_rows), :] = total

    @pl.when(step == steps - 1)
    def _():
        db_ref[...] = db_sum[...].astype(LOW)
        for last in range(max(steps - 2, 0), steps):
            far_copy(last, last % 2).wait_send()
        for last in range(steps):
            far_copy(last, last % 2).wait_recv()
        if size:
            for distance in order:
                beside(distance).wait_send()
                if distance:
                    across(distance).wait_recv()
                    home_ref[span(at[distance], home_rows), :] = z_land[distance]
                    across(distance).wait_send()


def expert_back(rows, cot_rows, mix_rows, forward, pieces, first, steps, number, going_home=None):
    gate_pieces, up_pieces, down_pieces = pieces
    world = len(gate_pieces)
    slots, features = rows.shape
    depth = gate_pieces[0].shape[0]
    tile = TILE
    once = pl.Buffered(1)
    whole = lambda value: pl.BlockSpec(value.shape, lambda i: (0, 0), pipeline_mode=once)
    kept = lambda width: pl.BlockSpec((slots, width), lambda i: (0, 0))
    tall = pl.BlockSpec((depth, tile), lambda i: (0, i + first))
    flat = pl.BlockSpec((tile, depth), lambda i: (i + first, 0))
    strip = pl.BlockSpec((slots, tile), lambda i: (0, i + first))
    low = lambda *shape: jax.ShapeDtypeStruct(shape, LOW)
    grads = low(steps, 3, features // 2, tile)
    operands = [rows, cot_rows, mix_rows, *forward, *gate_pieces, *up_pieces, *down_pieces]
    in_specs = [whole(rows), whole(cot_rows), whole(mix_rows)] + [strip] * 3
    in_specs += [tall] * (2 * world) + [flat] * world
    out_specs = [
        pl.BlockSpec((1, 3, features // 2, tile), lambda i: (i, 0, 0, 0)),
        pl.BlockSpec(memory_space=pl.ANY),
        kept(features),
        kept(HEAD),
    ]
    out_shape = [grads, grads, low(slots, features), jax.ShapeDtypeStruct((slots, HEAD), FULL)]
    scratch = [
        pltpu.VMEM((slots, features), FULL),
        pltpu.VMEM((features, slots), LOW),
        pltpu.VMEM((features, slots), LOW),
        pltpu.VMEM((2, 3, features // 2, tile), LOW),
        pltpu.SemaphoreType.DMA((2,)),
        pltpu.SemaphoreType.DMA((steps,)),
    ]
    size = 0
    if going_home is not None:
        size = lax.axis_size("ctx")
        operands.append(going_home)
        in_specs.append(whole(going_home))
        out_specs.append(kept(features // 2))
        out_shape.append(low(slots, features // 2))
        scratch += [pltpu.VMEM((size, slots // size, features // 2), LOW)] * 3
        scratch += [pltpu.SemaphoreType.DMA((size,))] * 4
    return pl.pallas_call(
        functools.partial(expert_back_kernel, world, steps, size),
        grid=(steps,),
        in_specs=in_specs,
        out_specs=out_specs,
        out_shape=out_shape,
        scratch_shapes=scratch,
        compiler_params=pltpu.CompilerParams(
            collective_id=number, has_side_effects=True, vmem_limit_bytes=VMEM_BYTES
        ),
        cost_estimate=pl.CostEstimate(
            flops=0, bytes_accessed=2 * slots * features, transcendentals=0
        ),
    )(*operands)


def scatter_rest(near, landed):
    pieces = lax.axis_size("fsdp")
    arrived, high, bit = [near, landed], near.shape[2], 2
    while True:
        total = arrived[0][:, :, high // 2 : high].astype(FULL)
        for block in arrived[1:]:
            total = total + block[:, :, high // 2 : high].astype(FULL)
        sent = total.astype(LOW)
        high //= 2
        if 2 * bit >= pieces:
            return sent, arrived
        arrived.append(swap(sent, "fsdp", bit))
        bit *= 2


def finish_kernel(count, steps_one, *refs):
    ones, twos = refs[:count], refs[count : 2 * count]
    outs = refs[2 * count :]

    def add_up(parts):
        for n, out in enumerate(outs):
            total = parts[0][0, n].astype(FULL)
            for part in parts[1:]:
                total = total + part[0, n].astype(FULL)
            out[...] = total.T if n == 2 else total

    @pl.when(pl.program_id(0) < steps_one)
    def _():
        add_up(ones)

    @pl.when(pl.program_id(0) >= steps_one)
    def _():
        add_up(twos)


def finish_experts(ones, twos):
    steps_one, steps_two = ones[0].shape[0], twos[0].shape[0]
    depth, tile = ones[-1].shape[2:]
    width = (steps_one + steps_two) * tile
    block = (1, 3, depth, tile)
    first = pl.BlockSpec(block, lambda i: (jnp.minimum(i, steps_one - 1), 0, 0, 0))
    second = pl.BlockSpec(block, lambda i: (jnp.maximum(i - steps_one, 0), 0, 0, 0))
    tall = pl.BlockSpec((depth, tile), lambda i: (0, i))
    return pl.pallas_call(
        functools.partial(finish_kernel, len(ones), steps_one),
        grid=(steps_one + steps_two,),
        in_specs=[first] * len(ones) + [second] * len(twos),
        out_specs=[tall, tall, pl.BlockSpec((tile, depth), lambda i: (i, 0))],
        out_shape=[jax.ShapeDtypeStruct((depth, width), FULL)] * 2
        + [jax.ShapeDtypeStruct((width, depth), FULL)],
        compiler_params=pltpu.CompilerParams(vmem_limit_bytes=VMEM_BYTES),
        cost_estimate=pl.CostEstimate(
            flops=0, bytes_accessed=30 * width * depth, transcendentals=0
        ),
    )(*ones, *twos)


def scatter_start(product, features, first_dim):
    pieces = lax.axis_size("fsdp")
    high, bit, arrived = features, 1, []

    def part(low, high):
        total = product(low, high)
        for block in arrived:
            total = total + lax.slice_in_dim(block, low, high, axis=first_dim).astype(FULL)
        return total

    while True:
        sent = part(high // 2, high).astype(LOW)
        high //= 2
        if 2 * bit >= pieces:
            break
        arrived.append(swap(sent, "fsdp", bit))
        bit *= 2

    def finish(last):
        arrived.append(last)
        return part(0, high)

    return sent, finish


def last_step(sent):
    return swap(sent, "fsdp", lax.axis_size("fsdp") // 2)


def turn_tables(length):
    half_head = HEAD // 2
    steps = np.arange(half_head, dtype=np.float32) * np.float32(2.0 / HEAD)
    frequency = np.power(np.float32(ROPE_BASE), -steps).astype(np.float32)
    angles = np.arange(length, dtype=np.float32)[:, None] * frequency[None, :]
    cosine = np.cos(angles.astype(np.float64)).astype(np.float32)
    sine = np.sin(angles.astype(np.float64)).astype(np.float32)
    return np.concatenate([cosine, cosine, -sine, sine], axis=1)


def turn(value, table):
    return value * table[:, :HEAD] + pltpu.roll(value, HEAD // 2, 1) * table[:, HEAD:]


def turn_back(value, table):
    return value * table[:, :HEAD] - pltpu.roll(value, HEAD // 2, 1) * table[:, HEAD:]


def attend_kernel(
    groups, scale, q_lin, k_lin, v_lin, q_table, k_table, q_low, k_low, v_low, heads, log_sum
):
    q_low[...] = turn(q_lin[...], q_table[...]).astype(LOW)
    k_low[...] = turn(k_lin[...], k_table[...]).astype(LOW)
    v_low[...] = v_lin[...].astype(LOW)
    rows = q_low.shape[0] // groups
    block = k_low.shape[0] // groups
    for group in range(groups):
        span = slice(group * rows, (group + 1) * rows)
        seen = slice(0, (group + 1) * block)
        scores = matmul_nt(q_low[span, :], k_low[seen, :]) * scale
        top = jnp.max(scores, axis=1, keepdims=True)
        weights = jnp.exp(scores - top)
        total = jnp.sum(weights, axis=1, keepdims=True)
        weights = (weights * (1.0 / total)).astype(LOW)
        heads[span, :] = matmul(weights, v_low[seen, :]).astype(LOW)
        log_sum[span, :] = jnp.broadcast_to(top + jnp.log(total), (rows, HEAD))


def attend(query_lin, kv_lin, query_table, key_table, groups):
    slots, width = query_lin.shape
    length = kv_lin.shape[0]
    count = width // HEAD
    by_head = lambda rows: pl.BlockSpec((rows, HEAD), lambda h: (0, h))
    whole = lambda rows: pl.BlockSpec((rows, 2 * HEAD), lambda h: (0, 0))
    return pl.pallas_call(
        functools.partial(attend_kernel, groups, 1.0 / math.sqrt(HEAD)),
        grid=(count,),
        in_specs=[
            by_head(slots),
            by_head(length),
            pl.BlockSpec((length, HEAD), lambda h: (0, h + count)),
            whole(slots),
            whole(length),
        ],
        out_specs=[by_head(slots), by_head(length), by_head(length), by_head(slots), by_head(slots)],
        out_shape=[
            jax.ShapeDtypeStruct((slots, width), LOW),
            jax.ShapeDtypeStruct((length, width), LOW),
            jax.ShapeDtypeStruct((length, width), LOW),
            jax.ShapeDtypeStruct((slots, width), LOW),
            jax.ShapeDtypeStruct((slots, width), FULL),
        ],
        compiler_params=pltpu.CompilerParams(vmem_limit_bytes=VMEM_BYTES),
        cost_estimate=pl.CostEstimate(
            flops=0, bytes_accessed=20 * length * width, transcendentals=0
        ),
    )(query_lin, kv_lin, kv_lin, query_table, key_table)


def attend_back_kernel(
    groups, scale, q_low, k_low, v_low, d_heads, log_sum, q_table, k_table, dq, dk, dv, dk_sum, dv_sum
):
    dk_sum[...] = jnp.zeros_like(dk_sum)
    dv_sum[...] = jnp.zeros_like(dv_sum)
    rows = q_low.shape[0] // groups
    block = k_low.shape[0] // groups
    for group in range(groups):
        span = slice(group * rows, (group + 1) * rows)
        seen = slice(0, (group + 1) * block)
        query, keys = q_low[span, :], k_low[seen, :]
        grads = d_heads[span, :]
        scores = matmul_nt(query, keys) * scale
        weights = jnp.exp(scores - log_sum[span, :1])
        d_weights = matmul_nt(grads, v_low[seen, :])
        delta = jnp.sum(weights * d_weights, axis=1, keepdims=True)
        d_scores = (weights * (d_weights - delta)).astype(LOW)
        dq[span, :] = turn_back(matmul(d_scores, keys) * scale, q_table[span, :]).astype(LOW)
        dk_sum[seen, :] += matmul_tn(d_scores, query) * scale
        dv_sum[seen, :] += matmul_tn(weights.astype(LOW), grads)
    dk[...] = turn_back(dk_sum[...], k_table[...]).astype(LOW)
    dv[...] = dv_sum[...].astype(LOW)


def attend_back(q_low, k_low, v_low, d_heads, log_sum, query_table, key_table, groups):
    slots, width = q_low.shape
    length = k_low.shape[0]
    count = width // HEAD
    by_head = lambda rows: pl.BlockSpec((rows, HEAD), lambda h: (0, h))
    whole = lambda rows: pl.BlockSpec((rows, 2 * HEAD), lambda h: (0, 0))
    return pl.pallas_call(
        functools.partial(attend_back_kernel, groups, 1.0 / math.sqrt(HEAD)),
        grid=(count,),
        in_specs=[
            by_head(slots),
            by_head(length),
            by_head(length),
            by_head(slots),
            by_head(slots),
            whole(slots),
            whole(length),
        ],
        out_specs=[by_head(slots), by_head(length), by_head(length)],
        out_shape=[
            jax.ShapeDtypeStruct((slots, width), LOW),
            jax.ShapeDtypeStruct((length, width), LOW),
            jax.ShapeDtypeStruct((length, width), LOW),
        ],
        scratch_shapes=[pltpu.VMEM((length, HEAD), FULL), pltpu.VMEM((length, HEAD), FULL)],
        compiler_params=pltpu.CompilerParams(vmem_limit_bytes=VMEM_BYTES),
        cost_estimate=pl.CostEstimate(
            flops=0, bytes_accessed=14 * length * width, transcendentals=0
        ),
    )(q_low, k_low, v_low, d_heads, log_sum, query_table, key_table)


def chosen_picks(routes, expert_count, capacity):
    experts = jnp.arange(expert_count, dtype=jnp.int32)
    onehot = (routes[:, :, None] == experts[None, None, :]).astype(jnp.int32)
    rows = routes.shape[0]
    below = (jnp.arange(rows)[:, None] > jnp.arange(rows)[None, :]).astype(LOW)
    order = matmul(below, jnp.sum(onehot, axis=1).astype(LOW)).astype(jnp.int32)
    slot = routes * capacity + jnp.sum(onehot * order[:, None, :], axis=2)
    slots = jnp.arange(expert_count * capacity, dtype=jnp.int32)
    picks = [(slot[:, k : k + 1] == slots[None, :]).astype(LOW) for k in range(routes.shape[1])]
    return picks, onehot.astype(FULL)


def expert_picks(routes_seq, expert, capacity):
    named = jnp.any(routes_seq == expert, axis=1)
    rows = named.shape[1]
    above = (jnp.arange(rows)[:, None] < jnp.arange(rows)[None, :]).astype(LOW)
    order = matmul(named.astype(LOW), above).astype(jnp.int32)
    slot = jnp.where(named, order, -1)
    return (slot[:, None, :] == jnp.arange(capacity, dtype=jnp.int32)[None, :, None]).astype(LOW)


def mix_of(logits, onehot):
    chosen = jnp.sum(onehot * logits[:, None, :], axis=2)
    return jax.nn.softmax(chosen, axis=1)


def logits_back(mix, mix_grad, probs, onehot, share_grad):
    d_chosen = mix * (mix_grad - jnp.sum(mix * mix_grad, axis=1, keepdims=True))
    d_logits = jnp.sum(onehot * d_chosen[:, :, None], axis=1)
    inner = jnp.sum(probs * share_grad[None, :], axis=1, keepdims=True)
    return d_logits + probs * (share_grad[None, :] - inner)


def through_router(d_logits, router_half):
    total = d_logits[:, 0:1] * router_half[:, 0][None, :]
    for expert in range(1, d_logits.shape[1]):
        total = total + d_logits[:, expert : expert + 1] * router_half[:, expert][None, :]
    return total


def on_device(
    tokens,
    cotangent,
    attn_routes,
    ffn_routes,
    norm_gain1,
    norm_gain2,
    attn_router,
    ffn_router,
    key_proj,
    value_proj,
    query_proj,
    out_proj,
    gate_proj,
    up_proj,
    down_proj,
):
    rows_here, features = tokens.shape
    half_width = features // 2
    picks_each = attn_routes.shape[1]
    expert_count = attn_router.shape[1]
    groups = lax.axis_size("ctx")
    mine = lax.axis_index("ctx")
    capacity = rows_here * picks_each // expert_count * 5 // 4
    slots = groups * capacity
    all_tokens = rows_here * lax.axis_size("fsdp") * groups

    attn_picks, attn_onehot = chosen_picks(attn_routes, expert_count, capacity)
    ffn_picks, ffn_onehot = chosen_picks(ffn_routes, expert_count, capacity)
    ffn_pick = ffn_picks[0]
    for pick in ffn_picks[1:]:
        ffn_pick = ffn_pick + pick
    cot_half = my_half(to_spread(cotangent, 1))
    cot_slots = matmul_tn(ffn_pick, cot_half).astype(LOW)

    tokens_spread = to_spread(tokens, 1)
    token_half = my_half(tokens_spread)
    routes_mine = jnp.concatenate([attn_routes.T, ffn_routes.T], axis=0)
    routes_mine = jnp.concatenate([routes_mine, jnp.zeros_like(routes_mine)], axis=0)
    kv_mine = jnp.concatenate([key_proj, value_proj], axis=1)
    seq_low, all_routes, kv_full, query_full, out_pieces, cot_beside = prologue(
        token_half,
        tokens_spread,
        routes_mine,
        kv_mine,
        query_proj[0],
        out_proj[0],
        block_for(cot_slots, 0),
        0,
    )
    seq_routes = all_routes[0]
    seq_tokens = jnp.concatenate([seq_low[0], seq_low[1]], axis=1).astype(FULL)
    out_full = jnp.concatenate([out_pieces[n] for n in range(lax.axis_size("fsdp"))], axis=1)

    gate_pieces = gather_pieces(after(gate_proj[0], all_routes))
    up_pieces = gather_pieces(after(up_proj[0], all_routes))
    down_pieces = gather_pieces(after(down_proj[0], all_routes))

    gain1 = to_spread(norm_gain1, 0)
    gain2_half = my_half(to_spread(norm_gain2, 0))
    router1 = to_spread(attn_router, 0)
    router2 = to_spread(ffn_router, 0)
    router1_half = my_half(router1.T).T.astype(FULL)
    router2_half = my_half(router2.T).T

    scale_seq = lax.rsqrt(jnp.mean(seq_tokens * seq_tokens, axis=1, keepdims=True) + EPSILON)
    a_seq = (seq_tokens * scale_seq * gain1).astype(LOW)
    a_mine = lax.dynamic_slice_in_dim(a_seq, mine * rows_here, rows_here, 0)
    scale_one = lax.dynamic_slice_in_dim(scale_seq, mine * rows_here, rows_here, 0)
    attn_logits = matmul(a_mine, router1)
    attn_probs = jax.nn.softmax(attn_logits, axis=1)
    attn_mix = mix_of(attn_logits, attn_onehot)

    later = after(cot_slots, all_routes)
    cot_blocks = [block_for(later, distance) for distance in range(groups)]
    cot_blocks[1:] = [swap(cot_blocks[distance], "ctx", distance) for distance in range(1, groups)]

    expert_onehot = expert_picks(seq_routes[:, :picks_each], mine, capacity)
    key_table = jnp.asarray(turn_tables(groups * rows_here))
    query_table = jnp.einsum(
        "bsr,brh->bsh",
        expert_onehot.astype(FULL),
        key_table.reshape(groups, rows_here, -1),
        precision=PRECISE,
    ).reshape(slots, -1)
    rows_in = (
        jnp.einsum(
            "bsr,brd->bsd",
            expert_onehot,
            a_seq.reshape(groups, rows_here, features),
            preferred_element_type=FULL,
        )
        .astype(LOW)
        .reshape(slots, features)
    )
    query_lin = matmul(rows_in, query_full)
    kv_lin = matmul(a_seq, kv_full)
    q_low, k_low, v_low, heads_low, log_sum = attend(
        query_lin, kv_lin, query_table, key_table, groups
    )
    cargo = [(item, "core") for item in gate_pieces + [up_proj[0], down_proj[0]]]
    attn_back, *known = send_home(
        after(matmul(heads_low, out_full).astype(LOW), *cot_blocks[1:]), 1, cargo=cargo
    )
    gate_known, up_known, down_known = known[:-2], known[-2:-1], known[-1:]

    input_half = my_half(tokens_spread).astype(FULL)
    attn_picked = [matmul(pick, attn_back) for pick in attn_picks]
    attended = input_half
    for k in range(picks_each):
        attended = attended + attn_mix[:, k : k + 1] * attn_picked[k]
    square_sum = tp_sum(jnp.sum(attended * attended, axis=1, keepdims=True))
    scale_two = lax.rsqrt(square_sum / features + EPSILON)
    b_half = (attended * scale_two * gain2_half).astype(LOW)
    gate_all = with_neighbours(gate_pieces, gate_known)
    b_slots = matmul_tn(ffn_pick, b_half).astype(LOW)
    up_all = with_neighbours(up_pieces, up_known, b_slots)
    ffn_rows = send_out(after(b_slots, up_all[-1]), 2)
    ffn_logits = tp_sum(matmul(b_half, router2_half))
    ffn_probs = jax.nn.softmax(ffn_logits, axis=1)
    ffn_mix = mix_of(ffn_logits, ffn_onehot)

    ffn_seq_routes = seq_routes[:, picks_each : 2 * picks_each]
    ffn_expert_onehot = expert_picks(ffn_seq_routes, mine, capacity).astype(FULL)
    row_routes = jnp.einsum(
        "bsr,bkr->bsk", ffn_expert_onehot, ffn_seq_routes.astype(FULL), precision=PRECISE
    ).reshape(slots, picks_each)
    row_onehot = row_routes[:, :, None] == jnp.arange(expert_count, dtype=FULL)[None, None, :]
    row_mix = mix_of(matmul(ffn_rows, router2), row_onehot.astype(FULL))
    mine_too = (row_routes == mine.astype(FULL)).astype(FULL)
    mix_rows = jnp.broadcast_to(jnp.sum(row_mix * mine_too, axis=1, keepdims=True), (slots, HEAD))
    *forward, cot_rows = expert_forward(ffn_rows, gate_all, up_all, cot_blocks, cot_beside, 6)
    down_all = with_neighbours(down_pieces, down_known, forward[0])
    ffn_out = expert_product(forward[0], down_all)
    pieces = (gate_all, up_all, down_all)
    tiles = gate_proj.shape[2] // TILE
    count_one = (tiles + 1) // 2
    near_one, landed_one, db_one, mix_grad_one, ffn_back = expert_back(
        ffn_rows, cot_rows, mix_rows, forward, pieces, 0, count_one, 7, going_home=ffn_out
    )
    sent_one, parts_one = scatter_rest(near_one, landed_one)
    back_one = last_step(sent_one)
    near_two, landed_two, db_two, mix_grad_two = expert_back(
        after(ffn_rows, sent_one), cot_rows, mix_rows, forward, pieces, count_one, tiles - count_one, 8
    )
    sent_two, parts_two = scatter_rest(near_two, landed_two)
    back_two = last_step(sent_two)
    db_rows = (db_one.astype(FULL) + db_two.astype(FULL)).astype(LOW)
    mix_grad_rows = jnp.pad(
        jnp.sum(mix_grad_one + mix_grad_two, axis=1).reshape(groups, 1, capacity),
        ((0, 0), (0, 7), (0, 256 - capacity)),
    )
    db_back, mix_grad_back = send_home(after(db_rows, sent_two), 3, extra=mix_grad_rows)
    db_back = after(db_back, back_one)
    mix_grad_back = mix_grad_back[:, 0, :capacity].reshape(1, slots)

    experts = jnp.arange(expert_count, dtype=jnp.int32)
    named = (all_routes[..., None] == experts).astype(FULL)
    hits = jnp.stack(
        [
            jnp.sum(named[:, :, :picks_each], axis=(0, 1, 2, 3)),
            jnp.sum(named[:, :, picks_each : 2 * picks_each], axis=(0, 1, 2, 3)),
        ]
    )
    share = hits / (all_tokens * picks_each)
    share_grad = AUX_WEIGHT * expert_count / all_tokens * share
    grad_half = cot_half.astype(FULL)
    d_normed2 = jnp.zeros((rows_here, half_width), FULL)
    ffn_mix_grad = []
    for pick in ffn_picks:
        d_normed2 = d_normed2 + matmul(pick, db_back)
        ffn_mix_grad.append(jnp.sum(pick.astype(FULL) * mix_grad_back, axis=1, keepdims=True))
    ffn_mix_grad = jnp.concatenate(ffn_mix_grad, axis=1)
    ffn_d_logits = logits_back(ffn_mix, ffn_mix_grad, ffn_probs, ffn_onehot, share_grad[1])
    d_normed2 = d_normed2 + through_router(ffn_d_logits, router2_half.astype(FULL))
    weighted2 = d_normed2 * gain2_half
    inner2 = tp_sum(jnp.sum(weighted2 * attended, axis=1, keepdims=True)) / features
    d_attended = grad_half + scale_two * weighted2 - attended * scale_two**3 * inner2
    gain2_part = jnp.sum(d_normed2 * attended * scale_two, axis=0)
    ffn_router_part = precise_tn(b_half.astype(FULL), ffn_d_logits)

    dy_slots = jnp.zeros((slots, half_width), FULL)
    for k in range(picks_each):
        dy_slots = dy_slots + matmul_tn(attn_picks[k], (attn_mix[:, k : k + 1] * d_attended).astype(LOW))
    dy_rows = send_out(dy_slots.astype(LOW), 4)
    d_heads = matmul_nt(dy_rows, out_full).astype(LOW)
    dq_low, dk_low, dv_low = attend_back(
        q_low, k_low, v_low, d_heads, log_sum, query_table, key_table, groups
    )
    dkv_low = after(jnp.concatenate([dk_low, dv_low], axis=1), back_two)
    da_rows = matmul_nt(dq_low, query_full).astype(LOW).reshape(groups, capacity, features)
    da_seq = jnp.einsum("bsr,bsd->brd", expert_onehot, da_rows, preferred_element_type=FULL)
    da_seq = da_seq.reshape(groups * rows_here, features) + matmul_nt(dkv_low, kv_full)
    out_sent, out_finish = scatter_start(
        lambda low, high: matmul_tn(heads_low, dy_rows[:, low:high]), features, 1
    )
    kv_sent, kv_finish = scatter_start(
        lambda low, high: matmul_tn(a_seq[:, low:high], dkv_low), features, 0
    )
    result = attended
    for k in range(picks_each):
        result = result + ffn_mix[:, k : k + 1] * matmul(ffn_picks[k], ffn_back)
    result_low = result.astype(LOW)
    da_half, kv_back, out_back, result_other = send_home(
        da_seq.astype(LOW),
        5,
        cargo=((kv_sent, "fsdp"), (out_sent, "fsdp"), (result_low, "tp")),
        add_up=True,
    )
    output = from_spread(join_halves(result_low, result_other), 1)
    kv_part = kv_finish(kv_back)
    query_sent, query_finish = scatter_start(
        lambda low, high: matmul_tn(rows_in[:, low:high], after(dq_low, kv_part)), features, 0
    )
    query_back = last_step(query_sent)
    kv_part_low = kv_part.astype(LOW)
    kv_arrived = [
        swap(block_for(kv_part_low, distance), "ctx", distance)
        for distance in far_first(groups)
        if distance
    ]
    query_grad = query_finish(query_back)
    out_grad = out_finish(out_back)
    back_one, back_two = lax.optimization_barrier((back_one, back_two, query_sent))[:2]
    gate_grad, up_grad, down_grad = finish_experts(parts_one + [back_one], parts_two + [back_two])
    kv_grad = block_for(kv_part, 0)
    for block in lax.optimization_barrier((*kv_arrived, gate_grad))[:-1]:
        kv_grad = kv_grad + block.astype(FULL)
    key_width = key_proj.shape[1]

    attn_mix_grad = tp_sum(
        jnp.concatenate(
            [jnp.sum(d_attended * picked, axis=1, keepdims=True) for picked in attn_picked], axis=1
        )
    )
    attn_d_logits = logits_back(attn_mix, attn_mix_grad, attn_probs, attn_onehot, share_grad[0])
    a_half = my_half(a_mine)
    attn_router_part = precise_tn(a_half.astype(FULL), attn_d_logits)

    d_normed1 = da_half + through_router(attn_d_logits, router1_half)
    gain1_half = my_half(gain1)
    weighted1 = d_normed1 * gain1_half
    inner1 = tp_sum(jnp.sum(weighted1 * input_half, axis=1, keepdims=True)) / features
    input_grad = d_attended + scale_one * weighted1 - input_half * scale_one**3 * inner1
    input_grad_low = input_grad.astype(LOW)
    input_grad = from_spread(join_halves(input_grad_low, swap(input_grad_low, "tp", 1)), 1).astype(FULL)
    gain1_part = jnp.sum(d_normed1 * input_half * scale_one, axis=0)

    small = jnp.concatenate(
        [gain1_part[None], gain2_part[None], attn_router_part.T, ffn_router_part.T], axis=0
    )
    small = from_spread(join_halves(small, swap(small, "tp", 1)), 1)
    prob_sums = jnp.concatenate([jnp.sum(attn_probs, axis=0), jnp.sum(ffn_probs, axis=0)])
    small = jnp.concatenate([small, jnp.pad(prob_sums, (0, features - prob_sums.shape[0]))[None]], axis=0)
    small = after(all_sum(small, ("fsdp",)), query_back, gate_grad)
    small = all_sum(small, ("ctx",))
    prob_sums = small[-1, : 2 * expert_count].reshape(2, expert_count)
    losses = expert_count * jnp.sum(share * prob_sums / all_tokens, axis=1)
    return (
        output,
        input_grad,
        losses[0],
        losses[1],
        small[0],
        small[1],
        small[2 : 2 + expert_count].T,
        small[2 + expert_count : 2 + 2 * expert_count].T,
        kv_grad[:, :key_width],
        kv_grad[:, key_width:],
        query_grad[None],
        out_grad[None],
        gate_grad[None],
        up_grad[None],
        down_grad[None],
    )


def solution(mesh):
    by_token = P(("fsdp", "ctx"), None)
    by_row = P(("fsdp", "ctx"), "tp")
    inward = P("ctx", "fsdp", "tp")
    outward = P("ctx", "tp", "fsdp")
    weights = (by_row, by_row, inward, outward, inward, inward, outward)
    return jax.shard_map(
        on_device,
        mesh=mesh,
        in_specs=(by_token,) * 4 + (P(),) * 4 + weights,
        out_specs=(by_token,) * 2 + (P(),) * 6 + weights,
        check_vma=False,
    )
```

```python
import functools
import math

import jax
import jax.numpy as jnp
import numpy as np
from jax import lax
from jax.experimental import pallas as pl
from jax.experimental.pallas import tpu as pltpu
from jax.sharding import PartitionSpec as P

HEAD = 128
EPSILON = 1e-06
ROPE_BASE = 10000.0
AUX_WEIGHT = 0.1
PRECISE = lax.Precision.HIGHEST
LOW = jnp.bfloat16
FULL = jnp.float32
VMEM_BYTES = 58 * 1024 * 1024
TILE = 256


def matmul(lhs, rhs):
    return jnp.dot(lhs, rhs, preferred_element_type=FULL)


def matmul_tn(lhs, rhs):
    return lax.dot_general(lhs, rhs, (((0,), (0,)), ((), ())), preferred_element_type=FULL)


def matmul_nt(lhs, rhs):
    return lax.dot_general(lhs, rhs, (((1,), (1,)), ((), ())), preferred_element_type=FULL)


def precise_tn(lhs, rhs):
    return lax.dot_general(lhs, rhs, (((0,), (0,)), ((), ())), precision=PRECISE)


def swap(value, axis, distance):
    size = lax.axis_size(axis)
    return lax.ppermute(value, axis, [(i, i ^ distance) for i in range(size)])


def after(value, *earlier):
    return lax.optimization_barrier((value,) + earlier)[0]


def bits_down(size):
    bit = size // 2
    while bit >= 1:
        yield bit
        bit //= 2


def spread_order(size):
    order = [0]
    for bit in bits_down(size):
        order = order + [place | bit for place in order]
    return order


def gather_pieces(piece):
    pieces = [piece]
    for bit in bits_down(lax.axis_size("fsdp")):
        if bit > 1:
            pieces = pieces + [swap(item, "fsdp", bit) for item in pieces]
    return pieces


def with_neighbours(pieces, known, *earlier):
    rest = [swap(after(item, *earlier), "fsdp", 1) for item in pieces[len(known) :]]
    return pieces + list(known) + rest


def flip_blocks(value, axis, index, count):
    parts = jnp.split(value, count, axis)
    for bit in bits_down(count):
        turned = (index // bit) % 2 == 1
        parts = [jnp.where(turned, parts[n ^ bit], parts[n]) for n in range(count)]
    return jnp.concatenate(parts, axis)


def to_spread(value, axis):
    size = lax.axis_size("fsdp")
    value = flip_blocks(value, axis, lax.axis_index("fsdp"), size)
    parts = jnp.split(value, size, axis)
    return jnp.concatenate([parts[place] for place in spread_order(size)], axis)


def from_spread(value, axis):
    size = lax.axis_size("fsdp")
    parts = jnp.split(value, size, axis)
    order = spread_order(size)
    value = jnp.concatenate([parts[order.index(place)] for place in range(size)], axis)
    return flip_blocks(value, axis, lax.axis_index("fsdp"), size)


def my_half(value):
    width = value.shape[-1] // 2
    return jnp.where(lax.axis_index("tp") == 0, value[..., :width], value[..., width:])


def other_half(value):
    width = value.shape[-1] // 2
    return jnp.where(lax.axis_index("tp") == 0, value[..., width:], value[..., :width])


def join_halves(mine, other):
    first = lax.axis_index("tp") == 0
    return jnp.concatenate([jnp.where(first, mine, other), jnp.where(first, other, mine)], -1)


def tp_sum(value):
    return value + swap(value, "tp", 1)


def all_sum(value, axes):
    for axis in axes:
        for bit in bits_down(lax.axis_size(axis)):
            value = value + swap(value, axis, bit)
    return value


def far_first(size):
    return list(range(size // 2, size)) + list(range(size // 2 - 1, -1, -1))


def place_blocks(blocks):
    index = lax.axis_index("ctx")
    rows = blocks[0].shape[0]
    total = jnp.zeros((rows * len(blocks),) + blocks[0].shape[1:], blocks[0].dtype)
    for distance, block in enumerate(blocks):
        total = lax.dynamic_update_slice_in_dim(total, block, (index ^ distance) * rows, 0)
    return total


def block_for(value, distance):
    size = lax.axis_size("ctx")
    rows = value.shape[0] // size
    return lax.dynamic_slice_in_dim(value, (lax.axis_index("ctx") ^ distance) * rows, rows, 0)


def xor_index(index, distance):
    result = index
    bit = 1
    while bit <= distance:
        if distance & bit:
            result = result + bit - 2 * bit * ((index // bit) % 2)
        bit *= 2
    return result


def span(start, size):
    return pl.ds(pl.multiple_of(start * size, 16), size)


def meet(peers):
    barrier = pltpu.get_barrier_semaphore()
    for device in peers:
        pl.semaphore_signal(barrier, inc=1, device_id=device, device_id_type=pl.DeviceIdType.MESH)
    pl.semaphore_wait(barrier, len(peers))


def remote(source, target, sems, index, device):
    return pltpu.make_async_remote_copy(
        src_ref=source,
        dst_ref=target,
        send_sem=sems[0].at[index],
        recv_sem=sems[1].at[index],
        device_id=device,
        device_id_type=pl.DeviceIdType.MESH,
    )


def near_first(size):
    return list(range(1, size))


def mixed_order(size):
    return [distance for distance in spread_order(size) if distance] + [0]


def cuts_of(rows):
    for count in (4, 2):
        if rows % (16 * count) == 0:
            return count
    return 1


def send_out_kernel(size, rows_ref, out_ref, z_land, y_land, z_send, z_recv, y_send, y_recv):
    mine, first = lax.axis_index("ctx"), lax.axis_index("tp") == 0
    other_tp = {"tp": 1 - lax.axis_index("tp")}
    rows, width = z_land.shape[1], z_land.shape[2]
    cuts = cuts_of(rows)
    part = rows // cuts
    at = [xor_index(mine, distance) for distance in range(size)]
    meet([{"ctx": at[distance]} for distance in range(1, size)] + [other_tp])
    order = [(distance, cut) for distance in near_first(size) for cut in range(cuts)]
    own = [(0, cut) for cut in range(cuts)]
    across, beside = {}, {}

    def source(distance, cut):
        start = pl.multiple_of(at[distance] * rows + cut * part, 16)
        return rows_ref.at[pl.ds(start, part)]

    def inside(distance, cut):
        return distance, pl.ds(cut * part, part)

    for distance, cut in order:
        across[distance, cut] = remote(
            source(distance, cut),
            z_land.at[inside(distance, cut)],
            (z_send, z_recv),
            distance * cuts + cut,
            {"ctx": at[distance]},
        )
        across[distance, cut].start()
    for distance, cut in own + order:
        if distance:
            across[distance, cut].wait_recv()
        beside[distance, cut] = remote(
            z_land.at[inside(distance, cut)] if distance else source(0, cut),
            y_land.at[inside(distance, cut)],
            (y_send, y_recv),
            distance * cuts + cut,
            other_tp,
        )
        beside[distance, cut].start()
    for distance, cut in own + order:
        beside[distance, cut].wait_recv()
        held = z_land[inside(distance, cut)] if distance else source(0, cut)[...]
        theirs = y_land[inside(distance, cut)]
        here = pl.ds(pl.multiple_of(at[distance] * rows + cut * part, 16), part)
        out_ref[here, :width] = jnp.where(first, held, theirs)
        out_ref[here, width:] = jnp.where(first, theirs, held)
    for item in order:
        across[item].wait_send()
    for item in own + order:
        beside[item].wait_send()


def send_out(half_rows, number):
    size = lax.axis_size("ctx")
    total, width = half_rows.shape
    land = pltpu.VMEM((size, total // size, width), half_rows.dtype)
    return pl.pallas_call(
        functools.partial(send_out_kernel, size),
        in_specs=[pl.BlockSpec(memory_space=pltpu.VMEM)],
        out_specs=pl.BlockSpec(memory_space=pltpu.VMEM),
        out_shape=jax.ShapeDtypeStruct((total, 2 * width), half_rows.dtype),
        scratch_shapes=[land, land] + [pltpu.SemaphoreType.DMA((size * cuts_of(total // size),))] * 4,
        compiler_params=pltpu.CompilerParams(
            collective_id=number, has_side_effects=True, vmem_limit_bytes=VMEM_BYTES
        ),
        cost_estimate=pl.CostEstimate(flops=0, bytes_accessed=12 * total * width, transcendentals=0),
    )(half_rows)


def send_home_kernel(size, adds, has_extra, cargo_axes, *refs):
    cargoes = len(cargo_axes)
    streams = len(adds)
    parts, refs = refs[:streams], refs[streams:]
    extra_ref, refs = (refs[0], refs[1:]) if has_extra else (None, refs)
    cargo_in, refs = refs[:cargoes], refs[cargoes:]
    outs, refs = refs[:streams], refs[streams:]
    extra_out, refs = (refs[0], refs[1:]) if has_extra else (None, refs)
    cargo_out, refs = refs[:cargoes], refs[cargoes:]
    lands, refs = [refs[7 * n : 7 * n + 7] for n in range(streams)], refs[7 * streams :]
    mine, first = lax.axis_index("ctx"), lax.axis_index("tp") == 0
    place = lax.axis_index("tp")
    other_tp = {"tp": 1 - place}
    at = [xor_index(mine, distance) for distance in range(size)]
    world = lax.axis_size("fsdp")
    spot = lax.axis_index("fsdp")
    along = {"tp": other_tp, "fsdp": {"fsdp": xor_index(spot, world // 2)}, "core": {"fsdp": xor_index(spot, 1)}}
    extra_peers = [along[axis] for axis in ("fsdp", "core") if axis in cargo_axes]
    meet([{"ctx": at[distance]} for distance in range(1, size)] + [other_tp] + extra_peers)
    order = mixed_order(size)
    beside, across, extras = {}, {}, {}
    cargo = [
        remote(cargo_in[n], cargo_out[n], refs[-2:], n, along[axis])
        for n, axis in enumerate(cargo_axes)
    ]
    for copy, axis in zip(cargo, cargo_axes):
        if axis != "tp":
            copy.start()
    if has_extra:
        ey_land, e_ready, ez_land, ey_send, ey_recv, ez_send, ez_recv = refs[:7]
        extra_beside = remote(extra_ref, ey_land, (ey_send, ey_recv), 0, other_tp)
        extra_beside.start()
    turns = []
    for n in range(streams):
        y_land, _, z_land, y_send, y_recv, _, _ = lands[n]
        rows, width = z_land.shape[1], z_land.shape[2]
        cuts = cuts_of(rows)
        part = rows // cuts
        columns = pl.ds(pl.multiple_of((1 - place) * width, 128), width)
        for distance in order:
            for cut in range(cuts):
                inside = distance, pl.ds(cut * part, part)
                here = pl.ds(pl.multiple_of(at[distance] * rows + cut * part, 16), part)
                number = distance * cuts + cut
                beside[n, number] = remote(
                    parts[n].at[here, columns], y_land.at[inside], (y_send, y_recv), number, other_tp
                )
                beside[n, number].start()
                turns.append((n, distance, cut, number, part, width, inside, here))
    for copy, axis in zip(cargo, cargo_axes):
        if axis == "tp":
            copy.start()
    if has_extra:
        extra_beside.wait_recv()
        e_ready[...] = extra_ref[...] + ey_land[...]
        for distance in order:
            if distance:
                extras[distance] = remote(
                    e_ready.at[at[distance]],
                    ez_land.at[distance],
                    (ez_send, ez_recv),
                    distance,
                    {"ctx": at[distance]},
                )
                extras[distance].start()
    for n, distance, cut, number, part, width, inside, here in turns:
        y_land, ready, z_land, _, _, z_send, z_recv = lands[n]
        beside[n, number].wait_recv()
        whole = parts[n][here, :]
        own = jnp.where(first, whole[:, :width], whole[:, width:])
        total = (own.astype(FULL) + y_land[inside].astype(FULL)).astype(LOW)
        if distance:
            ready[inside] = total
            across[n, number] = remote(
                ready.at[inside], z_land.at[inside], (z_send, z_recv), number, {"ctx": at[distance]}
            )
            across[n, number].start()
        elif adds[n]:
            outs[n][inside[1], :] = total.astype(FULL)
        else:
            outs[n][here, :] = total
    for n, distance, cut, number, part, width, inside, here in turns:
        if distance:
            across[n, number].wait_recv()
            if adds[n]:
                outs[n][inside[1], :] += lands[n][2][inside].astype(FULL)
            else:
                outs[n][here, :] = lands[n][2][inside]
    if has_extra:
        extra_out[mine] = e_ready[mine]
        for distance in order:
            if distance:
                extras[distance].wait_recv()
                extra_out[at[distance]] = ez_land[distance]
                extras[distance].wait_send()
        extra_beside.wait_send()
    for copy in list(beside.values()) + list(across.values()):
        copy.wait_send()
    for copy in cargo:
        copy.wait()


def send_home(partial_rows, number, extra=None, cargo=(), add_up=False, more=None):
    size = lax.axis_size("ctx")
    operands = [partial_rows] if more is None else [partial_rows, more]
    adds = (add_up, False)[: len(operands)]
    sems = [pltpu.SemaphoreType.DMA((size,))] * 4
    shapes, scratch, moved = [], [], 0
    for item, added in zip(operands, adds):
        total, width = item.shape[0], item.shape[1] // 2
        rows = total // size
        moved += 12 * total * width
        shapes.append(
            jax.ShapeDtypeStruct((rows, width), FULL) if added else jax.ShapeDtypeStruct((total, width), LOW)
        )
        scratch += [pltpu.VMEM((size, rows, width), LOW)] * 3
        scratch += [pltpu.SemaphoreType.DMA((size * cuts_of(rows),))] * 4
    if extra is not None:
        operands.append(extra)
        shapes.append(jax.ShapeDtypeStruct(extra.shape, FULL))
        scratch += [pltpu.VMEM(extra.shape, FULL)] * 3 + sems
    in_specs = [pl.BlockSpec(memory_space=pltpu.VMEM)] * len(operands)
    out_specs = [pl.BlockSpec(memory_space=pltpu.VMEM)] * len(shapes)
    for item, _ in cargo:
        operands.append(item)
        shapes.append(jax.ShapeDtypeStruct(item.shape, item.dtype))
        in_specs.append(pl.BlockSpec(memory_space=pl.ANY))
        out_specs.append(pl.BlockSpec(memory_space=pl.ANY))
    if cargo:
        scratch += [pltpu.SemaphoreType.DMA((len(cargo),))] * 2
    results = pl.pallas_call(
        functools.partial(send_home_kernel, size, adds, extra is not None, tuple(axis for _, axis in cargo)),
        in_specs=in_specs,
        out_specs=out_specs,
        out_shape=shapes,
        scratch_shapes=scratch,
        compiler_params=pltpu.CompilerParams(
            collective_id=number, has_side_effects=True, vmem_limit_bytes=VMEM_BYTES
        ),
        cost_estimate=pl.CostEstimate(flops=0, bytes_accessed=moved, transcendentals=0),
    )(*operands)
    return results if len(shapes) > 1 else results[0]


def prologue_kernel(sizes, *refs):
    groups, world = sizes
    half_in, own_in, routes_in, kv_in, query_in, out_in, cot_in = refs[:7]
    seq_ref, routes_ref, kv_ref, query_ref, out_ref, cot_ref = refs[7:13]
    local_sem = refs[13]
    pairs = [(refs[14 + 2 * n], refs[15 + 2 * n]) for n in range(16)]
    token_line, route_line, kv_line, token_pass, kv_pass = (pairs[2 * n : 2 * n + 2] for n in range(5))
    kv_own, fr, fk, fq, fo, cot_beside = pairs[10:]
    mine, place, spot = lax.axis_index("ctx"), lax.axis_index("tp"), lax.axis_index("fsdp")
    other_tp = {"tp": 1 - place}
    rows, width = half_in.shape
    sub = kv_in.shape[0]
    piece = sub * groups
    q_rows = query_in.shape[0]
    steps = list(bits_down(world))
    beside = {bit: {"fsdp": xor_index(spot, bit)} for bit in steps}
    first = steps[0]
    meet(
        [{"ctx": xor_index(mine, distance)} for distance in range(1, groups)]
        + [other_tp]
        + [beside[bit] for bit in steps]
    )
    locals_ = [
        pltpu.make_async_copy(
            own_in.at[:, pl.ds(n * width, width)], seq_ref.at[n, span(mine, rows)], local_sem.at[n]
        )
        for n in range(2)
    ] + [
        pltpu.make_async_copy(routes_in, routes_ref.at[0, mine], local_sem.at[2]),
        pltpu.make_async_copy(kv_in, kv_ref.at[span(mine, sub)], local_sem.at[3]),
        pltpu.make_async_copy(query_in, query_ref.at[pl.ds(0, q_rows)], local_sem.at[4]),
        pltpu.make_async_copy(out_in, out_ref.at[0], local_sem.at[5]),
    ]
    started, landed = [], set()

    def go(copy):
        copy.start()
        started.append(copy)
        return copy

    def arrived(copy):
        if id(copy) not in landed:
            copy.wait_recv()
            landed.add(id(copy))

    def wrap(index):
        return lax.rem(index + groups, groups)

    def outgoing(step):
        yield 0, jnp.logical_and(mine < groups - 1, mine >= step), wrap(mine - step), wrap(mine + 1)
        yield 1, jnp.logical_and(mine > 0, mine + step < groups), wrap(mine + step), wrap(mine - 1)

    def incoming(step):
        yield 0, mine >= step + 1, wrap(mine - 1 - step)
        yield 1, mine + step + 1 < groups, wrap(mine + 1 + step)

    def line_copy(own, place_of, sems, step, way, block, target):
        source = place_of(block) if step else own
        return remote(source, place_of(block), sems[way], step, {"ctx": target})

    def line_start(own, place_of, sems, step):
        for way, happens, block, target in outgoing(step):

            @pl.when(happens)
            def _():
                line_copy(own, place_of, sems, step, way, block, target).start()

    def line_wait(place_of, sems, step, passed):
        for way, happens, block in incoming(step):

            @pl.when(happens)
            def _():
                remote(place_of(block), place_of(block), sems[way], step, other_tp).wait_recv()
                if passed is not None:
                    passed(step, way, block).start()

    def line_end(own, place_of, sems, step, passed):
        for way, happens, block, target in outgoing(step):

            @pl.when(happens)
            def _():
                line_copy(own, place_of, sems, step, way, block, target).wait_send()

        if passed is None:
            return
        for way, happens, block in incoming(step):

            @pl.when(happens)
            def _():
                passed(step, way, block).wait_send()

    def passed_wait(step, passed):
        for way, happens, block in incoming(step):

            @pl.when(happens)
            def _():
                passed(step, way, block).wait_recv()

    route_place = lambda n: routes_ref.at[0, n]
    kv_place = lambda n: kv_ref.at[span(n, sub)]
    token_place = lambda n: seq_ref.at[place, span(n, rows)]

    def kv_along(step, way, block):
        target = kv_ref.at[pl.ds(pl.multiple_of(piece + block * sub, 16), sub)]
        return remote(kv_place(block), target, kv_pass[way], step, beside[first])

    def token_along(step, way, block):
        return remote(token_place(block), token_place(block), token_pass[way], step, other_tp)

    def token_landed(step, way, block):
        view = seq_ref.at[1 - place, span(block, rows)]
        return remote(view, view, token_pass[way], step, other_tp)

    kv_first = go(
        remote(
            kv_in,
            kv_ref.at[pl.ds(pl.multiple_of(piece + mine * sub, 16), sub)],
            kv_own,
            0,
            beside[first],
        )
    )
    query_view = lambda n: query_ref.at[pl.ds(n * q_rows, q_rows)]
    out_view = lambda n: out_ref.at[n]
    kv_view = lambda n: kv_ref.at[pl.ds(n * piece, piece)]
    query_copies = {1: go(remote(query_in, query_view(1), fq, 1, beside[first]))}
    out_copies = {}
    go(remote(cot_in, cot_ref, cot_beside, 0, other_tp))
    for copy in locals_:
        copy.start()
    for step in range(groups - 1):
        line_start(kv_in, kv_place, kv_line, step)
        line_start(routes_in, route_place, route_line, step)
        line_start(half_in, token_place, token_line, step)
        if step == 0:
            for copy in locals_:
                copy.wait()
            for bit in steps[1:]:
                n = world // (2 * bit)
                query_copies[n] = go(remote(query_in, query_view(n), fq, n, beside[bit]))
                out_copies[n] = go(remote(out_in, out_view(n), fo, n, beside[bit]))
        line_wait(kv_place, kv_line, step, kv_along)
        if step == groups - 2:
            out_copies[1] = go(remote(out_in, out_view(1), fo, 1, beside[first]))
        line_wait(route_place, route_line, step, None)
        line_wait(token_place, token_line, step, token_along)
    route_wait, kv_wait = {}, {}
    count = 1
    for bit in steps:
        for n in range(count):
            peer = beside[bit]
            if n in route_wait:
                arrived(route_wait[n])
            route_wait[count + n] = go(
                remote(routes_ref.at[n], routes_ref.at[count + n], fr, count + n, peer)
            )
            if bit == first:
                continue
            if n:
                arrived(query_copies[n])
                query_copies[count + n] = go(
                    remote(query_view(n), query_view(count + n), fq, count + n, peer)
                )
            if n == 1 and count == 2:
                arrived(kv_first)
                for step in range(groups - 1):
                    passed_wait(step, kv_along)
            if n > 1:
                arrived(kv_wait[n])
            kv_wait[count + n] = go(remote(kv_view(n), kv_view(count + n), fk, count + n, peer))
            if n:
                arrived(out_copies[n])
                out_copies[count + n] = go(remote(out_view(n), out_view(count + n), fo, count + n, peer))
        count *= 2
    if world == 2:
        arrived(kv_first)
        for step in range(groups - 1):
            passed_wait(step, kv_along)
    for copy in started:
        arrived(copy)
    for step in range(groups - 1):
        passed_wait(step, token_landed)
        line_end(kv_in, kv_place, kv_line, step, kv_along)
        line_end(routes_in, route_place, route_line, step, None)
        line_end(half_in, token_place, token_line, step, token_along)
    for copy in started:
        copy.wait_send()


def prologue(token_half, token_rows, routes, kv_rows, query_piece, out_piece, cot_block, number):
    groups, world = lax.axis_size("ctx"), lax.axis_size("fsdp")
    any_space = pl.BlockSpec(memory_space=pl.ANY)
    rows, features = token_rows.shape
    pair = lambda count: [pltpu.SemaphoreType.DMA((count,))] * 2
    return pl.pallas_call(
        functools.partial(prologue_kernel, (groups, world)),
        in_specs=[pl.BlockSpec(memory_space=pltpu.VMEM)] * 7,
        out_specs=[any_space] * 6,
        out_shape=[
            jax.ShapeDtypeStruct((2, groups * rows, features // 2), LOW),
            jax.ShapeDtypeStruct((world, groups) + routes.shape, jnp.int32),
            jax.ShapeDtypeStruct((world * groups * kv_rows.shape[0], kv_rows.shape[1]), LOW),
            jax.ShapeDtypeStruct((world * query_piece.shape[0], query_piece.shape[1]), LOW),
            jax.ShapeDtypeStruct((world,) + out_piece.shape, LOW),
            jax.ShapeDtypeStruct(cot_block.shape, LOW),
        ],
        scratch_shapes=[pltpu.SemaphoreType.DMA((6,))]
        + pair(groups) * 10
        + pair(1)
        + pair(world) * 4
        + pair(1),
        compiler_params=pltpu.CompilerParams(
            collective_id=number, has_side_effects=True, vmem_limit_bytes=VMEM_BYTES
        ),
        cost_estimate=pl.CostEstimate(flops=0, bytes_accessed=100000000, transcendentals=0),
    )(token_half, token_rows, routes, kv_rows, query_piece, out_piece, cot_block)


def expert_forward_kernel(world, size, *refs):
    rows_ref = refs[0]
    gates, ups = refs[1 : 1 + world], refs[1 + world : 1 + 2 * world]
    refs = refs[1 + 2 * world :]
    blocks, beside_ref, refs = refs[:size], refs[size], refs[size + 1 :]
    hidden_ref, by_gate_ref, by_up_ref, cot_ref, y_land, y_send, y_recv = refs
    width = rows_ref.shape[1] // world
    mine, place = lax.axis_index("ctx"), lax.axis_index("tp")
    other_tp = {"tp": 1 - place}
    beside = [
        remote(blocks[distance], y_land.at[distance], (y_send, y_recv), distance, other_tp)
        for distance in range(1, size)
    ]

    @pl.when(pl.program_id(0) == 0)
    def _():
        meet([other_tp])
        for copy in beside:
            copy.start()

    gate_lin, up_lin = None, None
    for n in range(world):
        columns = slice(n * width, (n + 1) * width)
        gate_term = matmul(rows_ref[:, columns], gates[n][...])
        up_term = matmul(rows_ref[:, columns], ups[n][...])
        gate_lin = gate_lin + gate_term if n else gate_term
        up_lin = up_lin + up_term if n else up_term
    sigmoid_gate = 1.0 / (1.0 + jnp.exp(-gate_lin))
    swish = gate_lin * sigmoid_gate
    hidden_ref[...] = (swish * up_lin).astype(LOW)
    by_gate_ref[...] = (up_lin * sigmoid_gate * (1.0 + gate_lin * (1.0 - sigmoid_gate))).astype(LOW)
    by_up_ref[...] = swish.astype(LOW)

    @pl.when(pl.program_id(0) == pl.num_programs(0) - 1)
    def _():
        rows, half = y_land.shape[1], y_land.shape[2]
        for distance in range(size):
            if distance:
                beside[distance - 1].wait_recv()
            own = blocks[distance][...]
            theirs = y_land[distance] if distance else beside_ref[...]
            here = span(xor_index(mine, distance), rows)
            cot_ref[here, :half] = jnp.where(place == 0, own, theirs)
            cot_ref[here, half:] = jnp.where(place == 0, theirs, own)
        for copy in beside:
            copy.wait_send()


def expert_forward(rows, gate_pieces, up_pieces, cot_blocks, cot_beside, number):
    world, size = len(gate_pieces), len(cot_blocks)
    slots, features = rows.shape
    depth, hidden_width = gate_pieces[0].shape
    tall = pl.BlockSpec((depth, TILE), lambda i: (0, i))
    strip = pl.BlockSpec((slots, TILE), lambda i: (0, i))
    whole = lambda value: pl.BlockSpec(value.shape, lambda i: (0, 0), pipeline_mode=pl.Buffered(1))
    return pl.pallas_call(
        functools.partial(expert_forward_kernel, world, size),
        grid=(hidden_width // TILE,),
        in_specs=[whole(rows)] + [tall] * (2 * world) + [whole(block) for block in cot_blocks] + [whole(cot_beside)],
        out_specs=[strip] * 3 + [pl.BlockSpec((slots, features), lambda i: (0, 0))],
        out_shape=[jax.ShapeDtypeStruct((slots, hidden_width), LOW)] * 3
        + [jax.ShapeDtypeStruct((slots, features), LOW)],
        scratch_shapes=[pltpu.VMEM((size,) + cot_blocks[0].shape, LOW)]
        + [pltpu.SemaphoreType.DMA((size,))] * 2,
        compiler_params=pltpu.CompilerParams(
            collective_id=number, has_side_effects=True, vmem_limit_bytes=VMEM_BYTES
        ),
        cost_estimate=pl.CostEstimate(flops=0, bytes_accessed=2 * slots * features, transcendentals=0),
    )(rows, *gate_pieces, *up_pieces, *cot_blocks, cot_beside)


def product_kernel(world, tiles, hidden_ref, *refs):
    downs, out_ref = refs[:world], refs[world]
    for n in range(world):

        @pl.when(pl.program_id(0) // tiles == n)
        def _():
            out_ref[...] = matmul(hidden_ref[...], downs[n][...]).astype(LOW)


def expert_product(hidden, down_pieces):
    world = len(down_pieces)
    depth, width = down_pieces[0].shape
    tiles = max(width // TILE, 1)
    tile = width // tiles

    def piece_spec(n):
        return pl.BlockSpec((depth, tile), lambda i: (0, jnp.clip(i - n * tiles, 0, tiles - 1)))

    return pl.pallas_call(
        functools.partial(product_kernel, world, tiles),
        grid=(world * tiles,),
        in_specs=[pl.BlockSpec(hidden.shape, lambda i: (0, 0), pipeline_mode=pl.Buffered(1))]
        + [piece_spec(n) for n in range(world)],
        out_specs=pl.BlockSpec((hidden.shape[0], tile), lambda i: (0, i)),
        out_shape=jax.ShapeDtypeStruct((hidden.shape[0], world * width), LOW),
        compiler_params=pltpu.CompilerParams(vmem_limit_bytes=VMEM_BYTES),
        cost_estimate=pl.CostEstimate(
            flops=2 * hidden.shape[0] * depth * world * width,
            bytes_accessed=2 * depth * world * width,
            transcendentals=0,
        ),
    )(hidden, *down_pieces)


def expert_back_kernel(world, steps, size, *refs):
    rows_ref, cot_ref, mix_ref, hidden_ref, by_gate_ref, by_up_ref = refs[:6]
    gates, ups, downs = (refs[6 + n * world : 6 + (n + 1) * world] for n in range(3))
    refs = refs[6 + 3 * world :]
    part_ref, refs = (refs[0], refs[1:]) if size else (None, refs)
    near_ref, landed_ref, db_ref, mix_grad_ref = refs[:4]
    home_ref, refs = (refs[4], refs[5:]) if size else (None, refs[4:])
    db_sum, rows_t_ref, cot_t_ref, far, send_sem, recv_sem = refs[:6]
    step = pl.program_id(0)
    slot = lax.rem(step, 2)
    features = rows_ref.shape[1]
    width = features // world
    half = features // 2
    tile = near_ref.shape[3]
    other_core = {"fsdp": xor_index(lax.axis_index("fsdp"), 1)}
    peers = [other_core]
    if size:
        y_land, ready, z_land, y_send, y_recv, z_send, z_recv = refs[6:]
        mine, place = lax.axis_index("ctx"), lax.axis_index("tp")
        other_tp = {"tp": 1 - place}
        at = [xor_index(mine, distance) for distance in range(size)]
        peers = peers + [other_tp] + [{"ctx": at[distance]} for distance in range(1, size)]
        home_rows, home_width = z_land.shape[1], z_land.shape[2]
        away = pl.ds(pl.multiple_of((1 - place) * home_width, 128), home_width)
        order = mixed_order(size)

        def beside(distance):
            return remote(
                part_ref.at[span(at[distance], home_rows), away],
                y_land.at[distance],
                (y_send, y_recv),
                distance,
                other_tp,
            )

        def across(distance):
            return remote(
                ready.at[distance],
                z_land.at[distance],
                (z_send, z_recv),
                distance,
                {"ctx": at[distance]},
            )

    def far_copy(at_step, at_slot):
        return pltpu.make_async_remote_copy(
            src_ref=far.at[at_slot],
            dst_ref=landed_ref.at[at_step],
            send_sem=send_sem.at[at_slot],
            recv_sem=recv_sem.at[at_step],
            device_id=other_core,
            device_id_type=pl.DeviceIdType.MESH,
        )

    @pl.when(step == 0)
    def _():
        meet(peers)
        if size:
            for distance in order:
                beside(distance).start()
        db_sum[...] = jnp.zeros_like(db_sum)
        mix_grad_ref[...] = jnp.zeros_like(mix_grad_ref)
        for place_at in range(0, features, tile):
            rows_t_ref[place_at : place_at + tile, :] = rows_ref[:, place_at : place_at + tile].T
            cot_t_ref[place_at : place_at + tile, :] = cot_ref[:, place_at : place_at + tile].T

    d_hidden = None
    for n in range(world):
        columns = slice(n * width, (n + 1) * width)
        term = matmul_nt(cot_ref[:, columns], downs[n][...])
        d_hidden = d_hidden + term if n else term
    hidden = hidden_ref[...].astype(FULL)
    mix_grad = hidden * d_hidden
    for place_at in range(0, tile, HEAD):
        mix_grad_ref[...] += mix_grad[:, place_at : place_at + HEAD]
    mix = jnp.concatenate([mix_ref[...]] * (tile // HEAD), axis=1)
    d_gated = d_hidden * mix
    mixed_low = (hidden * mix).astype(LOW)
    d_gate = (d_gated * by_gate_ref[...].astype(FULL)).astype(LOW)
    d_up = (d_gated * by_up_ref[...].astype(FULL)).astype(LOW)
    @pl.when(step >= 2)
    def _():
        far_copy(step - 2, slot).wait_send()

    pairs = ((rows_t_ref, d_gate), (rows_t_ref, d_up), (cot_t_ref, mixed_low))
    for n, (left, right) in enumerate(pairs):
        far[slot, n] = matmul(left[half:, :], right).astype(LOW)
    far_copy(step, slot).start()
    for n in range(world):
        columns = slice(n * width, (n + 1) * width)
        db_sum[:, columns] += matmul_nt(d_gate, gates[n][...]) + matmul_nt(d_up, ups[n][...])

    for n, (left, right) in enumerate(pairs):
        near_ref[0, n] = matmul(left[:half, :], right).astype(LOW)

    if size:
        for turn, distance in enumerate(order):

            @pl.when(step == min(turn + 1, steps - 1))
            def _():
                beside(distance).wait_recv()
                whole = part_ref[span(at[distance], home_rows), :]
                own = jnp.where(place == 0, whole[:, :home_width], whole[:, home_width:])
                total = (own.astype(FULL) + y_land[distance].astype(FULL)).astype(LOW)
                if distance:
                    ready[distance] = total
                    across(distance).start()
                else:
                    home_ref[span(mine, home_rows), :] = total

    @pl.when(step == steps - 1)
    def _():
        db_ref[...] = db_sum[...].astype(LOW)
        for last in range(max(steps - 2, 0), steps):
            far_copy(last, last % 2).wait_send()
        for last in range(steps):
            far_copy(last, last % 2).wait_recv()
        if size:
            for distance in order:
                beside(distance).wait_send()
                if distance:
                    across(distance).wait_recv()
                    home_ref[span(at[distance], home_rows), :] = z_land[distance]
                    across(distance).wait_send()


def expert_back(rows, cot_rows, mix_rows, forward, pieces, first, steps, number, going_home=None):
    gate_pieces, up_pieces, down_pieces = pieces
    world = len(gate_pieces)
    slots, features = rows.shape
    depth = gate_pieces[0].shape[0]
    tile = TILE
    once = pl.Buffered(1)
    whole = lambda value: pl.BlockSpec(value.shape, lambda i: (0, 0), pipeline_mode=once)
    kept = lambda width: pl.BlockSpec((slots, width), lambda i: (0, 0))
    tall = pl.BlockSpec((depth, tile), lambda i: (0, i + first))
    flat = pl.BlockSpec((tile, depth), lambda i: (i + first, 0))
    strip = pl.BlockSpec((slots, tile), lambda i: (0, i + first))
    low = lambda *shape: jax.ShapeDtypeStruct(shape, LOW)
    grads = low(steps, 3, features // 2, tile)
    operands = [rows, cot_rows, mix_rows, *forward, *gate_pieces, *up_pieces, *down_pieces]
    in_specs = [whole(rows), whole(cot_rows), whole(mix_rows)] + [strip] * 3
    in_specs += [tall] * (2 * world) + [flat] * world
    out_specs = [
        pl.BlockSpec((1, 3, features // 2, tile), lambda i: (i, 0, 0, 0)),
        pl.BlockSpec(memory_space=pl.ANY),
        kept(features),
        kept(HEAD),
    ]
    out_shape = [grads, grads, low(slots, features), jax.ShapeDtypeStruct((slots, HEAD), FULL)]
    scratch = [
        pltpu.VMEM((slots, features), FULL),
        pltpu.VMEM((features, slots), LOW),
        pltpu.VMEM((features, slots), LOW),
        pltpu.VMEM((2, 3, features // 2, tile), LOW),
        pltpu.SemaphoreType.DMA((2,)),
        pltpu.SemaphoreType.DMA((steps,)),
    ]
    size = 0
    if going_home is not None:
        size = lax.axis_size("ctx")
        operands.append(going_home)
        in_specs.append(whole(going_home))
        out_specs.append(kept(features // 2))
        out_shape.append(low(slots, features // 2))
        scratch += [pltpu.VMEM((size, slots // size, features // 2), LOW)] * 3
        scratch += [pltpu.SemaphoreType.DMA((size,))] * 4
    return pl.pallas_call(
        functools.partial(expert_back_kernel, world, steps, size),
        grid=(steps,),
        in_specs=in_specs,
        out_specs=out_specs,
        out_shape=out_shape,
        scratch_shapes=scratch,
        compiler_params=pltpu.CompilerParams(
            collective_id=number, has_side_effects=True, vmem_limit_bytes=VMEM_BYTES
        ),
        cost_estimate=pl.CostEstimate(
            flops=0, bytes_accessed=2 * slots * features, transcendentals=0
        ),
    )(*operands)


def scatter_rest(near, landed):
    pieces = lax.axis_size("fsdp")
    arrived, high, bit = [near, landed], near.shape[2], 2
    while True:
        total = arrived[0][:, :, high // 2 : high].astype(FULL)
        for block in arrived[1:]:
            total = total + block[:, :, high // 2 : high].astype(FULL)
        sent = total.astype(LOW)
        high //= 2
        if 2 * bit >= pieces:
            return sent, arrived
        arrived.append(swap(sent, "fsdp", bit))
        bit *= 2


def finish_kernel(count, steps_one, *refs):
    ones, twos = refs[:count], refs[count : 2 * count]
    outs = refs[2 * count :]

    def add_up(parts):
        for n, out in enumerate(outs):
            total = parts[0][0, n].astype(FULL)
            for part in parts[1:]:
                total = total + part[0, n].astype(FULL)
            out[...] = total.T if n == 2 else total

    @pl.when(pl.program_id(0) < steps_one)
    def _():
        add_up(ones)

    @pl.when(pl.program_id(0) >= steps_one)
    def _():
        add_up(twos)


def finish_experts(ones, twos):
    steps_one, steps_two = ones[0].shape[0], twos[0].shape[0]
    depth, tile = ones[-1].shape[2:]
    width = (steps_one + steps_two) * tile
    block = (1, 3, depth, tile)
    first = pl.BlockSpec(block, lambda i: (jnp.minimum(i, steps_one - 1), 0, 0, 0))
    second = pl.BlockSpec(block, lambda i: (jnp.maximum(i - steps_one, 0), 0, 0, 0))
    tall = pl.BlockSpec((depth, tile), lambda i: (0, i))
    return pl.pallas_call(
        functools.partial(finish_kernel, len(ones), steps_one),
        grid=(steps_one + steps_two,),
        in_specs=[first] * len(ones) + [second] * len(twos),
        out_specs=[tall, tall, pl.BlockSpec((tile, depth), lambda i: (i, 0))],
        out_shape=[jax.ShapeDtypeStruct((depth, width), FULL)] * 2
        + [jax.ShapeDtypeStruct((width, depth), FULL)],
        compiler_params=pltpu.CompilerParams(vmem_limit_bytes=VMEM_BYTES),
        cost_estimate=pl.CostEstimate(
            flops=0, bytes_accessed=30 * width * depth, transcendentals=0
        ),
    )(*ones, *twos)


def scatter_start(product, features, first_dim):
    pieces = lax.axis_size("fsdp")
    high, bit, arrived = features, 1, []

    def part(low, high):
        total = product(low, high)
        for block in arrived:
            total = total + lax.slice_in_dim(block, low, high, axis=first_dim).astype(FULL)
        return total

    while True:
        sent = part(high // 2, high).astype(LOW)
        high //= 2
        if 2 * bit >= pieces:
            break
        arrived.append(swap(sent, "fsdp", bit))
        bit *= 2

    def finish(last):
        arrived.append(last)
        return part(0, high)

    return sent, finish


def last_step(sent):
    return swap(sent, "fsdp", lax.axis_size("fsdp") // 2)


def turn_tables(length):
    half_head = HEAD // 2
    steps = np.arange(half_head, dtype=np.float32) * np.float32(2.0 / HEAD)
    frequency = np.power(np.float32(ROPE_BASE), -steps).astype(np.float32)
    angles = np.arange(length, dtype=np.float32)[:, None] * frequency[None, :]
    cosine = np.cos(angles.astype(np.float64)).astype(np.float32)
    sine = np.sin(angles.astype(np.float64)).astype(np.float32)
    return np.concatenate([cosine, cosine, -sine, sine], axis=1)


def turn(value, table):
    return value * table[:, :HEAD] + pltpu.roll(value, HEAD // 2, 1) * table[:, HEAD:]


def turn_back(value, table):
    return value * table[:, :HEAD] - pltpu.roll(value, HEAD // 2, 1) * table[:, HEAD:]


def attend_kernel(
    groups, scale, q_lin, k_lin, v_lin, q_table, k_table, q_low, k_low, v_low, heads, log_sum
):
    q_low[...] = turn(q_lin[...], q_table[...]).astype(LOW)
    k_low[...] = turn(k_lin[...], k_table[...]).astype(LOW)
    v_low[...] = v_lin[...].astype(LOW)
    rows = q_low.shape[0] // groups
    block = k_low.shape[0] // groups
    for group in range(groups):
        span = slice(group * rows, (group + 1) * rows)
        seen = slice(0, (group + 1) * block)
        scores = matmul_nt(q_low[span, :], k_low[seen, :]) * scale
        top = jnp.max(scores, axis=1, keepdims=True)
        weights = jnp.exp(scores - top)
        total = jnp.sum(weights, axis=1, keepdims=True)
        weights = (weights * (1.0 / total)).astype(LOW)
        heads[span, :] = matmul(weights, v_low[seen, :]).astype(LOW)
        log_sum[span, :] = jnp.broadcast_to(top + jnp.log(total), (rows, HEAD))


def attend(query_lin, kv_lin, query_table, key_table, groups):
    slots, width = query_lin.shape
    length = kv_lin.shape[0]
    count = width // HEAD
    by_head = lambda rows: pl.BlockSpec((rows, HEAD), lambda h: (0, h))
    whole = lambda rows: pl.BlockSpec((rows, 2 * HEAD), lambda h: (0, 0))
    return pl.pallas_call(
        functools.partial(attend_kernel, groups, 1.0 / math.sqrt(HEAD)),
        grid=(count,),
        in_specs=[
            by_head(slots),
            by_head(length),
            pl.BlockSpec((length, HEAD), lambda h: (0, h + count)),
            whole(slots),
            whole(length),
        ],
        out_specs=[by_head(slots), by_head(length), by_head(length), by_head(slots), by_head(slots)],
        out_shape=[
            jax.ShapeDtypeStruct((slots, width), LOW),
            jax.ShapeDtypeStruct((length, width), LOW),
            jax.ShapeDtypeStruct((length, width), LOW),
            jax.ShapeDtypeStruct((slots, width), LOW),
            jax.ShapeDtypeStruct((slots, width), FULL),
        ],
        compiler_params=pltpu.CompilerParams(vmem_limit_bytes=VMEM_BYTES),
        cost_estimate=pl.CostEstimate(
            flops=0, bytes_accessed=20 * length * width, transcendentals=0
        ),
    )(query_lin, kv_lin, kv_lin, query_table, key_table)


def attend_back_kernel(
    groups, scale, q_low, k_low, v_low, d_heads, log_sum, q_table, k_table, dq, dk, dv, dk_sum, dv_sum
):
    dk_sum[...] = jnp.zeros_like(dk_sum)
    dv_sum[...] = jnp.zeros_like(dv_sum)
    rows = q_low.shape[0] // groups
    block = k_low.shape[0] // groups
    for group in range(groups):
        span = slice(group * rows, (group + 1) * rows)
        seen = slice(0, (group + 1) * block)
        query, keys = q_low[span, :], k_low[seen, :]
        grads = d_heads[span, :]
        scores = matmul_nt(query, keys) * scale
        weights = jnp.exp(scores - log_sum[span, :1])
        d_weights = matmul_nt(grads, v_low[seen, :])
        delta = jnp.sum(weights * d_weights, axis=1, keepdims=True)
        d_scores = (weights * (d_weights - delta)).astype(LOW)
        dq[span, :] = turn_back(matmul(d_scores, keys) * scale, q_table[span, :]).astype(LOW)
        dk_sum[seen, :] += matmul_tn(d_scores, query) * scale
        dv_sum[seen, :] += matmul_tn(weights.astype(LOW), grads)
    dk[...] = turn_back(dk_sum[...], k_table[...]).astype(LOW)
    dv[...] = dv_sum[...].astype(LOW)


def attend_back(q_low, k_low, v_low, d_heads, log_sum, query_table, key_table, groups):
    slots, width = q_low.shape
    length = k_low.shape[0]
    count = width // HEAD
    by_head = lambda rows: pl.BlockSpec((rows, HEAD), lambda h: (0, h))
    whole = lambda rows: pl.BlockSpec((rows, 2 * HEAD), lambda h: (0, 0))
    return pl.pallas_call(
        functools.partial(attend_back_kernel, groups, 1.0 / math.sqrt(HEAD)),
        grid=(count,),
        in_specs=[
            by_head(slots),
            by_head(length),
            by_head(length),
            by_head(slots),
            by_head(slots),
            whole(slots),
            whole(length),
        ],
        out_specs=[by_head(slots), by_head(length), by_head(length)],
        out_shape=[
            jax.ShapeDtypeStruct((slots, width), LOW),
            jax.ShapeDtypeStruct((length, width), LOW),
            jax.ShapeDtypeStruct((length, width), LOW),
        ],
        scratch_shapes=[pltpu.VMEM((length, HEAD), FULL), pltpu.VMEM((length, HEAD), FULL)],
        compiler_params=pltpu.CompilerParams(vmem_limit_bytes=VMEM_BYTES),
        cost_estimate=pl.CostEstimate(
            flops=0, bytes_accessed=14 * length * width, transcendentals=0
        ),
    )(q_low, k_low, v_low, d_heads, log_sum, query_table, key_table)


def chosen_picks(routes, expert_count, capacity):
    experts = jnp.arange(expert_count, dtype=jnp.int32)
    onehot = (routes[:, :, None] == experts[None, None, :]).astype(jnp.int32)
    rows = routes.shape[0]
    below = (jnp.arange(rows)[:, None] > jnp.arange(rows)[None, :]).astype(LOW)
    order = matmul(below, jnp.sum(onehot, axis=1).astype(LOW)).astype(jnp.int32)
    slot = routes * capacity + jnp.sum(onehot * order[:, None, :], axis=2)
    slots = jnp.arange(expert_count * capacity, dtype=jnp.int32)
    picks = [(slot[:, k : k + 1] == slots[None, :]).astype(LOW) for k in range(routes.shape[1])]
    return picks, onehot.astype(FULL)


def expert_picks(routes_seq, expert, capacity):
    named = jnp.any(routes_seq == expert, axis=1)
    rows = named.shape[1]
    above = (jnp.arange(rows)[:, None] < jnp.arange(rows)[None, :]).astype(LOW)
    order = matmul(named.astype(LOW), above).astype(jnp.int32)
    slot = jnp.where(named, order, -1)
    return (slot[:, None, :] == jnp.arange(capacity, dtype=jnp.int32)[None, :, None]).astype(LOW)


def mix_of(logits, onehot):
    chosen = jnp.sum(onehot * logits[:, None, :], axis=2)
    return jax.nn.softmax(chosen, axis=1)


def logits_back(mix, mix_grad, probs, onehot, share_grad):
    d_chosen = mix * (mix_grad - jnp.sum(mix * mix_grad, axis=1, keepdims=True))
    d_logits = jnp.sum(onehot * d_chosen[:, :, None], axis=1)
    inner = jnp.sum(probs * share_grad[None, :], axis=1, keepdims=True)
    return d_logits + probs * (share_grad[None, :] - inner)


def through_router(d_logits, router_half):
    total = d_logits[:, 0:1] * router_half[:, 0][None, :]
    for expert in range(1, d_logits.shape[1]):
        total = total + d_logits[:, expert : expert + 1] * router_half[:, expert][None, :]
    return total


def on_device(
    tokens,
    cotangent,
    attn_routes,
    ffn_routes,
    norm_gain1,
    norm_gain2,
    attn_router,
    ffn_router,
    key_proj,
    value_proj,
    query_proj,
    out_proj,
    gate_proj,
    up_proj,
    down_proj,
):
    rows_here, features = tokens.shape
    half_width = features // 2
    picks_each = attn_routes.shape[1]
    expert_count = attn_router.shape[1]
    groups = lax.axis_size("ctx")
    mine = lax.axis_index("ctx")
    capacity = rows_here * picks_each // expert_count * 5 // 4
    slots = groups * capacity
    all_tokens = rows_here * lax.axis_size("fsdp") * groups

    attn_picks, attn_onehot = chosen_picks(attn_routes, expert_count, capacity)
    ffn_picks, ffn_onehot = chosen_picks(ffn_routes, expert_count, capacity)
    ffn_pick = ffn_picks[0]
    for pick in ffn_picks[1:]:
        ffn_pick = ffn_pick + pick
    cot_half = my_half(to_spread(cotangent, 1))
    cot_slots = matmul_tn(ffn_pick, cot_half).astype(LOW)

    tokens_spread = to_spread(tokens, 1)
    token_half = my_half(tokens_spread)
    routes_mine = jnp.concatenate([attn_routes.T, ffn_routes.T], axis=0)
    routes_mine = jnp.concatenate([routes_mine, jnp.zeros_like(routes_mine)], axis=0)
    kv_mine = jnp.concatenate([key_proj, value_proj], axis=1)
    seq_low, all_routes, kv_full, query_full, out_pieces, cot_beside = prologue(
        token_half,
        tokens_spread,
        routes_mine,
        kv_mine,
        query_proj[0],
        out_proj[0],
        block_for(cot_slots, 0),
        0,
    )
    seq_routes = all_routes[0]
    seq_tokens = jnp.concatenate([seq_low[0], seq_low[1]], axis=1).astype(FULL)
    out_full = jnp.concatenate([out_pieces[n] for n in range(lax.axis_size("fsdp"))], axis=1)

    gate_pieces = gather_pieces(after(gate_proj[0], all_routes))
    up_pieces = gather_pieces(after(up_proj[0], all_routes))
    down_pieces = gather_pieces(after(down_proj[0], all_routes))

    gain1 = to_spread(norm_gain1, 0)
    gain2_half = my_half(to_spread(norm_gain2, 0))
    router1 = to_spread(attn_router, 0)
    router2 = to_spread(ffn_router, 0)
    router1_half = my_half(router1.T).T.astype(FULL)
    router2_half = my_half(router2.T).T

    scale_seq = lax.rsqrt(jnp.mean(seq_tokens * seq_tokens, axis=1, keepdims=True) + EPSILON)
    a_seq = (seq_tokens * scale_seq * gain1).astype(LOW)
    a_mine = lax.dynamic_slice_in_dim(a_seq, mine * rows_here, rows_here, 0)
    scale_one = lax.dynamic_slice_in_dim(scale_seq, mine * rows_here, rows_here, 0)
    attn_logits = matmul(a_mine, router1)
    attn_probs = jax.nn.softmax(attn_logits, axis=1)
    attn_mix = mix_of(attn_logits, attn_onehot)

    later = after(cot_slots, all_routes)
    cot_blocks = [block_for(later, distance) for distance in range(groups)]
    cot_blocks[1:] = [swap(cot_blocks[distance], "ctx", distance) for distance in range(1, groups)]

    expert_onehot = expert_picks(seq_routes[:, :picks_each], mine, capacity)
    key_table = jnp.asarray(turn_tables(groups * rows_here))
    query_table = jnp.einsum(
        "bsr,brh->bsh",
        expert_onehot.astype(FULL),
        key_table.reshape(groups, rows_here, -1),
        precision=PRECISE,
    ).reshape(slots, -1)
    rows_in = (
        jnp.einsum(
            "bsr,brd->bsd",
            expert_onehot,
            a_seq.reshape(groups, rows_here, features),
            preferred_element_type=FULL,
        )
        .astype(LOW)
        .reshape(slots, features)
    )
    query_lin = matmul(rows_in, query_full)
    kv_lin = matmul(a_seq, kv_full)
    q_low, k_low, v_low, heads_low, log_sum = attend(
        query_lin, kv_lin, query_table, key_table, groups
    )
    cargo = [(item, "core") for item in gate_pieces + [up_proj[0], down_proj[0]]]
    attn_back, *known = send_home(
        after(matmul(heads_low, out_full).astype(LOW), *cot_blocks[1:]), 1, cargo=cargo
    )
    gate_known, up_known, down_known = known[:-2], known[-2:-1], known[-1:]

    input_half = my_half(tokens_spread).astype(FULL)
    attn_picked = [matmul(pick, attn_back) for pick in attn_picks]
    attended = input_half
    for k in range(picks_each):
        attended = attended + attn_mix[:, k : k + 1] * attn_picked[k]
    square_sum = tp_sum(jnp.sum(attended * attended, axis=1, keepdims=True))
    scale_two = lax.rsqrt(square_sum / features + EPSILON)
    b_half = (attended * scale_two * gain2_half).astype(LOW)
    gate_all = with_neighbours(gate_pieces, gate_known)
    b_slots = matmul_tn(ffn_pick, b_half).astype(LOW)
    up_all = with_neighbours(up_pieces, up_known, b_slots)
    ffn_rows = send_out(after(b_slots, up_all[-1]), 2)
    ffn_logits = tp_sum(matmul(b_half, router2_half))
    ffn_probs = jax.nn.softmax(ffn_logits, axis=1)
    ffn_mix = mix_of(ffn_logits, ffn_onehot)

    ffn_seq_routes = seq_routes[:, picks_each : 2 * picks_each]
    ffn_expert_onehot = expert_picks(ffn_seq_routes, mine, capacity).astype(FULL)
    row_routes = jnp.einsum(
        "bsr,bkr->bsk", ffn_expert_onehot, ffn_seq_routes.astype(FULL), precision=PRECISE
    ).reshape(slots, picks_each)
    row_onehot = row_routes[:, :, None] == jnp.arange(expert_count, dtype=FULL)[None, None, :]
    row_mix = mix_of(matmul(ffn_rows, router2), row_onehot.astype(FULL))
    mine_too = (row_routes == mine.astype(FULL)).astype(FULL)
    mix_rows = jnp.broadcast_to(jnp.sum(row_mix * mine_too, axis=1, keepdims=True), (slots, HEAD))
    *forward, cot_rows = expert_forward(ffn_rows, gate_all, up_all, cot_blocks, cot_beside, 6)
    down_all = with_neighbours(down_pieces, down_known, forward[0])
    ffn_out = expert_product(forward[0], down_all)
    pieces = (gate_all, up_all, down_all)
    tiles = gate_proj.shape[2] // TILE
    count_one = (tiles + 1) // 2
    near_one, landed_one, db_one, mix_grad_one, ffn_back = expert_back(
        ffn_rows, cot_rows, mix_rows, forward, pieces, 0, count_one, 7, going_home=ffn_out
    )
    sent_one, parts_one = scatter_rest(near_one, landed_one)
    back_one = last_step(sent_one)
    near_two, landed_two, db_two, mix_grad_two = expert_back(
        after(ffn_rows, sent_one), cot_rows, mix_rows, forward, pieces, count_one, tiles - count_one, 8
    )
    sent_two, parts_two = scatter_rest(near_two, landed_two)
    back_two = last_step(sent_two)
    db_rows = (db_one.astype(FULL) + db_two.astype(FULL)).astype(LOW)
    mix_grad_rows = jnp.pad(
        jnp.sum(mix_grad_one + mix_grad_two, axis=1).reshape(groups, 1, capacity),
        ((0, 0), (0, 7), (0, 256 - capacity)),
    )
    db_back, mix_grad_back = send_home(after(db_rows, sent_two), 3, extra=mix_grad_rows)
    db_back = after(db_back, back_one)
    mix_grad_back = mix_grad_back[:, 0, :capacity].reshape(1, slots)

    experts = jnp.arange(expert_count, dtype=jnp.int32)
    named = (all_routes[..., None] == experts).astype(FULL)
    hits = jnp.stack(
        [
            jnp.sum(named[:, :, :picks_each], axis=(0, 1, 2, 3)),
            jnp.sum(named[:, :, picks_each : 2 * picks_each], axis=(0, 1, 2, 3)),
        ]
    )
    share = hits / (all_tokens * picks_each)
    share_grad = AUX_WEIGHT * expert_count / all_tokens * share
    grad_half = cot_half.astype(FULL)
    d_normed2 = jnp.zeros((rows_here, half_width), FULL)
    ffn_mix_grad = []
    for pick in ffn_picks:
        d_normed2 = d_normed2 + matmul(pick, db_back)
        ffn_mix_grad.append(jnp.sum(pick.astype(FULL) * mix_grad_back, axis=1, keepdims=True))
    ffn_mix_grad = jnp.concatenate(ffn_mix_grad, axis=1)
    ffn_d_logits = logits_back(ffn_mix, ffn_mix_grad, ffn_probs, ffn_onehot, share_grad[1])
    d_normed2 = d_normed2 + through_router(ffn_d_logits, router2_half.astype(FULL))
    weighted2 = d_normed2 * gain2_half
    inner2 = tp_sum(jnp.sum(weighted2 * attended, axis=1, keepdims=True)) / features
    d_attended = grad_half + scale_two * weighted2 - attended * scale_two**3 * inner2
    gain2_part = jnp.sum(d_normed2 * attended * scale_two, axis=0)
    ffn_router_part = precise_tn(b_half.astype(FULL), ffn_d_logits)

    dy_slots = jnp.zeros((slots, half_width), FULL)
    for k in range(picks_each):
        dy_slots = dy_slots + matmul_tn(attn_picks[k], (attn_mix[:, k : k + 1] * d_attended).astype(LOW))
    dy_rows = send_out(dy_slots.astype(LOW), 4)
    out_sent, out_finish = scatter_start(
        lambda low, high: matmul_tn(heads_low, dy_rows[:, low:high]), features, 1
    )
    out_back = last_step(out_sent)
    d_heads = after(matmul_nt(dy_rows, out_full).astype(LOW), out_sent)
    dq_low, dk_low, dv_low = attend_back(
        q_low, k_low, v_low, d_heads, log_sum, query_table, key_table, groups
    )
    dkv_low = after(jnp.concatenate([dk_low, dv_low], axis=1), back_two)
    da_rows = matmul_nt(dq_low, query_full).astype(LOW).reshape(groups, capacity, features)
    da_seq = jnp.einsum("bsr,bsd->brd", expert_onehot, da_rows, preferred_element_type=FULL)
    da_seq = da_seq.reshape(groups * rows_here, features) + matmul_nt(dkv_low, kv_full)
    kv_sent, kv_finish = scatter_start(
        lambda low, high: matmul_tn(a_seq[:, low:high], dkv_low), features, 0
    )
    result = attended
    for k in range(picks_each):
        result = result + ffn_mix[:, k : k + 1] * matmul(ffn_picks[k], ffn_back)
    result_low = result.astype(LOW)
    da_half, kv_back, result_other = send_home(
        after(da_seq.astype(LOW), out_back),
        5,
        cargo=((kv_sent, "fsdp"), (result_low, "tp")),
        add_up=True,
    )
    output = from_spread(join_halves(result_low, result_other), 1)
    kv_part = kv_finish(kv_back)
    query_sent, query_finish = scatter_start(
        lambda low, high: matmul_tn(rows_in[:, low:high], after(dq_low, kv_part)), features, 0
    )
    query_back = last_step(query_sent)
    kv_part_low = kv_part.astype(LOW)
    kv_arrived = [
        swap(block_for(kv_part_low, distance), "ctx", distance)
        for distance in far_first(groups)
        if distance
    ]
    query_grad = query_finish(query_back)
    out_grad = out_finish(after(out_back, da_half))
    back_one, back_two = lax.optimization_barrier((back_one, back_two, query_sent))[:2]
    gate_grad, up_grad, down_grad = finish_experts(parts_one + [back_one], parts_two + [back_two])
    kv_grad = block_for(kv_part, 0)
    for block in lax.optimization_barrier((*kv_arrived, gate_grad))[:-1]:
        kv_grad = kv_grad + block.astype(FULL)
    key_width = key_proj.shape[1]

    attn_mix_grad = tp_sum(
        jnp.concatenate(
            [jnp.sum(d_attended * picked, axis=1, keepdims=True) for picked in attn_picked], axis=1
        )
    )
    attn_d_logits = logits_back(attn_mix, attn_mix_grad, attn_probs, attn_onehot, share_grad[0])
    a_half = my_half(a_mine)
    attn_router_part = precise_tn(a_half.astype(FULL), attn_d_logits)

    d_normed1 = da_half + through_router(attn_d_logits, router1_half)
    gain1_half = my_half(gain1)
    weighted1 = d_normed1 * gain1_half
    inner1 = tp_sum(jnp.sum(weighted1 * input_half, axis=1, keepdims=True)) / features
    input_grad = d_attended + scale_one * weighted1 - input_half * scale_one**3 * inner1
    input_grad_low = input_grad.astype(LOW)
    input_grad_other = after(swap(input_grad_low, "tp", 1), gate_grad)
    input_grad = from_spread(join_halves(input_grad_low, input_grad_other), 1).astype(FULL)
    gain1_part = jnp.sum(d_normed1 * input_half * scale_one, axis=0)

    small = jnp.concatenate(
        [gain1_part[None], gain2_part[None], attn_router_part.T, ffn_router_part.T], axis=0
    )
    small = from_spread(join_halves(small, swap(small, "tp", 1)), 1)
    prob_sums = jnp.concatenate([jnp.sum(attn_probs, axis=0), jnp.sum(ffn_probs, axis=0)])
    small = jnp.concatenate([small, jnp.pad(prob_sums, (0, features - prob_sums.shape[0]))[None]], axis=0)
    small = after(all_sum(small, ("fsdp",)), query_back, gate_grad)
    small = all_sum(small, ("ctx",))
    prob_sums = small[-1, : 2 * expert_count].reshape(2, expert_count)
    losses = expert_count * jnp.sum(share * prob_sums / all_tokens, axis=1)
    return (
        output,
        input_grad,
        losses[0],
        losses[1],
        small[0],
        small[1],
        small[2 : 2 + expert_count].T,
        small[2 + expert_count : 2 + 2 * expert_count].T,
        kv_grad[:, :key_width],
        kv_grad[:, key_width:],
        query_grad[None],
        out_grad[None],
        gate_grad[None],
        up_grad[None],
        down_grad[None],
    )


def solution(mesh):
    by_token = P(("fsdp", "ctx"), None)
    by_row = P(("fsdp", "ctx"), "tp")
    inward = P("ctx", "fsdp", "tp")
    outward = P("ctx", "tp", "fsdp")
    weights = (by_row, by_row, inward, outward, inward, inward, outward)
    return jax.shard_map(
        on_device,
        mesh=mesh,
        in_specs=(by_token,) * 4 + (P(),) * 4 + weights,
        out_specs=(by_token,) * 2 + (P(),) * 6 + weights,
        check_vma=False,
    )
```

```python
import functools
import math

import jax
import jax.numpy as jnp
import numpy as np
from jax import lax
from jax.experimental import pallas as pl
from jax.experimental.pallas import tpu as pltpu
from jax.sharding import PartitionSpec as P

HEAD = 128
EPSILON = 1e-06
ROPE_BASE = 10000.0
AUX_WEIGHT = 0.1
PRECISE = lax.Precision.HIGHEST
LOW = jnp.bfloat16
FULL = jnp.float32
VMEM_BYTES = 58 * 1024 * 1024
TILE = 256


def matmul(lhs, rhs):
    return jnp.dot(lhs, rhs, preferred_element_type=FULL)


def matmul_tn(lhs, rhs):
    return lax.dot_general(lhs, rhs, (((0,), (0,)), ((), ())), preferred_element_type=FULL)


def matmul_nt(lhs, rhs):
    return lax.dot_general(lhs, rhs, (((1,), (1,)), ((), ())), preferred_element_type=FULL)


def precise_tn(lhs, rhs):
    return lax.dot_general(lhs, rhs, (((0,), (0,)), ((), ())), precision=PRECISE)


def swap(value, axis, distance):
    size = lax.axis_size(axis)
    return lax.ppermute(value, axis, [(i, i ^ distance) for i in range(size)])


def after(value, *earlier):
    return lax.optimization_barrier((value,) + earlier)[0]


def bits_down(size):
    bit = size // 2
    while bit >= 1:
        yield bit
        bit //= 2


def spread_order(size):
    order = [0]
    for bit in bits_down(size):
        order = order + [place | bit for place in order]
    return order


def gather_pieces(piece):
    pieces = [piece]
    for bit in bits_down(lax.axis_size("fsdp")):
        if bit > 1:
            pieces = pieces + [swap(item, "fsdp", bit) for item in pieces]
    return pieces


def with_neighbours(pieces, known, *earlier):
    rest = [swap(after(item, *earlier), "fsdp", 1) for item in pieces[len(known) :]]
    return pieces + list(known) + rest


def flip_blocks(value, axis, index, count):
    parts = jnp.split(value, count, axis)
    for bit in bits_down(count):
        turned = (index // bit) % 2 == 1
        parts = [jnp.where(turned, parts[n ^ bit], parts[n]) for n in range(count)]
    return jnp.concatenate(parts, axis)


def to_spread(value, axis):
    size = lax.axis_size("fsdp")
    value = flip_blocks(value, axis, lax.axis_index("fsdp"), size)
    parts = jnp.split(value, size, axis)
    return jnp.concatenate([parts[place] for place in spread_order(size)], axis)


def from_spread(value, axis):
    size = lax.axis_size("fsdp")
    parts = jnp.split(value, size, axis)
    order = spread_order(size)
    value = jnp.concatenate([parts[order.index(place)] for place in range(size)], axis)
    return flip_blocks(value, axis, lax.axis_index("fsdp"), size)


def my_half(value):
    width = value.shape[-1] // 2
    return jnp.where(lax.axis_index("tp") == 0, value[..., :width], value[..., width:])


def other_half(value):
    width = value.shape[-1] // 2
    return jnp.where(lax.axis_index("tp") == 0, value[..., width:], value[..., :width])


def join_halves(mine, other):
    first = lax.axis_index("tp") == 0
    return jnp.concatenate([jnp.where(first, mine, other), jnp.where(first, other, mine)], -1)


def tp_sum(value):
    return value + swap(value, "tp", 1)


def all_sum(value, axes):
    for axis in axes:
        for bit in bits_down(lax.axis_size(axis)):
            value = value + swap(value, axis, bit)
    return value


def far_first(size):
    return list(range(size // 2, size)) + list(range(size // 2 - 1, -1, -1))


def place_blocks(blocks):
    index = lax.axis_index("ctx")
    rows = blocks[0].shape[0]
    total = jnp.zeros((rows * len(blocks),) + blocks[0].shape[1:], blocks[0].dtype)
    for distance, block in enumerate(blocks):
        total = lax.dynamic_update_slice_in_dim(total, block, (index ^ distance) * rows, 0)
    return total


def block_for(value, distance):
    size = lax.axis_size("ctx")
    rows = value.shape[0] // size
    return lax.dynamic_slice_in_dim(value, (lax.axis_index("ctx") ^ distance) * rows, rows, 0)


def xor_index(index, distance):
    result = index
    bit = 1
    while bit <= distance:
        if distance & bit:
            result = result + bit - 2 * bit * ((index // bit) % 2)
        bit *= 2
    return result


def span(start, size):
    return pl.ds(pl.multiple_of(start * size, 16), size)


def meet(peers):
    barrier = pltpu.get_barrier_semaphore()
    for device in peers:
        pl.semaphore_signal(barrier, inc=1, device_id=device, device_id_type=pl.DeviceIdType.MESH)
    pl.semaphore_wait(barrier, len(peers))


def remote(source, target, sems, index, device):
    return pltpu.make_async_remote_copy(
        src_ref=source,
        dst_ref=target,
        send_sem=sems[0].at[index],
        recv_sem=sems[1].at[index],
        device_id=device,
        device_id_type=pl.DeviceIdType.MESH,
    )


def near_first(size):
    return list(range(1, size))


def mixed_order(size):
    return [distance for distance in spread_order(size) if distance] + [0]


def cuts_of(rows):
    for count in (5, 4, 2):
        if rows % (16 * count) == 0:
            return count
    return 1


def send_out_kernel(size, rows_ref, out_ref, z_land, y_land, z_send, z_recv, y_send, y_recv):
    mine, first = lax.axis_index("ctx"), lax.axis_index("tp") == 0
    other_tp = {"tp": 1 - lax.axis_index("tp")}
    rows, width = z_land.shape[1], z_land.shape[2]
    cuts = cuts_of(rows)
    part = rows // cuts
    at = [xor_index(mine, distance) for distance in range(size)]
    meet([{"ctx": at[distance]} for distance in range(1, size)] + [other_tp])
    order = [(distance, cut) for distance in near_first(size) for cut in range(cuts)]
    own = [(0, cut) for cut in range(cuts)]
    across, beside = {}, {}

    def source(distance, cut):
        start = pl.multiple_of(at[distance] * rows + cut * part, 16)
        return rows_ref.at[pl.ds(start, part)]

    def inside(distance, cut):
        return distance, pl.ds(cut * part, part)

    for distance, cut in order:
        across[distance, cut] = remote(
            source(distance, cut),
            z_land.at[inside(distance, cut)],
            (z_send, z_recv),
            distance * cuts + cut,
            {"ctx": at[distance]},
        )
        across[distance, cut].start()
    for distance, cut in own + order:
        if distance:
            across[distance, cut].wait_recv()
        beside[distance, cut] = remote(
            z_land.at[inside(distance, cut)] if distance else source(0, cut),
            y_land.at[inside(distance, cut)],
            (y_send, y_recv),
            distance * cuts + cut,
            other_tp,
        )
        beside[distance, cut].start()
    for distance, cut in own + order:
        beside[distance, cut].wait_recv()
        held = z_land[inside(distance, cut)] if distance else source(0, cut)[...]
        theirs = y_land[inside(distance, cut)]
        here = pl.ds(pl.multiple_of(at[distance] * rows + cut * part, 16), part)
        out_ref[here, :width] = jnp.where(first, held, theirs)
        out_ref[here, width:] = jnp.where(first, theirs, held)
    for item in order:
        across[item].wait_send()
    for item in own + order:
        beside[item].wait_send()


def send_out(half_rows, number):
    size = lax.axis_size("ctx")
    total, width = half_rows.shape
    land = pltpu.VMEM((size, total // size, width), half_rows.dtype)
    return pl.pallas_call(
        functools.partial(send_out_kernel, size),
        in_specs=[pl.BlockSpec(memory_space=pltpu.VMEM)],
        out_specs=pl.BlockSpec(memory_space=pltpu.VMEM),
        out_shape=jax.ShapeDtypeStruct((total, 2 * width), half_rows.dtype),
        scratch_shapes=[land, land] + [pltpu.SemaphoreType.DMA((size * cuts_of(total // size),))] * 4,
        compiler_params=pltpu.CompilerParams(
            collective_id=number, has_side_effects=True, vmem_limit_bytes=VMEM_BYTES
        ),
        cost_estimate=pl.CostEstimate(flops=0, bytes_accessed=12 * total * width, transcendentals=0),
    )(half_rows)


def send_home_kernel(size, adds, has_extra, cargo_axes, *refs):
    cargoes = len(cargo_axes)
    streams = len(adds)
    parts, refs = refs[:streams], refs[streams:]
    extra_ref, refs = (refs[0], refs[1:]) if has_extra else (None, refs)
    cargo_in, refs = refs[:cargoes], refs[cargoes:]
    outs, refs = refs[:streams], refs[streams:]
    extra_out, refs = (refs[0], refs[1:]) if has_extra else (None, refs)
    cargo_out, refs = refs[:cargoes], refs[cargoes:]
    lands, refs = [refs[7 * n : 7 * n + 7] for n in range(streams)], refs[7 * streams :]
    mine, first = lax.axis_index("ctx"), lax.axis_index("tp") == 0
    place = lax.axis_index("tp")
    other_tp = {"tp": 1 - place}
    at = [xor_index(mine, distance) for distance in range(size)]
    world = lax.axis_size("fsdp")
    spot = lax.axis_index("fsdp")
    along = {"tp": other_tp, "fsdp": {"fsdp": xor_index(spot, world // 2)}, "core": {"fsdp": xor_index(spot, 1)}}
    extra_peers = [along[axis] for axis in ("fsdp", "core") if axis in cargo_axes]
    meet([{"ctx": at[distance]} for distance in range(1, size)] + [other_tp] + extra_peers)
    order = mixed_order(size)
    beside, across, extras = {}, {}, {}
    cargo = [
        remote(cargo_in[n], cargo_out[n], refs[-2:], n, along[axis])
        for n, axis in enumerate(cargo_axes)
    ]
    for copy, axis in zip(cargo, cargo_axes):
        if axis != "tp":
            copy.start()
    if has_extra:
        ey_land, e_ready, ez_land, ey_send, ey_recv, ez_send, ez_recv = refs[:7]
        extra_beside = remote(extra_ref, ey_land, (ey_send, ey_recv), 0, other_tp)
        extra_beside.start()
    turns = []
    for n in range(streams):
        y_land, _, z_land, y_send, y_recv, _, _ = lands[n]
        rows, width = z_land.shape[1], z_land.shape[2]
        cuts = cuts_of(rows)
        part = rows // cuts
        columns = pl.ds(pl.multiple_of((1 - place) * width, 128), width)
        for distance in order:
            for cut in range(cuts):
                inside = distance, pl.ds(cut * part, part)
                here = pl.ds(pl.multiple_of(at[distance] * rows + cut * part, 16), part)
                number = distance * cuts + cut
                beside[n, number] = remote(
                    parts[n].at[here, columns], y_land.at[inside], (y_send, y_recv), number, other_tp
                )
                beside[n, number].start()
                turns.append((n, distance, cut, number, part, width, inside, here))
    for copy, axis in zip(cargo, cargo_axes):
        if axis == "tp":
            copy.start()
    if has_extra:
        extra_beside.wait_recv()
        e_ready[...] = extra_ref[...] + ey_land[...]
        for distance in order:
            if distance:
                extras[distance] = remote(
                    e_ready.at[at[distance]],
                    ez_land.at[distance],
                    (ez_send, ez_recv),
                    distance,
                    {"ctx": at[distance]},
                )
                extras[distance].start()
    for n, distance, cut, number, part, width, inside, here in turns:
        y_land, ready, z_land, _, _, z_send, z_recv = lands[n]
        beside[n, number].wait_recv()
        whole = parts[n][here, :]
        own = jnp.where(first, whole[:, :width], whole[:, width:])
        total = (own.astype(FULL) + y_land[inside].astype(FULL)).astype(LOW)
        if distance:
            ready[inside] = total
            across[n, number] = remote(
                ready.at[inside], z_land.at[inside], (z_send, z_recv), number, {"ctx": at[distance]}
            )
            across[n, number].start()
        elif adds[n]:
            outs[n][inside[1], :] = total.astype(FULL)
        else:
            outs[n][here, :] = total
    for n, distance, cut, number, part, width, inside, here in turns:
        if distance:
            across[n, number].wait_recv()
            if adds[n]:
                outs[n][inside[1], :] += lands[n][2][inside].astype(FULL)
            else:
                outs[n][here, :] = lands[n][2][inside]
    if has_extra:
        extra_out[mine] = e_ready[mine]
        for distance in order:
            if distance:
                extras[distance].wait_recv()
                extra_out[at[distance]] = ez_land[distance]
                extras[distance].wait_send()
        extra_beside.wait_send()
    for copy in list(beside.values()) + list(across.values()):
        copy.wait_send()
    for copy in cargo:
        copy.wait()


def send_home(partial_rows, number, extra=None, cargo=(), add_up=False, more=None):
    size = lax.axis_size("ctx")
    operands = [partial_rows] if more is None else [partial_rows, more]
    adds = (add_up, False)[: len(operands)]
    sems = [pltpu.SemaphoreType.DMA((size,))] * 4
    shapes, scratch, moved = [], [], 0
    for item, added in zip(operands, adds):
        total, width = item.shape[0], item.shape[1] // 2
        rows = total // size
        moved += 12 * total * width
        shapes.append(
            jax.ShapeDtypeStruct((rows, width), FULL) if added else jax.ShapeDtypeStruct((total, width), LOW)
        )
        scratch += [pltpu.VMEM((size, rows, width), LOW)] * 3
        scratch += [pltpu.SemaphoreType.DMA((size * cuts_of(rows),))] * 4
    if extra is not None:
        operands.append(extra)
        shapes.append(jax.ShapeDtypeStruct(extra.shape, FULL))
        scratch += [pltpu.VMEM(extra.shape, FULL)] * 3 + sems
    in_specs = [pl.BlockSpec(memory_space=pltpu.VMEM)] * len(operands)
    out_specs = [pl.BlockSpec(memory_space=pltpu.VMEM)] * len(shapes)
    for item, _ in cargo:
        operands.append(item)
        shapes.append(jax.ShapeDtypeStruct(item.shape, item.dtype))
        in_specs.append(pl.BlockSpec(memory_space=pl.ANY))
        out_specs.append(pl.BlockSpec(memory_space=pl.ANY))
    if cargo:
        scratch += [pltpu.SemaphoreType.DMA((len(cargo),))] * 2
    results = pl.pallas_call(
        functools.partial(send_home_kernel, size, adds, extra is not None, tuple(axis for _, axis in cargo)),
        in_specs=in_specs,
        out_specs=out_specs,
        out_shape=shapes,
        scratch_shapes=scratch,
        compiler_params=pltpu.CompilerParams(
            collective_id=number, has_side_effects=True, vmem_limit_bytes=VMEM_BYTES
        ),
        cost_estimate=pl.CostEstimate(flops=0, bytes_accessed=moved, transcendentals=0),
    )(*operands)
    return results if len(shapes) > 1 else results[0]


def prologue_kernel(sizes, *refs):
    groups, world = sizes
    half_in, own_in, routes_in, kv_in, query_in, out_in, cot_in = refs[:7]
    seq_ref, routes_ref, kv_ref, query_ref, out_ref, cot_ref = refs[7:13]
    local_sem = refs[13]
    pairs = [(refs[14 + 2 * n], refs[15 + 2 * n]) for n in range(16)]
    token_line, route_line, kv_line, token_pass, kv_pass = (pairs[2 * n : 2 * n + 2] for n in range(5))
    kv_own, fr, fk, fq, fo, cot_beside = pairs[10:]
    mine, place, spot = lax.axis_index("ctx"), lax.axis_index("tp"), lax.axis_index("fsdp")
    other_tp = {"tp": 1 - place}
    rows, width = half_in.shape
    sub = kv_in.shape[0]
    piece = sub * groups
    q_rows = query_in.shape[0]
    steps = list(bits_down(world))
    beside = {bit: {"fsdp": xor_index(spot, bit)} for bit in steps}
    first = steps[0]
    meet(
        [{"ctx": xor_index(mine, distance)} for distance in range(1, groups)]
        + [other_tp]
        + [beside[bit] for bit in steps]
    )
    locals_ = [
        pltpu.make_async_copy(
            own_in.at[:, pl.ds(n * width, width)], seq_ref.at[n, span(mine, rows)], local_sem.at[n]
        )
        for n in range(2)
    ] + [
        pltpu.make_async_copy(routes_in, routes_ref.at[0, mine], local_sem.at[2]),
        pltpu.make_async_copy(kv_in, kv_ref.at[span(mine, sub)], local_sem.at[3]),
        pltpu.make_async_copy(query_in, query_ref.at[pl.ds(0, q_rows)], local_sem.at[4]),
        pltpu.make_async_copy(out_in, out_ref.at[0], local_sem.at[5]),
    ]
    started, landed = [], set()

    def go(copy):
        copy.start()
        started.append(copy)
        return copy

    def arrived(copy):
        if id(copy) not in landed:
            copy.wait_recv()
            landed.add(id(copy))

    def wrap(index):
        return lax.rem(index + groups, groups)

    def outgoing(step):
        yield 0, jnp.logical_and(mine < groups - 1, mine >= step), wrap(mine - step), wrap(mine + 1)
        yield 1, jnp.logical_and(mine > 0, mine + step < groups), wrap(mine + step), wrap(mine - 1)

    def incoming(step):
        yield 0, mine >= step + 1, wrap(mine - 1 - step)
        yield 1, mine + step + 1 < groups, wrap(mine + 1 + step)

    def line_copy(own, place_of, sems, step, way, block, target):
        source = place_of(block) if step else own
        return remote(source, place_of(block), sems[way], step, {"ctx": target})

    def line_start(own, place_of, sems, step):
        for way, happens, block, target in outgoing(step):

            @pl.when(happens)
            def _():
                line_copy(own, place_of, sems, step, way, block, target).start()

    def line_wait(place_of, sems, step, passed):
        for way, happens, block in incoming(step):

            @pl.when(happens)
            def _():
                remote(place_of(block), place_of(block), sems[way], step, other_tp).wait_recv()
                if passed is not None:
                    passed(step, way, block).start()

    def line_end(own, place_of, sems, step, passed):
        for way, happens, block, target in outgoing(step):

            @pl.when(happens)
            def _():
                line_copy(own, place_of, sems, step, way, block, target).wait_send()

        if passed is None:
            return
        for way, happens, block in incoming(step):

            @pl.when(happens)
            def _():
                passed(step, way, block).wait_send()

    def passed_wait(step, passed):
        for way, happens, block in incoming(step):

            @pl.when(happens)
            def _():
                passed(step, way, block).wait_recv()

    route_place = lambda n: routes_ref.at[0, n]
    kv_place = lambda n: kv_ref.at[span(n, sub)]
    token_place = lambda n: seq_ref.at[place, span(n, rows)]

    def kv_along(step, way, block):
        target = kv_ref.at[pl.ds(pl.multiple_of(piece + block * sub, 16), sub)]
        return remote(kv_place(block), target, kv_pass[way], step, beside[first])

    def token_along(step, way, block):
        return remote(token_place(block), token_place(block), token_pass[way], step, other_tp)

    def token_landed(step, way, block):
        view = seq_ref.at[1 - place, span(block, rows)]
        return remote(view, view, token_pass[way], step, other_tp)

    kv_first = go(
        remote(
            kv_in,
            kv_ref.at[pl.ds(pl.multiple_of(piece + mine * sub, 16), sub)],
            kv_own,
            0,
            beside[first],
        )
    )
    query_view = lambda n: query_ref.at[pl.ds(n * q_rows, q_rows)]
    out_view = lambda n: out_ref.at[n]
    kv_view = lambda n: kv_ref.at[pl.ds(n * piece, piece)]
    query_copies = {1: go(remote(query_in, query_view(1), fq, 1, beside[first]))}
    out_copies = {}
    go(remote(cot_in, cot_ref, cot_beside, 0, other_tp))
    for copy in locals_:
        copy.start()
    for step in range(groups - 1):
        line_start(kv_in, kv_place, kv_line, step)
        line_start(routes_in, route_place, route_line, step)
        line_start(half_in, token_place, token_line, step)
        if step == 0:
            for copy in locals_:
                copy.wait()
            for bit in steps[1:]:
                n = world // (2 * bit)
                query_copies[n] = go(remote(query_in, query_view(n), fq, n, beside[bit]))
                out_copies[n] = go(remote(out_in, out_view(n), fo, n, beside[bit]))
        line_wait(kv_place, kv_line, step, kv_along)
        if step == groups - 2:
            out_copies[1] = go(remote(out_in, out_view(1), fo, 1, beside[first]))
        line_wait(route_place, route_line, step, None)
        line_wait(token_place, token_line, step, token_along)
    route_wait, kv_wait = {}, {}
    count = 1
    for bit in steps:
        for n in range(count):
            peer = beside[bit]
            if n in route_wait:
                arrived(route_wait[n])
            route_wait[count + n] = go(
                remote(routes_ref.at[n], routes_ref.at[count + n], fr, count + n, peer)
            )
            if bit == first:
                continue
            if n:
                arrived(query_copies[n])
                query_copies[count + n] = go(
                    remote(query_view(n), query_view(count + n), fq, count + n, peer)
                )
            if n == 1 and count == 2:
                arrived(kv_first)
                for step in range(groups - 1):
                    passed_wait(step, kv_along)
            if n > 1:
                arrived(kv_wait[n])
            kv_wait[count + n] = go(remote(kv_view(n), kv_view(count + n), fk, count + n, peer))
            if n:
                arrived(out_copies[n])
                out_copies[count + n] = go(remote(out_view(n), out_view(count + n), fo, count + n, peer))
        count *= 2
    if world == 2:
        arrived(kv_first)
        for step in range(groups - 1):
            passed_wait(step, kv_along)
    for copy in started:
        arrived(copy)
    for step in range(groups - 1):
        passed_wait(step, token_landed)
        line_end(kv_in, kv_place, kv_line, step, kv_along)
        line_end(routes_in, route_place, route_line, step, None)
        line_end(half_in, token_place, token_line, step, token_along)
    for copy in started:
        copy.wait_send()


def prologue(token_half, token_rows, routes, kv_rows, query_piece, out_piece, cot_block, number):
    groups, world = lax.axis_size("ctx"), lax.axis_size("fsdp")
    any_space = pl.BlockSpec(memory_space=pl.ANY)
    rows, features = token_rows.shape
    pair = lambda count: [pltpu.SemaphoreType.DMA((count,))] * 2
    return pl.pallas_call(
        functools.partial(prologue_kernel, (groups, world)),
        in_specs=[pl.BlockSpec(memory_space=pltpu.VMEM)] * 7,
        out_specs=[any_space] * 6,
        out_shape=[
            jax.ShapeDtypeStruct((2, groups * rows, features // 2), LOW),
            jax.ShapeDtypeStruct((world, groups) + routes.shape, jnp.int32),
            jax.ShapeDtypeStruct((world * groups * kv_rows.shape[0], kv_rows.shape[1]), LOW),
            jax.ShapeDtypeStruct((world * query_piece.shape[0], query_piece.shape[1]), LOW),
            jax.ShapeDtypeStruct((world,) + out_piece.shape, LOW),
            jax.ShapeDtypeStruct(cot_block.shape, LOW),
        ],
        scratch_shapes=[pltpu.SemaphoreType.DMA((6,))]
        + pair(groups) * 10
        + pair(1)
        + pair(world) * 4
        + pair(1),
        compiler_params=pltpu.CompilerParams(
            collective_id=number, has_side_effects=True, vmem_limit_bytes=VMEM_BYTES
        ),
        cost_estimate=pl.CostEstimate(flops=0, bytes_accessed=100000000, transcendentals=0),
    )(token_half, token_rows, routes, kv_rows, query_piece, out_piece, cot_block)


def expert_forward_kernel(world, size, *refs):
    rows_ref = refs[0]
    gates, ups = refs[1 : 1 + world], refs[1 + world : 1 + 2 * world]
    refs = refs[1 + 2 * world :]
    blocks, beside_ref, refs = refs[:size], refs[size], refs[size + 1 :]
    hidden_ref, by_gate_ref, by_up_ref, cot_ref, y_land, y_send, y_recv = refs
    width = rows_ref.shape[1] // world
    mine, place = lax.axis_index("ctx"), lax.axis_index("tp")
    other_tp = {"tp": 1 - place}
    beside = [
        remote(blocks[distance], y_land.at[distance], (y_send, y_recv), distance, other_tp)
        for distance in range(1, size)
    ]

    @pl.when(pl.program_id(0) == 0)
    def _():
        meet([other_tp])
        for copy in beside:
            copy.start()

    gate_lin, up_lin = None, None
    for n in range(world):
        columns = slice(n * width, (n + 1) * width)
        gate_term = matmul(rows_ref[:, columns], gates[n][...])
        up_term = matmul(rows_ref[:, columns], ups[n][...])
        gate_lin = gate_lin + gate_term if n else gate_term
        up_lin = up_lin + up_term if n else up_term
    sigmoid_gate = 1.0 / (1.0 + jnp.exp(-gate_lin))
    swish = gate_lin * sigmoid_gate
    hidden_ref[...] = (swish * up_lin).astype(LOW)
    by_gate_ref[...] = (up_lin * sigmoid_gate * (1.0 + gate_lin * (1.0 - sigmoid_gate))).astype(LOW)
    by_up_ref[...] = swish.astype(LOW)

    @pl.when(pl.program_id(0) == pl.num_programs(0) - 1)
    def _():
        rows, half = y_land.shape[1], y_land.shape[2]
        for distance in range(size):
            if distance:
                beside[distance - 1].wait_recv()
            own = blocks[distance][...]
            theirs = y_land[distance] if distance else beside_ref[...]
            here = span(xor_index(mine, distance), rows)
            cot_ref[here, :half] = jnp.where(place == 0, own, theirs)
            cot_ref[here, half:] = jnp.where(place == 0, theirs, own)
        for copy in beside:
            copy.wait_send()


def expert_forward(rows, gate_pieces, up_pieces, cot_blocks, cot_beside, number):
    world, size = len(gate_pieces), len(cot_blocks)
    slots, features = rows.shape
    depth, hidden_width = gate_pieces[0].shape
    tall = pl.BlockSpec((depth, TILE), lambda i: (0, i))
    strip = pl.BlockSpec((slots, TILE), lambda i: (0, i))
    whole = lambda value: pl.BlockSpec(value.shape, lambda i: (0, 0), pipeline_mode=pl.Buffered(1))
    return pl.pallas_call(
        functools.partial(expert_forward_kernel, world, size),
        grid=(hidden_width // TILE,),
        in_specs=[whole(rows)] + [tall] * (2 * world) + [whole(block) for block in cot_blocks] + [whole(cot_beside)],
        out_specs=[strip] * 3 + [pl.BlockSpec((slots, features), lambda i: (0, 0))],
        out_shape=[jax.ShapeDtypeStruct((slots, hidden_width), LOW)] * 3
        + [jax.ShapeDtypeStruct((slots, features), LOW)],
        scratch_shapes=[pltpu.VMEM((size,) + cot_blocks[0].shape, LOW)]
        + [pltpu.SemaphoreType.DMA((size,))] * 2,
        compiler_params=pltpu.CompilerParams(
            collective_id=number, has_side_effects=True, vmem_limit_bytes=VMEM_BYTES
        ),
        cost_estimate=pl.CostEstimate(flops=0, bytes_accessed=2 * slots * features, transcendentals=0),
    )(rows, *gate_pieces, *up_pieces, *cot_blocks, cot_beside)


def product_kernel(world, tiles, hidden_ref, *refs):
    downs, out_ref = refs[:world], refs[world]
    for n in range(world):

        @pl.when(pl.program_id(0) // tiles == n)
        def _():
            out_ref[...] = matmul(hidden_ref[...], downs[n][...]).astype(LOW)


def expert_product(hidden, down_pieces):
    world = len(down_pieces)
    depth, width = down_pieces[0].shape
    tiles = max(width // TILE, 1)
    tile = width // tiles

    def piece_spec(n):
        return pl.BlockSpec((depth, tile), lambda i: (0, jnp.clip(i - n * tiles, 0, tiles - 1)))

    return pl.pallas_call(
        functools.partial(product_kernel, world, tiles),
        grid=(world * tiles,),
        in_specs=[pl.BlockSpec(hidden.shape, lambda i: (0, 0), pipeline_mode=pl.Buffered(1))]
        + [piece_spec(n) for n in range(world)],
        out_specs=pl.BlockSpec((hidden.shape[0], tile), lambda i: (0, i)),
        out_shape=jax.ShapeDtypeStruct((hidden.shape[0], world * width), LOW),
        compiler_params=pltpu.CompilerParams(vmem_limit_bytes=VMEM_BYTES),
        cost_estimate=pl.CostEstimate(
            flops=2 * hidden.shape[0] * depth * world * width,
            bytes_accessed=2 * depth * world * width,
            transcendentals=0,
        ),
    )(hidden, *down_pieces)


def expert_back_kernel(world, steps, size, *refs):
    rows_ref, cot_ref, mix_ref, hidden_ref, by_gate_ref, by_up_ref = refs[:6]
    gates, ups, downs = (refs[6 + n * world : 6 + (n + 1) * world] for n in range(3))
    refs = refs[6 + 3 * world :]
    part_ref, refs = (refs[0], refs[1:]) if size else (None, refs)
    near_ref, landed_ref, db_ref, mix_grad_ref = refs[:4]
    home_ref, refs = (refs[4], refs[5:]) if size else (None, refs[4:])
    db_sum, rows_t_ref, cot_t_ref, far, send_sem, recv_sem = refs[:6]
    step = pl.program_id(0)
    slot = lax.rem(step, 2)
    features = rows_ref.shape[1]
    width = features // world
    half = features // 2
    tile = near_ref.shape[3]
    other_core = {"fsdp": xor_index(lax.axis_index("fsdp"), 1)}
    peers = [other_core]
    if size:
        y_land, ready, z_land, y_send, y_recv, z_send, z_recv = refs[6:]
        mine, place = lax.axis_index("ctx"), lax.axis_index("tp")
        other_tp = {"tp": 1 - place}
        at = [xor_index(mine, distance) for distance in range(size)]
        peers = peers + [other_tp] + [{"ctx": at[distance]} for distance in range(1, size)]
        home_rows, home_width = z_land.shape[1], z_land.shape[2]
        away = pl.ds(pl.multiple_of((1 - place) * home_width, 128), home_width)
        order = mixed_order(size)

        def beside(distance):
            return remote(
                part_ref.at[span(at[distance], home_rows), away],
                y_land.at[distance],
                (y_send, y_recv),
                distance,
                other_tp,
            )

        def across(distance):
            return remote(
                ready.at[distance],
                z_land.at[distance],
                (z_send, z_recv),
                distance,
                {"ctx": at[distance]},
            )

    def far_copy(at_step, at_slot):
        return pltpu.make_async_remote_copy(
            src_ref=far.at[at_slot],
            dst_ref=landed_ref.at[at_step],
            send_sem=send_sem.at[at_slot],
            recv_sem=recv_sem.at[at_step],
            device_id=other_core,
            device_id_type=pl.DeviceIdType.MESH,
        )

    @pl.when(step == 0)
    def _():
        meet(peers)
        if size:
            for distance in order:
                beside(distance).start()
        db_sum[...] = jnp.zeros_like(db_sum)
        mix_grad_ref[...] = jnp.zeros_like(mix_grad_ref)
        for place_at in range(0, features, tile):
            rows_t_ref[place_at : place_at + tile, :] = rows_ref[:, place_at : place_at + tile].T
            cot_t_ref[place_at : place_at + tile, :] = cot_ref[:, place_at : place_at + tile].T

    d_hidden = None
    for n in range(world):
        columns = slice(n * width, (n + 1) * width)
        term = matmul_nt(cot_ref[:, columns], downs[n][...])
        d_hidden = d_hidden + term if n else term
    hidden = hidden_ref[...].astype(FULL)
    mix_grad = hidden * d_hidden
    for place_at in range(0, tile, HEAD):
        mix_grad_ref[...] += mix_grad[:, place_at : place_at + HEAD]
    mix = jnp.concatenate([mix_ref[...]] * (tile // HEAD), axis=1)
    d_gated = d_hidden * mix
    mixed_low = (hidden * mix).astype(LOW)
    d_gate = (d_gated * by_gate_ref[...].astype(FULL)).astype(LOW)
    d_up = (d_gated * by_up_ref[...].astype(FULL)).astype(LOW)
    @pl.when(step >= 2)
    def _():
        far_copy(step - 2, slot).wait_send()

    pairs = ((rows_t_ref, d_gate), (rows_t_ref, d_up), (cot_t_ref, mixed_low))
    for n, (left, right) in enumerate(pairs):
        far[slot, n] = matmul(left[half:, :], right).astype(LOW)
    far_copy(step, slot).start()
    for n in range(world):
        columns = slice(n * width, (n + 1) * width)
        db_sum[:, columns] += matmul_nt(d_gate, gates[n][...]) + matmul_nt(d_up, ups[n][...])

    for n, (left, right) in enumerate(pairs):
        near_ref[0, n] = matmul(left[:half, :], right).astype(LOW)

    if size:
        for turn, distance in enumerate(order):

            @pl.when(step == min(turn + 1, steps - 1))
            def _():
                beside(distance).wait_recv()
                whole = part_ref[span(at[distance], home_rows), :]
                own = jnp.where(place == 0, whole[:, :home_width], whole[:, home_width:])
                total = (own.astype(FULL) + y_land[distance].astype(FULL)).astype(LOW)
                if distance:
                    ready[distance] = total
                    across(distance).start()
                else:
                    home_ref[span(mine, home_rows), :] = total

    @pl.when(step == steps - 1)
    def _():
        db_ref[...] = db_sum[...].astype(LOW)
        for last in range(max(steps - 2, 0), steps):
            far_copy(last, last % 2).wait_send()
        for last in range(steps):
            far_copy(last, last % 2).wait_recv()
        if size:
            for distance in order:
                beside(distance).wait_send()
                if distance:
                    across(distance).wait_recv()
                    home_ref[span(at[distance], home_rows), :] = z_land[distance]
                    across(distance).wait_send()


def expert_back(rows, cot_rows, mix_rows, forward, pieces, first, steps, number, going_home=None):
    gate_pieces, up_pieces, down_pieces = pieces
    world = len(gate_pieces)
    slots, features = rows.shape
    depth = gate_pieces[0].shape[0]
    tile = TILE
    once = pl.Buffered(1)
    whole = lambda value: pl.BlockSpec(value.shape, lambda i: (0, 0), pipeline_mode=once)
    kept = lambda width: pl.BlockSpec((slots, width), lambda i: (0, 0))
    tall = pl.BlockSpec((depth, tile), lambda i: (0, i + first))
    flat = pl.BlockSpec((tile, depth), lambda i: (i + first, 0))
    strip = pl.BlockSpec((slots, tile), lambda i: (0, i + first))
    low = lambda *shape: jax.ShapeDtypeStruct(shape, LOW)
    grads = low(steps, 3, features // 2, tile)
    operands = [rows, cot_rows, mix_rows, *forward, *gate_pieces, *up_pieces, *down_pieces]
    in_specs = [whole(rows), whole(cot_rows), whole(mix_rows)] + [strip] * 3
    in_specs += [tall] * (2 * world) + [flat] * world
    out_specs = [
        pl.BlockSpec((1, 3, features // 2, tile), lambda i: (i, 0, 0, 0)),
        pl.BlockSpec(memory_space=pl.ANY),
        kept(features),
        kept(HEAD),
    ]
    out_shape = [grads, grads, low(slots, features), jax.ShapeDtypeStruct((slots, HEAD), FULL)]
    scratch = [
        pltpu.VMEM((slots, features), FULL),
        pltpu.VMEM((features, slots), LOW),
        pltpu.VMEM((features, slots), LOW),
        pltpu.VMEM((2, 3, features // 2, tile), LOW),
        pltpu.SemaphoreType.DMA((2,)),
        pltpu.SemaphoreType.DMA((steps,)),
    ]
    size = 0
    if going_home is not None:
        size = lax.axis_size("ctx")
        operands.append(going_home)
        in_specs.append(whole(going_home))
        out_specs.append(kept(features // 2))
        out_shape.append(low(slots, features // 2))
        scratch += [pltpu.VMEM((size, slots // size, features // 2), LOW)] * 3
        scratch += [pltpu.SemaphoreType.DMA((size,))] * 4
    return pl.pallas_call(
        functools.partial(expert_back_kernel, world, steps, size),
        grid=(steps,),
        in_specs=in_specs,
        out_specs=out_specs,
        out_shape=out_shape,
        scratch_shapes=scratch,
        compiler_params=pltpu.CompilerParams(
            collective_id=number, has_side_effects=True, vmem_limit_bytes=VMEM_BYTES
        ),
        cost_estimate=pl.CostEstimate(
            flops=0, bytes_accessed=2 * slots * features, transcendentals=0
        ),
    )(*operands)


def scatter_rest(near, landed):
    pieces = lax.axis_size("fsdp")
    arrived, high, bit = [near, landed], near.shape[2], 2
    while True:
        total = arrived[0][:, :, high // 2 : high].astype(FULL)
        for block in arrived[1:]:
            total = total + block[:, :, high // 2 : high].astype(FULL)
        sent = total.astype(LOW)
        high //= 2
        if 2 * bit >= pieces:
            return sent, arrived
        arrived.append(swap(sent, "fsdp", bit))
        bit *= 2


def finish_kernel(count, steps_one, *refs):
    ones, twos = refs[:count], refs[count : 2 * count]
    outs = refs[2 * count :]

    def add_up(parts):
        for n, out in enumerate(outs):
            total = parts[0][0, n].astype(FULL)
            for part in parts[1:]:
                total = total + part[0, n].astype(FULL)
            out[...] = total.T if n == 2 else total

    @pl.when(pl.program_id(0) < steps_one)
    def _():
        add_up(ones)

    @pl.when(pl.program_id(0) >= steps_one)
    def _():
        add_up(twos)


def finish_experts(ones, twos):
    steps_one, steps_two = ones[0].shape[0], twos[0].shape[0]
    depth, tile = ones[-1].shape[2:]
    width = (steps_one + steps_two) * tile
    block = (1, 3, depth, tile)
    first = pl.BlockSpec(block, lambda i: (jnp.minimum(i, steps_one - 1), 0, 0, 0))
    second = pl.BlockSpec(block, lambda i: (jnp.maximum(i - steps_one, 0), 0, 0, 0))
    tall = pl.BlockSpec((depth, tile), lambda i: (0, i))
    return pl.pallas_call(
        functools.partial(finish_kernel, len(ones), steps_one),
        grid=(steps_one + steps_two,),
        in_specs=[first] * len(ones) + [second] * len(twos),
        out_specs=[tall, tall, pl.BlockSpec((tile, depth), lambda i: (i, 0))],
        out_shape=[jax.ShapeDtypeStruct((depth, width), FULL)] * 2
        + [jax.ShapeDtypeStruct((width, depth), FULL)],
        compiler_params=pltpu.CompilerParams(vmem_limit_bytes=VMEM_BYTES),
        cost_estimate=pl.CostEstimate(
            flops=0, bytes_accessed=30 * width * depth, transcendentals=0
        ),
    )(*ones, *twos)


def scatter_start(product, features, first_dim):
    pieces = lax.axis_size("fsdp")
    high, bit, arrived = features, 1, []

    def part(low, high):
        total = product(low, high)
        for block in arrived:
            total = total + lax.slice_in_dim(block, low, high, axis=first_dim).astype(FULL)
        return total

    while True:
        sent = part(high // 2, high).astype(LOW)
        high //= 2
        if 2 * bit >= pieces:
            break
        arrived.append(swap(sent, "fsdp", bit))
        bit *= 2

    def finish(last):
        arrived.append(last)
        return part(0, high)

    return sent, finish


def last_step(sent):
    return swap(sent, "fsdp", lax.axis_size("fsdp") // 2)


def turn_tables(length):
    half_head = HEAD // 2
    steps = np.arange(half_head, dtype=np.float32) * np.float32(2.0 / HEAD)
    frequency = np.power(np.float32(ROPE_BASE), -steps).astype(np.float32)
    angles = np.arange(length, dtype=np.float32)[:, None] * frequency[None, :]
    cosine = np.cos(angles.astype(np.float64)).astype(np.float32)
    sine = np.sin(angles.astype(np.float64)).astype(np.float32)
    return np.concatenate([cosine, cosine, -sine, sine], axis=1)


def turn(value, table):
    return value * table[:, :HEAD] + pltpu.roll(value, HEAD // 2, 1) * table[:, HEAD:]


def turn_back(value, table):
    return value * table[:, :HEAD] - pltpu.roll(value, HEAD // 2, 1) * table[:, HEAD:]


def attend_kernel(
    groups, scale, q_lin, k_lin, v_lin, q_table, k_table, q_low, k_low, v_low, heads, log_sum
):
    q_low[...] = turn(q_lin[...], q_table[...]).astype(LOW)
    k_low[...] = turn(k_lin[...], k_table[...]).astype(LOW)
    v_low[...] = v_lin[...].astype(LOW)
    rows = q_low.shape[0] // groups
    block = k_low.shape[0] // groups
    for group in range(groups):
        span = slice(group * rows, (group + 1) * rows)
        seen = slice(0, (group + 1) * block)
        scores = matmul_nt(q_low[span, :], k_low[seen, :]) * scale
        top = jnp.max(scores, axis=1, keepdims=True)
        weights = jnp.exp(scores - top)
        total = jnp.sum(weights, axis=1, keepdims=True)
        weights = (weights * (1.0 / total)).astype(LOW)
        heads[span, :] = matmul(weights, v_low[seen, :]).astype(LOW)
        log_sum[span, :] = jnp.broadcast_to(top + jnp.log(total), (rows, HEAD))


def attend(query_lin, kv_lin, query_table, key_table, groups):
    slots, width = query_lin.shape
    length = kv_lin.shape[0]
    count = width // HEAD
    by_head = lambda rows: pl.BlockSpec((rows, HEAD), lambda h: (0, h))
    whole = lambda rows: pl.BlockSpec((rows, 2 * HEAD), lambda h: (0, 0))
    return pl.pallas_call(
        functools.partial(attend_kernel, groups, 1.0 / math.sqrt(HEAD)),
        grid=(count,),
        in_specs=[
            by_head(slots),
            by_head(length),
            pl.BlockSpec((length, HEAD), lambda h: (0, h + count)),
            whole(slots),
            whole(length),
        ],
        out_specs=[by_head(slots), by_head(length), by_head(length), by_head(slots), by_head(slots)],
        out_shape=[
            jax.ShapeDtypeStruct((slots, width), LOW),
            jax.ShapeDtypeStruct((length, width), LOW),
            jax.ShapeDtypeStruct((length, width), LOW),
            jax.ShapeDtypeStruct((slots, width), LOW),
            jax.ShapeDtypeStruct((slots, width), FULL),
        ],
        compiler_params=pltpu.CompilerParams(vmem_limit_bytes=VMEM_BYTES),
        cost_estimate=pl.CostEstimate(
            flops=0, bytes_accessed=20 * length * width, transcendentals=0
        ),
    )(query_lin, kv_lin, kv_lin, query_table, key_table)


def attend_back_kernel(
    groups, scale, q_low, k_low, v_low, d_heads, log_sum, q_table, k_table, dq, dk, dv, dk_sum, dv_sum
):
    dk_sum[...] = jnp.zeros_like(dk_sum)
    dv_sum[...] = jnp.zeros_like(dv_sum)
    rows = q_low.shape[0] // groups
    block = k_low.shape[0] // groups
    for group in range(groups):
        span = slice(group * rows, (group + 1) * rows)
        seen = slice(0, (group + 1) * block)
        query, keys = q_low[span, :], k_low[seen, :]
        grads = d_heads[span, :]
        scores = matmul_nt(query, keys) * scale
        weights = jnp.exp(scores - log_sum[span, :1])
        d_weights = matmul_nt(grads, v_low[seen, :])
        delta = jnp.sum(weights * d_weights, axis=1, keepdims=True)
        d_scores = (weights * (d_weights - delta)).astype(LOW)
        dq[span, :] = turn_back(matmul(d_scores, keys) * scale, q_table[span, :]).astype(LOW)
        dk_sum[seen, :] += matmul_tn(d_scores, query) * scale
        dv_sum[seen, :] += matmul_tn(weights.astype(LOW), grads)
    dk[...] = turn_back(dk_sum[...], k_table[...]).astype(LOW)
    dv[...] = dv_sum[...].astype(LOW)


def attend_back(q_low, k_low, v_low, d_heads, log_sum, query_table, key_table, groups):
    slots, width = q_low.shape
    length = k_low.shape[0]
    count = width // HEAD
    by_head = lambda rows: pl.BlockSpec((rows, HEAD), lambda h: (0, h))
    whole = lambda rows: pl.BlockSpec((rows, 2 * HEAD), lambda h: (0, 0))
    return pl.pallas_call(
        functools.partial(attend_back_kernel, groups, 1.0 / math.sqrt(HEAD)),
        grid=(count,),
        in_specs=[
            by_head(slots),
            by_head(length),
            by_head(length),
            by_head(slots),
            by_head(slots),
            whole(slots),
            whole(length),
        ],
        out_specs=[by_head(slots), by_head(length), by_head(length)],
        out_shape=[
            jax.ShapeDtypeStruct((slots, width), LOW),
            jax.ShapeDtypeStruct((length, width), LOW),
            jax.ShapeDtypeStruct((length, width), LOW),
        ],
        scratch_shapes=[pltpu.VMEM((length, HEAD), FULL), pltpu.VMEM((length, HEAD), FULL)],
        compiler_params=pltpu.CompilerParams(vmem_limit_bytes=VMEM_BYTES),
        cost_estimate=pl.CostEstimate(
            flops=0, bytes_accessed=14 * length * width, transcendentals=0
        ),
    )(q_low, k_low, v_low, d_heads, log_sum, query_table, key_table)


def chosen_picks(routes, expert_count, capacity):
    experts = jnp.arange(expert_count, dtype=jnp.int32)
    onehot = (routes[:, :, None] == experts[None, None, :]).astype(jnp.int32)
    rows = routes.shape[0]
    below = (jnp.arange(rows)[:, None] > jnp.arange(rows)[None, :]).astype(LOW)
    order = matmul(below, jnp.sum(onehot, axis=1).astype(LOW)).astype(jnp.int32)
    slot = routes * capacity + jnp.sum(onehot * order[:, None, :], axis=2)
    slots = jnp.arange(expert_count * capacity, dtype=jnp.int32)
    picks = [(slot[:, k : k + 1] == slots[None, :]).astype(LOW) for k in range(routes.shape[1])]
    return picks, onehot.astype(FULL)


def expert_picks(routes_seq, expert, capacity):
    named = jnp.any(routes_seq == expert, axis=1)
    rows = named.shape[1]
    above = (jnp.arange(rows)[:, None] < jnp.arange(rows)[None, :]).astype(LOW)
    order = matmul(named.astype(LOW), above).astype(jnp.int32)
    slot = jnp.where(named, order, -1)
    return (slot[:, None, :] == jnp.arange(capacity, dtype=jnp.int32)[None, :, None]).astype(LOW)


def mix_of(logits, onehot):
    chosen = jnp.sum(onehot * logits[:, None, :], axis=2)
    return jax.nn.softmax(chosen, axis=1)


def logits_back(mix, mix_grad, probs, onehot, share_grad):
    d_chosen = mix * (mix_grad - jnp.sum(mix * mix_grad, axis=1, keepdims=True))
    d_logits = jnp.sum(onehot * d_chosen[:, :, None], axis=1)
    inner = jnp.sum(probs * share_grad[None, :], axis=1, keepdims=True)
    return d_logits + probs * (share_grad[None, :] - inner)


def through_router(d_logits, router_half):
    total = d_logits[:, 0:1] * router_half[:, 0][None, :]
    for expert in range(1, d_logits.shape[1]):
        total = total + d_logits[:, expert : expert + 1] * router_half[:, expert][None, :]
    return total


def on_device(
    tokens,
    cotangent,
    attn_routes,
    ffn_routes,
    norm_gain1,
    norm_gain2,
    attn_router,
    ffn_router,
    key_proj,
    value_proj,
    query_proj,
    out_proj,
    gate_proj,
    up_proj,
    down_proj,
):
    rows_here, features = tokens.shape
    half_width = features // 2
    picks_each = attn_routes.shape[1]
    expert_count = attn_router.shape[1]
    groups = lax.axis_size("ctx")
    mine = lax.axis_index("ctx")
    capacity = rows_here * picks_each // expert_count * 5 // 4
    slots = groups * capacity
    all_tokens = rows_here * lax.axis_size("fsdp") * groups

    attn_picks, attn_onehot = chosen_picks(attn_routes, expert_count, capacity)
    ffn_picks, ffn_onehot = chosen_picks(ffn_routes, expert_count, capacity)
    ffn_pick = ffn_picks[0]
    for pick in ffn_picks[1:]:
        ffn_pick = ffn_pick + pick
    cot_half = my_half(to_spread(cotangent, 1))
    cot_slots = matmul_tn(ffn_pick, cot_half).astype(LOW)

    tokens_spread = to_spread(tokens, 1)
    token_half = my_half(tokens_spread)
    routes_mine = jnp.concatenate([attn_routes.T, ffn_routes.T], axis=0)
    routes_mine = jnp.concatenate([routes_mine, jnp.zeros_like(routes_mine)], axis=0)
    kv_mine = jnp.concatenate([key_proj, value_proj], axis=1)
    seq_low, all_routes, kv_full, query_full, out_pieces, cot_beside = prologue(
        token_half,
        tokens_spread,
        routes_mine,
        kv_mine,
        query_proj[0],
        out_proj[0],
        block_for(cot_slots, 0),
        0,
    )
    seq_routes = all_routes[0]
    seq_tokens = jnp.concatenate([seq_low[0], seq_low[1]], axis=1).astype(FULL)
    out_full = jnp.concatenate([out_pieces[n] for n in range(lax.axis_size("fsdp"))], axis=1)

    gate_pieces = gather_pieces(after(gate_proj[0], all_routes))
    up_pieces = gather_pieces(after(up_proj[0], all_routes))
    down_pieces = gather_pieces(after(down_proj[0], all_routes))

    gain1 = to_spread(norm_gain1, 0)
    gain2_half = my_half(to_spread(norm_gain2, 0))
    router1 = to_spread(attn_router, 0)
    router2 = to_spread(ffn_router, 0)
    router1_half = my_half(router1.T).T.astype(FULL)
    router2_half = my_half(router2.T).T

    scale_seq = lax.rsqrt(jnp.mean(seq_tokens * seq_tokens, axis=1, keepdims=True) + EPSILON)
    a_seq = (seq_tokens * scale_seq * gain1).astype(LOW)
    a_mine = lax.dynamic_slice_in_dim(a_seq, mine * rows_here, rows_here, 0)
    scale_one = lax.dynamic_slice_in_dim(scale_seq, mine * rows_here, rows_here, 0)
    attn_logits = matmul(a_mine, router1)
    attn_probs = jax.nn.softmax(attn_logits, axis=1)
    attn_mix = mix_of(attn_logits, attn_onehot)

    later = after(cot_slots, all_routes)
    cot_blocks = [block_for(later, distance) for distance in range(groups)]
    cot_blocks[1:] = [swap(cot_blocks[distance], "ctx", distance) for distance in range(1, groups)]

    expert_onehot = expert_picks(seq_routes[:, :picks_each], mine, capacity)
    key_table = jnp.asarray(turn_tables(groups * rows_here))
    query_table = jnp.einsum(
        "bsr,brh->bsh",
        expert_onehot.astype(FULL),
        key_table.reshape(groups, rows_here, -1),
        precision=PRECISE,
    ).reshape(slots, -1)
    rows_in = (
        jnp.einsum(
            "bsr,brd->bsd",
            expert_onehot,
            a_seq.reshape(groups, rows_here, features),
            preferred_element_type=FULL,
        )
        .astype(LOW)
        .reshape(slots, features)
    )
    query_lin = matmul(rows_in, query_full)
    kv_lin = matmul(a_seq, kv_full)
    q_low, k_low, v_low, heads_low, log_sum = attend(
        query_lin, kv_lin, query_table, key_table, groups
    )
    cargo = [(item, "core") for item in gate_pieces + [up_proj[0], down_proj[0]]]
    attn_back, *known = send_home(
        after(matmul(heads_low, out_full).astype(LOW), *cot_blocks[1:]), 1, cargo=cargo
    )
    gate_known, up_known, down_known = known[:-2], known[-2:-1], known[-1:]

    input_half = my_half(tokens_spread).astype(FULL)
    attn_picked = [matmul(pick, attn_back) for pick in attn_picks]
    attended = input_half
    for k in range(picks_each):
        attended = attended + attn_mix[:, k : k + 1] * attn_picked[k]
    square_sum = tp_sum(jnp.sum(attended * attended, axis=1, keepdims=True))
    scale_two = lax.rsqrt(square_sum / features + EPSILON)
    b_half = (attended * scale_two * gain2_half).astype(LOW)
    gate_all = with_neighbours(gate_pieces, gate_known)
    b_slots = matmul_tn(ffn_pick, b_half).astype(LOW)
    up_all = with_neighbours(up_pieces, up_known, b_slots)
    ffn_rows = send_out(after(b_slots, up_all[-1]), 2)
    ffn_logits = tp_sum(matmul(b_half, router2_half))
    ffn_probs = jax.nn.softmax(ffn_logits, axis=1)
    ffn_mix = mix_of(ffn_logits, ffn_onehot)

    ffn_seq_routes = seq_routes[:, picks_each : 2 * picks_each]
    ffn_expert_onehot = expert_picks(ffn_seq_routes, mine, capacity).astype(FULL)
    row_routes = jnp.einsum(
        "bsr,bkr->bsk", ffn_expert_onehot, ffn_seq_routes.astype(FULL), precision=PRECISE
    ).reshape(slots, picks_each)
    row_onehot = row_routes[:, :, None] == jnp.arange(expert_count, dtype=FULL)[None, None, :]
    row_mix = mix_of(matmul(ffn_rows, router2), row_onehot.astype(FULL))
    mine_too = (row_routes == mine.astype(FULL)).astype(FULL)
    mix_rows = jnp.broadcast_to(jnp.sum(row_mix * mine_too, axis=1, keepdims=True), (slots, HEAD))
    *forward, cot_rows = expert_forward(ffn_rows, gate_all, up_all, cot_blocks, cot_beside, 6)
    down_all = with_neighbours(down_pieces, down_known, forward[0])
    ffn_out = expert_product(forward[0], down_all)
    pieces = (gate_all, up_all, down_all)
    tiles = gate_proj.shape[2] // TILE
    count_one = (tiles + 1) // 2
    near_one, landed_one, db_one, mix_grad_one, ffn_back = expert_back(
        ffn_rows, cot_rows, mix_rows, forward, pieces, 0, count_one, 7, going_home=ffn_out
    )
    sent_one, parts_one = scatter_rest(near_one, landed_one)
    back_one = last_step(sent_one)
    near_two, landed_two, db_two, mix_grad_two = expert_back(
        after(ffn_rows, sent_one), cot_rows, mix_rows, forward, pieces, count_one, tiles - count_one, 8
    )
    sent_two, parts_two = scatter_rest(near_two, landed_two)
    back_two = last_step(sent_two)
    db_rows = (db_one.astype(FULL) + db_two.astype(FULL)).astype(LOW)
    mix_grad_rows = jnp.pad(
        jnp.sum(mix_grad_one + mix_grad_two, axis=1).reshape(groups, 1, capacity),
        ((0, 0), (0, 7), (0, 256 - capacity)),
    )
    db_back, mix_grad_back = send_home(after(db_rows, sent_two), 3, extra=mix_grad_rows)
    db_back = after(db_back, back_one)
    mix_grad_back = mix_grad_back[:, 0, :capacity].reshape(1, slots)

    experts = jnp.arange(expert_count, dtype=jnp.int32)
    named = (all_routes[..., None] == experts).astype(FULL)
    hits = jnp.stack(
        [
            jnp.sum(named[:, :, :picks_each], axis=(0, 1, 2, 3)),
            jnp.sum(named[:, :, picks_each : 2 * picks_each], axis=(0, 1, 2, 3)),
        ]
    )
    share = hits / (all_tokens * picks_each)
    share_grad = AUX_WEIGHT * expert_count / all_tokens * share
    grad_half = cot_half.astype(FULL)
    d_normed2 = jnp.zeros((rows_here, half_width), FULL)
    ffn_mix_grad = []
    for pick in ffn_picks:
        d_normed2 = d_normed2 + matmul(pick, db_back)
        ffn_mix_grad.append(jnp.sum(pick.astype(FULL) * mix_grad_back, axis=1, keepdims=True))
    ffn_mix_grad = jnp.concatenate(ffn_mix_grad, axis=1)
    ffn_d_logits = logits_back(ffn_mix, ffn_mix_grad, ffn_probs, ffn_onehot, share_grad[1])
    d_normed2 = d_normed2 + through_router(ffn_d_logits, router2_half.astype(FULL))
    weighted2 = d_normed2 * gain2_half
    inner2 = tp_sum(jnp.sum(weighted2 * attended, axis=1, keepdims=True)) / features
    d_attended = grad_half + scale_two * weighted2 - attended * scale_two**3 * inner2
    gain2_part = jnp.sum(d_normed2 * attended * scale_two, axis=0)
    ffn_router_part = precise_tn(b_half.astype(FULL), ffn_d_logits)

    dy_slots = jnp.zeros((slots, half_width), FULL)
    for k in range(picks_each):
        dy_slots = dy_slots + matmul_tn(attn_picks[k], (attn_mix[:, k : k + 1] * d_attended).astype(LOW))
    dy_rows = send_out(dy_slots.astype(LOW), 4)
    out_sent, out_finish = scatter_start(
        lambda low, high: matmul_tn(heads_low, dy_rows[:, low:high]), features, 1
    )
    out_back = last_step(out_sent)
    d_heads = after(matmul_nt(dy_rows, out_full).astype(LOW), out_sent)
    dq_low, dk_low, dv_low = attend_back(
        q_low, k_low, v_low, d_heads, log_sum, query_table, key_table, groups
    )
    dkv_low = after(jnp.concatenate([dk_low, dv_low], axis=1), back_two)
    da_rows = matmul_nt(dq_low, query_full).astype(LOW).reshape(groups, capacity, features)
    da_seq = jnp.einsum("bsr,bsd->brd", expert_onehot, da_rows, preferred_element_type=FULL)
    da_seq = da_seq.reshape(groups * rows_here, features) + matmul_nt(dkv_low, kv_full)
    kv_sent, kv_finish = scatter_start(
        lambda low, high: matmul_tn(a_seq[:, low:high], dkv_low), features, 0
    )
    result = attended
    for k in range(picks_each):
        result = result + ffn_mix[:, k : k + 1] * matmul(ffn_picks[k], ffn_back)
    result_low = result.astype(LOW)
    da_half, kv_back, result_other = send_home(
        after(da_seq.astype(LOW), out_back),
        5,
        cargo=((kv_sent, "fsdp"), (result_low, "tp")),
        add_up=True,
    )
    output = from_spread(join_halves(result_low, result_other), 1)
    kv_part = kv_finish(kv_back)
    query_sent, query_finish = scatter_start(
        lambda low, high: matmul_tn(rows_in[:, low:high], after(dq_low, kv_part)), features, 0
    )
    query_back = last_step(query_sent)
    kv_part_low = kv_part.astype(LOW)
    kv_arrived = [
        swap(block_for(kv_part_low, distance), "ctx", distance)
        for distance in far_first(groups)
        if distance
    ]
    query_grad = query_finish(query_back)
    out_grad = out_finish(after(out_back, da_half))
    back_one, back_two = lax.optimization_barrier((back_one, back_two, query_sent))[:2]
    gate_grad, up_grad, down_grad = finish_experts(parts_one + [back_one], parts_two + [back_two])
    kv_grad = block_for(kv_part, 0)
    for block in lax.optimization_barrier((*kv_arrived, gate_grad))[:-1]:
        kv_grad = kv_grad + block.astype(FULL)
    key_width = key_proj.shape[1]

    attn_mix_grad = tp_sum(
        jnp.concatenate(
            [jnp.sum(d_attended * picked, axis=1, keepdims=True) for picked in attn_picked], axis=1
        )
    )
    attn_d_logits = logits_back(attn_mix, attn_mix_grad, attn_probs, attn_onehot, share_grad[0])
    a_half = my_half(a_mine)
    attn_router_part = precise_tn(a_half.astype(FULL), attn_d_logits)

    d_normed1 = da_half + through_router(attn_d_logits, router1_half)
    gain1_half = my_half(gain1)
    weighted1 = d_normed1 * gain1_half
    inner1 = tp_sum(jnp.sum(weighted1 * input_half, axis=1, keepdims=True)) / features
    input_grad = d_attended + scale_one * weighted1 - input_half * scale_one**3 * inner1
    input_grad_low = input_grad.astype(LOW)
    input_grad_other = after(swap(input_grad_low, "tp", 1), gate_grad)
    input_grad = from_spread(join_halves(input_grad_low, input_grad_other), 1).astype(FULL)
    gain1_part = jnp.sum(d_normed1 * input_half * scale_one, axis=0)

    small = jnp.concatenate(
        [gain1_part[None], gain2_part[None], attn_router_part.T, ffn_router_part.T], axis=0
    )
    small = from_spread(join_halves(small, swap(small, "tp", 1)), 1)
    prob_sums = jnp.concatenate([jnp.sum(attn_probs, axis=0), jnp.sum(ffn_probs, axis=0)])
    small = jnp.concatenate([small, jnp.pad(prob_sums, (0, features - prob_sums.shape[0]))[None]], axis=0)
    small = after(all_sum(small, ("fsdp",)), query_back, gate_grad)
    small = all_sum(small, ("ctx",))
    prob_sums = small[-1, : 2 * expert_count].reshape(2, expert_count)
    losses = expert_count * jnp.sum(share * prob_sums / all_tokens, axis=1)
    return (
        output,
        input_grad,
        losses[0],
        losses[1],
        small[0],
        small[1],
        small[2 : 2 + expert_count].T,
        small[2 + expert_count : 2 + 2 * expert_count].T,
        kv_grad[:, :key_width],
        kv_grad[:, key_width:],
        query_grad[None],
        out_grad[None],
        gate_grad[None],
        up_grad[None],
        down_grad[None],
    )


def solution(mesh):
    by_token = P(("fsdp", "ctx"), None)
    by_row = P(("fsdp", "ctx"), "tp")
    inward = P("ctx", "fsdp", "tp")
    outward = P("ctx", "tp", "fsdp")
    weights = (by_row, by_row, inward, outward, inward, inward, outward)
    return jax.shard_map(
        on_device,
        mesh=mesh,
        in_specs=(by_token,) * 4 + (P(),) * 4 + weights,
        out_specs=(by_token,) * 2 + (P(),) * 6 + weights,
        check_vma=False,
    )
```
